32 devices in a mesh: dp: 4 (over x, core), fsdp: 8 (over z, y).
Axes of the slice: x: 2, y: 2, z: 4, core: 2. Of those that a mesh axis runs over, the one named last changes fastest.
Arguments:
- token_ids: int32 [64, 512], P(('dp', 'fsdp')), may hold values from 0 to 30521
- lengths: int32 [64], P(('dp', 'fsdp')), may hold values from 128 to 512
- pair_ids: int32 [3, 24], replicated, may hold values from 0 to 63
- scores: float32 [2, 24], replicated, may hold values from -0.5 to 1
- word_table: float32 [30720, 768], P('fsdp'), may hold values from -0.21875 to 0.21875
- pos_table: float32 [512, 768], P('fsdp'), may hold values from -0.21875 to 0.21875
- qkv_weight: float32 [768, 2304], P('fsdp'), may hold values from -0.21875 to 0.21875
- out_weight: float32 [768, 768], P('fsdp'), may hold values from -1.75 to 1.75
- up_weight: float32 [768, 3072], P('fsdp'), may hold values from -0.21875 to 0.21875
- down_weight: float32 [3072, 768], P('fsdp'), may hold values from -0.21875 to 0.21875
- small_params: float32 [14, 768], P(None, 'fsdp')
- word_moment: float32 [30720, 768], P('fsdp'), may hold values from -1.5258789e-05 to 1.5258789e-05
- pos_moment: float32 [512, 768], P('fsdp'), may hold values from -0.00015258789 to 0.00015258789
- qkv_moment: float32 [768, 2304], P('fsdp'), may hold values from -0.00015258789 to 0.00015258789
- out_moment: float32 [768, 768], P('fsdp'), may hold values from -0.00015258789 to 0.00015258789
- up_moment: float32 [768, 3072], P('fsdp'), may hold values from -0.00015258789 to 0.00015258789
- down_moment: float32 [3072, 768], P('fsdp'), may hold values from -0.00015258789 to 0.00015258789
- small_moment: float32 [14, 768], P(None, 'fsdp'), may hold values from -0.0004272461 to 0.0004272461
- word_average: float32 [30720, 768], P('fsdp'), may hold values from -0.21875 to 0.21875
- pos_average: float32 [512, 768], P('fsdp'), may hold values from -0.21875 to 0.21875
- qkv_average: float32 [768, 2304], P('fsdp'), may hold values from -0.21875 to 0.21875
- out_average: float32 [768, 768], P('fsdp'), may hold values from -1.75 to 1.75
- up_average: float32 [768, 3072], P('fsdp'), may hold values from -0.21875 to 0.21875
- down_average: float32 [3072, 768], P('fsdp'), may hold values from -0.21875 to 0.21875
- small_average: float32 [14, 768], P(None, 'fsdp'), may hold values from 0.5 to 1.5
Outputs:
- loss_sum: float32 [], replicated
- grad_norm: float32 [], replicated
- new_word_table: float32 [30720, 768], P('fsdp')
- new_pos_table: float32 [512, 768], P('fsdp')
- new_qkv_weight: float32 [768, 2304], P('fsdp')
- new_out_weight: float32 [768, 768], P('fsdp')
- new_up_weight: float32 [768, 3072], P('fsdp')
- new_down_weight: float32 [3072, 768], P('fsdp')
- new_small_params: float32 [14, 768], P(None, 'fsdp')
- new_word_moment: float32 [30720, 768], P('fsdp')
- new_pos_moment: float32 [512, 768], P('fsdp')
- new_qkv_moment: float32 [768, 2304], P('fsdp')
- new_out_moment: float32 [768, 768], P('fsdp')
- new_up_moment: float32 [768, 3072], P('fsdp')
- new_down_moment: float32 [3072, 768], P('fsdp')
- new_small_moment: float32 [14, 768], P(None, 'fsdp')
- new_word_average: float32 [30720, 768], P('fsdp')
- new_pos_average: float32 [512, 768], P('fsdp')
- new_qkv_average: float32 [768, 2304], P('fsdp')
- new_out_average: float32 [768, 768], P('fsdp')
- new_up_average: float32 [768, 3072], P('fsdp')
- new_down_average: float32 [3072, 768], P('fsdp')
- new_small_average: float32 [14, 768], P(None, 'fsdp')
The draws below stay inside these ranges and needn't reach their ends.
All inputs are finite; a program needn't handle non-finite values.
Results may differ from the reference program's by a relative error of at most 0.013.
The reference program's roundings to bfloat16 on the way count: a program that leaves them out, or rounds other values in their place, can miss the bound.
Values may be sent and summed in bfloat16 or wider, within the bound.
A program may use at most 576 MiB of HBM per device.

```python
import math
import jax
import jax.numpy as jnp
from jax import lax

D = 768
H = 12
FF = 3072
VOCAB = 30720
LEN = 512
SENTENCES = 64
ANCH = 24


def draw_small_params(key, part):
    gain_key, bias_key = jax.random.split(jax.random.fold_in(key, 11))
    ramp = 0.6 + 1.2 * jnp.arange(D, dtype=jnp.float32) / D
    spread = 0.12 * jax.random.normal(gain_key, (14, D), jnp.float32)
    shift = 0.1 * jax.random.normal(bias_key, (14, D), jnp.float32)
    rows = jnp.arange(14)
    is_gain = (rows == 0) | (rows == 5) | (rows == 12)
    return jnp.where(is_gain[:, None], ramp[None, :] * (1.0 + spread), shift).astype(jnp.float32)


def set_ends(values, rng, smallest, top_value):
    longest = values.shape.index(max(values.shape))
    spots = []
    for shift in (0, 1):
        where = [jax.random.randint(jax.random.fold_in(rng, axis), (), 0, length) for axis, length in enumerate(values.shape)]
        where[longest] = (where[longest] + shift) % values.shape[longest]
        spots.append(tuple(where))
    return values.at[spots[0]].set(smallest).at[spots[1]].set(top_value)


def block_levels(stream_key, extent, pieces, smallest, high):
    def one(axis_at, parts):
        steps = jax.random.uniform(jax.random.fold_in(jax.random.fold_in(stream_key, 6), axis_at), (parts,), jnp.float32, smallest / len(pieces), high / len(pieces))
        return jnp.repeat(jnp.exp(steps), extent[axis_at] // parts).reshape((-1,) + (1,) * (len(extent) - axis_at - 1))

    factor_of = one(*pieces[0])
    for cut in pieces[1:]:
        factor_of = factor_of * one(*cut)
    return factor_of


def noise(stream_key, shape, scale, most, shards=(), held_as=jnp.bfloat16):
    loudness = block_levels(stream_key, shape, shards, -0.22, 0.18) if shards else 1.0
    values = jax.random.normal(stream_key, shape, jnp.float32) * scale * loudness
    return jnp.minimum(jnp.maximum(values, -most), most).astype(held_as)


def setup_inputs(seed: int = 0) -> dict:
    key_of = jax.random.split(jax.random.key(seed), 26)
    return {
        "token_ids": set_ends(jax.random.randint(key_of[0], (SENTENCES, LEN), 0, min(VOCAB, 30522)), jax.random.fold_in(key_of[0], 1), 0, (min(VOCAB, 30522)) - 1).astype(jnp.int32),
        "lengths": set_ends(jax.random.randint(key_of[1], (SENTENCES,), LEN // 4, LEN + 1), jax.random.fold_in(key_of[1], 1), LEN // 4, LEN).astype(jnp.int32),
        "pair_ids": set_ends(jax.random.randint(key_of[2], (3, ANCH), 0, SENTENCES), jax.random.fold_in(key_of[2], 1), 0, SENTENCES - 1).astype(jnp.int32),
        "scores": jnp.clip(jax.random.uniform(key_of[3], (2, ANCH), jnp.float32, -0.5, 1.0), -0.5, 1.0),
        "word_table": noise(key_of[4], (VOCAB, D), D ** -0.5, 0.21875, ((0, 8),), jnp.float32),
        "pos_table": noise(key_of[5], (LEN, D), D ** -0.5, 0.21875, ((0, 8),), jnp.float32),
        "qkv_weight": noise(key_of[6], (D, 3 * D), D ** -0.5, 0.21875, ((0, 8),), jnp.float32),
        "out_weight": noise(key_of[7], (D, D), (D // 64) ** -0.5, 1.75, ((0, 8),), jnp.float32),
        "up_weight": noise(key_of[8], (D, FF), D ** -0.5, 0.21875, ((0, 8),), jnp.float32),
        "down_weight": noise(key_of[9], (FF, D), (FF // 4) ** -0.5, 0.21875, ((0, 8),), jnp.float32),
        "small_params": draw_small_params(jax.random.fold_in(key_of[25], 71), 0),
        "word_moment": noise(key_of[11], (VOCAB, D), 0.000001, 1.52587890625e-05, ((0, 8),), jnp.float32),
        "pos_moment": noise(key_of[12], (LEN, D), 0.00001, 0.00015258789, ((0, 8),), jnp.float32),
        "qkv_moment": noise(key_of[13], (D, 3 * D), 0.00001, 0.00015258789, ((0, 8),), jnp.float32),
        "out_moment": noise(key_of[14], (D, D), 0.00001, 0.00015258789, ((0, 8),), jnp.float32),
        "up_moment": noise(key_of[15], (D, FF), 0.00001, 0.00015258789, ((0, 8),), jnp.float32),
        "down_moment": noise(key_of[16], (FF, D), 0.00001, 0.00015258789, ((0, 8),), jnp.float32),
        "small_moment": noise(key_of[17], (14, D), 0.00003, 0.0004272461, ((1, 8),), jnp.float32),
        "word_average": noise(key_of[18], (VOCAB, D), D ** -0.5, 0.21875, ((0, 8),), jnp.float32),
        "pos_average": noise(key_of[19], (LEN, D), D ** -0.5, 0.21875, ((0, 8),), jnp.float32),
        "qkv_average": noise(key_of[20], (D, 3 * D), D ** -0.5, 0.21875, ((0, 8),), jnp.float32),
        "out_average": noise(key_of[21], (D, D), (D // 64) ** -0.5, 1.75, ((0, 8),), jnp.float32),
        "up_average": noise(key_of[22], (D, FF), D ** -0.5, 0.21875, ((0, 8),), jnp.float32),
        "down_average": noise(key_of[23], (FF, D), (FF // 4) ** -0.5, 0.21875, ((0, 8),), jnp.float32),
        "small_average": jnp.clip(1.0 + 0.1 * jax.random.normal(key_of[24], (14, D), jnp.float32), 0.5, 1.5),
    }


@jax.custom_vjp
def low(v):
    return lax.optimization_barrier(v.astype(jnp.bfloat16)).astype(jnp.float32)

@jax.custom_vjp
def low_back(v):
    return v

def low_keep(v):
    return (low(v), None)

def low_pass(kept, grad):
    return (grad,)

def back_keep(v):
    return (v, None)

def back_low(kept, grad):
    return (low(grad),)
low.defvjp(low_keep, low_pass)
low_back.defvjp(back_keep, back_low)
HIGH = lax.Precision.HIGHEST
MOMENTUM = 0.9
RATE = 3000.0
KEEP = 0.9

def layer_norm(v, gain, shift):
    mean = lax.optimization_barrier(jnp.mean(v, -1, keepdims=True))
    cent = v - mean
    var = lax.optimization_barrier(jnp.mean(cent * cent, -1, keepdims=True))
    return cent * lax.rsqrt(var + 1e-12) * gain + shift

def sentence_pooled(ids, length, weights):
    word, pos, qkv_w, out_w, up_w, down_w, small = weights
    seq = ids.shape[0]
    size = D // H
    x = word[ids] + pos
    h0 = layer_norm(x, small[0], small[1])
    qkv_bias = jnp.concatenate([small[2], jnp.zeros_like(small[2]), small[3]])
    qkv = low_back(jnp.dot(low(h0), qkv_w, precision=HIGH)) + qkv_bias
    heads = low(qkv).reshape(seq, 3, H, size)
    query, keys, values = (heads[:, 0], heads[:, 1], heads[:, 2])
    live = jnp.arange(seq) < length
    raw = jnp.einsum('qhd,khd->hqk', query, keys, precision=HIGH) * size ** (-0.5)
    logits = low_back(raw) + jnp.where(live, 0.0, -1000000000.0)[None, None, :]
    probs = jax.nn.softmax(logits, -1)
    mixed = low(low_back(jnp.einsum('hqk,khd->qhd', low(probs), values, precision=HIGH))).reshape(seq, D)
    att = low_back(jnp.dot(mixed, out_w, precision=HIGH)) + small[4]
    h1 = layer_norm(h0 + att, small[5], small[6])
    up = low_back(jnp.dot(low(h1), up_w, precision=HIGH)) + small[7:11].reshape(-1)
    act = low(jax.nn.gelu(up, approximate=False))
    ffn = low_back(jnp.dot(act, down_w, precision=HIGH)) + small[11]
    h2 = layer_norm(h1 + ffn, small[12], small[13])
    weight = live.astype(h2.dtype)
    return lax.optimization_barrier(jnp.sum(h2 * weight[:, None], 0)) / length.astype(h2.dtype)

def cosine(first, second):
    dots = lax.optimization_barrier(jnp.sum(first * second, -1))
    return dots * lax.rsqrt(lax.optimization_barrier(jnp.sum(first * first, -1)) + 1e-06) * lax.rsqrt(lax.optimization_barrier(jnp.sum(second * second, -1)) + 1e-06)

def pair_loss(pooled, pair_ids, scores):
    anchors = pooled[pair_ids[0]]
    near = cosine(anchors, pooled[pair_ids[1]]) - scores[0]
    far = cosine(anchors, pooled[pair_ids[2]]) - scores[1]
    return jnp.sum(near * near) + jnp.sum(far * far)

def reference(token_ids, lengths, pair_ids, scores, word_table, pos_table, qkv_weight, out_weight, up_weight, down_weight, small_params, word_moment, pos_moment, qkv_moment, out_moment, up_moment, down_moment, small_moment, word_average, pos_average, qkv_average, out_average, up_average, down_average, small_average):
    weights = (word_table, pos_table, qkv_weight, out_weight, up_weight, down_weight, small_params)
    moments = (word_moment, pos_moment, qkv_moment, out_moment, up_moment, down_moment, small_moment)
    averages = (word_average, pos_average, qkv_average, out_average, up_average, down_average, small_average)
    groups = token_ids.reshape(-1, 8, LEN)
    group_lens = lengths.reshape(-1, 8)

    def loss_fn(params):
        lowered = tuple((low(w) for w in params))

        def group(carry, item):
            ids, lens = item
            return (carry, jax.vmap(sentence_pooled, (0, 0, None))(ids, lens, lowered))
        _, pooled = lax.scan(jax.checkpoint(group), jnp.zeros((), jnp.float32), (groups, group_lens))
        return pair_loss(pooled.reshape(-1, D), pair_ids, scores)
    loss, pullback = jax.vjp(loss_fn, weights)
    grads = pullback(jnp.ones_like(loss))[0]
    total = jnp.zeros((), jnp.float32)
    for grad in grads:
        total = total + jnp.sum(grad * grad)
    norm = jnp.sqrt(total)
    limit = 1e-05 * math.sqrt((VOCAB + LEN + 4 * D + 2 * FF + 14) * D)
    factor = jnp.minimum(1.0, limit / (norm + 1e-06))
    new_w = []
    new_m = []
    new_a = []
    for weight, moment, average, grad in zip(weights, moments, averages, grads):
        step = factor * grad
        buffer = MOMENTUM * moment + step
        fresh = weight - RATE * (step + MOMENTUM * buffer)
        new_w.append(fresh)
        new_m.append(buffer)
        new_a.append(KEEP * average + (1.0 - KEEP) * fresh)
    return (loss, norm, new_w[0], new_w[1], new_w[2], new_w[3], new_w[4], new_w[5], new_w[6], new_m[0], new_m[1], new_m[2], new_m[3], new_m[4], new_m[5], new_m[6], new_a[0], new_a[1], new_a[2], new_a[3], new_a[4], new_a[5], new_a[6])
```

```python
import functools
import math

import jax
import jax.numpy as jnp
from jax import lax
from jax.experimental import pallas as pl
from jax.experimental.pallas import tpu as pltpu
from jax.sharding import PartitionSpec as P

D = 768
H = 12
FF = 3072
VOCAB = 30720
LEN = 512


MOMENTUM = 0.9
RATE = 3000.0
KEEP = 0.9


def layer_norm(v, gain, shift):
    mean = jnp.mean(v, -1, keepdims=True)
    cent = v - mean
    var = jnp.mean(cent * cent, -1, keepdims=True)
    return cent * lax.rsqrt(var + 1e-12) * gain + shift


def gelu_exact(v):
    return jax.nn.gelu(v, approximate=False)


def matmul(left, right):
    return jnp.dot(left, right, preferred_element_type=jnp.float32)


def outer_sum(left, right):
    return lax.dot_general(
        left, right, (((0,), (0,)), ((), ())), preferred_element_type=jnp.float32
    )


def back_mul(grad, weight):
    return lax.dot_general(
        grad, weight, (((1,), (1,)), ((), ())), preferred_element_type=jnp.float32
    )


def cosine(first, second):
    dots = jnp.sum(first * second, -1)
    return (
        dots
        * lax.rsqrt(jnp.sum(first * first, -1) + 1e-06)
        * lax.rsqrt(jnp.sum(second * second, -1) + 1e-06)
    )


def pair_loss(pooled, pair_ids, scores):
    anchors = pooled[pair_ids[0]]
    near = cosine(anchors, pooled[pair_ids[1]]) - scores[0]
    far = cosine(anchors, pooled[pair_ids[2]]) - scores[1]
    return jnp.sum(near * near) + jnp.sum(far * far)


MESH = pl.DeviceIdType.MESH


def gather_kernel(sizes, whole, src, out, send, recv, local):
    dp, fsdp = sizes
    count = dp * fsdp if whole else fsdp
    row, col = lax.axis_index("dp"), lax.axis_index("fsdp")
    me = row * fsdp + col if whole else col

    def target(step):
        other = lax.rem(me + step, count)
        return (other // fsdp, lax.rem(other, fsdp)) if whole else (row, other)

    barrier = pltpu.get_barrier_semaphore()

    def greet(step, carry):
        pl.semaphore_signal(barrier, inc=1, device_id=target(step), device_id_type=MESH)
        return carry

    lax.fori_loop(1, count, greet, 0)
    pl.semaphore_wait(barrier, count - 1)
    own = pltpu.make_async_copy(src, out.at[me], local)
    own.start()

    def copy(step):
        return pltpu.make_async_remote_copy(
            src_ref=src,
            dst_ref=out.at[me],
            send_sem=send.at[step],
            recv_sem=recv.at[step],
            device_id=target(step),
            device_id_type=MESH,
        )

    def begin(step, carry):
        copy(step).start()
        return carry

    def end(step, carry):
        copy(step).wait()
        return carry

    lax.fori_loop(1, count, begin, 0)
    lax.fori_loop(1, count, end, 0)
    own.wait()


def gather_small(value, whole, collective):
    dp, fsdp = lax.axis_size("dp"), lax.axis_size("fsdp")
    count = dp * fsdp if whole else fsdp
    return pl.pallas_call(
        functools.partial(gather_kernel, (dp, fsdp), whole),
        out_shape=jax.ShapeDtypeStruct((count,) + value.shape, value.dtype),
        in_specs=[pl.BlockSpec(memory_space=pltpu.VMEM)],
        out_specs=pl.BlockSpec(memory_space=pltpu.VMEM),
        scratch_shapes=[
            pltpu.SemaphoreType.DMA((count,)),
            pltpu.SemaphoreType.DMA((count,)),
            pltpu.SemaphoreType.DMA,
        ],
        compiler_params=pltpu.CompilerParams(collective_id=collective, has_side_effects=True),
    )(value)


LOOP = {8: (0, 2, 4, 6, 7, 5, 3, 1)}


def swap_core(value):
    return lax.ppermute(value, "dp", [(i, i ^ 1) for i in range(lax.axis_size("dp"))])


def swap_x(value):
    count = lax.axis_size("dp")
    return lax.ppermute(value, "dp", [(i, (i + 2) % count) for i in range(count)])


def sum_x(value):
    count = lax.axis_size("dp")
    total = value
    for hop in range(2, count, 2):
        moved = lax.ppermute(value, "dp", [(i, (i + hop) % count) for i in range(count)])
        total = total.astype(jnp.float32) + moved.astype(jnp.float32)
    return total


def shift(value, step):
    loop = LOOP[lax.axis_size("fsdp")]
    size = len(loop)
    return lax.ppermute(
        value, "fsdp", [(loop[i], loop[(i + step) % size]) for i in range(size)]
    )


def loop_place():
    loop = LOOP[lax.axis_size("fsdp")]
    place = [0] * len(loop)
    for i, device in enumerate(loop):
        place[device] = i
    return jnp.array(place, jnp.int32)[lax.axis_index("fsdp")], jnp.array(loop, jnp.int32)


def ring_gather(part, sign):
    size = lax.axis_size("fsdp")
    place, loop = loop_place()
    out = jnp.zeros((size,) + part.shape, part.dtype)

    def put(out, block, offset):
        at = loop[lax.rem(place + offset + size, size)]
        return lax.dynamic_update_slice(out, block[None], (at, 0, 0))

    out = put(out, part, 0)
    ahead = behind = part
    for hop in range(1, size // 2 + 1):
        ahead = shift(ahead, sign)
        out = put(out, ahead, -sign * hop)
        if hop < size - size // 2:
            behind = shift(behind, -sign)
            out = put(out, behind, sign * hop)
    return out


def ring_reduce(parts, sign):
    size = lax.axis_size("fsdp")
    place, loop = loop_place()

    def local(offset):
        at = loop[lax.rem(place + offset + size, size)]
        return lax.dynamic_index_in_dim(parts, at, 0, keepdims=False).astype(jnp.float32)

    def flow(direction, hops):
        arrived = None
        for hop in range(hops):
            value = local(direction * (hops - hop))
            if arrived is not None:
                value = value + arrived.astype(jnp.float32)
            arrived = shift(value.astype(jnp.bfloat16), direction)
        return arrived

    far = flow(sign, size // 2)
    near = flow(-sign, size - size // 2 - 1)
    return local(0) + far.astype(jnp.float32) + near.astype(jnp.float32)


def gather_halves(first, second, sign):
    core = lax.rem(lax.axis_index("dp"), 2)
    if lax.axis_size("fsdp") not in LOOP:
        return lax.all_gather(first, "fsdp", axis=0), lax.all_gather(second, "fsdp", axis=0)
    mine = ring_gather(jnp.where(core == 0, first, second), sign)
    other = swap_core(mine)
    return jnp.where(core == 0, mine, other), jnp.where(core == 0, other, mine)


def reduce_halves(first, second, sign):
    core = lax.rem(lax.axis_index("dp"), 2)
    give = jnp.where(core == 0, second, first).astype(jnp.bfloat16)
    keep = jnp.where(core == 0, first, second).astype(jnp.float32)
    chip = (keep + swap_core(give).astype(jnp.float32)).astype(jnp.bfloat16)
    if lax.axis_size("fsdp") in LOOP:
        block = ring_reduce(chip, sign)
    else:
        block = lax.psum_scatter(chip.astype(jnp.float32), "fsdp", scatter_dimension=0)
    total = sum_x(block.astype(jnp.bfloat16)).astype(jnp.bfloat16)
    other = swap_core(total)
    low = jnp.where(core == 0, total, other).astype(jnp.float32)
    high = jnp.where(core == 0, other, total).astype(jnp.float32)
    return low, high


def split_rows(weight, parts):
    return jnp.concatenate(jnp.split(weight, parts, axis=1), axis=0)


def join_rows(blocks, parts):
    count, rows, width = blocks.shape
    return (
        blocks.reshape(count, parts, rows // parts, width)
        .transpose(0, 2, 1, 3)
        .reshape(count * rows // parts, parts * width)
    )


def cut_rows(grad, count, parts):
    rows, width = grad.shape[0] // count, grad.shape[1] // parts
    return (
        grad.reshape(count, rows, parts, width)
        .transpose(0, 2, 1, 3)
        .reshape(count, parts * rows, width)
    )


def pad_rows(value, rows):
    return jnp.pad(value, [(0, 0)] * (value.ndim - 2) + [(0, rows - value.shape[-2]), (0, 0)])


def round_up(value, step):
    return -(-value // step) * step


def bucket_size(tokens, owners):
    mean = tokens / owners
    return min(tokens, round_up(int(mean + 5.6 * math.sqrt(mean)), 16))


def one_hot(index, count):
    return (index[:, None] == lax.iota(jnp.int32, count)[None, :]).astype(jnp.bfloat16)


class Routes:
    def __init__(self, everyone, own_rows):
        fsdp = lax.axis_size("fsdp")
        self.rows = own_rows
        tokens = everyone.shape[1]
        self.cap = bucket_size(tokens, fsdp)
        me = lax.axis_index("fsdp")
        group = lax.dynamic_slice_in_dim(everyone, lax.axis_index("dp") * fsdp, fsdp, 0)
        mine = lax.dynamic_index_in_dim(group, me, 0, keepdims=False)
        owners = lax.iota(jnp.int32, fsdp)
        every_count = jnp.sum(
            (everyone // own_rows)[:, :, None] == owners[None, None, :], 1, dtype=jnp.int32
        )
        self.rounds = (jnp.max(every_count) + self.cap - 1) // self.cap
        self.inner = group - me * own_rows
        self.held = (self.inner >= 0) & (self.inner < own_rows)
        self.held_place = jnp.cumsum(self.held.astype(jnp.int32), 1) - 1
        self.owner = mine // own_rows
        hot = (self.owner[None, :] == owners[:, None])
        place = jnp.cumsum(hot.astype(jnp.int32), 1) - 1
        self.hot = hot
        self.place = place
        self.my_place = jnp.sum(jnp.where(hot, place, 0), 0)

    def slots(self, flag, place, value, turn):
        slot = lax.iota(jnp.int32, self.cap)[None, :, None] + turn * self.cap
        hit = flag[:, None, :] & (place[:, None, :] == slot)
        return (jnp.sum(jnp.where(hit, value[:, None, :] + 1, 0), -1) - 1).reshape(-1)

    def owner_rows(self, turn):
        return self.slots(self.held, self.held_place, self.inner, turn)

    def asker_tokens(self, turn):
        tokens = lax.iota(jnp.int32, self.owner.shape[0])[None, :]
        return self.slots(self.hot, self.place, tokens, turn)

    def asker_slots(self, turn):
        place = self.my_place - turn * self.cap
        inside = (place >= 0) & (place < self.cap)
        return jnp.where(inside, self.owner * self.cap + place, -1)


def exchange(rows):
    fsdp = lax.axis_size("fsdp")
    blocks = rows.reshape(fsdp, rows.shape[0] // fsdp, rows.shape[1])
    return lax.all_to_all(blocks, "fsdp", 0, 0).reshape(rows.shape)


def fetch_round(table_low, routes, turn):
    sent = matmul(one_hot(routes.owner_rows(turn), routes.rows), table_low).astype(jnp.bfloat16)
    got = exchange(sent)
    return matmul(one_hot(routes.asker_slots(turn), got.shape[0]), got)


def fetch_rows(table_low, routes):
    first = fetch_round(table_low, routes, 0)

    def more(carry):
        return carry[0] < routes.rounds

    def body(carry):
        turn, words = carry
        return turn + 1, words + fetch_round(table_low, routes, turn)

    return lax.while_loop(more, body, (jnp.int32(1), first))[1]


def return_round(grad_low, routes, turn):
    tokens = grad_low.shape[0]
    sent = matmul(one_hot(routes.asker_tokens(turn), tokens), grad_low).astype(jnp.bfloat16)
    got = exchange(sent)
    return outer_sum(one_hot(routes.owner_rows(turn), routes.rows), got)


def return_rows(grad_low, routes):
    first = return_round(grad_low, routes, 0)

    def more(carry):
        return carry[0] < routes.rounds

    def body(carry):
        turn, total = carry
        return turn + 1, total + return_round(grad_low, routes, turn)

    return lax.while_loop(more, body, (jnp.int32(1), first))[1]


def sum_groups(table):
    core = lax.rem(lax.axis_index("dp"), 2)
    half = table.shape[0] // 2
    low = table.astype(jnp.bfloat16)
    keep = lax.dynamic_slice_in_dim(table, core * half, half, 0)
    give = lax.dynamic_slice_in_dim(low, (1 - core) * half, half, 0)
    chip = (keep + swap_core(give).astype(jnp.float32)).astype(jnp.bfloat16)
    total = sum_x(chip).astype(jnp.bfloat16)
    other = swap_core(total)
    return jnp.concatenate(
        [jnp.where(core == 0, total, other), jnp.where(core == 0, other, total)], 0
    ).astype(jnp.float32)


def attention_logits(query, keys, live_bias, scale):
    raw = jnp.einsum("bqhd,bkhd->bhqk", query, keys, preferred_element_type=jnp.float32) * scale
    return raw + live_bias[:, None, None, :]


def layer_forward(x, params, live_bias, batch, seq):
    qkv_w, out_w, up_w, down_w, small = params
    width = x.shape[1]
    size = width // H
    scale = size ** (-0.5)
    h0 = layer_norm(x, small[0], small[1])
    qkv_bias = jnp.concatenate([small[2], jnp.zeros_like(small[2]), small[3]])
    qkv = matmul(h0.astype(jnp.bfloat16), qkv_w) + qkv_bias
    parts = qkv.astype(jnp.bfloat16).reshape(batch, seq, 3, H, size)
    query, keys, values = (parts[:, :, 0], parts[:, :, 1], parts[:, :, 2])
    logits = attention_logits(query, keys, live_bias, scale)
    top = jnp.max(logits, -1, keepdims=True)
    total_log = top + jnp.log(jnp.sum(jnp.exp(logits - top), -1, keepdims=True))
    probs = jnp.exp(logits - total_log).astype(jnp.bfloat16)
    mixed = jnp.einsum("bhqk,bkhd->bqhd", probs, values, preferred_element_type=jnp.float32)
    mixed = mixed.astype(jnp.bfloat16).reshape(-1, width)
    first_sum = h0 + (matmul(mixed, out_w) + small[4])
    h1 = layer_norm(first_sum, small[5], small[6])
    up = matmul(h1.astype(jnp.bfloat16), up_w) + small[7:11].reshape(-1)
    act = gelu_exact(up).astype(jnp.bfloat16)
    second_sum = h1 + (matmul(act, down_w) + small[11])
    h2 = layer_norm(second_sum, small[12], small[13])
    kept = (x, h0, query, keys, values, total_log, mixed, first_sum, h1, up, act, second_sum)
    return (h2, kept)


def layer_backward(grad_h2, kept, params, live_bias):
    qkv_w, out_w, up_w, down_w, small = params
    x, h0, query, keys, values, total_log, mixed, first_sum, h1, up, act, second_sum = kept
    batch, seq, heads, size = query.shape
    width = heads * size
    scale = size ** (-0.5)
    _, pull_two = jax.vjp(layer_norm, second_sum, small[12], small[13])
    grad_r2, grad_g2, grad_b2 = pull_two(grad_h2)
    grad_ffn = grad_r2.astype(jnp.bfloat16)
    grad_down = outer_sum(act, grad_ffn)
    grad_act = back_mul(grad_ffn, down_w)
    _, pull_gelu = jax.vjp(gelu_exact, up)
    grad_up = pull_gelu(grad_act)[0]
    grad_upb = grad_up.astype(jnp.bfloat16)
    grad_upw = outer_sum(h1.astype(jnp.bfloat16), grad_upb)
    grad_h1 = grad_r2 + back_mul(grad_upb, up_w)
    _, pull_one = jax.vjp(layer_norm, first_sum, small[5], small[6])
    grad_r1, grad_g1, grad_b1 = pull_one(grad_h1)
    grad_att = grad_r1.astype(jnp.bfloat16)
    grad_outw = outer_sum(mixed, grad_att)
    grad_mixed = back_mul(grad_att, out_w).astype(jnp.bfloat16).reshape(batch, seq, heads, size)
    logits = attention_logits(query, keys, live_bias, scale)
    probs = jnp.exp(logits - total_log)
    grad_probs = jnp.einsum(
        "bqhd,bkhd->bhqk", grad_mixed, values, preferred_element_type=jnp.float32
    )
    grad_values = jnp.einsum(
        "bhqk,bqhd->bkhd",
        probs.astype(jnp.bfloat16),
        grad_mixed,
        preferred_element_type=jnp.float32,
    )
    inner = jnp.sum(probs * grad_probs, -1, keepdims=True)
    grad_logits = (probs * (grad_probs - inner)).astype(jnp.bfloat16)
    grad_query = (
        jnp.einsum("bhqk,bkhd->bqhd", grad_logits, keys, preferred_element_type=jnp.float32) * scale
    )
    grad_keys = (
        jnp.einsum("bhqk,bqhd->bkhd", grad_logits, query, preferred_element_type=jnp.float32)
        * scale
    )
    grad_qkv = jnp.stack([grad_query, grad_keys, grad_values], 2).reshape(-1, 3 * width)
    grad_qkvb = grad_qkv.astype(jnp.bfloat16)
    grad_qkvw = outer_sum(h0.astype(jnp.bfloat16), grad_qkvb)
    grad_h0 = grad_r1 + back_mul(grad_qkvb, qkv_w)
    _, pull_zero = jax.vjp(layer_norm, x, small[0], small[1])
    grad_x, grad_g0, grad_b0 = pull_zero(grad_h0)
    column_sums = jnp.sum(grad_qkv, 0)
    head_rows = jnp.stack(
        [
            grad_g0,
            grad_b0,
            column_sums[:width],
            column_sums[2 * width :],
            jnp.sum(grad_r1, 0),
            grad_g1,
            grad_b1,
        ]
    )
    tail_rows = jnp.stack([jnp.sum(grad_r2, 0), grad_g2, grad_b2])
    grad_small = jnp.concatenate([head_rows, jnp.sum(grad_up, 0).reshape(4, width), tail_rows], 0)
    return (grad_x, (grad_qkvw, grad_outw, grad_upw, grad_down, grad_small))


def renew(weight, moment, average, grad, factor):
    step = factor * grad
    buffer = MOMENTUM * moment + step
    fresh = weight - RATE * (step + MOMENTUM * buffer)
    return (fresh, buffer, KEEP * average + (1.0 - KEEP) * fresh)


def shards(
    token_ids,
    lengths,
    pair_ids,
    scores,
    word_table,
    pos_table,
    qkv_weight,
    out_weight,
    up_weight,
    down_weight,
    small_params,
    word_moment,
    pos_moment,
    qkv_moment,
    out_moment,
    up_moment,
    down_moment,
    small_moment,
    word_average,
    pos_average,
    qkv_average,
    out_average,
    up_average,
    down_average,
    small_average,
):
    batch, seq = token_ids.shape
    width = D
    fsdp = lax.axis_size("fsdp")
    me = lax.axis_index("fsdp")
    pos_low = pos_table.astype(jnp.bfloat16)
    qkv_low = split_rows(qkv_weight.astype(jnp.bfloat16), 3)
    out_low = out_weight.astype(jnp.bfloat16)
    up_low = split_rows(up_weight.astype(jnp.bfloat16), 4)
    down_low = down_weight.astype(jnp.bfloat16)
    small_low = small_params.astype(jnp.bfloat16)
    word_low = word_table.astype(jnp.bfloat16)
    tokens = batch * seq
    everyone = gather_small(token_ids.reshape(-1, 128), True, 0).reshape(-1, tokens)
    routes = Routes(everyone, word_table.shape[0])
    shard = qkv_weight.shape[0]
    pos_rows = pos_table.shape[0]
    small_cols = small_params.shape[1]
    small_block = jnp.pad(small_low, ((0, 2), (0, width - small_cols)))
    tail = round_up(max(2 * shard, shard + pos_rows + 16), 16)
    first_a = pad_rows(qkv_low[: 2 * shard], tail)
    first_b = pad_rows(jnp.concatenate([qkv_low[2 * shard :], pos_low, small_block], 0), tail)
    half = shard // 2
    second_a = jnp.concatenate([down_low, out_low[:half]], 0)
    second_b = jnp.concatenate([up_low, out_low[half:]], 0)
    got_a, got_b = gather_halves(first_a, first_b, 1)
    words = fetch_rows(word_low, routes)
    got_c, got_d = gather_halves(second_a, second_b, -1)
    qkv_full = join_rows(
        jnp.concatenate([got_a[:, : 2 * shard], got_b[:, :shard]], 1), 3
    )
    pos_full = got_b[:, shard : shard + pos_rows].reshape(-1, width)
    small_full = (
        got_b[:, shard + pos_rows : shard + pos_rows + 14, :small_cols]
        .transpose(1, 0, 2)
        .reshape(14, width)
    )
    down_rows = down_weight.shape[0]
    down_full = got_c[:, :down_rows].reshape(-1, width)
    up_full = join_rows(got_d[:, :down_rows], 4)
    out_full = jnp.concatenate([got_c[:, down_rows:], got_d[:, down_rows:]], 1).reshape(-1, width)
    params = (qkv_full, out_full, up_full, down_full, small_full.astype(jnp.float32))
    x = (words.reshape(batch, seq, width) + pos_full.astype(jnp.float32)[None]).reshape(
        -1, width
    )
    live = lax.iota(jnp.int32, seq)[None, :] < lengths[:, None]
    live_bias = jnp.where(live, 0.0, -1000000000.0).astype(jnp.float32)
    live_f = live.astype(jnp.float32)
    counts = lengths.astype(jnp.float32)
    h2, kept = layer_forward(x, params, live_bias, batch, seq)
    pooled = jnp.sum(h2.reshape(batch, seq, width) * live_f[:, :, None], 1) / counts[:, None]
    pooled_all = gather_small(pooled.reshape(-1, 128), True, 1).reshape(-1, width)
    loss, pull_loss = jax.vjp(lambda rows: pair_loss(rows, pair_ids, scores), pooled_all)
    grad_all = pull_loss(jnp.ones((), jnp.float32))[0]
    grad_pooled = lax.dynamic_slice_in_dim(
        grad_all, lax.axis_index(("dp", "fsdp")) * batch, batch, 0
    )
    grad_h2 = (live_f[:, :, None] * (grad_pooled / counts[:, None])[:, None, :]).reshape(-1, width)
    grad_x, layer_grads = layer_backward(grad_h2, kept, params, live_bias)
    grad_qkvw, grad_outw, grad_upw, grad_downw, grad_small = layer_grads
    sum_down, sum_up = reduce_halves(
        cut_rows(grad_downw, fsdp, 1), cut_rows(grad_upw, fsdp, 4), 1
    )
    grad_table = return_rows(grad_x.astype(jnp.bfloat16), routes)
    grad_pos = jnp.sum(grad_x.reshape(batch, seq, width), 0)
    qkv_cut = cut_rows(grad_qkvw, fsdp, 3)
    small_cut = jnp.pad(
        grad_small.reshape(14, fsdp, small_cols).transpose(1, 0, 2),
        ((0, 0), (0, 2), (0, width - small_cols)),
    )
    half_pos = pos_rows // 2
    pos_cut = grad_pos.reshape(fsdp, pos_rows, width)
    low_cut = jnp.concatenate([qkv_cut[:, : 2 * shard], pos_cut[:, :half_pos], small_cut], 1)
    high_cut = pad_rows(
        jnp.concatenate(
            [qkv_cut[:, 2 * shard :], cut_rows(grad_outw, fsdp, 1), pos_cut[:, half_pos:]], 1
        ),
        low_cut.shape[1],
    )
    sum_low, sum_high = reduce_halves(low_cut, high_cut, -1)
    sum_qkv = join_rows(
        jnp.concatenate([sum_low[: 2 * shard], sum_high[:shard]], 0)[None], 3
    )
    sum_out = sum_high[shard : 2 * shard]
    sum_pos = jnp.concatenate(
        [sum_low[2 * shard : 2 * shard + half_pos], sum_high[2 * shard : 2 * shard + half_pos]], 0
    )
    small_at = 2 * shard + half_pos
    sum_small = sum_low[small_at : small_at + 14, :small_cols]
    sum_upw = join_rows(sum_up[None], 4)
    summed = (
        sum_groups(grad_table),
        sum_pos,
        sum_qkv,
        sum_out,
        sum_upw,
        sum_down,
        sum_small,
    )
    local_squares = jnp.zeros((), jnp.float32)
    for grad in summed:
        local_squares = local_squares + jnp.sum(grad * grad)
    total = jnp.sum(gather_small(jnp.full((8, 128), local_squares), False, 2)[:, 0, 0])
    norm = jnp.sqrt(total)
    limit = 1e-05 * math.sqrt((VOCAB + LEN + 4 * D + 2 * FF + 14) * D)
    factor = jnp.minimum(1.0, limit / (norm + 1e-06))
    weights = (word_table, pos_table, qkv_weight, out_weight, up_weight, down_weight, small_params)
    moments = (
        word_moment,
        pos_moment,
        qkv_moment,
        out_moment,
        up_moment,
        down_moment,
        small_moment,
    )
    averages = (
        word_average,
        pos_average,
        qkv_average,
        out_average,
        up_average,
        down_average,
        small_average,
    )
    new_w = []
    new_m = []
    new_a = []
    for weight, moment, average, grad in zip(weights, moments, averages, summed):
        fresh, buffer, mean_new = renew(weight, moment, average, grad, factor)
        new_w.append(fresh)
        new_m.append(buffer)
        new_a.append(mean_new)
    return (
        loss,
        norm,
        new_w[0],
        new_w[1],
        new_w[2],
        new_w[3],
        new_w[4],
        new_w[5],
        new_w[6],
        new_m[0],
        new_m[1],
        new_m[2],
        new_m[3],
        new_m[4],
        new_m[5],
        new_m[6],
        new_a[0],
        new_a[1],
        new_a[2],
        new_a[3],
        new_a[4],
        new_a[5],
        new_a[6],
    )


def solution(mesh):
    placed = (
        P(("dp", "fsdp"), None),
        P(("dp", "fsdp")),
        P(),
        P(),
        P("fsdp", None),
        P("fsdp", None),
        P("fsdp", None),
        P("fsdp", None),
        P("fsdp", None),
        P("fsdp", None),
        P(None, "fsdp"),
        P("fsdp", None),
        P("fsdp", None),
        P("fsdp", None),
        P("fsdp", None),
        P("fsdp", None),
        P("fsdp", None),
        P(None, "fsdp"),
        P("fsdp", None),
        P("fsdp", None),
        P("fsdp", None),
        P("fsdp", None),
        P("fsdp", None),
        P("fsdp", None),
        P(None, "fsdp"),
    )
    return jax.shard_map(
        shards,
        mesh=mesh,
        in_specs=placed,
        out_specs=(
            P(),
            P(),
            P("fsdp", None),
            P("fsdp", None),
            P("fsdp", None),
            P("fsdp", None),
            P("fsdp", None),
            P("fsdp", None),
            P(None, "fsdp"),
            P("fsdp", None),
            P("fsdp", None),
            P("fsdp", None),
            P("fsdp", None),
            P("fsdp", None),
            P("fsdp", None),
            P(None, "fsdp"),
            P("fsdp", None),
            P("fsdp", None),
            P("fsdp", None),
            P("fsdp", None),
            P("fsdp", None),
            P("fsdp", None),
            P(None, "fsdp"),
        ),
        check_vma=False,
    )
```

```python
import functools
import math

import jax
import jax.numpy as jnp
from jax import lax
from jax.experimental import pallas as pl
from jax.experimental.pallas import tpu as pltpu
from jax.sharding import PartitionSpec as P

D = 768
H = 12
FF = 3072
VOCAB = 30720
LEN = 512


MOMENTUM = 0.9
RATE = 3000.0
KEEP = 0.9


def matmul(left, right):
    return jnp.dot(left, right, preferred_element_type=jnp.float32)


def outer_sum(left, right):
    return lax.dot_general(
        left, right, (((0,), (0,)), ((), ())), preferred_element_type=jnp.float32
    )


def back_mul(grad, weight):
    return lax.dot_general(
        grad, weight, (((1,), (1,)), ((), ())), preferred_element_type=jnp.float32
    )


TILE = 256
EPS = 1e-12
VMEM_GRANT = 60 * 1024 * 1024


def whole_spec(shape):
    return pl.BlockSpec(shape, lambda *_: (0,) * len(shape))


def rows_spec(width, rows=TILE):
    return pl.BlockSpec((rows, width), lambda i, *_: (i, 0))


def weight_spec(rows, at):
    return pl.BlockSpec((rows, D), lambda i, *_: (at, 0))


def call(kernel, name, grid, in_specs, out_specs, out_shape, scratch=(), prefetch=0, flops=0, moved=0):
    return pl.pallas_call(
        kernel,
        name=name,
        grid_spec=pltpu.PrefetchScalarGridSpec(
            num_scalar_prefetch=prefetch,
            grid=grid,
            in_specs=in_specs,
            out_specs=out_specs,
            scratch_shapes=scratch,
        ),
        out_shape=out_shape,
        compiler_params=pltpu.CompilerParams(vmem_limit_bytes=VMEM_GRANT),
        cost_estimate=pl.CostEstimate(flops=flops, bytes_accessed=moved, transcendentals=0),
    )


def normed(v):
    mean = jnp.mean(v, -1, keepdims=True)
    cent = v - mean
    scale = lax.rsqrt(jnp.mean(cent * cent, -1, keepdims=True) + EPS)
    return cent * scale, scale


def norm_back(grad, hat, scale, gain):
    inner = grad * gain
    middle = jnp.mean(inner, -1, keepdims=True)
    along = jnp.mean(inner * hat, -1, keepdims=True)
    return (
        scale * (inner - middle - hat * along),
        jnp.sum(grad * hat, 0, keepdims=True),
        jnp.sum(grad, 0, keepdims=True),
    )


def add_row(ref, row, value):
    ref[row : row + 1, :] += value


def embed_kernel(slot, got, extra, pos, weight, small, x_out, h0_out, qkv_out):
    count = got.shape[0]
    pick = (slot[:, 0:1] == lax.broadcasted_iota(jnp.int32, (slot.shape[0], count), 1)).astype(
        jnp.bfloat16
    )
    words = matmul(pick, got[...]) + extra[...].astype(jnp.float32)
    x = words + pos[...].astype(jnp.float32)
    hat, _ = normed(x)
    h0 = hat * small[0:1, :] + small[1:2, :]
    x_out[...] = x
    h0_out[...] = h0
    low = h0.astype(jnp.bfloat16)
    for third, bias in enumerate((2, None, 3)):
        value = matmul(low, weight[third * D : (third + 1) * D, :])
        if bias is not None:
            value = value + small[bias : bias + 1, :]
        qkv_out[:, third * D : (third + 1) * D] = value.astype(jnp.bfloat16)


def embed(slot, got, extra, pos, weight, small):
    tokens = slot.shape[0]
    turns = pos.shape[0] // TILE
    return call(
        embed_kernel,
        "embed_qkv",
        (tokens // TILE,),
        [
            rows_spec(128),
            whole_spec(got.shape),
            rows_spec(D),
            pl.BlockSpec((TILE, D), lambda i: (lax.rem(i, turns), 0)),
            weight_spec(3 * D, 0),
            whole_spec(small.shape),
        ],
        [rows_spec(D), rows_spec(D), rows_spec(3 * D)],
        [
            jax.ShapeDtypeStruct((tokens, D), jnp.float32),
            jax.ShapeDtypeStruct((tokens, D), jnp.float32),
            jax.ShapeDtypeStruct((tokens, 3 * D), jnp.bfloat16),
        ],
        flops=2 * tokens * D * (3 * D + got.shape[0]),
        moved=tokens * D * 20,
    )(slot, got, extra, pos, weight, small)


def head_masks(rows):
    lane = lax.broadcasted_iota(jnp.int32, (rows, 128), 1)
    return (lane < 64, lane >= 64)


def live_row(length, seq):
    return jnp.where(
        lax.broadcasted_iota(jnp.int32, (1, seq), 1) < length, 0.0, -1000000000.0
    ).astype(jnp.float32)


def attend_kernel(lengths, qkv, mixed_out, log_out):
    seq = qkv.shape[0]
    bias = live_row(lengths[pl.program_id(0)], seq)
    masks = head_masks(seq)
    lane = lax.broadcasted_iota(jnp.int32, (seq, 128), 1)
    logs = jnp.zeros((seq, 128), jnp.float32)
    for pair in range(H // 2):
        at = pair * 128
        query = qkv[:, at : at + 128] * jnp.bfloat16(0.125)
        keys = qkv[:, D + at : D + at + 128]
        values = qkv[:, 2 * D + at : 2 * D + at + 128]
        sides = []
        for side, mask in enumerate(masks):
            logits = back_mul(jnp.where(mask, query, jnp.zeros_like(query)), keys) + bias
            top = jnp.max(logits, -1, keepdims=True)
            raised = jnp.exp(logits - top)
            total = jnp.sum(raised, -1, keepdims=True)
            probs = (raised * (1.0 / total)).astype(jnp.bfloat16)
            sides.append(matmul(probs, values))
            logs = jnp.where(lane == 2 * pair + side, top + jnp.log(total), logs)
        mixed_out[:, at : at + 128] = jnp.where(masks[0], sides[0], sides[1]).astype(jnp.bfloat16)
    log_out[...] = logs


def attend(lengths, qkv, seq):
    tokens = qkv.shape[0]
    return call(
        attend_kernel,
        "attention",
        (tokens // seq,),
        [rows_spec(3 * D, seq)],
        [rows_spec(D, seq), rows_spec(128, seq)],
        [
            jax.ShapeDtypeStruct((tokens, D), jnp.bfloat16),
            jax.ShapeDtypeStruct((tokens, 128), jnp.float32),
        ],
        prefetch=1,
        flops=4 * tokens * seq * D,
        moved=tokens * D * 8,
    )(lengths, qkv)


def feed_kernel(
    lengths, mixed, h0, out_w, up_w, down_w, small, r1_out, h1_out, act_out, slope_out, r2_out, pooled
):
    step = pl.program_id(0)
    turns = LEN // TILE
    r1 = h0[...] + (matmul(mixed[...], out_w[...]) + small[4:5, :])
    hat, _ = normed(r1)
    h1 = hat * small[5:6, :] + small[6:7, :]
    low = h1.astype(jnp.bfloat16)
    r1_out[...] = r1
    h1_out[...] = low
    ffn = jnp.zeros(r1.shape, jnp.float32)
    for part in range(FF // D):
        up = matmul(low, up_w[part * D : (part + 1) * D, :]) + small[7 + part : 8 + part, :]
        below = 0.5 * (1.0 + lax.erf(up * math.sqrt(0.5)))
        act = (up * below).astype(jnp.bfloat16)
        slope = below + up * jnp.exp(-0.5 * up * up) * (1.0 / math.sqrt(2.0 * math.pi))
        act_out[:, part * D : (part + 1) * D] = act
        slope_out[:, part * D : (part + 1) * D] = slope.astype(jnp.bfloat16)
        ffn = ffn + matmul(act, down_w[part * D : (part + 1) * D, :])
    r2 = h1 + (ffn + small[11:12, :])
    r2_out[...] = r2
    hat2, _ = normed(r2)
    h2 = hat2 * small[12:13, :] + small[13:14, :]
    length = lengths[step // turns]
    at = lax.rem(step, turns) * TILE + lax.broadcasted_iota(jnp.int32, (TILE, 1), 0)
    part_sum = jnp.sum(jnp.where(at < length, h2, 0.0), 0, keepdims=True)

    @pl.when(lax.rem(step, turns) == 0)
    def _():
        pooled[...] = jnp.zeros_like(pooled)

    pooled[0, 0:1, :] += part_sum / length.astype(jnp.float32)


def feed(lengths, mixed, h0, weight, small):
    tokens = mixed.shape[0]
    turns = LEN // TILE
    return call(
        feed_kernel,
        "feed_forward",
        (tokens // TILE,),
        [
            rows_spec(D),
            rows_spec(D),
            weight_spec(D, 3),
            weight_spec(FF, 1),
            weight_spec(FF, 2),
            whole_spec(small.shape),
        ],
        [
            rows_spec(D),
            rows_spec(D),
            rows_spec(FF),
            rows_spec(FF),
            rows_spec(D),
            pl.BlockSpec((1, 8, D), lambda i, *_: (i // turns, 0, 0)),
        ],
        [
            jax.ShapeDtypeStruct((tokens, D), jnp.float32),
            jax.ShapeDtypeStruct((tokens, D), jnp.bfloat16),
            jax.ShapeDtypeStruct((tokens, FF), jnp.bfloat16),
            jax.ShapeDtypeStruct((tokens, FF), jnp.bfloat16),
            jax.ShapeDtypeStruct((tokens, D), jnp.float32),
            jax.ShapeDtypeStruct((tokens // LEN, 8, D), jnp.float32),
        ],
        prefetch=1,
        flops=2 * tokens * D * (D + 2 * FF),
        moved=tokens * D * 32,
    )(lengths, mixed, h0, weight, weight, weight, small)


def feed_back_kernel(
    lengths, share, r1, r2, slope, out_w, up_w, down_w, small, f_out, u_out, r1_grad, a_out, mixed_out, sums
):
    step = pl.program_id(0)
    turns = LEN // TILE

    @pl.when(step == 0)
    def _():
        sums[...] = jnp.zeros_like(sums)

    length = lengths[step // turns]
    at = lax.rem(step, turns) * TILE + lax.broadcasted_iota(jnp.int32, (TILE, 1), 0)
    grad_h2 = jnp.where(at < length, share[0, 0:1, :], 0.0)
    hat2, scale2 = normed(r2[...])
    grad_r2, gain2, shift2 = norm_back(grad_h2, hat2, scale2, small[12:13, :])
    add_row(sums, 12, gain2)
    add_row(sums, 13, shift2)
    add_row(sums, 11, jnp.sum(grad_r2, 0, keepdims=True))
    low_f = grad_r2.astype(jnp.bfloat16)
    f_out[...] = low_f
    grad_h1 = grad_r2
    for part in range(FF // D):
        span = slice(part * D, (part + 1) * D)
        grad_up = back_mul(low_f, down_w[span, :]) * slope[:, span].astype(jnp.float32)
        add_row(sums, 7 + part, jnp.sum(grad_up, 0, keepdims=True))
        low_u = grad_up.astype(jnp.bfloat16)
        u_out[:, span] = low_u
        grad_h1 = grad_h1 + back_mul(low_u, up_w[span, :])
    hat1, scale1 = normed(r1[...])
    grad_r1, gain1, shift1 = norm_back(grad_h1, hat1, scale1, small[5:6, :])
    add_row(sums, 5, gain1)
    add_row(sums, 6, shift1)
    add_row(sums, 4, jnp.sum(grad_r1, 0, keepdims=True))
    r1_grad[...] = grad_r1
    low_a = grad_r1.astype(jnp.bfloat16)
    a_out[...] = low_a
    mixed_out[...] = back_mul(low_a, out_w[...]).astype(jnp.bfloat16)


def feed_back(lengths, share, r1, r2, slope, weight, small):
    tokens = r1.shape[0]
    turns = LEN // TILE
    return call(
        feed_back_kernel,
        "feed_forward_back",
        (tokens // TILE,),
        [
            pl.BlockSpec((1, 8, D), lambda i, *_: (i // turns, 0, 0)),
            rows_spec(D),
            rows_spec(D),
            rows_spec(FF),
            weight_spec(D, 3),
            weight_spec(FF, 1),
            weight_spec(FF, 2),
            whole_spec(small.shape),
        ],
        [
            rows_spec(D),
            rows_spec(FF),
            rows_spec(D),
            rows_spec(D),
            rows_spec(D),
            whole_spec((16, D)),
        ],
        [
            jax.ShapeDtypeStruct((tokens, D), jnp.bfloat16),
            jax.ShapeDtypeStruct((tokens, FF), jnp.bfloat16),
            jax.ShapeDtypeStruct((tokens, D), jnp.float32),
            jax.ShapeDtypeStruct((tokens, D), jnp.bfloat16),
            jax.ShapeDtypeStruct((tokens, D), jnp.bfloat16),
            jax.ShapeDtypeStruct((16, D), jnp.float32),
        ],
        prefetch=1,
        flops=2 * tokens * D * (D + 2 * FF),
        moved=tokens * D * 32,
    )(lengths, share, r1, r2, slope, weight, weight, weight, small)


def outer_kernel(act, low_f, low_h1, low_u, mixed, low_a, out):
    step = pl.program_id(0)
    parts = FF // D

    @pl.when(step < parts)
    def _():
        out[...] = outer_sum(act[...], low_f[...]).astype(jnp.bfloat16)

    @pl.when((step >= parts) & (step < 2 * parts))
    def _():
        out[...] = outer_sum(low_h1[...], low_u[...]).astype(jnp.bfloat16)

    @pl.when(step == 2 * parts)
    def _():
        out[...] = outer_sum(mixed[...], low_a[...]).astype(jnp.bfloat16)


def feed_weights(act, low_f, low_h1, low_u, mixed, low_a):
    tokens = act.shape[0]
    parts = FF // D
    return call(
        outer_kernel,
        "feed_forward_weights",
        (2 * parts + 1,),
        [
            pl.BlockSpec((tokens, D), lambda i: (0, jnp.minimum(i, parts - 1))),
            whole_spec((tokens, D)),
            whole_spec((tokens, D)),
            pl.BlockSpec((tokens, D), lambda i: (0, jnp.clip(i - parts, 0, parts - 1))),
            whole_spec((tokens, D)),
            whole_spec((tokens, D)),
        ],
        [pl.BlockSpec((D, D), lambda i: (i, 0))],
        [jax.ShapeDtypeStruct(((2 * parts + 1) * D, D), jnp.bfloat16)],
        flops=2 * tokens * D * (D + 2 * FF),
        moved=tokens * D * 24,
    )(act, low_f, low_h1, low_u, mixed, low_a)[0]


def attend_back_kernel(lengths, qkv, grad_mixed, logs, out, sums):
    seq = qkv.shape[0]
    bias = live_row(lengths[pl.program_id(0)], seq)
    masks = head_masks(seq)

    @pl.when(pl.program_id(0) == 0)
    def _():
        sums[...] = jnp.zeros_like(sums)

    for pair in range(H // 2):
        at = pair * 128
        query = qkv[:, at : at + 128] * jnp.bfloat16(0.125)
        keys = qkv[:, D + at : D + at + 128]
        values = qkv[:, 2 * D + at : 2 * D + at + 128]
        above = grad_mixed[:, at : at + 128]
        queries = []
        key_sum = value_sum = None
        for side, mask in enumerate(masks):
            head = 2 * pair + side
            side_query = jnp.where(mask, query, jnp.zeros_like(query))
            side_above = jnp.where(mask, above, jnp.zeros_like(above))
            probs = jnp.exp(back_mul(side_query, keys) + (bias - logs[:, head : head + 1]))
            grad_probs = back_mul(side_above, values)
            inner = jnp.sum(probs * grad_probs, -1, keepdims=True)
            grad_logits = (probs * (grad_probs - inner)).astype(jnp.bfloat16)
            side_value = outer_sum(probs.astype(jnp.bfloat16), side_above)
            side_key = outer_sum(grad_logits, side_query)
            queries.append(matmul(grad_logits, keys))
            value_sum = side_value if side == 0 else value_sum + side_value
            key_sum = side_key if side == 0 else key_sum + side_key
        grad_query = jnp.where(masks[0], queries[0], queries[1]) * 0.125
        out[:, at : at + 128] = grad_query.astype(jnp.bfloat16)
        out[:, D + at : D + at + 128] = key_sum.astype(jnp.bfloat16)
        out[:, 2 * D + at : 2 * D + at + 128] = value_sum.astype(jnp.bfloat16)
        sums[2:3, at : at + 128] += jnp.sum(grad_query, 0, keepdims=True)
        sums[3:4, at : at + 128] += jnp.sum(value_sum, 0, keepdims=True)


def attend_back(lengths, qkv, grad_mixed, logs, seq):
    tokens = qkv.shape[0]
    return call(
        attend_back_kernel,
        "attention_back",
        (tokens // seq,),
        [rows_spec(3 * D, seq), rows_spec(D, seq), rows_spec(128, seq)],
        [rows_spec(3 * D, seq), whole_spec((16, D))],
        [
            jax.ShapeDtypeStruct((tokens, 3 * D), jnp.bfloat16),
            jax.ShapeDtypeStruct((16, D), jnp.float32),
        ],
        prefetch=1,
        flops=10 * tokens * seq * D,
        moved=tokens * D * 16,
    )(lengths, qkv, grad_mixed, logs)


def embed_back_kernel(grad_r1, grad_qkv, weight, x, small, x_out, pos_out, sums):
    spot, sentence = pl.program_id(0), pl.program_id(1)

    @pl.when((spot == 0) & (sentence == 0))
    def _():
        sums[...] = jnp.zeros_like(sums)

    @pl.when(sentence == 0)
    def _():
        pos_out[...] = jnp.zeros_like(pos_out)

    grad_h0 = grad_r1[...]
    for third in range(3):
        span = slice(third * D, (third + 1) * D)
        grad_h0 = grad_h0 + back_mul(grad_qkv[:, span], weight[span, :])
    hat, scale = normed(x[...])
    grad_x, gain, shift = norm_back(grad_h0, hat, scale, small[0:1, :])
    add_row(sums, 0, gain)
    add_row(sums, 1, shift)
    x_out[...] = grad_x.astype(jnp.bfloat16)
    pos_out[...] += grad_x


def embed_back(grad_r1, grad_qkv, weight, x, small, seq):
    tokens = x.shape[0]
    turns = seq // TILE

    def rows(width):
        return pl.BlockSpec((TILE, width), lambda p, b: (b * turns + p, 0))

    return call(
        embed_back_kernel,
        "embed_back",
        (turns, tokens // seq),
        [rows(D), rows(3 * D), whole_spec((3 * D, D)), rows(D), whole_spec(small.shape)],
        [rows(D), pl.BlockSpec((TILE, D), lambda p, b: (p, 0)), whole_spec((16, D))],
        [
            jax.ShapeDtypeStruct((tokens, D), jnp.bfloat16),
            jax.ShapeDtypeStruct((seq, D), jnp.float32),
            jax.ShapeDtypeStruct((16, D), jnp.float32),
        ],
        flops=6 * tokens * D * D,
        moved=tokens * D * 20,
    )(grad_r1, grad_qkv, weight, x, small)


def qkv_outer_kernel(h0, grad_qkv, out, low):
    @pl.when(pl.program_id(0) == 0)
    def _():
        low[...] = h0[...].astype(jnp.bfloat16)

    out[...] = outer_sum(low[...], grad_qkv[...]).astype(jnp.bfloat16)


def qkv_weights(h0, grad_qkv):
    tokens = h0.shape[0]
    return call(
        qkv_outer_kernel,
        "qkv_weights",
        (3,),
        [whole_spec((tokens, D)), pl.BlockSpec((tokens, D), lambda i: (0, i))],
        [pl.BlockSpec((D, D), lambda i: (i, 0))],
        [jax.ShapeDtypeStruct((3 * D, D), jnp.bfloat16)],
        scratch=[pltpu.VMEM((tokens, D), jnp.bfloat16)],
        flops=6 * tokens * D * D,
        moved=tokens * D * 12,
    )(h0, grad_qkv)[0]


def bucket_kernel(slot, grad, out):
    size = out.shape[0]
    at = pl.program_id(0) * size + lax.broadcasted_iota(jnp.int32, (size, slot.shape[1]), 0)
    pick = (slot[...] == at).astype(jnp.bfloat16)
    out[...] = matmul(pick, grad[...]).astype(jnp.bfloat16)


def bucket_rows(slot, grad, count):
    tokens = grad.shape[0]
    size = count // 4
    return call(
        bucket_kernel,
        "bucket_rows",
        (count // size,),
        [whole_spec((1, tokens)), whole_spec((tokens, D))],
        [pl.BlockSpec((size, D), lambda i: (i, 0))],
        [jax.ShapeDtypeStruct((count, D), jnp.bfloat16)],
        flops=2 * tokens * D * count,
        moved=tokens * D * 4,
    )(slot, grad)[0]


def scatter_kernel(row, got, out):
    size = out.shape[0]
    at = pl.program_id(0) * size + lax.broadcasted_iota(jnp.int32, (size, row.shape[1]), 0)
    pick = (row[...] == at).astype(jnp.bfloat16)
    out[...] = matmul(pick, got[...])


def scatter_rows(row, got, rows):
    size = math.gcd(rows, 480)
    count = got.shape[0]
    return call(
        scatter_kernel,
        "scatter_rows",
        (rows // size,),
        [whole_spec((1, count)), whole_spec((count, D))],
        [pl.BlockSpec((size, D), lambda i: (i, 0))],
        [jax.ShapeDtypeStruct((rows, D), jnp.float32)],
        flops=2 * rows * D * count,
        moved=rows * D * 8,
    )(row, got)[0]


def cosine(first, second):
    dots = jnp.sum(first * second, -1)
    return (
        dots
        * lax.rsqrt(jnp.sum(first * first, -1) + 1e-06)
        * lax.rsqrt(jnp.sum(second * second, -1) + 1e-06)
    )


def pair_loss(pooled, pair_ids, scores):
    anchors = pooled[pair_ids[0]]
    near = cosine(anchors, pooled[pair_ids[1]]) - scores[0]
    far = cosine(anchors, pooled[pair_ids[2]]) - scores[1]
    return jnp.sum(near * near) + jnp.sum(far * far)


MESH = pl.DeviceIdType.MESH


def gather_kernel(sizes, whole, src, out, send, recv, local):
    dp, fsdp = sizes
    count = dp * fsdp if whole else fsdp
    row, col = lax.axis_index("dp"), lax.axis_index("fsdp")
    me = row * fsdp + col if whole else col

    def target(step):
        other = lax.rem(me + step, count)
        return (other // fsdp, lax.rem(other, fsdp)) if whole else (row, other)

    barrier = pltpu.get_barrier_semaphore()

    def greet(step, carry):
        pl.semaphore_signal(barrier, inc=1, device_id=target(step), device_id_type=MESH)
        return carry

    lax.fori_loop(1, count, greet, 0)
    pl.semaphore_wait(barrier, count - 1)
    own = pltpu.make_async_copy(src, out.at[me], local)
    own.start()

    def copy(step):
        return pltpu.make_async_remote_copy(
            src_ref=src,
            dst_ref=out.at[me],
            send_sem=send.at[step],
            recv_sem=recv.at[step],
            device_id=target(step),
            device_id_type=MESH,
        )

    def begin(step, carry):
        copy(step).start()
        return carry

    def end(step, carry):
        copy(step).wait()
        return carry

    lax.fori_loop(1, count, begin, 0)
    lax.fori_loop(1, count, end, 0)
    own.wait()


def gather_small(value, whole, collective):
    dp, fsdp = lax.axis_size("dp"), lax.axis_size("fsdp")
    count = dp * fsdp if whole else fsdp
    return pl.pallas_call(
        functools.partial(gather_kernel, (dp, fsdp), whole),
        out_shape=jax.ShapeDtypeStruct((count,) + value.shape, value.dtype),
        in_specs=[pl.BlockSpec(memory_space=pltpu.VMEM)],
        out_specs=pl.BlockSpec(memory_space=pltpu.VMEM),
        scratch_shapes=[
            pltpu.SemaphoreType.DMA((count,)),
            pltpu.SemaphoreType.DMA((count,)),
            pltpu.SemaphoreType.DMA,
        ],
        compiler_params=pltpu.CompilerParams(collective_id=collective, has_side_effects=True),
    )(value)


LOOP_SIZE = 8
CHUNK = 480


def grid_place(device):
    z, y = device // 2, lax.rem(device, 2)
    return z + y * (LOOP_SIZE - 1 - 2 * z)


def grid_device(place):
    place = lax.rem(place + LOOP_SIZE, LOOP_SIZE)
    y = place // (LOOP_SIZE // 2)
    return 2 * (place + y * (LOOP_SIZE - 1 - 2 * place)) + y


def fetch_kernel(
    cap,
    own_rows,
    ids,
    pieces,
    pos_low,
    small,
    table,
    everyone,
    weight,
    pos,
    smalls,
    got,
    held_rows,
    asker_row,
    asker_col,
    most,
    stage,
    table_low,
    sent,
    before,
    id_send,
    id_recv,
    hop_send,
    hop_recv,
    word_send,
    word_recv,
    small_send,
    small_recv,
    stage_sem,
    local_sem,
):
    fsdp = LOOP_SIZE
    row, col = lax.axis_index("dp"), lax.axis_index("fsdp")
    count = lax.axis_size("dp") * fsdp
    tokens = ids.shape[1]
    me = row * fsdp + col
    shard = pieces.shape[0] // 12
    pos_rows = pos_low.shape[0]
    quarter = row
    place = grid_place(col)
    core_mate = row + 1 - 2 * lax.rem(row, 2)
    x_mate = lax.rem(row + 2, 4)
    right = (row, grid_device(place + 1))
    left = (row, grid_device(place - 1))

    def anyone(step):
        other = lax.rem(me + step, count)
        return (other // fsdp, lax.rem(other, fsdp))

    barrier = pltpu.get_barrier_semaphore()

    def greet(step, carry):
        pl.semaphore_signal(barrier, inc=1, device_id=anyone(step), device_id_type=MESH)
        return carry

    lax.fori_loop(1, count, greet, 0)
    pl.semaphore_wait(barrier, count - 1)

    def id_copy(step):
        return pltpu.make_async_remote_copy(
            src_ref=ids,
            dst_ref=everyone.at[me],
            send_sem=id_send.at[step],
            recv_sem=id_recv.at[step],
            device_id=anyone(step),
            device_id_type=MESH,
        )

    def id_start(step, carry):
        id_copy(step).start()
        return carry

    lax.fori_loop(1, count, id_start, 0)
    everyone[pl.ds(me, 1)] = ids[...][None]

    def weight_at(piece, block):
        late = piece // 8
        early_at = piece * D + block * shard
        late_at = 8 * D + block * 4 * shard + (piece - 8) * shard
        return pl.ds(pl.multiple_of(early_at + late * (late_at - early_at), 16), shard)

    def pos_at(part, block):
        size = pos_rows // 4
        return pl.ds(pl.multiple_of(block * pos_rows + part * size, 16), size)

    def hop(slot, block, part, target, own=False):
        copies = []
        for i in range(4):
            if i < 3:
                piece = part * 3 + i
                there = weight.at[weight_at(piece, block), :]
                here = there
                if own:
                    here = pieces.at[pl.ds(pl.multiple_of(piece * shard, 16), shard), :]
            else:
                there = pos.at[pos_at(part, block), :]
                here = there
                if own:
                    size = pos_rows // 4
                    here = pos_low.at[pl.ds(pl.multiple_of(part * size, 16), size), :]
            copies.append(
                pltpu.make_async_remote_copy(
                    src_ref=here,
                    dst_ref=there,
                    send_sem=hop_send.at[4 * slot + i],
                    recv_sem=hop_recv.at[4 * slot + i],
                    device_id=target,
                    device_id_type=MESH,
                )
            )
        return copies

    started = []

    def begin(copies):
        for copy in copies:
            copy.start()
        started.extend(copies)

    def arrive(copies):
        for copy in copies:
            copy.wait_recv()

    events = []
    for k in range(1, LOOP_SIZE // 2 + 1):
        events.append((k, 1))
        if k < LOOP_SIZE // 2:
            events.append((k, -1))
    slot_of = {event: i for i, event in enumerate(events)}
    total = len(events)

    def block_of(event):
        return grid_device(place - event[0] * event[1])

    begin(hop(slot_of[(1, 1)], col, quarter, right, own=True))
    begin(hop(slot_of[(1, -1)], col, quarter, left, own=True))

    def small_copy(step):
        return pltpu.make_async_remote_copy(
            src_ref=small,
            dst_ref=smalls.at[col],
            send_sem=small_send.at[step],
            recv_sem=small_recv.at[step],
            device_id=(row, lax.rem(col + step, fsdp)),
            device_id_type=MESH,
        )

    for step in range(1, fsdp):
        small_copy(step).start()
    local = [pltpu.make_async_copy(small, smalls.at[col], local_sem.at[0])]
    local.append(
        pltpu.make_async_copy(
            pos_low, pos.at[pl.ds(pl.multiple_of(col * pos_rows, 16), pos_rows), :], local_sem.at[1]
        )
    )
    local.append(
        pltpu.make_async_copy(
            pieces.at[pl.ds(8 * shard, 4 * shard), :],
            weight.at[pl.ds(pl.multiple_of(8 * D + col * 4 * shard, 16), 4 * shard), :],
            local_sem.at[2],
        )
    )
    for piece in range(8):
        local.append(
            pltpu.make_async_copy(
                pieces.at[pl.ds(piece * shard, shard), :],
                weight.at[pl.ds(pl.multiple_of(piece * D + col * shard, 16), shard), :],
                local_sem.at[3 + piece],
            )
        )
    for copy in local:
        copy.start()

    chunks = own_rows // CHUNK

    def stage_copy(chunk, slot):
        return pltpu.make_async_copy(
            table.at[pl.ds(chunk * CHUNK, CHUNK), :], stage.at[slot], stage_sem.at[slot]
        )

    stage_copy(0, 0).start()
    across = lax.broadcasted_iota(jnp.int32, (tokens, tokens), 1)
    down = lax.broadcasted_iota(jnp.int32, (tokens, tokens), 0)
    before[...] = (down <= across).astype(jnp.float32).astype(jnp.bfloat16)
    for chunk in range(chunks):
        if chunk + 1 < chunks:
            stage_copy(chunk + 1, (chunk + 1) % 2).start()
        stage_copy(chunk, chunk % 2).wait()
        table_low[chunk * CHUNK : (chunk + 1) * CHUNK, :] = stage[chunk % 2].astype(jnp.bfloat16)

    mine = jnp.broadcast_to(ids[...], (8, tokens))
    owner = lax.broadcasted_iota(jnp.int32, (8, tokens), 0)
    hot = (mine >= owner * own_rows) & (mine < (owner + 1) * own_rows)
    so_far = matmul(hot.astype(jnp.float32).astype(jnp.bfloat16), before[...]).astype(jnp.int32) - 1
    slot = jnp.sum(
        jnp.where(hot & (so_far < cap), owner * cap + so_far + 1, 0), 0, keepdims=True
    ) - 1
    asker_row[...] = slot
    asker_col[...] = jnp.broadcast_to(slot, (128, tokens)).T

    def word_copy(step):
        return pltpu.make_async_remote_copy(
            src_ref=sent.at[lax.rem(col + step, fsdp)],
            dst_ref=got.at[col],
            send_sem=word_send.at[step],
            recv_sem=word_recv.at[step],
            device_id=(row, lax.rem(col + step, fsdp)),
            device_id_type=MESH,
        )

    def bucket(step):
        asker = lax.rem(col + step, fsdp)
        if step:
            id_copy(lax.rem(me - row * fsdp - asker + count, count)).wait_recv()
        theirs = everyone[row * fsdp + asker] - col * own_rows
        held = (theirs >= 0) & (theirs < own_rows)
        flag = jnp.broadcast_to(held, (8, tokens)).astype(jnp.float32).astype(jnp.bfloat16)
        rank = matmul(flag, before[...])[0:1, :].astype(jnp.int32) - 1
        rank = jnp.where(held, rank, -1)
        hit = lax.broadcasted_iota(jnp.int32, (cap, tokens), 0) == rank
        inner = jnp.sum(jnp.where(hit, theirs + 1, 0), 1, keepdims=True) - 1
        held_rows[pl.ds(asker, 1)] = jnp.broadcast_to(inner, (cap, 128)).T[0:1, :][None]
        rows = jnp.zeros((cap, D), jnp.float32)
        wide = own_rows // 4
        for part in range(4):
            pick = inner == part * wide + lax.broadcasted_iota(jnp.int32, (cap, wide), 1)
            rows = rows + matmul(
                pick.astype(jnp.float32).astype(jnp.bfloat16),
                table_low[part * wide : (part + 1) * wide, :],
            )
        sent[pl.ds(asker, 1)] = rows.astype(jnp.bfloat16)[None]
        if step:
            word_copy(step).start()

    def spread(index):
        event = events[index]
        hops, sign = event
        block = block_of(event)
        here = hop(index, block, quarter, right)
        arrive(here)
        follow = (hops + 1, sign)
        if follow in slot_of:
            begin(hop(slot_of[follow], block, quarter, right if sign == 1 else left))
        begin(hop(total + index, block, quarter, (x_mate, col)))
        begin(hop(2 * total + index, block, quarter, (core_mate, col)))

    def pass_on(index):
        block = block_of(events[index])
        arrive(hop(total + index, block, x_mate, (x_mate, col)))
        begin(hop(3 * total + index, block, x_mate, (core_mate, col)))

    for step in range(1, fsdp):
        bucket(step)
        if step >= 2 and step - 2 < total:
            spread(step - 2)
        if step >= 4 and step - 4 < total:
            pass_on(step - 4)
    bucket(0)
    own_words = pltpu.make_async_copy(sent.at[col], got.at[col], local_sem.at[11])
    own_words.start()
    spread(fsdp - 2)
    for index in range(fsdp - 4, total):
        pass_on(index)

    def id_end(step, carry):
        copy = id_copy(step)
        copy.wait_send()

        @pl.when(lax.rem(lax.rem(me - step + count, count) // fsdp - row + count, count) != 0)
        def _():
            copy.wait_recv()

        return carry

    lax.fori_loop(1, count, id_end, 0)
    ids_all = everyone[...]
    largest = jnp.zeros((1, 1), jnp.int32)
    for part in range(fsdp):
        inside = (ids_all >= part * own_rows) & (ids_all < (part + 1) * own_rows)
        number = jnp.sum(inside.astype(jnp.int32), -1)
        largest = jnp.maximum(largest, jnp.max(number, 0, keepdims=True))
    most[...] = jnp.broadcast_to(largest, (8, 128))
    for index in range(total):
        block = block_of(events[index])
        arrive(hop(2 * total + index, block, core_mate, (core_mate, col)))
        arrive(hop(3 * total + index, block, lax.rem(core_mate + 2, 4), (core_mate, col)))
    for step in range(1, fsdp):
        small_copy(step).wait()
        word_copy(step).wait()
    own_words.wait()
    for copy in local:
        copy.wait()
    for copy in started:
        copy.wait_send()


def fetch(ids, pieces, pos_low, small, table, cap):
    fsdp = lax.axis_size("fsdp")
    count = lax.axis_size("dp") * fsdp
    tokens = ids.shape[1]
    own_rows = table.shape[0]
    hops = 16 * (fsdp - 1)
    vmem = pl.BlockSpec(memory_space=pltpu.VMEM)
    anywhere = pl.BlockSpec(memory_space=pl.ANY)
    return pl.pallas_call(
        functools.partial(fetch_kernel, cap, own_rows),
        name="fetch",
        in_specs=[vmem, anywhere, anywhere, anywhere, anywhere],
        out_specs=[vmem, anywhere, anywhere, anywhere, anywhere, vmem, vmem, vmem, vmem],
        out_shape=[
            jax.ShapeDtypeStruct((count, 1, tokens), jnp.int32),
            jax.ShapeDtypeStruct((12 * D, D), jnp.bfloat16),
            jax.ShapeDtypeStruct((fsdp * pos_low.shape[0], D), jnp.bfloat16),
            jax.ShapeDtypeStruct((fsdp,) + small.shape, jnp.bfloat16),
            jax.ShapeDtypeStruct((fsdp, cap, D), jnp.bfloat16),
            jax.ShapeDtypeStruct((fsdp, 1, cap), jnp.int32),
            jax.ShapeDtypeStruct((1, tokens), jnp.int32),
            jax.ShapeDtypeStruct((tokens, 128), jnp.int32),
            jax.ShapeDtypeStruct((8, 128), jnp.int32),
        ],
        scratch_shapes=[
            pltpu.VMEM((2, CHUNK, D), jnp.float32),
            pltpu.VMEM((own_rows, D), jnp.bfloat16),
            pltpu.VMEM((fsdp, cap, D), jnp.bfloat16),
            pltpu.VMEM((tokens, tokens), jnp.bfloat16),
            pltpu.SemaphoreType.DMA((count,)),
            pltpu.SemaphoreType.DMA((count,)),
            pltpu.SemaphoreType.DMA((hops,)),
            pltpu.SemaphoreType.DMA((hops,)),
            pltpu.SemaphoreType.DMA((fsdp,)),
            pltpu.SemaphoreType.DMA((fsdp,)),
            pltpu.SemaphoreType.DMA((fsdp,)),
            pltpu.SemaphoreType.DMA((fsdp,)),
            pltpu.SemaphoreType.DMA((2,)),
            pltpu.SemaphoreType.DMA((12,)),
        ],
        compiler_params=pltpu.CompilerParams(
            collective_id=0, has_side_effects=True, vmem_limit_bytes=VMEM_GRANT
        ),
    )(ids, pieces, pos_low, small, table)


LOOP = {8: (0, 2, 4, 6, 7, 5, 3, 1)}


def swap_core(value):
    return lax.ppermute(value, "dp", [(i, i ^ 1) for i in range(lax.axis_size("dp"))])


def swap_x(value):
    count = lax.axis_size("dp")
    return lax.ppermute(value, "dp", [(i, (i + 2) % count) for i in range(count)])


def sum_x(value):
    count = lax.axis_size("dp")
    total = value
    for hop in range(2, count, 2):
        moved = lax.ppermute(value, "dp", [(i, (i + hop) % count) for i in range(count)])
        total = total.astype(jnp.float32) + moved.astype(jnp.float32)
    return total


def shift(value, step):
    loop = LOOP[lax.axis_size("fsdp")]
    size = len(loop)
    return lax.ppermute(
        value, "fsdp", [(loop[i], loop[(i + step) % size]) for i in range(size)]
    )


def loop_place():
    loop = LOOP[lax.axis_size("fsdp")]
    place = [0] * len(loop)
    for i, device in enumerate(loop):
        place[device] = i
    return jnp.array(place, jnp.int32)[lax.axis_index("fsdp")], jnp.array(loop, jnp.int32)


def ring_gather(part, sign):
    size = lax.axis_size("fsdp")
    place, loop = loop_place()
    out = jnp.zeros((size,) + part.shape, part.dtype)

    def put(out, block, offset):
        at = loop[lax.rem(place + offset + size, size)]
        return lax.dynamic_update_slice(out, block[None], (at, 0, 0))

    out = put(out, part, 0)
    ahead = behind = part
    for hop in range(1, size // 2 + 1):
        ahead = shift(ahead, sign)
        out = put(out, ahead, -sign * hop)
        if hop < size - size // 2:
            behind = shift(behind, -sign)
            out = put(out, behind, sign * hop)
    return out


def ring_reduce(parts, sign):
    size = lax.axis_size("fsdp")
    place, loop = loop_place()

    def local(offset):
        at = loop[lax.rem(place + offset + size, size)]
        return lax.dynamic_index_in_dim(parts, at, 0, keepdims=False).astype(jnp.float32)

    def flow(direction, hops):
        arrived = None
        for hop in range(hops):
            value = local(direction * (hops - hop))
            if arrived is not None:
                value = value + arrived.astype(jnp.float32)
            arrived = shift(value.astype(jnp.bfloat16), direction)
        return arrived

    far = flow(sign, size // 2)
    near = flow(-sign, size - size // 2 - 1)
    return local(0) + far.astype(jnp.float32) + near.astype(jnp.float32)


def gather_halves(first, second, sign):
    core = lax.rem(lax.axis_index("dp"), 2)
    if lax.axis_size("fsdp") not in LOOP:
        return lax.all_gather(first, "fsdp", axis=0), lax.all_gather(second, "fsdp", axis=0)
    mine = ring_gather(jnp.where(core == 0, first, second), sign)
    other = swap_core(mine)
    return jnp.where(core == 0, mine, other), jnp.where(core == 0, other, mine)


def reduce_halves(first, second, sign):
    core = lax.rem(lax.axis_index("dp"), 2)
    give = jnp.where(core == 0, second, first).astype(jnp.bfloat16)
    keep = jnp.where(core == 0, first, second).astype(jnp.float32)
    chip = (keep + swap_core(give).astype(jnp.float32)).astype(jnp.bfloat16)
    if lax.axis_size("fsdp") in LOOP:
        block = ring_reduce(chip, sign)
    else:
        block = lax.psum_scatter(chip.astype(jnp.float32), "fsdp", scatter_dimension=0)
    total = sum_x(block.astype(jnp.bfloat16)).astype(jnp.bfloat16)
    other = swap_core(total)
    low = jnp.where(core == 0, total, other).astype(jnp.float32)
    high = jnp.where(core == 0, other, total).astype(jnp.float32)
    return low, high


def split_rows(weight, parts):
    return jnp.concatenate(jnp.split(weight, parts, axis=1), axis=0)


def join_rows(blocks, parts):
    count, rows, width = blocks.shape
    return (
        blocks.reshape(count, parts, rows // parts, width)
        .transpose(0, 2, 1, 3)
        .reshape(count * rows // parts, parts * width)
    )


def cut_parts(grad, count, parts):
    width = grad.shape[-1]
    return (
        grad.reshape(parts, count, -1, width).transpose(1, 0, 2, 3).reshape(count, -1, width)
    )


def pad_rows(value, rows):
    return jnp.pad(value, [(0, 0)] * (value.ndim - 2) + [(0, rows - value.shape[-2]), (0, 0)])


def round_up(value, step):
    return -(-value // step) * step


def bucket_size(tokens, owners):
    mean = tokens / owners
    return min(tokens, round_up(int(mean + 5.6 * math.sqrt(mean)), 16))


def one_hot(index, count):
    return (index[:, None] == lax.iota(jnp.int32, count)[None, :]).astype(jnp.bfloat16)


class Routes:
    def __init__(self, everyone, own_rows):
        fsdp = lax.axis_size("fsdp")
        self.rows = own_rows
        tokens = everyone.shape[1]
        self.cap = bucket_size(tokens, fsdp)
        me = lax.axis_index("fsdp")
        group = lax.dynamic_slice_in_dim(everyone, lax.axis_index("dp") * fsdp, fsdp, 0)
        mine = lax.dynamic_index_in_dim(group, me, 0, keepdims=False)
        owners = lax.iota(jnp.int32, fsdp)
        every_count = jnp.sum(
            (everyone // own_rows)[:, :, None] == owners[None, None, :], 1, dtype=jnp.int32
        )
        self.rounds = (jnp.max(every_count) + self.cap - 1) // self.cap
        self.inner = group - me * own_rows
        self.held = (self.inner >= 0) & (self.inner < own_rows)
        self.held_place = jnp.cumsum(self.held.astype(jnp.int32), 1) - 1
        self.owner = mine // own_rows
        hot = (self.owner[None, :] == owners[:, None])
        place = jnp.cumsum(hot.astype(jnp.int32), 1) - 1
        self.hot = hot
        self.place = place
        self.my_place = jnp.sum(jnp.where(hot, place, 0), 0)

    def slots(self, flag, place, value, turn):
        slot = lax.iota(jnp.int32, self.cap)[None, :, None] + turn * self.cap
        hit = flag[:, None, :] & (place[:, None, :] == slot)
        return (jnp.sum(jnp.where(hit, value[:, None, :] + 1, 0), -1) - 1).reshape(-1)

    def owner_rows(self, turn):
        return self.slots(self.held, self.held_place, self.inner, turn)

    def asker_tokens(self, turn):
        tokens = lax.iota(jnp.int32, self.owner.shape[0])[None, :]
        return self.slots(self.hot, self.place, tokens, turn)

    def asker_slots(self, turn):
        place = self.my_place - turn * self.cap
        inside = (place >= 0) & (place < self.cap)
        return jnp.where(inside, self.owner * self.cap + place, -1)


def exchange(rows):
    fsdp = lax.axis_size("fsdp")
    blocks = rows.reshape(fsdp, rows.shape[0] // fsdp, rows.shape[1])
    return lax.all_to_all(blocks, "fsdp", 0, 0).reshape(rows.shape)


def gather_table(table_low, routes, turn):
    return matmul(one_hot(routes.owner_rows(turn), routes.rows), table_low).astype(jnp.bfloat16)


def more_words(everyone, table, rounds, tokens):
    def more(carry):
        return carry[0] < rounds

    def body(carry):
        turn, words = carry
        ids, turn = lax.optimization_barrier((everyone, turn))
        routes = Routes(ids, table.shape[0])
        got = exchange(gather_table(table.astype(jnp.bfloat16), routes, turn))
        mine = matmul(one_hot(routes.asker_slots(turn), got.shape[0]), got)
        return turn + 1, words + mine.astype(jnp.bfloat16)

    start = (jnp.int32(1), jnp.zeros((tokens, D), jnp.bfloat16))
    return lax.while_loop(more, body, start)[1]


def return_round(grad_low, asker, held, rows):
    sent = bucket_rows(asker, grad_low, held.shape[1])
    return scatter_rows(held, exchange(sent), rows)


def return_rows(grad_low, plan, rows):
    first = return_round(grad_low, plan.asker_row, plan.held_rows, rows)

    def more(carry):
        return carry[0] < plan.rounds

    def body(carry):
        turn, total = carry
        ids, turn = lax.optimization_barrier((plan.everyone, turn))
        routes = Routes(ids, rows)
        asker, held = routes.asker_slots(turn)[None, :], routes.owner_rows(turn)[None, :]
        return turn + 1, total + return_round(grad_low, asker, held, rows)

    return lax.while_loop(more, body, (jnp.int32(1), first))[1]


class Plan:
    def __init__(self, ids, pieces, pos_low, small, table):
        fsdp = lax.axis_size("fsdp")
        tokens = ids.shape[0]
        cap = bucket_size(tokens, fsdp)
        cols = small.shape[1]
        block = jnp.pad(small, ((0, 2), (0, 128 - cols)))
        if fsdp == LOOP_SIZE and lax.axis_size("dp") == 4:
            everyone, self.weight, self.pos, smalls, got, held, row, col, most = fetch(
                ids.reshape(1, tokens), pieces, pos_low, block, table, cap
            )
            self.everyone = everyone.reshape(-1, tokens)
            self.rounds = (most[0, 0] + cap - 1) // cap
            self.asker_row, self.asker_col = row, col
            self.held_rows = held.reshape(1, -1)
            self.got = got.reshape(-1, D)
        else:
            self.everyone = gather_small(ids.reshape(-1, 128), True, 0).reshape(-1, tokens)
            routes = Routes(self.everyone, table.shape[0])
            self.rounds = routes.rounds
            slot = routes.asker_slots(0)
            self.asker_row = slot[None, :]
            self.asker_col = jnp.broadcast_to(slot[:, None], (tokens, 128))
            self.held_rows = routes.owner_rows(0)[None, :]
            self.got = exchange(gather_table(table.astype(jnp.bfloat16), routes, 0))
            both = lax.all_gather(pieces, "fsdp", axis=0)
            early = pieces.shape[0] * 2 // 3
            self.weight = jnp.concatenate(
                [
                    both[:, :early].reshape(fsdp, 8, -1, D).transpose(1, 0, 2, 3).reshape(-1, D),
                    both[:, early:].reshape(-1, D),
                ],
                0,
            )
            self.pos = lax.all_gather(pos_low, "fsdp", axis=0, tiled=True)
            smalls = lax.all_gather(block, "fsdp", axis=0)
        self.small = (
            smalls[:, :, :cols].transpose(1, 0, 2).reshape(16, D).astype(jnp.float32)
        )
        self.extra = more_words(self.everyone, table, self.rounds, tokens)


def sum_groups(table):
    core = lax.rem(lax.axis_index("dp"), 2)
    half = table.shape[0] // 2
    low = table.astype(jnp.bfloat16)
    keep = lax.dynamic_slice_in_dim(table, core * half, half, 0)
    give = lax.dynamic_slice_in_dim(low, (1 - core) * half, half, 0)
    chip = (keep + swap_core(give).astype(jnp.float32)).astype(jnp.bfloat16)
    total = sum_x(chip).astype(jnp.bfloat16)
    other = swap_core(total)
    return jnp.concatenate(
        [jnp.where(core == 0, total, other), jnp.where(core == 0, other, total)], 0
    ).astype(jnp.float32)


def renew(weight, moment, average, grad, factor):
    step = factor * grad
    buffer = MOMENTUM * moment + step
    fresh = weight - RATE * (step + MOMENTUM * buffer)
    return (fresh, buffer, KEEP * average + (1.0 - KEEP) * fresh)


def shards(
    token_ids,
    lengths,
    pair_ids,
    scores,
    word_table,
    pos_table,
    qkv_weight,
    out_weight,
    up_weight,
    down_weight,
    small_params,
    word_moment,
    pos_moment,
    qkv_moment,
    out_moment,
    up_moment,
    down_moment,
    small_moment,
    word_average,
    pos_average,
    qkv_average,
    out_average,
    up_average,
    down_average,
    small_average,
):
    batch, seq = token_ids.shape
    width = D
    fsdp = lax.axis_size("fsdp")
    tokens = batch * seq
    shard = qkv_weight.shape[0]
    pos_rows = pos_table.shape[0]
    small_cols = small_params.shape[1]
    pieces = jnp.concatenate(
        [
            split_rows(qkv_weight.astype(jnp.bfloat16), 3),
            out_weight.astype(jnp.bfloat16),
            split_rows(up_weight.astype(jnp.bfloat16), 4),
            down_weight.astype(jnp.bfloat16),
        ],
        0,
    )
    plan = Plan(
        token_ids.reshape(-1),
        pieces,
        pos_table.astype(jnp.bfloat16),
        small_params.astype(jnp.bfloat16),
        word_table,
    )
    weight, small_full = plan.weight, plan.small
    half_pos = pos_rows // 2
    x, h0, qkv = embed(plan.asker_col, plan.got, plan.extra, plan.pos, weight, small_full)
    mixed, logs = attend(lengths, qkv, seq)
    r1, low_h1, act, slope, r2, pooled = feed(lengths, mixed, h0, weight, small_full)
    pooled_all = gather_small(pooled[:, 0].reshape(-1, 128), True, 1).reshape(-1, width)
    loss, pull_loss = jax.vjp(lambda rows: pair_loss(rows, pair_ids, scores), pooled_all)
    grad_all = pull_loss(jnp.ones((), jnp.float32))[0]
    grad_pooled = lax.dynamic_slice_in_dim(
        grad_all, lax.axis_index(("dp", "fsdp")) * batch, batch, 0
    )
    share = jnp.broadcast_to(
        (grad_pooled / lengths.astype(jnp.float32)[:, None])[:, None, :], (batch, 8, width)
    )
    low_f, low_u, grad_r1, low_a, grad_mixed, sums_feed = feed_back(
        lengths, share, r1, r2, slope, weight, small_full
    )
    feed_grads = feed_weights(act, low_f, low_h1, low_u, mixed, low_a)
    sum_down, sum_up = reduce_halves(
        feed_grads[:FF].reshape(fsdp, -1, width),
        cut_parts(feed_grads[FF : 2 * FF], fsdp, 4),
        1,
    )
    grad_qkv, sums_attend = attend_back(lengths, qkv, grad_mixed, logs, seq)
    grad_x, grad_pos, sums_embed = embed_back(grad_r1, grad_qkv, weight, x, small_full, seq)
    grad_table = return_rows(grad_x, plan, word_table.shape[0])
    qkv_cut = cut_parts(qkv_weights(h0, grad_qkv), fsdp, 3)
    grad_small = sums_feed + sums_attend + sums_embed
    small_cut = jnp.pad(
        grad_small.reshape(16, fsdp, small_cols).transpose(1, 0, 2),
        ((0, 0), (0, 0), (0, width - small_cols)),
    ).astype(jnp.bfloat16)
    pos_cut = grad_pos.reshape(fsdp, pos_rows, width).astype(jnp.bfloat16)
    low_cut = jnp.concatenate([qkv_cut[:, : 2 * shard], pos_cut[:, :half_pos], small_cut], 1)
    high_cut = pad_rows(
        jnp.concatenate(
            [
                qkv_cut[:, 2 * shard :],
                feed_grads[2 * FF :].reshape(fsdp, shard, width),
                pos_cut[:, half_pos:],
            ],
            1,
        ),
        low_cut.shape[1],
    )
    sum_low, sum_high = reduce_halves(low_cut, high_cut, -1)
    sum_qkv = join_rows(
        jnp.concatenate([sum_low[: 2 * shard], sum_high[:shard]], 0)[None], 3
    )
    sum_out = sum_high[shard : 2 * shard]
    sum_pos = jnp.concatenate(
        [sum_low[2 * shard : 2 * shard + half_pos], sum_high[2 * shard : 2 * shard + half_pos]], 0
    )
    small_at = 2 * shard + half_pos
    sum_small = sum_low[small_at : small_at + 14, :small_cols]
    sum_upw = join_rows(sum_up[None], 4)
    summed = (
        sum_groups(grad_table),
        sum_pos,
        sum_qkv,
        sum_out,
        sum_upw,
        sum_down,
        sum_small,
    )
    local_squares = jnp.zeros((), jnp.float32)
    for grad in summed:
        local_squares = local_squares + jnp.sum(grad * grad)
    total = jnp.sum(gather_small(jnp.full((8, 128), local_squares), False, 2)[:, 0, 0])
    norm = jnp.sqrt(total)
    limit = 1e-05 * math.sqrt((VOCAB + LEN + 4 * D + 2 * FF + 14) * D)
    factor = jnp.minimum(1.0, limit / (norm + 1e-06))
    weights = (word_table, pos_table, qkv_weight, out_weight, up_weight, down_weight, small_params)
    moments = (
        word_moment,
        pos_moment,
        qkv_moment,
        out_moment,
        up_moment,
        down_moment,
        small_moment,
    )
    averages = (
        word_average,
        pos_average,
        qkv_average,
        out_average,
        up_average,
        down_average,
        small_average,
    )
    new_w = []
    new_m = []
    new_a = []
    for weight, moment, average, grad in zip(weights, moments, averages, summed):
        fresh, buffer, mean_new = renew(weight, moment, average, grad, factor)
        new_w.append(fresh)
        new_m.append(buffer)
        new_a.append(mean_new)
    return (
        loss,
        norm,
        new_w[0],
        new_w[1],
        new_w[2],
        new_w[3],
        new_w[4],
        new_w[5],
        new_w[6],
        new_m[0],
        new_m[1],
        new_m[2],
        new_m[3],
        new_m[4],
        new_m[5],
        new_m[6],
        new_a[0],
        new_a[1],
        new_a[2],
        new_a[3],
        new_a[4],
        new_a[5],
        new_a[6],
    )


def solution(mesh):
    placed = (
        P(("dp", "fsdp"), None),
        P(("dp", "fsdp")),
        P(),
        P(),
        P("fsdp", None),
        P("fsdp", None),
        P("fsdp", None),
        P("fsdp", None),
        P("fsdp", None),
        P("fsdp", None),
        P(None, "fsdp"),
        P("fsdp", None),
        P("fsdp", None),
        P("fsdp", None),
        P("fsdp", None),
        P("fsdp", None),
        P("fsdp", None),
        P(None, "fsdp"),
        P("fsdp", None),
        P("fsdp", None),
        P("fsdp", None),
        P("fsdp", None),
        P("fsdp", None),
        P("fsdp", None),
        P(None, "fsdp"),
    )
    return jax.shard_map(
        shards,
        mesh=mesh,
        in_specs=placed,
        out_specs=(
            P(),
            P(),
            P("fsdp", None),
            P("fsdp", None),
            P("fsdp", None),
            P("fsdp", None),
            P("fsdp", None),
            P("fsdp", None),
            P(None, "fsdp"),
            P("fsdp", None),
            P("fsdp", None),
            P("fsdp", None),
            P("fsdp", None),
            P("fsdp", None),
            P("fsdp", None),
            P(None, "fsdp"),
            P("fsdp", None),
            P("fsdp", None),
            P("fsdp", None),
            P("fsdp", None),
            P("fsdp", None),
            P("fsdp", None),
            P(None, "fsdp"),
        ),
        check_vma=False,
    )
```

```python
import functools
import math

import jax
import jax.numpy as jnp
from jax import lax
from jax.experimental import pallas as pl
from jax.experimental.pallas import tpu as pltpu
from jax.sharding import PartitionSpec as P

D = 768
H = 12
FF = 3072
VOCAB = 30720
LEN = 512


MOMENTUM = 0.9
RATE = 3000.0
KEEP = 0.9


def matmul(left, right):
    return jnp.dot(left, right, preferred_element_type=jnp.float32)


def outer_sum(left, right):
    return lax.dot_general(
        left, right, (((0,), (0,)), ((), ())), preferred_element_type=jnp.float32
    )


def back_mul(grad, weight):
    return lax.dot_general(
        grad, weight, (((1,), (1,)), ((), ())), preferred_element_type=jnp.float32
    )


TILE = 256
EPS = 1e-12
VMEM_GRANT = 60 * 1024 * 1024


def whole_spec(shape):
    return pl.BlockSpec(shape, lambda *_: (0,) * len(shape))


def rows_spec(width, rows=TILE):
    return pl.BlockSpec((rows, width), lambda i, *_: (i, 0))


def weight_spec(rows, at):
    return pl.BlockSpec((rows, D), lambda i, *_: (at, 0))


def call(kernel, name, grid, in_specs, out_specs, out_shape, scratch=(), prefetch=0, flops=0, moved=0):
    return pl.pallas_call(
        kernel,
        name=name,
        grid_spec=pltpu.PrefetchScalarGridSpec(
            num_scalar_prefetch=prefetch,
            grid=grid,
            in_specs=in_specs,
            out_specs=out_specs,
            scratch_shapes=scratch,
        ),
        out_shape=out_shape,
        compiler_params=pltpu.CompilerParams(vmem_limit_bytes=VMEM_GRANT),
        cost_estimate=pl.CostEstimate(flops=flops, bytes_accessed=moved, transcendentals=0),
    )


def normed(v):
    mean = jnp.mean(v, -1, keepdims=True)
    cent = v - mean
    scale = lax.rsqrt(jnp.mean(cent * cent, -1, keepdims=True) + EPS)
    return cent * scale, scale


def norm_back(grad, hat, scale, gain):
    inner = grad * gain
    middle = jnp.mean(inner, -1, keepdims=True)
    along = jnp.mean(inner * hat, -1, keepdims=True)
    return (
        scale * (inner - middle - hat * along),
        jnp.sum(grad * hat, 0, keepdims=True),
        jnp.sum(grad, 0, keepdims=True),
    )


def add_row(ref, row, value):
    ref[row : row + 1, :] += value


def embed_kernel(slot, got, extra, pos, weight, small, x_out, h0_out, qkv_out):
    count = got.shape[0]
    pick = (slot[:, 0:1] == lax.broadcasted_iota(jnp.int32, (slot.shape[0], count), 1)).astype(
        jnp.bfloat16
    )
    words = matmul(pick, got[...]) + extra[...].astype(jnp.float32)
    x = words + pos[...].astype(jnp.float32)
    hat, _ = normed(x)
    h0 = hat * small[0:1, :] + small[1:2, :]
    x_out[...] = x
    h0_out[...] = h0
    low = h0.astype(jnp.bfloat16)
    for third, bias in enumerate((2, None, 3)):
        value = matmul(low, weight[third * D : (third + 1) * D, :])
        if bias is not None:
            value = value + small[bias : bias + 1, :]
        qkv_out[:, third * D : (third + 1) * D] = value.astype(jnp.bfloat16)


def embed(slot, got, extra, pos, weight, small):
    tokens = slot.shape[0]
    turns = pos.shape[0] // TILE
    return call(
        embed_kernel,
        "embed_qkv",
        (tokens // TILE,),
        [
            rows_spec(128),
            whole_spec(got.shape),
            rows_spec(D),
            pl.BlockSpec((TILE, D), lambda i: (lax.rem(i, turns), 0)),
            weight_spec(3 * D, 0),
            whole_spec(small.shape),
        ],
        [rows_spec(D), rows_spec(D), rows_spec(3 * D)],
        [
            jax.ShapeDtypeStruct((tokens, D), jnp.float32),
            jax.ShapeDtypeStruct((tokens, D), jnp.float32),
            jax.ShapeDtypeStruct((tokens, 3 * D), jnp.bfloat16),
        ],
        flops=2 * tokens * D * (3 * D + got.shape[0]),
        moved=tokens * D * 20,
    )(slot, got, extra, pos, weight, small)


def head_masks(rows):
    lane = lax.broadcasted_iota(jnp.int32, (rows, 128), 1)
    return (lane < 64, lane >= 64)


def live_row(length, seq):
    return jnp.where(
        lax.broadcasted_iota(jnp.int32, (1, seq), 1) < length, 0.0, -1000000000.0
    ).astype(jnp.float32)


def attend_kernel(lengths, qkv, mixed_out, log_out):
    seq = qkv.shape[0]
    bias = live_row(lengths[pl.program_id(0)], seq)
    masks = head_masks(seq)
    lane = lax.broadcasted_iota(jnp.int32, (seq, 128), 1)
    logs = jnp.zeros((seq, 128), jnp.float32)
    for pair in range(H // 2):
        at = pair * 128
        query = qkv[:, at : at + 128] * jnp.bfloat16(0.125)
        keys = qkv[:, D + at : D + at + 128]
        values = qkv[:, 2 * D + at : 2 * D + at + 128]
        sides = []
        for side, mask in enumerate(masks):
            logits = back_mul(jnp.where(mask, query, jnp.zeros_like(query)), keys) + bias
            top = jnp.max(logits, -1, keepdims=True)
            raised = jnp.exp(logits - top)
            total = jnp.sum(raised, -1, keepdims=True)
            probs = (raised * (1.0 / total)).astype(jnp.bfloat16)
            sides.append(matmul(probs, values))
            logs = jnp.where(lane == 2 * pair + side, top + jnp.log(total), logs)
        mixed_out[:, at : at + 128] = jnp.where(masks[0], sides[0], sides[1]).astype(jnp.bfloat16)
    log_out[...] = logs


def attend(lengths, qkv, seq):
    tokens = qkv.shape[0]
    return call(
        attend_kernel,
        "attention",
        (tokens // seq,),
        [rows_spec(3 * D, seq)],
        [rows_spec(D, seq), rows_spec(128, seq)],
        [
            jax.ShapeDtypeStruct((tokens, D), jnp.bfloat16),
            jax.ShapeDtypeStruct((tokens, 128), jnp.float32),
        ],
        prefetch=1,
        flops=4 * tokens * seq * D,
        moved=tokens * D * 8,
    )(lengths, qkv)


def feed_kernel(
    lengths, mixed, h0, out_w, up_w, down_w, small, r1_out, h1_out, act_out, slope_out, r2_out, pooled
):
    step = pl.program_id(0)
    turns = LEN // TILE
    r1 = h0[...] + (matmul(mixed[...], out_w[...]) + small[4:5, :])
    hat, _ = normed(r1)
    h1 = hat * small[5:6, :] + small[6:7, :]
    low = h1.astype(jnp.bfloat16)
    r1_out[...] = r1
    h1_out[...] = low
    ffn = jnp.zeros(r1.shape, jnp.float32)
    for part in range(FF // D):
        up = matmul(low, up_w[part * D : (part + 1) * D, :]) + small[7 + part : 8 + part, :]
        below = 0.5 * (1.0 + lax.erf(up * math.sqrt(0.5)))
        act = (up * below).astype(jnp.bfloat16)
        slope = below + up * jnp.exp(-0.5 * up * up) * (1.0 / math.sqrt(2.0 * math.pi))
        act_out[:, part * D : (part + 1) * D] = act
        slope_out[:, part * D : (part + 1) * D] = slope.astype(jnp.bfloat16)
        ffn = ffn + matmul(act, down_w[part * D : (part + 1) * D, :])
    r2 = h1 + (ffn + small[11:12, :])
    r2_out[...] = r2
    hat2, _ = normed(r2)
    h2 = hat2 * small[12:13, :] + small[13:14, :]
    length = lengths[step // turns]
    at = lax.rem(step, turns) * TILE + lax.broadcasted_iota(jnp.int32, (TILE, 1), 0)
    part_sum = jnp.sum(jnp.where(at < length, h2, 0.0), 0, keepdims=True)

    @pl.when(lax.rem(step, turns) == 0)
    def _():
        pooled[...] = jnp.zeros_like(pooled)

    pooled[0, 0:1, :] += part_sum / length.astype(jnp.float32)


def feed(lengths, mixed, h0, weight, small):
    tokens = mixed.shape[0]
    turns = LEN // TILE
    return call(
        feed_kernel,
        "feed_forward",
        (tokens // TILE,),
        [
            rows_spec(D),
            rows_spec(D),
            weight_spec(D, 3),
            weight_spec(FF, 1),
            weight_spec(FF, 2),
            whole_spec(small.shape),
        ],
        [
            rows_spec(D),
            rows_spec(D),
            rows_spec(FF),
            rows_spec(FF),
            rows_spec(D),
            pl.BlockSpec((1, 8, D), lambda i, *_: (i // turns, 0, 0)),
        ],
        [
            jax.ShapeDtypeStruct((tokens, D), jnp.float32),
            jax.ShapeDtypeStruct((tokens, D), jnp.bfloat16),
            jax.ShapeDtypeStruct((tokens, FF), jnp.bfloat16),
            jax.ShapeDtypeStruct((tokens, FF), jnp.bfloat16),
            jax.ShapeDtypeStruct((tokens, D), jnp.float32),
            jax.ShapeDtypeStruct((tokens // LEN, 8, D), jnp.float32),
        ],
        prefetch=1,
        flops=2 * tokens * D * (D + 2 * FF),
        moved=tokens * D * 32,
    )(lengths, mixed, h0, weight, weight, weight, small)


def feed_back_kernel(
    lengths, share, r1, r2, slope, out_w, up_w, down_w, small, f_out, u_out, r1_grad, a_out, mixed_out, sums
):
    step = pl.program_id(0)
    turns = LEN // TILE

    @pl.when(step == 0)
    def _():
        sums[...] = jnp.zeros_like(sums)

    length = lengths[step // turns]
    at = lax.rem(step, turns) * TILE + lax.broadcasted_iota(jnp.int32, (TILE, 1), 0)
    grad_h2 = jnp.where(at < length, share[0, 0:1, :], 0.0)
    hat2, scale2 = normed(r2[...])
    grad_r2, gain2, shift2 = norm_back(grad_h2, hat2, scale2, small[12:13, :])
    add_row(sums, 12, gain2)
    add_row(sums, 13, shift2)
    add_row(sums, 11, jnp.sum(grad_r2, 0, keepdims=True))
    low_f = grad_r2.astype(jnp.bfloat16)
    f_out[...] = low_f
    grad_h1 = grad_r2
    for part in range(FF // D):
        span = slice(part * D, (part + 1) * D)
        grad_up = back_mul(low_f, down_w[span, :]) * slope[:, span].astype(jnp.float32)
        add_row(sums, 7 + part, jnp.sum(grad_up, 0, keepdims=True))
        low_u = grad_up.astype(jnp.bfloat16)
        u_out[:, span] = low_u
        grad_h1 = grad_h1 + back_mul(low_u, up_w[span, :])
    hat1, scale1 = normed(r1[...])
    grad_r1, gain1, shift1 = norm_back(grad_h1, hat1, scale1, small[5:6, :])
    add_row(sums, 5, gain1)
    add_row(sums, 6, shift1)
    add_row(sums, 4, jnp.sum(grad_r1, 0, keepdims=True))
    r1_grad[...] = grad_r1
    low_a = grad_r1.astype(jnp.bfloat16)
    a_out[...] = low_a
    mixed_out[...] = back_mul(low_a, out_w[...]).astype(jnp.bfloat16)


def feed_back(lengths, share, r1, r2, slope, weight, small):
    tokens = r1.shape[0]
    turns = LEN // TILE
    return call(
        feed_back_kernel,
        "feed_forward_back",
        (tokens // TILE,),
        [
            pl.BlockSpec((1, 8, D), lambda i, *_: (i // turns, 0, 0)),
            rows_spec(D),
            rows_spec(D),
            rows_spec(FF),
            weight_spec(D, 3),
            weight_spec(FF, 1),
            weight_spec(FF, 2),
            whole_spec(small.shape),
        ],
        [
            rows_spec(D),
            rows_spec(FF),
            rows_spec(D),
            rows_spec(D),
            rows_spec(D),
            whole_spec((16, D)),
        ],
        [
            jax.ShapeDtypeStruct((tokens, D), jnp.bfloat16),
            jax.ShapeDtypeStruct((tokens, FF), jnp.bfloat16),
            jax.ShapeDtypeStruct((tokens, D), jnp.float32),
            jax.ShapeDtypeStruct((tokens, D), jnp.bfloat16),
            jax.ShapeDtypeStruct((tokens, D), jnp.bfloat16),
            jax.ShapeDtypeStruct((16, D), jnp.float32),
        ],
        prefetch=1,
        flops=2 * tokens * D * (D + 2 * FF),
        moved=tokens * D * 32,
    )(lengths, share, r1, r2, slope, weight, weight, weight, small)


def outer_kernel(act, low_f, low_h1, low_u, mixed, low_a, out):
    step = pl.program_id(0)
    parts = FF // D

    @pl.when(step < parts)
    def _():
        out[...] = outer_sum(act[...], low_f[...]).astype(jnp.bfloat16)

    @pl.when((step >= parts) & (step < 2 * parts))
    def _():
        out[...] = outer_sum(low_h1[...], low_u[...]).astype(jnp.bfloat16)

    @pl.when(step == 2 * parts)
    def _():
        out[...] = outer_sum(mixed[...], low_a[...]).astype(jnp.bfloat16)


def feed_weights(act, low_f, low_h1, low_u, mixed, low_a):
    tokens = act.shape[0]
    parts = FF // D
    return call(
        outer_kernel,
        "feed_forward_weights",
        (2 * parts + 1,),
        [
            pl.BlockSpec((tokens, D), lambda i: (0, jnp.minimum(i, parts - 1))),
            whole_spec((tokens, D)),
            whole_spec((tokens, D)),
            pl.BlockSpec((tokens, D), lambda i: (0, jnp.clip(i - parts, 0, parts - 1))),
            whole_spec((tokens, D)),
            whole_spec((tokens, D)),
        ],
        [pl.BlockSpec((D, D), lambda i: (i, 0))],
        [jax.ShapeDtypeStruct(((2 * parts + 1) * D, D), jnp.bfloat16)],
        flops=2 * tokens * D * (D + 2 * FF),
        moved=tokens * D * 24,
    )(act, low_f, low_h1, low_u, mixed, low_a)[0]


def attend_back_kernel(lengths, qkv, grad_mixed, logs, out, sums):
    seq = qkv.shape[0]
    bias = live_row(lengths[pl.program_id(0)], seq)
    masks = head_masks(seq)

    @pl.when(pl.program_id(0) == 0)
    def _():
        sums[...] = jnp.zeros_like(sums)

    for pair in range(H // 2):
        attend_back_pair(
            qkv, grad_mixed, logs, bias, masks, out, sums, slice(0, seq), pair
        )


def attend_back(lengths, qkv, grad_mixed, logs, seq):
    tokens = qkv.shape[0]
    return call(
        attend_back_kernel,
        "attention_back",
        (tokens // seq,),
        [rows_spec(3 * D, seq), rows_spec(D, seq), rows_spec(128, seq)],
        [rows_spec(3 * D, seq), whole_spec((16, D))],
        [
            jax.ShapeDtypeStruct((tokens, 3 * D), jnp.bfloat16),
            jax.ShapeDtypeStruct((16, D), jnp.float32),
        ],
        prefetch=1,
        flops=10 * tokens * seq * D,
        moved=tokens * D * 16,
    )(lengths, qkv, grad_mixed, logs)


def embed_back_kernel(grad_r1, grad_qkv, weight, x, small, x_out, pos_out, sums):
    spot, sentence = pl.program_id(0), pl.program_id(1)

    @pl.when((spot == 0) & (sentence == 0))
    def _():
        sums[...] = jnp.zeros_like(sums)

    @pl.when(sentence == 0)
    def _():
        pos_out[...] = jnp.zeros_like(pos_out)

    grad_h0 = grad_r1[...]
    for third in range(3):
        span = slice(third * D, (third + 1) * D)
        grad_h0 = grad_h0 + back_mul(grad_qkv[:, span], weight[span, :])
    hat, scale = normed(x[...])
    grad_x, gain, shift = norm_back(grad_h0, hat, scale, small[0:1, :])
    add_row(sums, 0, gain)
    add_row(sums, 1, shift)
    x_out[...] = grad_x.astype(jnp.bfloat16)
    pos_out[...] += grad_x


def embed_back(grad_r1, grad_qkv, weight, x, small, seq):
    tokens = x.shape[0]
    turns = seq // TILE

    def rows(width):
        return pl.BlockSpec((TILE, width), lambda p, b: (b * turns + p, 0))

    return call(
        embed_back_kernel,
        "embed_back",
        (turns, tokens // seq),
        [rows(D), rows(3 * D), whole_spec((3 * D, D)), rows(D), whole_spec(small.shape)],
        [rows(D), pl.BlockSpec((TILE, D), lambda p, b: (p, 0)), whole_spec((16, D))],
        [
            jax.ShapeDtypeStruct((tokens, D), jnp.bfloat16),
            jax.ShapeDtypeStruct((seq, D), jnp.float32),
            jax.ShapeDtypeStruct((16, D), jnp.float32),
        ],
        flops=6 * tokens * D * D,
        moved=tokens * D * 20,
    )(grad_r1, grad_qkv, weight, x, small)


def qkv_outer_kernel(h0, grad_qkv, out, low):
    @pl.when(pl.program_id(0) == 0)
    def _():
        low[...] = h0[...].astype(jnp.bfloat16)

    out[...] = outer_sum(low[...], grad_qkv[...]).astype(jnp.bfloat16)


def qkv_weights(h0, grad_qkv):
    tokens = h0.shape[0]
    return call(
        qkv_outer_kernel,
        "qkv_weights",
        (3,),
        [whole_spec((tokens, D)), pl.BlockSpec((tokens, D), lambda i: (0, i))],
        [pl.BlockSpec((D, D), lambda i: (i, 0))],
        [jax.ShapeDtypeStruct((3 * D, D), jnp.bfloat16)],
        scratch=[pltpu.VMEM((tokens, D), jnp.bfloat16)],
        flops=6 * tokens * D * D,
        moved=tokens * D * 12,
    )(h0, grad_qkv)[0]


def bucket_kernel(slot, grad, out):
    size = out.shape[0]
    at = pl.program_id(0) * size + lax.broadcasted_iota(jnp.int32, (size, slot.shape[1]), 0)
    pick = (slot[...] == at).astype(jnp.bfloat16)
    out[...] = matmul(pick, grad[...]).astype(jnp.bfloat16)


def bucket_rows(slot, grad, count):
    tokens = grad.shape[0]
    size = count // 4
    return call(
        bucket_kernel,
        "bucket_rows",
        (count // size,),
        [whole_spec((1, tokens)), whole_spec((tokens, D))],
        [pl.BlockSpec((size, D), lambda i: (i, 0))],
        [jax.ShapeDtypeStruct((count, D), jnp.bfloat16)],
        flops=2 * tokens * D * count,
        moved=tokens * D * 4,
    )(slot, grad)[0]


def scatter_kernel(row, got, out):
    size = out.shape[0]
    at = pl.program_id(0) * size + lax.broadcasted_iota(jnp.int32, (size, row.shape[1]), 0)
    pick = (row[...] == at).astype(jnp.bfloat16)
    out[...] = matmul(pick, got[...])


def scatter_rows(row, got, rows):
    size = math.gcd(rows, 480)
    count = got.shape[0]
    return call(
        scatter_kernel,
        "scatter_rows",
        (rows // size,),
        [whole_spec((1, count)), whole_spec((count, D))],
        [pl.BlockSpec((size, D), lambda i: (i, 0))],
        [jax.ShapeDtypeStruct((rows, D), jnp.float32)],
        flops=2 * rows * D * count,
        moved=rows * D * 8,
    )(row, got)[0]


def cosine(first, second):
    dots = jnp.sum(first * second, -1)
    return (
        dots
        * lax.rsqrt(jnp.sum(first * first, -1) + 1e-06)
        * lax.rsqrt(jnp.sum(second * second, -1) + 1e-06)
    )


def pair_loss(pooled, pair_ids, scores):
    anchors = pooled[pair_ids[0]]
    near = cosine(anchors, pooled[pair_ids[1]]) - scores[0]
    far = cosine(anchors, pooled[pair_ids[2]]) - scores[1]
    return jnp.sum(near * near) + jnp.sum(far * far)


MESH = pl.DeviceIdType.MESH


def gather_kernel(sizes, whole, src, out, send, recv, local):
    dp, fsdp = sizes
    count = dp * fsdp if whole else fsdp
    row, col = lax.axis_index("dp"), lax.axis_index("fsdp")
    me = row * fsdp + col if whole else col

    def target(step):
        other = lax.rem(me + step, count)
        return (other // fsdp, lax.rem(other, fsdp)) if whole else (row, other)

    barrier = pltpu.get_barrier_semaphore()

    def greet(step, carry):
        pl.semaphore_signal(barrier, inc=1, device_id=target(step), device_id_type=MESH)
        return carry

    lax.fori_loop(1, count, greet, 0)
    pl.semaphore_wait(barrier, count - 1)
    own = pltpu.make_async_copy(src, out.at[me], local)
    own.start()

    def copy(step):
        return pltpu.make_async_remote_copy(
            src_ref=src,
            dst_ref=out.at[me],
            send_sem=send.at[step],
            recv_sem=recv.at[step],
            device_id=target(step),
            device_id_type=MESH,
        )

    def begin(step, carry):
        copy(step).start()
        return carry

    def end(step, carry):
        copy(step).wait()
        return carry

    lax.fori_loop(1, count, begin, 0)
    lax.fori_loop(1, count, end, 0)
    own.wait()


def gather_small(value, whole, collective):
    dp, fsdp = lax.axis_size("dp"), lax.axis_size("fsdp")
    count = dp * fsdp if whole else fsdp
    return pl.pallas_call(
        functools.partial(gather_kernel, (dp, fsdp), whole),
        out_shape=jax.ShapeDtypeStruct((count,) + value.shape, value.dtype),
        in_specs=[pl.BlockSpec(memory_space=pltpu.VMEM)],
        out_specs=pl.BlockSpec(memory_space=pltpu.VMEM),
        scratch_shapes=[
            pltpu.SemaphoreType.DMA((count,)),
            pltpu.SemaphoreType.DMA((count,)),
            pltpu.SemaphoreType.DMA,
        ],
        compiler_params=pltpu.CompilerParams(collective_id=collective, has_side_effects=True),
    )(value)


LOOP_SIZE = 8
CHUNK = 480


def grid_place(device):
    z, y = device // 2, lax.rem(device, 2)
    return z + y * (LOOP_SIZE - 1 - 2 * z)


def grid_device(place):
    place = lax.rem(place + LOOP_SIZE, LOOP_SIZE)
    y = place // (LOOP_SIZE // 2)
    return 2 * (place + y * (LOOP_SIZE - 1 - 2 * place)) + y


def fetch_kernel(
    cap,
    own_rows,
    ids,
    pieces,
    pos_low,
    small,
    table,
    everyone,
    weight,
    pos,
    smalls,
    got,
    held_rows,
    asker_row,
    asker_col,
    most,
    stage,
    table_low,
    sent,
    before,
    id_send,
    id_recv,
    hop_send,
    hop_recv,
    word_send,
    word_recv,
    small_send,
    small_recv,
    held_send,
    held_recv,
    stage_sem,
    local_sem,
):
    fsdp = LOOP_SIZE
    row, col = lax.axis_index("dp"), lax.axis_index("fsdp")
    count = lax.axis_size("dp") * fsdp
    tokens = ids.shape[1]
    me = row * fsdp + col
    shard = pieces.shape[0] // 12
    pos_rows = pos_low.shape[0]
    quarter = row
    place = grid_place(col)
    core_mate = row + 1 - 2 * lax.rem(row, 2)
    x_mate = lax.rem(row + 2, 4)
    right = (row, grid_device(place + 1))
    left = (row, grid_device(place - 1))

    def anyone(step):
        other = lax.rem(me + step, count)
        return (other // fsdp, lax.rem(other, fsdp))

    barrier = pltpu.get_barrier_semaphore()

    def greet(step, carry):
        pl.semaphore_signal(barrier, inc=1, device_id=anyone(step), device_id_type=MESH)
        return carry

    lax.fori_loop(1, count, greet, 0)
    pl.semaphore_wait(barrier, count - 1)

    def id_copy(step):
        return pltpu.make_async_remote_copy(
            src_ref=ids,
            dst_ref=everyone.at[me],
            send_sem=id_send.at[step],
            recv_sem=id_recv.at[step],
            device_id=anyone(step),
            device_id_type=MESH,
        )

    def id_start(step, carry):
        id_copy(step).start()
        return carry

    lax.fori_loop(1, count, id_start, 0)
    everyone[pl.ds(me, 1)] = ids[...][None]

    def weight_at(piece, block):
        late = piece // 8
        early_at = piece * D + block * shard
        late_at = 8 * D + block * 4 * shard + (piece - 8) * shard
        return pl.ds(pl.multiple_of(early_at + late * (late_at - early_at), 16), shard)

    def pos_at(part, block):
        size = pos_rows // 4
        return pl.ds(pl.multiple_of(block * pos_rows + part * size, 16), size)

    def hop(slot, block, part, target, own=False):
        copies = []
        for i in range(4):
            if i < 3:
                piece = part * 3 + i
                there = weight.at[weight_at(piece, block), :]
                here = there
                if own:
                    here = pieces.at[pl.ds(pl.multiple_of(piece * shard, 16), shard), :]
            else:
                there = pos.at[pos_at(part, block), :]
                here = there
                if own:
                    size = pos_rows // 4
                    here = pos_low.at[pl.ds(pl.multiple_of(part * size, 16), size), :]
            copies.append(
                pltpu.make_async_remote_copy(
                    src_ref=here,
                    dst_ref=there,
                    send_sem=hop_send.at[4 * slot + i],
                    recv_sem=hop_recv.at[4 * slot + i],
                    device_id=target,
                    device_id_type=MESH,
                )
            )
        return copies

    started = []

    def begin(copies):
        for copy in copies:
            copy.start()
        started.extend(copies)

    def arrive(copies):
        for copy in copies:
            copy.wait_recv()

    events = []
    for k in range(1, LOOP_SIZE // 2 + 1):
        events.append((k, 1))
        if k < LOOP_SIZE // 2:
            events.append((k, -1))
    slot_of = {event: i for i, event in enumerate(events)}
    total = len(events)

    def block_of(event):
        return grid_device(place - event[0] * event[1])

    begin(hop(slot_of[(1, 1)], col, quarter, right, own=True))
    begin(hop(slot_of[(1, -1)], col, quarter, left, own=True))

    def small_copy(step):
        return pltpu.make_async_remote_copy(
            src_ref=small,
            dst_ref=smalls.at[col],
            send_sem=small_send.at[step],
            recv_sem=small_recv.at[step],
            device_id=(row, lax.rem(col + step, fsdp)),
            device_id_type=MESH,
        )

    for step in range(1, fsdp):
        small_copy(step).start()
    local = [pltpu.make_async_copy(small, smalls.at[col], local_sem.at[0])]
    local.append(
        pltpu.make_async_copy(
            pos_low, pos.at[pl.ds(pl.multiple_of(col * pos_rows, 16), pos_rows), :], local_sem.at[1]
        )
    )
    local.append(
        pltpu.make_async_copy(
            pieces.at[pl.ds(8 * shard, 4 * shard), :],
            weight.at[pl.ds(pl.multiple_of(8 * D + col * 4 * shard, 16), 4 * shard), :],
            local_sem.at[2],
        )
    )
    for piece in range(8):
        local.append(
            pltpu.make_async_copy(
                pieces.at[pl.ds(piece * shard, shard), :],
                weight.at[pl.ds(pl.multiple_of(piece * D + col * shard, 16), shard), :],
                local_sem.at[3 + piece],
            )
        )
    for copy in local:
        copy.start()

    chunks = own_rows // CHUNK

    def stage_copy(chunk, slot):
        return pltpu.make_async_copy(
            table.at[pl.ds(chunk * CHUNK, CHUNK), :], stage.at[slot], stage_sem.at[slot]
        )

    stage_copy(0, 0).start()
    across = lax.broadcasted_iota(jnp.int32, (tokens, tokens), 1)
    down = lax.broadcasted_iota(jnp.int32, (tokens, tokens), 0)
    before[...] = (down <= across).astype(jnp.float32).astype(jnp.bfloat16)
    for chunk in range(chunks):
        if chunk + 1 < chunks:
            stage_copy(chunk + 1, (chunk + 1) % 2).start()
        stage_copy(chunk, chunk % 2).wait()
        table_low[chunk * CHUNK : (chunk + 1) * CHUNK, :] = stage[chunk % 2].astype(jnp.bfloat16)

    mine = jnp.broadcast_to(ids[...], (8, tokens))
    owner = lax.broadcasted_iota(jnp.int32, (8, tokens), 0)
    hot = (mine >= owner * own_rows) & (mine < (owner + 1) * own_rows)
    so_far = matmul(hot.astype(jnp.float32).astype(jnp.bfloat16), before[...]).astype(jnp.int32) - 1
    slot = jnp.sum(
        jnp.where(hot & (so_far < cap), owner * cap + so_far + 1, 0), 0, keepdims=True
    ) - 1
    asker_row[...] = slot
    asker_col[...] = jnp.broadcast_to(slot, (128, tokens)).T

    def word_copy(step):
        return pltpu.make_async_remote_copy(
            src_ref=sent.at[lax.rem(col + step, fsdp)],
            dst_ref=got.at[col],
            send_sem=word_send.at[step],
            recv_sem=word_recv.at[step],
            device_id=(row, lax.rem(col + step, fsdp)),
            device_id_type=MESH,
        )

    def bucket(step):
        asker = lax.rem(col + step, fsdp)
        if step:
            id_copy(lax.rem(me - row * fsdp - asker + count, count)).wait_recv()
        theirs = everyone[row * fsdp + asker] - col * own_rows
        held = (theirs >= 0) & (theirs < own_rows)
        flag = jnp.broadcast_to(held, (8, tokens)).astype(jnp.float32).astype(jnp.bfloat16)
        rank = matmul(flag, before[...])[0:1, :].astype(jnp.int32) - 1
        rank = jnp.where(held, rank, -1)
        hit = lax.broadcasted_iota(jnp.int32, (cap, tokens), 0) == rank
        inner = jnp.sum(jnp.where(hit, theirs + 1, 0), 1, keepdims=True) - 1
        held_rows[pl.ds(row, 1), step] = jnp.broadcast_to(inner, (cap, 128)).T[0:1, :][None]
        rows = jnp.zeros((cap, D), jnp.float32)
        wide = own_rows // 4
        for part in range(4):
            pick = inner == part * wide + lax.broadcasted_iota(jnp.int32, (cap, wide), 1)
            rows = rows + matmul(
                pick.astype(jnp.float32).astype(jnp.bfloat16),
                table_low[part * wide : (part + 1) * wide, :],
            )
        sent[pl.ds(asker, 1)] = rows.astype(jnp.bfloat16)[None]
        if step:
            word_copy(step).start()

    def spread(index):
        event = events[index]
        hops, sign = event
        block = block_of(event)
        here = hop(index, block, quarter, right)
        arrive(here)
        follow = (hops + 1, sign)
        if follow in slot_of:
            begin(hop(slot_of[follow], block, quarter, right if sign == 1 else left))
        begin(hop(total + index, block, quarter, (x_mate, col)))
        begin(hop(2 * total + index, block, quarter, (core_mate, col)))

    def pass_on(index):
        block = block_of(events[index])
        arrive(hop(total + index, block, x_mate, (x_mate, col)))
        begin(hop(3 * total + index, block, x_mate, (core_mate, col)))

    for step in range(1, fsdp):
        bucket(step)
        if step >= 2 and step - 2 < total:
            spread(step - 2)
        if step >= 4 and step - 4 < total:
            pass_on(step - 4)
    bucket(0)
    own_words = pltpu.make_async_copy(sent.at[col], got.at[col], local_sem.at[11])
    own_words.start()

    def held_copy(index):
        target = (core_mate, x_mate, lax.rem(core_mate + 2, 4))[index]
        return pltpu.make_async_remote_copy(
            src_ref=held_rows.at[row],
            dst_ref=held_rows.at[row],
            send_sem=held_send.at[index],
            recv_sem=held_recv.at[index],
            device_id=(target, col),
            device_id_type=MESH,
        )

    for index in range(3):
        held_copy(index).start()
    spread(fsdp - 2)
    for index in range(fsdp - 4, total):
        pass_on(index)

    def id_end(step, carry):
        copy = id_copy(step)
        copy.wait_send()

        @pl.when(lax.rem(lax.rem(me - step + count, count) // fsdp - row + count, count) != 0)
        def _():
            copy.wait_recv()

        return carry

    lax.fori_loop(1, count, id_end, 0)
    ids_all = everyone[...]
    largest = jnp.zeros((1, 1), jnp.int32)
    for part in range(fsdp):
        inside = (ids_all >= part * own_rows) & (ids_all < (part + 1) * own_rows)
        number = jnp.sum(inside.astype(jnp.int32), -1)
        largest = jnp.maximum(largest, jnp.max(number, 0, keepdims=True))
    most[...] = jnp.broadcast_to(largest, (8, 128))
    for index in range(total):
        block = block_of(events[index])
        arrive(hop(2 * total + index, block, core_mate, (core_mate, col)))
        arrive(hop(3 * total + index, block, lax.rem(core_mate + 2, 4), (core_mate, col)))
    for step in range(1, fsdp):
        small_copy(step).wait()
        word_copy(step).wait()
    for index in range(3):
        held_copy(index).wait()
    own_words.wait()
    for copy in local:
        copy.wait()
    for copy in started:
        copy.wait_send()


def fetch(ids, pieces, pos_low, small, table, cap):
    fsdp = lax.axis_size("fsdp")
    count = lax.axis_size("dp") * fsdp
    tokens = ids.shape[1]
    own_rows = table.shape[0]
    hops = 16 * (fsdp - 1)
    vmem = pl.BlockSpec(memory_space=pltpu.VMEM)
    anywhere = pl.BlockSpec(memory_space=pl.ANY)
    return pl.pallas_call(
        functools.partial(fetch_kernel, cap, own_rows),
        name="fetch",
        in_specs=[vmem, anywhere, anywhere, anywhere, anywhere],
        out_specs=[vmem, anywhere, anywhere, anywhere, anywhere, vmem, vmem, vmem, vmem],
        out_shape=[
            jax.ShapeDtypeStruct((count, 1, tokens), jnp.int32),
            jax.ShapeDtypeStruct((12 * D, D), jnp.bfloat16),
            jax.ShapeDtypeStruct((fsdp * pos_low.shape[0], D), jnp.bfloat16),
            jax.ShapeDtypeStruct((fsdp,) + small.shape, jnp.bfloat16),
            jax.ShapeDtypeStruct((fsdp, cap, D), jnp.bfloat16),
            jax.ShapeDtypeStruct((4, fsdp, 1, cap), jnp.int32),
            jax.ShapeDtypeStruct((1, tokens), jnp.int32),
            jax.ShapeDtypeStruct((tokens, 128), jnp.int32),
            jax.ShapeDtypeStruct((8, 128), jnp.int32),
        ],
        scratch_shapes=[
            pltpu.VMEM((2, CHUNK, D), jnp.float32),
            pltpu.VMEM((own_rows, D), jnp.bfloat16),
            pltpu.VMEM((fsdp, cap, D), jnp.bfloat16),
            pltpu.VMEM((tokens, tokens), jnp.bfloat16),
            pltpu.SemaphoreType.DMA((count,)),
            pltpu.SemaphoreType.DMA((count,)),
            pltpu.SemaphoreType.DMA((hops,)),
            pltpu.SemaphoreType.DMA((hops,)),
            pltpu.SemaphoreType.DMA((fsdp,)),
            pltpu.SemaphoreType.DMA((fsdp,)),
            pltpu.SemaphoreType.DMA((fsdp,)),
            pltpu.SemaphoreType.DMA((fsdp,)),
            pltpu.SemaphoreType.DMA((3,)),
            pltpu.SemaphoreType.DMA((3,)),
            pltpu.SemaphoreType.DMA((2,)),
            pltpu.SemaphoreType.DMA((12,)),
        ],
        compiler_params=pltpu.CompilerParams(
            collective_id=0, has_side_effects=True, vmem_limit_bytes=VMEM_GRANT
        ),
    )(ids, pieces, pos_low, small, table)


class Ring:
    def __init__(self, parts, sign, send, recv, base):
        self.parts, self.send, self.recv, self.base = parts, send, recv, base
        self.row, col = lax.axis_index("dp"), lax.axis_index("fsdp")
        self.col, self.place = col, grid_place(col)
        self.hops = {sign: LOOP_SIZE // 2, -sign: LOOP_SIZE - LOOP_SIZE // 2 - 1}
        self.events = []
        for k in range(1, LOOP_SIZE // 2 + 1):
            for direction in (sign, -sign):
                if k <= self.hops[direction]:
                    self.events.append((k, direction))
        self.slot = {event: i for i, event in enumerate(self.events)}
        self.sign = sign
        self.started = []

    def copies(self, source, event):
        slot = self.slot[event]
        target = (self.row, grid_device(self.place + event[1]))
        return [
            pltpu.make_async_remote_copy(
                src_ref=box.at[source],
                dst_ref=box.at[slot],
                send_sem=self.send.at[self.base + len(self.parts) * slot + i],
                recv_sem=self.recv.at[self.base + len(self.parts) * slot + i],
                device_id=target,
                device_id_type=MESH,
            )
            for i, (_, _, box) in enumerate(self.parts)
        ]

    def depart(self, source, event):
        for copy in self.copies(source, event):
            copy.start()
            self.started.append(copy)

    def add(self, slot, block, arrived):
        for keep, mate, box in self.parts:
            terms = [keep.at[block], mate.at[block]] + ([box.at[slot]] if arrived else [])
            sum_rows(box.at[slot], terms)

    def first(self):
        for i, direction in enumerate((self.sign, -self.sign)):
            block = grid_device(self.place + direction * self.hops[direction])
            self.add(len(self.events) + i, block, False)
            self.depart(len(self.events) + i, (1, direction))

    def step(self, index):
        hop, direction = self.events[index]
        for copy in self.copies(index, self.events[index]):
            copy.wait_recv()
        left = self.hops[direction] - hop
        if left:
            self.add(index, grid_device(self.place + direction * left), True)
            self.depart(index, (hop + 1, direction))

    def last(self, totals):
        far = self.slot[(self.hops[self.sign], self.sign)]
        near = self.slot[(self.hops[-self.sign], -self.sign)]
        for (keep, mate, box), total in zip(self.parts, totals):
            sum_rows(total, [keep.at[self.col], mate.at[self.col], box.at[far], box.at[near]])

    def drain(self):
        for copy in self.started:
            copy.wait_send()


def sum_rows(out, terms):
    rows = min(out.shape[0], 32)

    def body(i, carry):
        span = pl.ds(pl.multiple_of(i * rows, rows), rows)
        total = terms[0][span, :].astype(jnp.float32)
        for term in terms[1:]:
            total = total + term[span, :].astype(jnp.float32)
        out[span, :] = total.astype(out.dtype)
        return carry

    lax.fori_loop(0, out.shape[0] // rows, body, 0)


def add_squares(squares, value):
    rows = min(value.shape[0], 32)

    def body(i, carry):
        part = value[pl.ds(pl.multiple_of(i * rows, rows), rows), :].astype(jnp.float32)
        squares[0:1, 0 : part.shape[1]] += jnp.sum(part * part, 0, keepdims=True)
        return carry

    lax.fori_loop(0, value.shape[0] // rows, body, 0)


def finish_kernel(
    cap,
    own_rows,
    grad,
    slot,
    held,
    feed_grads,
    qkv_grads,
    pos_grads,
    small_grads,
    depart,
    own,
    table_out,
    sum_a,
    sum_b,
    sum_small,
    norm_out,
    got,
    sent,
    total,
    half_low,
    last_a,
    keep_b,
    mate_b,
    box_b,
    keep_s,
    mate_s,
    box_s,
    out_a,
    in_a,
    out_b,
    in_b,
    out_s,
    in_s,
    squares,
    share,
    shares,
    word_send,
    word_recv,
    ring_send,
    ring_recv,
    pair_send,
    pair_recv,
    norm_send,
    norm_recv,
    local_sem,
):
    fsdp = LOOP_SIZE
    row, col = lax.axis_index("dp"), lax.axis_index("fsdp")
    core = lax.rem(row, 2)
    core_mate = row + 1 - 2 * core
    x_mate = lax.rem(row + 2, 4)
    far_mate = lax.rem(core_mate + 2, 4)
    half = own_rows // 2
    tokens = grad.shape[0]

    barrier = pltpu.get_barrier_semaphore()
    for step in range(1, fsdp):
        there = (row, lax.rem(col + step, fsdp))
        pl.semaphore_signal(barrier, inc=1, device_id=there, device_id_type=MESH)
    for step in range(fsdp):
        there = (core_mate, lax.rem(col + step, fsdp))
        pl.semaphore_signal(barrier, inc=1, device_id=there, device_id_type=MESH)
    pl.semaphore_signal(barrier, inc=1, device_id=(x_mate, col), device_id_type=MESH)
    pl.semaphore_wait(barrier, 2 * fsdp)

    def remote(src, dst, sems, index, target):
        return pltpu.make_async_remote_copy(
            src_ref=src,
            dst_ref=dst,
            send_sem=sems[0].at[index],
            recv_sem=sems[1].at[index],
            device_id=target,
            device_id_type=MESH,
        )

    pair = (pair_send, pair_recv)
    mate = (core_mate, col)
    shard = feed_grads.shape[1]

    def b_parts(which, target):
        pos_half = pos_grads.shape[1] // 2
        if which == 0:
            first, second = qkv_grads.at[pl.ds(0, 8)], qkv_grads.at[pl.ds(8, 8)]
        else:
            first, second = qkv_grads.at[pl.ds(16, 8)], feed_grads.at[pl.ds(64, 8)]
        return [
            (first, target.at[:, pl.ds(0, shard)]),
            (second, target.at[:, pl.ds(shard, shard)]),
            (pos_grads.at[:, pl.ds(which * pos_half, pos_half)], target.at[:, pl.ds(2 * shard, pos_half)]),
        ]

    def s_parts(which, target):
        return [(small_grads.at[:, pl.ds(8 * which, 8)], target)]

    for which in range(2):

        @pl.when(core == which)
        def _(which=which):
            for index, (parts, keep, mates) in enumerate(
                ((b_parts, keep_b, mate_b), (s_parts, keep_s, mate_s))
            ):
                for src, dst in parts(1 - which, mates):
                    remote(src, dst, pair, index, mate).start()
                for src, dst in parts(which, keep):
                    pltpu.make_async_copy(src, dst, local_sem.at[index]).start()

    def halves_in(index):
        keep, mates = ((keep_b, mate_b), (keep_s, mate_s))[index]
        pltpu.make_async_copy(keep, keep, local_sem.at[index]).wait()
        remote(mates, mates, pair, index, mate).wait_recv()

    def word_copy(step):
        return remote(
            sent.at[step],
            got.at[row, step],
            (word_send, word_recv),
            step,
            (row, lax.rem(col - step + fsdp, fsdp)),
        )

    def word_hand(kind, step):
        group, target = ((row, (x_mate, col)), (row, mate), (x_mate, mate))[kind]
        place = got.at[group, step]
        return remote(place, place, (word_send, word_recv), fsdp * (kind + 1) + step, target)

    def bucket(step):
        base = lax.rem(col - step + fsdp, fsdp) * cap
        pick = slot[...] == base + lax.broadcasted_iota(jnp.int32, (cap, tokens), 0)
        rows = matmul(pick.astype(jnp.float32).astype(jnp.bfloat16), grad[...]).astype(jnp.bfloat16)
        if step:
            sent[step] = rows
            word_copy(step).start()
        else:
            got[pl.ds(row, 1), 0] = rows[None]

    handed = []

    def spread(step):
        if step:
            word_copy(step).wait_recv()
        for kind in (0, 1):
            copy = word_hand(kind, step)
            copy.start()
            handed.append(copy)

    def pass_on(step):
        place = got.at[x_mate, step]
        remote(place, place, (word_send, word_recv), fsdp + step, (x_mate, col)).wait_recv()
        copy = word_hand(2, step)
        copy.start()
        handed.append(copy)

    def from_mate(group, kind, step):
        place = got.at[group, step]
        remote(place, place, (word_send, word_recv), fsdp * (kind + 1) + step, mate).wait_recv()

    def accumulate(side, parity, part, fresh):
        chip = row - core if side == 0 else x_mate - core
        group = chip + parity
        width = 4 * cap
        size = half // 4

        def tile(i, carry):
            at = core * half + i * size + lax.broadcasted_iota(jnp.int32, (size, width), 0)
            pick = held[pl.ds(group, 1), 0, part * width : (part + 1) * width] == at
            rows = got[pl.ds(group, 1), 4 * part : 4 * part + 4].reshape(width, D)
            value = matmul(pick.astype(jnp.float32).astype(jnp.bfloat16), rows)
            span = pl.ds(pl.multiple_of(i * size, size), size)
            if fresh:
                total[side, span, :] = value
            else:
                total[side, span, :] += value
            return carry

        lax.fori_loop(0, 4, tile, 0)

    def arrived_here(part):
        for step in range(4 * part, 4 * part + 4):
            from_mate(core_mate, 1, step)

    def arrived_far(part):
        for step in range(4 * part, 4 * part + 4):
            from_mate(far_mate, 2, step)

    def last_hop():
        return remote(
            depart, last_a, (ring_send, ring_recv), 14, (row, grid_device(grid_place(col) + 1))
        )

    ring_b = Ring(
        [(keep_b, mate_b, box_b), (keep_s, mate_s, box_s)],
        -1,
        ring_send,
        ring_recv,
        0,
    )
    squares[...] = jnp.zeros_like(squares)

    def swap_x(ring, totals, incoming, index):
        ring.last(totals)
        for i, (mine, theirs) in enumerate(zip(totals, incoming)):
            remote(mine, theirs, pair, index + i, (x_mate, col)).start()

    def settle(totals, incoming, finals, index, back):
        for i, (mine, theirs, final) in enumerate(zip(totals, incoming, finals)):
            remote(mine, theirs, pair, index + i, (x_mate, col)).wait_recv()
            sum_rows(final.at[core], [mine, theirs])
            add_squares(squares, final.at[core])
            remote(final.at[core], final.at[core], pair, back + i, mate).start()

    last_hop().start()
    for step in range(1, fsdp):
        bucket(step)
    bucket(0)
    spread(0)
    halves_in(0)
    halves_in(1)
    ring_b.first()
    spread(1)
    last_hop().wait_recv()
    sum_rows(out_a, [own, last_a])
    remote(out_a, in_a, pair, 5, (x_mate, col)).start()
    spread(2)
    pass_on(0)
    spread(3)
    ring_b.step(0)
    ring_b.step(1)
    pass_on(1)
    pass_on(2)
    arrived_here(0)
    accumulate(0, 0, 0, True)
    accumulate(0, 1, 0, False)
    spread(4)
    pass_on(3)
    ring_b.step(2)
    ring_b.step(3)
    spread(5)
    arrived_far(0)
    accumulate(1, 0, 0, True)
    accumulate(1, 1, 0, False)
    spread(6)
    pass_on(4)
    ring_b.step(4)
    ring_b.step(5)
    spread(7)
    pass_on(5)
    arrived_here(1)
    accumulate(0, 0, 1, False)
    accumulate(0, 1, 1, False)
    ring_b.step(6)
    swap_x(ring_b, (out_b, out_s), (in_b, in_s), 3)
    pass_on(6)
    pass_on(7)
    settle((out_a,), (in_a,), (sum_a,), 5, 9)
    arrived_far(1)
    accumulate(1, 0, 1, False)
    accumulate(1, 1, 1, False)

    def close(i, carry):
        span = pl.ds(pl.multiple_of(i * 32, 32), 32)
        value = (total[0, span, :] + total[1, span, :]).astype(jnp.bfloat16)
        half_low[span, :] = value
        wide = value.astype(jnp.float32)
        squares[0:1, :] += jnp.sum(wide * wide, 0, keepdims=True)
        return carry

    lax.fori_loop(0, half // 32, close, 0)
    mine = table_out.at[pl.ds(pl.multiple_of(core * half, 32), half), :]
    kept = pltpu.make_async_copy(half_low, mine, local_sem.at[3])
    kept.start()
    given = remote(half_low, mine, pair, 6, mate)
    given.start()
    settle((out_b, out_s), (in_b, in_s), (sum_b, sum_small), 3, 7)

    here = core * fsdp + col
    share[...] = jnp.broadcast_to(jnp.sum(squares[0:1, :], 1, keepdims=True), (8, 128))
    shares[pl.ds(here, 1)] = share[...][None]

    def norm_copy(step):
        other = lax.rem(here + step, 2 * fsdp)
        target = (row - core + other // fsdp, lax.rem(other, fsdp))
        return remote(share, shares.at[here], (norm_send, norm_recv), step, target)

    for step in range(1, 2 * fsdp):
        norm_copy(step).start()
    for step in range(1, 2 * fsdp):
        norm_copy(step).wait()
    norm = shares[0]
    for step in range(1, 2 * fsdp):
        norm = norm + shares[step]
    norm_out[...] = norm

    kept.wait()
    given.wait()
    for i, final in enumerate((sum_b, sum_small, sum_a)):
        other = final.at[1 - core]
        remote(other, other, pair, 7 + i, mate).wait()
    for index, (mine_out, theirs) in enumerate(((out_b, in_b), (out_s, in_s), (out_a, in_a))):
        remote(mine_out, theirs, pair, 3 + index, (x_mate, col)).wait_send()
    for index, mates in enumerate((mate_b, mate_s)):
        remote(mates, mates, pair, index, mate).wait_send()
    for step in range(1, fsdp):
        word_copy(step).wait_send()
    for copy in handed:
        copy.wait_send()
    last_hop().wait_send()
    ring_b.drain()


class flat_blocks:
    def __init__(self, ref):
        self.ref = ref

    @property
    def at(self):
        return self

    def __getitem__(self, block):
        return flat_rows(self.ref, block)


class flat_rows:
    def __init__(self, ref, block):
        self.ref, self.block = ref, block

    def __getitem__(self, key):
        span = key[0]
        rows = self.ref.shape[2]
        return self.ref[self.block, span.start // rows, pl.ds(lax.rem(span.start, rows), span.size), :]


def finish(grad, slot, held, feed_grads, qkv_grads, pos_grads, small_grads, depart, own, own_rows, cap):
    fsdp = LOOP_SIZE
    tokens = grad.shape[0]
    shard = D // fsdp
    pos_rows = pos_grads.shape[0] // fsdp
    rows_a, rows_b = 4 * shard, 2 * shard + pos_rows // 2
    half = own_rows // 2
    vmem = pl.BlockSpec(memory_space=pltpu.VMEM)
    anywhere = pl.BlockSpec(memory_space=pl.ANY)
    low, wide = jnp.bfloat16, jnp.float32
    return pl.pallas_call(
        functools.partial(finish_kernel, cap, own_rows),
        name="finish",
        in_specs=[vmem, vmem, vmem, anywhere, anywhere, anywhere, anywhere, vmem, vmem],
        out_specs=[anywhere, vmem, vmem, vmem, vmem],
        out_shape=[
            jax.ShapeDtypeStruct((own_rows, D), low),
            jax.ShapeDtypeStruct((2, rows_a, D), low),
            jax.ShapeDtypeStruct((2, rows_b, D), low),
            jax.ShapeDtypeStruct((2, 8, 128), wide),
            jax.ShapeDtypeStruct((8, 128), wide),
        ],
        scratch_shapes=[
            pltpu.VMEM((4, fsdp, cap, D), low),
            pltpu.VMEM((fsdp, cap, D), low),
            pltpu.VMEM((2, half, D), wide),
            pltpu.VMEM((half, D), low),
            pltpu.VMEM((rows_a, D), low),
            pltpu.VMEM((fsdp, rows_b, D), low),
            pltpu.VMEM((fsdp, rows_b, D), low),
            pltpu.VMEM((fsdp + 1, rows_b, D), low),
            pltpu.VMEM((fsdp, 8, 128), wide),
            pltpu.VMEM((fsdp, 8, 128), wide),
            pltpu.VMEM((fsdp + 1, 8, 128), wide),
            pltpu.VMEM((rows_a, D), low),
            pltpu.VMEM((rows_a, D), low),
            pltpu.VMEM((rows_b, D), low),
            pltpu.VMEM((rows_b, D), low),
            pltpu.VMEM((8, 128), wide),
            pltpu.VMEM((8, 128), wide),
            pltpu.VMEM((8, D), wide),
            pltpu.VMEM((8, 128), wide),
            pltpu.VMEM((2 * fsdp, 8, 128), wide),
            pltpu.SemaphoreType.DMA((4 * fsdp,)),
            pltpu.SemaphoreType.DMA((4 * fsdp,)),
            pltpu.SemaphoreType.DMA((15,)),
            pltpu.SemaphoreType.DMA((15,)),
            pltpu.SemaphoreType.DMA((10,)),
            pltpu.SemaphoreType.DMA((10,)),
            pltpu.SemaphoreType.DMA((2 * fsdp,)),
            pltpu.SemaphoreType.DMA((2 * fsdp,)),
            pltpu.SemaphoreType.DMA((4,)),
        ],
        compiler_params=pltpu.CompilerParams(
            collective_id=3, has_side_effects=True, vmem_limit_bytes=VMEM_GRANT
        ),
    )(
        grad,
        slot,
        held,
        feed_grads.reshape(-1, shard, D),
        qkv_grads.reshape(-1, shard, D),
        pos_grads.reshape(fsdp, pos_rows, D),
        small_grads,
        depart,
        own,
    )


def attend_back_pair(qkv, grad_mixed, logs, bias, masks, out, sums, rows, pair):
    at = pair * 128
    query = qkv[rows, at : at + 128] * jnp.bfloat16(0.125)
    keys = qkv[rows, D + at : D + at + 128]
    values = qkv[rows, 2 * D + at : 2 * D + at + 128]
    above = grad_mixed[rows, at : at + 128]
    queries = []
    key_sum = value_sum = None
    for side, mask in enumerate(masks):
        head = 2 * pair + side
        side_query = jnp.where(mask, query, jnp.zeros_like(query))
        side_above = jnp.where(mask, above, jnp.zeros_like(above))
        probs = jnp.exp(back_mul(side_query, keys) + (bias - logs[rows, head : head + 1]))
        grad_probs = back_mul(side_above, values)
        inner = jnp.sum(probs * grad_probs, -1, keepdims=True)
        grad_logits = (probs * (grad_probs - inner)).astype(jnp.bfloat16)
        side_value = outer_sum(probs.astype(jnp.bfloat16), side_above)
        side_key = outer_sum(grad_logits, side_query)
        queries.append(matmul(grad_logits, keys))
        value_sum = side_value if side == 0 else value_sum + side_value
        key_sum = side_key if side == 0 else key_sum + side_key
    grad_query = jnp.where(masks[0], queries[0], queries[1]) * 0.125
    out[rows, at : at + 128] = grad_query.astype(jnp.bfloat16)
    out[rows, D + at : D + at + 128] = key_sum.astype(jnp.bfloat16)
    out[rows, 2 * D + at : 2 * D + at + 128] = value_sum.astype(jnp.bfloat16)
    sums[2:3, at : at + 128] += jnp.sum(grad_query, 0, keepdims=True)
    sums[3:4, at : at + 128] += jnp.sum(value_sum, 0, keepdims=True)


def back_kernel(
    lengths,
    qkv,
    grad_mixed,
    logs,
    small,
    grad_r1,
    x,
    weight,
    feed_grads,
    x_out,
    pos_out,
    qkv_out,
    sums,
    depart,
    own,
    grad_qkv,
    r1_in,
    x_in,
    weight_in,
    low_h0,
    pos_sum,
    keep,
    mates,
    box,
    ring_send,
    ring_recv,
    pair_send,
    pair_recv,
    local_sem,
):
    fsdp = LOOP_SIZE
    row, col = lax.axis_index("dp"), lax.axis_index("fsdp")
    core = lax.rem(row, 2)
    mate = (row + 1 - 2 * core, col)
    place = grid_place(col)
    seq = LEN
    sentences = qkv.shape[0] // seq

    barrier = pltpu.get_barrier_semaphore()
    for there in (mate, (row, grid_device(place + 1)), (row, grid_device(place - 1))):
        pl.semaphore_signal(barrier, inc=1, device_id=there, device_id_type=MESH)
    pl.semaphore_wait(barrier, 3)

    def pair_copy(src, dst):
        return pltpu.make_async_remote_copy(
            src_ref=src,
            dst_ref=dst,
            send_sem=pair_send,
            recv_sem=pair_recv,
            device_id=mate,
            device_id_type=MESH,
        )

    def halves(which, target):
        if which == 0:
            return [(feed_grads.at[pl.ds(4 * b, 4)], target.at[b]) for b in range(fsdp)]
        return [(feed_grads.at[pl.ds(32 + 8 * j, 8)], target.at[:, j]) for j in range(4)]

    for which in range(2):

        @pl.when(core == which)
        def _(which=which):
            for src, dst in halves(1 - which, mates):
                pair_copy(src, dst).start()
            for src, dst in halves(which, keep):
                pltpu.make_async_copy(src, dst, local_sem.at[0]).start()

    fills = [
        pltpu.make_async_copy(grad_r1, r1_in, local_sem.at[1]),
        pltpu.make_async_copy(x, x_in, local_sem.at[2]),
        pltpu.make_async_copy(weight.at[pl.ds(0, 3 * D), :], weight_in, local_sem.at[3]),
    ]
    for fill in fills:
        fill.start()

    ring = Ring([(flat_blocks(keep), flat_blocks(mates), box)], 1, ring_send, ring_recv, 0)
    sums[...] = jnp.zeros_like(sums)
    masks = head_masks(seq)
    done = 0
    for sentence in range(sentences):
        bias = live_row(lengths[sentence], seq)
        rows = slice(sentence * seq, (sentence + 1) * seq)
        for pair in range(H // 2):
            attend_back_pair(qkv, grad_mixed, logs, bias, masks, grad_qkv, sums, rows, pair)
            done += 1
            if done == 4:
                pltpu.make_async_copy(keep, keep, local_sem.at[0]).wait()
                pair_copy(mates, mates).wait_recv()
                ring.first()
            if done == 10:
                ring.step(0)
                ring.step(1)
    for fill in fills:
        fill.wait()
    pos_sum[...] = jnp.zeros_like(pos_sum)

    def tile(i, carry):
        span = pl.ds(pl.multiple_of(i * TILE, TILE), TILE)
        grad_h0 = r1_in[span, :]
        for third in range(3):
            cols = slice(third * D, (third + 1) * D)
            grad_h0 = grad_h0 + back_mul(grad_qkv[span, cols], weight_in[cols, :])
        hat, scale = normed(x_in[span, :])
        low_h0[span, :] = (hat * small[0:1, :] + small[1:2, :]).astype(jnp.bfloat16)
        grad_x, gain, shift = norm_back(grad_h0, hat, scale, small[0:1, :])
        add_row(sums, 0, gain)
        add_row(sums, 1, shift)
        x_out[span, :] = grad_x.astype(jnp.bfloat16)
        spot = pl.ds(pl.multiple_of(lax.rem(i, seq // TILE) * TILE, TILE), TILE)
        pos_sum[spot, :] += grad_x
        return carry

    lax.fori_loop(0, sentences * seq // TILE, tile, 0)
    pos_out[...] = pos_sum[...].astype(jnp.bfloat16)
    ring.step(2)
    ring.step(3)
    for third in range(3):
        cols = slice(third * D, (third + 1) * D)
        qkv_out[cols, :] = outer_sum(low_h0[...], grad_qkv[:, cols]).astype(jnp.bfloat16)
    right, left = ring.slot[(3, 1)], ring.slot[(3, -1)]
    for slot in (right, left):
        for copy in ring.copies(slot, ring.events[slot]):
            copy.wait_recv()
    ahead = grid_device(place + 1)
    sum_rows(depart, [ring.parts[0][0].at[ahead], ring.parts[0][1].at[ahead], box.at[right]])
    sum_rows(own, [ring.parts[0][0].at[col], ring.parts[0][1].at[col], box.at[left]])
    pair_copy(mates, mates).wait_send()
    ring.drain()


def back(lengths, qkv, grad_mixed, logs, small, grad_r1, x, weight, feed_grads):
    fsdp = LOOP_SIZE
    tokens = qkv.shape[0]
    shard = D // fsdp
    vmem = pl.BlockSpec(memory_space=pltpu.VMEM)
    anywhere = pl.BlockSpec(memory_space=pl.ANY)
    low, wide = jnp.bfloat16, jnp.float32
    return pl.pallas_call(
        back_kernel,
        name="back",
        in_specs=[pl.BlockSpec(memory_space=pltpu.SMEM)] + [vmem] * 4 + [anywhere] * 4,
        out_specs=[vmem] * 6,
        out_shape=[
            jax.ShapeDtypeStruct((tokens, D), low),
            jax.ShapeDtypeStruct((LEN, D), low),
            jax.ShapeDtypeStruct((3 * D, D), low),
            jax.ShapeDtypeStruct((16, D), wide),
            jax.ShapeDtypeStruct((4 * shard, D), low),
            jax.ShapeDtypeStruct((4 * shard, D), wide),
        ],
        scratch_shapes=[
            pltpu.VMEM((tokens, 3 * D), low),
            pltpu.VMEM((tokens, D), wide),
            pltpu.VMEM((tokens, D), wide),
            pltpu.VMEM((3 * D, D), low),
            pltpu.VMEM((tokens, D), low),
            pltpu.VMEM((LEN, D), wide),
            pltpu.VMEM((fsdp, 4, shard, D), low),
            pltpu.VMEM((fsdp, 4, shard, D), low),
            pltpu.VMEM((fsdp + 1, 4 * shard, D), low),
            pltpu.SemaphoreType.DMA((7,)),
            pltpu.SemaphoreType.DMA((7,)),
            pltpu.SemaphoreType.DMA,
            pltpu.SemaphoreType.DMA,
            pltpu.SemaphoreType.DMA((4,)),
        ],
        compiler_params=pltpu.CompilerParams(
            collective_id=4, has_side_effects=True, vmem_limit_bytes=VMEM_GRANT
        ),
    )(lengths, qkv, grad_mixed, logs, small, grad_r1, x, weight, feed_grads.reshape(-1, shard, D))


LOOP = {8: (0, 2, 4, 6, 7, 5, 3, 1)}


def swap_core(value):
    return lax.ppermute(value, "dp", [(i, i ^ 1) for i in range(lax.axis_size("dp"))])


def swap_x(value):
    count = lax.axis_size("dp")
    return lax.ppermute(value, "dp", [(i, (i + 2) % count) for i in range(count)])


def sum_x(value):
    count = lax.axis_size("dp")
    total = value
    for hop in range(2, count, 2):
        moved = lax.ppermute(value, "dp", [(i, (i + hop) % count) for i in range(count)])
        total = total.astype(jnp.float32) + moved.astype(jnp.float32)
    return total


def shift(value, step):
    loop = LOOP[lax.axis_size("fsdp")]
    size = len(loop)
    return lax.ppermute(
        value, "fsdp", [(loop[i], loop[(i + step) % size]) for i in range(size)]
    )


def loop_place():
    loop = LOOP[lax.axis_size("fsdp")]
    place = [0] * len(loop)
    for i, device in enumerate(loop):
        place[device] = i
    return jnp.array(place, jnp.int32)[lax.axis_index("fsdp")], jnp.array(loop, jnp.int32)


def ring_gather(part, sign):
    size = lax.axis_size("fsdp")
    place, loop = loop_place()
    out = jnp.zeros((size,) + part.shape, part.dtype)

    def put(out, block, offset):
        at = loop[lax.rem(place + offset + size, size)]
        return lax.dynamic_update_slice(out, block[None], (at, 0, 0))

    out = put(out, part, 0)
    ahead = behind = part
    for hop in range(1, size // 2 + 1):
        ahead = shift(ahead, sign)
        out = put(out, ahead, -sign * hop)
        if hop < size - size // 2:
            behind = shift(behind, -sign)
            out = put(out, behind, sign * hop)
    return out


def ring_reduce(parts, sign):
    size = lax.axis_size("fsdp")
    place, loop = loop_place()

    def local(offset):
        at = loop[lax.rem(place + offset + size, size)]
        return lax.dynamic_index_in_dim(parts, at, 0, keepdims=False).astype(jnp.float32)

    def flow(direction, hops):
        arrived = None
        for hop in range(hops):
            value = local(direction * (hops - hop))
            if arrived is not None:
                value = value + arrived.astype(jnp.float32)
            arrived = shift(value.astype(jnp.bfloat16), direction)
        return arrived

    far = flow(sign, size // 2)
    near = flow(-sign, size - size // 2 - 1)
    return local(0) + far.astype(jnp.float32) + near.astype(jnp.float32)


def gather_halves(first, second, sign):
    core = lax.rem(lax.axis_index("dp"), 2)
    if lax.axis_size("fsdp") not in LOOP:
        return lax.all_gather(first, "fsdp", axis=0), lax.all_gather(second, "fsdp", axis=0)
    mine = ring_gather(jnp.where(core == 0, first, second), sign)
    other = swap_core(mine)
    return jnp.where(core == 0, mine, other), jnp.where(core == 0, other, mine)


def reduce_halves(first, second, sign):
    core = lax.rem(lax.axis_index("dp"), 2)
    give = jnp.where(core == 0, second, first).astype(jnp.bfloat16)
    keep = jnp.where(core == 0, first, second).astype(jnp.float32)
    chip = (keep + swap_core(give).astype(jnp.float32)).astype(jnp.bfloat16)
    if lax.axis_size("fsdp") in LOOP:
        block = ring_reduce(chip, sign)
    else:
        block = lax.psum_scatter(chip.astype(jnp.float32), "fsdp", scatter_dimension=0)
    total = sum_x(block.astype(jnp.bfloat16)).astype(jnp.bfloat16)
    other = swap_core(total)
    low = jnp.where(core == 0, total, other).astype(jnp.float32)
    high = jnp.where(core == 0, other, total).astype(jnp.float32)
    return low, high


def split_rows(weight, parts):
    return jnp.concatenate(jnp.split(weight, parts, axis=1), axis=0)


def join_rows(blocks, parts):
    count, rows, width = blocks.shape
    return (
        blocks.reshape(count, parts, rows // parts, width)
        .transpose(0, 2, 1, 3)
        .reshape(count * rows // parts, parts * width)
    )


def cut_parts(grad, count, parts):
    width = grad.shape[-1]
    return (
        grad.reshape(parts, count, -1, width).transpose(1, 0, 2, 3).reshape(count, -1, width)
    )


def pad_rows(value, rows):
    return jnp.pad(value, [(0, 0)] * (value.ndim - 2) + [(0, rows - value.shape[-2]), (0, 0)])


def round_up(value, step):
    return -(-value // step) * step


def bucket_size(tokens, owners):
    mean = tokens / owners
    return min(tokens, round_up(int(mean + 5.6 * math.sqrt(mean)), 16))


def one_hot(index, count):
    return (index[:, None] == lax.iota(jnp.int32, count)[None, :]).astype(jnp.bfloat16)


class Routes:
    def __init__(self, everyone, own_rows):
        fsdp = lax.axis_size("fsdp")
        self.rows = own_rows
        tokens = everyone.shape[1]
        self.cap = bucket_size(tokens, fsdp)
        me = lax.axis_index("fsdp")
        group = lax.dynamic_slice_in_dim(everyone, lax.axis_index("dp") * fsdp, fsdp, 0)
        mine = lax.dynamic_index_in_dim(group, me, 0, keepdims=False)
        owners = lax.iota(jnp.int32, fsdp)
        every_count = jnp.sum(
            (everyone // own_rows)[:, :, None] == owners[None, None, :], 1, dtype=jnp.int32
        )
        self.rounds = (jnp.max(every_count) + self.cap - 1) // self.cap
        self.inner = group - me * own_rows
        self.held = (self.inner >= 0) & (self.inner < own_rows)
        self.held_place = jnp.cumsum(self.held.astype(jnp.int32), 1) - 1
        self.owner = mine // own_rows
        hot = (self.owner[None, :] == owners[:, None])
        place = jnp.cumsum(hot.astype(jnp.int32), 1) - 1
        self.hot = hot
        self.place = place
        self.my_place = jnp.sum(jnp.where(hot, place, 0), 0)

    def slots(self, flag, place, value, turn):
        slot = lax.iota(jnp.int32, self.cap)[None, :, None] + turn * self.cap
        hit = flag[:, None, :] & (place[:, None, :] == slot)
        return (jnp.sum(jnp.where(hit, value[:, None, :] + 1, 0), -1) - 1).reshape(-1)

    def owner_rows(self, turn):
        return self.slots(self.held, self.held_place, self.inner, turn)

    def asker_tokens(self, turn):
        tokens = lax.iota(jnp.int32, self.owner.shape[0])[None, :]
        return self.slots(self.hot, self.place, tokens, turn)

    def asker_slots(self, turn):
        place = self.my_place - turn * self.cap
        inside = (place >= 0) & (place < self.cap)
        return jnp.where(inside, self.owner * self.cap + place, -1)


def exchange(rows):
    fsdp = lax.axis_size("fsdp")
    blocks = rows.reshape(fsdp, rows.shape[0] // fsdp, rows.shape[1])
    return lax.all_to_all(blocks, "fsdp", 0, 0).reshape(rows.shape)


def pick_kernel(index, table, out):
    rows = lax.broadcasted_iota(jnp.int32, (index.shape[0], table.shape[0]), 1)
    pick = (index[:, 0:1] == rows).astype(jnp.bfloat16)
    out[...] = matmul(pick, table[...].astype(jnp.bfloat16)).astype(jnp.bfloat16)


def gather_table(table, routes, turn):
    index = routes.owner_rows(turn)
    size = routes.cap
    return call(
        pick_kernel,
        "pick_rows",
        (index.shape[0] // size,),
        [rows_spec(128, size), whole_spec(table.shape)],
        [rows_spec(D, size)],
        [jax.ShapeDtypeStruct((index.shape[0], D), jnp.bfloat16)],
        flops=2 * index.shape[0] * D * table.shape[0],
        moved=table.shape[0] * D * 4,
    )(jnp.broadcast_to(index[:, None], (index.shape[0], 128)), table)[0]


def more_words(everyone, table, rounds, tokens):
    def more(carry):
        return carry[0] < rounds

    def body(carry):
        turn, words = carry
        ids, turn, rows = lax.optimization_barrier((everyone, turn, table))
        routes = Routes(ids, table.shape[0])
        got = exchange(gather_table(rows, routes, turn))
        mine = matmul(one_hot(routes.asker_slots(turn), got.shape[0]), got)
        return turn + 1, words + mine.astype(jnp.bfloat16)

    start = (jnp.int32(1), jnp.zeros((tokens, D), jnp.bfloat16))
    return lax.while_loop(more, body, start)[1]


def return_round(grad_low, everyone, turn, rows):
    routes = Routes(everyone, rows)
    held = routes.owner_rows(turn)[None, :]
    sent = bucket_rows(routes.asker_slots(turn)[None, :], grad_low, held.shape[1])
    return scatter_rows(held, exchange(sent), rows)


def return_rows(grad_low, everyone, rounds, rows):
    def more(carry):
        return carry[0] < rounds

    def body(carry):
        turn, total = carry
        ids, turn = lax.optimization_barrier((everyone, turn))
        return turn + 1, total + return_round(grad_low, ids, turn, rows)

    return lax.while_loop(more, body, (jnp.int32(0), jnp.zeros((rows, D), jnp.float32)))[1]


def more_grads(grad_low, plan, table, squares):
    def more(carry):
        return carry[0] < plan.rounds

    def body(carry):
        turn, table, squares = carry
        ids, turn = lax.optimization_barrier((plan.everyone, turn))
        before = table.astype(jnp.float32)
        after = (before + sum_groups(return_round(grad_low, ids, turn, table.shape[0]))).astype(
            jnp.bfloat16
        )
        change = jnp.sum(after.astype(jnp.float32) ** 2) - jnp.sum(before * before)
        return turn + 1, after, squares + lax.psum(change, "fsdp")

    return lax.while_loop(more, body, (jnp.int32(1), table, squares))[1:]


def total_grads(everyone, rounds, grad_x, feed_grads, qkv_grads, grad_pos, grad_small, own_rows):
    fsdp = lax.axis_size("fsdp")
    down, up = reduce_halves(
        feed_grads[:FF].reshape(fsdp, -1, D), cut_parts(feed_grads[FF : 2 * FF], fsdp, 4), 1
    )
    qkv_cut = cut_parts(qkv_grads, fsdp, 3)
    shard = qkv_cut.shape[1] // 3
    pos_cut = grad_pos.reshape(fsdp, -1, D)
    half_pos = pos_cut.shape[1] // 2
    low, high = reduce_halves(
        jnp.concatenate([qkv_cut[:, : 2 * shard], pos_cut[:, :half_pos]], 1),
        jnp.concatenate(
            [
                qkv_cut[:, 2 * shard :],
                feed_grads[2 * FF :].reshape(fsdp, shard, D),
                pos_cut[:, half_pos:],
            ],
            1,
        ),
        -1,
    )
    cols = D // fsdp
    small = lax.dynamic_slice_in_dim(
        lax.psum(grad_small, ("dp", "fsdp")), lax.axis_index("fsdp") * cols, cols, 1
    )
    small = jnp.pad(small, ((0, 0), (0, 128 - cols)))
    table = sum_groups(return_rows(grad_x, everyone, rounds, own_rows))
    squares = sum(jnp.sum(part * part) for part in (table, down, up, low, high, small))
    squares = jnp.sum(gather_small(jnp.full((8, 128), squares), False, 2)[:, 0, 0])
    return (
        table.astype(jnp.bfloat16),
        jnp.stack([down, up]).astype(jnp.bfloat16),
        jnp.stack([low, high]).astype(jnp.bfloat16),
        small,
        squares,
    )


class Plan:
    def __init__(self, ids, pieces, pos_low, small, table):
        fsdp = lax.axis_size("fsdp")
        tokens = ids.shape[0]
        cap = self.cap = bucket_size(tokens, fsdp)
        cols = small.shape[1]
        block = jnp.pad(small, ((0, 2), (0, 128 - cols)))
        if fsdp == LOOP_SIZE and lax.axis_size("dp") == 4:
            everyone, self.weight, self.pos, smalls, got, held, row, col, most = fetch(
                ids.reshape(1, tokens), pieces, pos_low, block, table, cap
            )
            self.everyone = everyone.reshape(-1, tokens)
            self.rounds = (most[0, 0] + cap - 1) // cap
            self.direct = True
            self.asker_row, self.asker_col = row, col
            self.held = held.reshape(4, 1, -1)
            self.got = got.reshape(-1, D)
        else:
            self.direct = False
            self.everyone = gather_small(ids.reshape(-1, 128), True, 0).reshape(-1, tokens)
            routes = Routes(self.everyone, table.shape[0])
            self.rounds = routes.rounds
            slot = routes.asker_slots(0)
            self.asker_col = jnp.broadcast_to(slot[:, None], (tokens, 128))
            self.got = exchange(gather_table(table, routes, 0))
            both = lax.all_gather(pieces, "fsdp", axis=0)
            early = pieces.shape[0] * 2 // 3
            self.weight = jnp.concatenate(
                [
                    both[:, :early].reshape(fsdp, 8, -1, D).transpose(1, 0, 2, 3).reshape(-1, D),
                    both[:, early:].reshape(-1, D),
                ],
                0,
            )
            self.pos = lax.all_gather(pos_low, "fsdp", axis=0, tiled=True)
            smalls = lax.all_gather(block, "fsdp", axis=0)
        self.small = (
            smalls[:, :, :cols].transpose(1, 0, 2).reshape(16, D).astype(jnp.float32)
        )
        self.extra = more_words(self.everyone, table, self.rounds, tokens)


def sum_groups(table):
    core = lax.rem(lax.axis_index("dp"), 2)
    half = table.shape[0] // 2
    low = table.astype(jnp.bfloat16)
    keep = lax.dynamic_slice_in_dim(table, core * half, half, 0)
    give = lax.dynamic_slice_in_dim(low, (1 - core) * half, half, 0)
    chip = (keep + swap_core(give).astype(jnp.float32)).astype(jnp.bfloat16)
    total = sum_x(chip).astype(jnp.bfloat16)
    other = swap_core(total)
    return jnp.concatenate(
        [jnp.where(core == 0, total, other), jnp.where(core == 0, other, total)], 0
    ).astype(jnp.float32)


def renew(weight, moment, average, grad, factor):
    step = factor * grad
    buffer = MOMENTUM * moment + step
    fresh = weight - RATE * (step + MOMENTUM * buffer)
    return (fresh, buffer, KEEP * average + (1.0 - KEEP) * fresh)


def shards(
    token_ids,
    lengths,
    pair_ids,
    scores,
    word_table,
    pos_table,
    qkv_weight,
    out_weight,
    up_weight,
    down_weight,
    small_params,
    word_moment,
    pos_moment,
    qkv_moment,
    out_moment,
    up_moment,
    down_moment,
    small_moment,
    word_average,
    pos_average,
    qkv_average,
    out_average,
    up_average,
    down_average,
    small_average,
):
    batch, seq = token_ids.shape
    width = D
    fsdp = lax.axis_size("fsdp")
    tokens = batch * seq
    shard = qkv_weight.shape[0]
    pos_rows = pos_table.shape[0]
    small_cols = small_params.shape[1]
    pieces = jnp.concatenate(
        [
            split_rows(qkv_weight.astype(jnp.bfloat16), 3),
            out_weight.astype(jnp.bfloat16),
            split_rows(up_weight.astype(jnp.bfloat16), 4),
            down_weight.astype(jnp.bfloat16),
        ],
        0,
    )
    plan = Plan(
        token_ids.reshape(-1),
        pieces,
        pos_table.astype(jnp.bfloat16),
        small_params.astype(jnp.bfloat16),
        word_table,
    )
    weight, small_full = plan.weight, plan.small
    x, h0, qkv = embed(plan.asker_col, plan.got, plan.extra, plan.pos, weight, small_full)
    mixed, logs = attend(lengths, qkv, seq)
    r1, low_h1, act, slope, r2, pooled = feed(lengths, mixed, h0, weight, small_full)
    pooled_all = gather_small(pooled[:, 0].reshape(-1, 128), True, 1).reshape(-1, width)
    loss, pull_loss = jax.vjp(lambda rows: pair_loss(rows, pair_ids, scores), pooled_all)
    grad_all = pull_loss(jnp.ones((), jnp.float32))[0]
    grad_pooled = lax.dynamic_slice_in_dim(
        grad_all, lax.axis_index(("dp", "fsdp")) * batch, batch, 0
    )
    share = jnp.broadcast_to(
        (grad_pooled / lengths.astype(jnp.float32)[:, None])[:, None, :], (batch, 8, width)
    )
    low_f, low_u, grad_r1, low_a, grad_mixed, sums_feed = feed_back(
        lengths, share, r1, r2, slope, weight, small_full
    )
    feed_grads = feed_weights(act, low_f, low_h1, low_u, mixed, low_a)
    own_rows = word_table.shape[0]
    if plan.direct:
        grad_x, low_pos, qkv_grads, sums_back, depart, own = back(
            lengths, qkv, grad_mixed, logs, small_full, grad_r1, x, weight, feed_grads
        )
        grad_small = sums_feed + sums_back
        small_cut = jnp.pad(
            grad_small.reshape(16, fsdp, small_cols).transpose(1, 0, 2),
            ((0, 0), (0, 0), (0, 128 - small_cols)),
        )
        table, sum_a, sum_b, small, squares = finish(
            grad_x,
            plan.asker_row,
            plan.held,
            feed_grads,
            qkv_grads,
            low_pos,
            small_cut,
            depart,
            own,
            own_rows,
            plan.cap,
        )
        small = small.reshape(16, 128)
        table, total = more_grads(grad_x, plan, table, squares[0, 0])
    else:
        grad_qkv, sums_attend = attend_back(lengths, qkv, grad_mixed, logs, seq)
        grad_x, grad_pos, sums_embed = embed_back(grad_r1, grad_qkv, weight, x, small_full, seq)
        qkv_grads = qkv_weights(h0, grad_qkv)
        grad_small = sums_feed + sums_attend + sums_embed
        table, sum_a, sum_b, small, total = total_grads(
            plan.everyone,
            plan.rounds,
            grad_x,
            feed_grads,
            qkv_grads,
            grad_pos.astype(jnp.bfloat16),
            grad_small,
            own_rows,
        )
    wide_b = sum_b.astype(jnp.float32)
    summed = (
        table.astype(jnp.float32),
        wide_b[:, 2 * shard :].reshape(pos_rows, width),
        jnp.concatenate([wide_b[0, :shard], wide_b[0, shard : 2 * shard], wide_b[1, :shard]], 1),
        wide_b[1, shard : 2 * shard],
        join_rows(sum_a[1][None], 4).astype(jnp.float32),
        sum_a[0].astype(jnp.float32),
        small[:14, :small_cols],
    )
    norm = jnp.sqrt(total)
    limit = 1e-05 * math.sqrt((VOCAB + LEN + 4 * D + 2 * FF + 14) * D)
    factor = jnp.minimum(1.0, limit / (norm + 1e-06))
    weights = (word_table, pos_table, qkv_weight, out_weight, up_weight, down_weight, small_params)
    moments = (
        word_moment,
        pos_moment,
        qkv_moment,
        out_moment,
        up_moment,
        down_moment,
        small_moment,
    )
    averages = (
        word_average,
        pos_average,
        qkv_average,
        out_average,
        up_average,
        down_average,
        small_average,
    )
    new_w = []
    new_m = []
    new_a = []
    for weight, moment, average, grad in zip(weights, moments, averages, summed):
        fresh, buffer, mean_new = renew(weight, moment, average, grad, factor)
        new_w.append(fresh)
        new_m.append(buffer)
        new_a.append(mean_new)
    return (
        loss,
        norm,
        new_w[0],
        new_w[1],
        new_w[2],
        new_w[3],
        new_w[4],
        new_w[5],
        new_w[6],
        new_m[0],
        new_m[1],
        new_m[2],
        new_m[3],
        new_m[4],
        new_m[5],
        new_m[6],
        new_a[0],
        new_a[1],
        new_a[2],
        new_a[3],
        new_a[4],
        new_a[5],
        new_a[6],
    )


def solution(mesh):
    placed = (
        P(("dp", "fsdp"), None),
        P(("dp", "fsdp")),
        P(),
        P(),
        P("fsdp", None),
        P("fsdp", None),
        P("fsdp", None),
        P("fsdp", None),
        P("fsdp", None),
        P("fsdp", None),
        P(None, "fsdp"),
        P("fsdp", None),
        P("fsdp", None),
        P("fsdp", None),
        P("fsdp", None),
        P("fsdp", None),
        P("fsdp", None),
        P(None, "fsdp"),
        P("fsdp", None),
        P("fsdp", None),
        P("fsdp", None),
        P("fsdp", None),
        P("fsdp", None),
        P("fsdp", None),
        P(None, "fsdp"),
    )
    return jax.shard_map(
        shards,
        mesh=mesh,
        in_specs=placed,
        out_specs=(
            P(),
            P(),
            P("fsdp", None),
            P("fsdp", None),
            P("fsdp", None),
            P("fsdp", None),
            P("fsdp", None),
            P("fsdp", None),
            P(None, "fsdp"),
            P("fsdp", None),
            P("fsdp", None),
            P("fsdp", None),
            P("fsdp", None),
            P("fsdp", None),
            P("fsdp", None),
            P(None, "fsdp"),
            P("fsdp", None),
            P("fsdp", None),
            P("fsdp", None),
            P("fsdp", None),
            P("fsdp", None),
            P("fsdp", None),
            P(None, "fsdp"),
        ),
        check_vma=False,
    )
```

```python
import functools
import math

import jax
import jax.numpy as jnp
from jax import lax
from jax.experimental import pallas as pl
from jax.experimental.pallas import tpu as pltpu
from jax.sharding import PartitionSpec as P

D = 768
H = 12
FF = 3072
VOCAB = 30720
LEN = 512


MOMENTUM = 0.9
RATE = 3000.0
KEEP = 0.9


def matmul(left, right):
    return jnp.dot(left, right, preferred_element_type=jnp.float32)


def outer_sum(left, right):
    return lax.dot_general(
        left, right, (((0,), (0,)), ((), ())), preferred_element_type=jnp.float32
    )


def back_mul(grad, weight):
    return lax.dot_general(
        grad, weight, (((1,), (1,)), ((), ())), preferred_element_type=jnp.float32
    )


TILE = 256
EPS = 1e-12
VMEM_GRANT = 60 * 1024 * 1024


def whole_spec(shape):
    return pl.BlockSpec(shape, lambda *_: (0,) * len(shape))


def rows_spec(width, rows=TILE):
    return pl.BlockSpec((rows, width), lambda i, *_: (i, 0))


def weight_spec(rows, at):
    return pl.BlockSpec((rows, D), lambda i, *_: (at, 0))


def call(kernel, name, grid, in_specs, out_specs, out_shape, scratch=(), prefetch=0, flops=0, moved=0):
    return pl.pallas_call(
        kernel,
        name=name,
        grid_spec=pltpu.PrefetchScalarGridSpec(
            num_scalar_prefetch=prefetch,
            grid=grid,
            in_specs=in_specs,
            out_specs=out_specs,
            scratch_shapes=scratch,
        ),
        out_shape=out_shape,
        compiler_params=pltpu.CompilerParams(vmem_limit_bytes=VMEM_GRANT),
        cost_estimate=pl.CostEstimate(flops=flops, bytes_accessed=moved, transcendentals=0),
    )


def normed(v):
    mean = jnp.mean(v, -1, keepdims=True)
    cent = v - mean
    scale = lax.rsqrt(jnp.mean(cent * cent, -1, keepdims=True) + EPS)
    return cent * scale, scale


def norm_back(grad, hat, scale, gain):
    inner = grad * gain
    middle = jnp.mean(inner, -1, keepdims=True)
    along = jnp.mean(inner * hat, -1, keepdims=True)
    return (
        scale * (inner - middle - hat * along),
        jnp.sum(grad * hat, 0, keepdims=True),
        jnp.sum(grad, 0, keepdims=True),
    )


def add_row(ref, row, value):
    ref[row : row + 1, :] += value


def embed_kernel(slot, got, extra, pos, weight, small, x_out, h0_out, qkv_out):
    count = got.shape[0]
    pick = (slot[:, 0:1] == lax.broadcasted_iota(jnp.int32, (slot.shape[0], count), 1)).astype(
        jnp.bfloat16
    )
    words = matmul(pick, got[...]) + extra[...].astype(jnp.float32)
    x = words + pos[...].astype(jnp.float32)
    hat, _ = normed(x)
    h0 = hat * small[0:1, :] + small[1:2, :]
    x_out[...] = x
    h0_out[...] = h0
    low = h0.astype(jnp.bfloat16)
    for third, bias in enumerate((2, None, 3)):
        value = matmul(low, weight[third * D : (third + 1) * D, :])
        if bias is not None:
            value = value + small[bias : bias + 1, :]
        qkv_out[:, third * D : (third + 1) * D] = value.astype(jnp.bfloat16)


def embed(slot, got, extra, pos, weight, small):
    tokens = slot.shape[0]
    turns = pos.shape[0] // TILE
    return call(
        embed_kernel,
        "embed_qkv",
        (tokens // TILE,),
        [
            rows_spec(128),
            whole_spec(got.shape),
            rows_spec(D),
            pl.BlockSpec((TILE, D), lambda i: (lax.rem(i, turns), 0)),
            weight_spec(3 * D, 0),
            whole_spec(small.shape),
        ],
        [rows_spec(D), rows_spec(D), rows_spec(3 * D)],
        [
            jax.ShapeDtypeStruct((tokens, D), jnp.float32),
            jax.ShapeDtypeStruct((tokens, D), jnp.float32),
            jax.ShapeDtypeStruct((tokens, 3 * D), jnp.bfloat16),
        ],
        flops=2 * tokens * D * (3 * D + got.shape[0]),
        moved=tokens * D * 20,
    )(slot, got, extra, pos, weight, small)


def head_masks(rows):
    lane = lax.broadcasted_iota(jnp.int32, (rows, 128), 1)
    return (lane < 64, lane >= 64)


def live_row(length, seq):
    return jnp.where(
        lax.broadcasted_iota(jnp.int32, (1, seq), 1) < length, 0.0, -1000000000.0
    ).astype(jnp.float32)


def attend_pair(qkv, bias, masks, logs, mixed_out, rows, pair):
    at = pair * 128
    query = qkv[rows, at : at + 128] * jnp.bfloat16(0.125)
    keys = qkv[rows, D + at : D + at + 128]
    values = qkv[rows, 2 * D + at : 2 * D + at + 128]
    lane = lax.broadcasted_iota(jnp.int32, logs.shape, 1)
    sides = []
    for side, mask in enumerate(masks):
        logits = back_mul(jnp.where(mask, query, jnp.zeros_like(query)), keys) + bias
        top = jnp.max(logits, -1, keepdims=True)
        raised = jnp.exp(logits - top)
        total = jnp.sum(raised, -1, keepdims=True)
        probs = (raised * (1.0 / total)).astype(jnp.bfloat16)
        sides.append(matmul(probs, values))
        logs = jnp.where(lane == 2 * pair + side, top + jnp.log(total), logs)
    mixed_out[rows, at : at + 128] = jnp.where(masks[0], sides[0], sides[1]).astype(jnp.bfloat16)
    return logs


def attend_kernel(lengths, qkv, mixed_out, log_out):
    seq = qkv.shape[0]
    bias = live_row(lengths[pl.program_id(0)], seq)
    masks = head_masks(seq)
    logs = jnp.zeros((seq, 128), jnp.float32)
    for pair in range(H // 2):
        logs = attend_pair(qkv, bias, masks, logs, mixed_out, slice(0, seq), pair)
    log_out[...] = logs


def attend(lengths, qkv, seq):
    tokens = qkv.shape[0]
    return call(
        attend_kernel,
        "attention",
        (tokens // seq,),
        [rows_spec(3 * D, seq)],
        [rows_spec(D, seq), rows_spec(128, seq)],
        [
            jax.ShapeDtypeStruct((tokens, D), jnp.bfloat16),
            jax.ShapeDtypeStruct((tokens, 128), jnp.float32),
        ],
        prefetch=1,
        flops=4 * tokens * seq * D,
        moved=tokens * D * 8,
    )(lengths, qkv)


def feed_kernel(
    lengths, mixed, h0, out_w, up_w, down_w, small, r1_out, h1_out, act_out, slope_out, r2_out, pooled
):
    step = pl.program_id(0)
    turns = LEN // TILE
    r1 = h0[...] + (matmul(mixed[...], out_w[...]) + small[4:5, :])
    hat, _ = normed(r1)
    h1 = hat * small[5:6, :] + small[6:7, :]
    low = h1.astype(jnp.bfloat16)
    r1_out[...] = r1
    h1_out[...] = low
    ffn = jnp.zeros(r1.shape, jnp.float32)
    for part in range(FF // D):
        up = matmul(low, up_w[part * D : (part + 1) * D, :]) + small[7 + part : 8 + part, :]
        below = 0.5 * (1.0 + lax.erf(up * math.sqrt(0.5)))
        act = (up * below).astype(jnp.bfloat16)
        slope = below + up * jnp.exp(-0.5 * up * up) * (1.0 / math.sqrt(2.0 * math.pi))
        act_out[:, part * D : (part + 1) * D] = act
        slope_out[:, part * D : (part + 1) * D] = slope.astype(jnp.bfloat16)
        ffn = ffn + matmul(act, down_w[part * D : (part + 1) * D, :])
    r2 = h1 + (ffn + small[11:12, :])
    r2_out[...] = r2
    hat2, _ = normed(r2)
    h2 = hat2 * small[12:13, :] + small[13:14, :]
    length = lengths[step // turns]
    at = lax.rem(step, turns) * TILE + lax.broadcasted_iota(jnp.int32, (TILE, 1), 0)
    part_sum = jnp.sum(jnp.where(at < length, h2, 0.0), 0, keepdims=True)

    @pl.when(lax.rem(step, turns) == 0)
    def _():
        pooled[...] = jnp.zeros_like(pooled)

    pooled[0, 0:1, :] += part_sum / length.astype(jnp.float32)


def feed(lengths, mixed, h0, first, second, small):
    tokens = mixed.shape[0]
    turns = LEN // TILE
    return call(
        feed_kernel,
        "feed_forward",
        (tokens // TILE,),
        [
            rows_spec(D),
            rows_spec(D),
            weight_spec(D, 3),
            weight_spec(FF, 0),
            weight_spec(FF, 1),
            whole_spec(small.shape),
        ],
        [
            rows_spec(D),
            rows_spec(D),
            rows_spec(FF),
            rows_spec(FF),
            rows_spec(D),
            pl.BlockSpec((1, 8, D), lambda i, *_: (i // turns, 0, 0)),
        ],
        [
            jax.ShapeDtypeStruct((tokens, D), jnp.float32),
            jax.ShapeDtypeStruct((tokens, D), jnp.bfloat16),
            jax.ShapeDtypeStruct((tokens, FF), jnp.bfloat16),
            jax.ShapeDtypeStruct((tokens, FF), jnp.bfloat16),
            jax.ShapeDtypeStruct((tokens, D), jnp.float32),
            jax.ShapeDtypeStruct((tokens // LEN, 8, D), jnp.float32),
        ],
        prefetch=1,
        flops=2 * tokens * D * (D + 2 * FF),
        moved=tokens * D * 32,
    )(lengths, mixed, h0, first, second, second, small)


def feed_back_kernel(
    lengths, share, r1, r2, slope, out_w, up_w, down_w, small, f_out, u_out, r1_grad, a_out, mixed_out, sums
):
    step = pl.program_id(0)
    turns = LEN // TILE

    @pl.when(step == 0)
    def _():
        sums[...] = jnp.zeros_like(sums)

    length = lengths[step // turns]
    at = lax.rem(step, turns) * TILE + lax.broadcasted_iota(jnp.int32, (TILE, 1), 0)
    grad_h2 = jnp.where(at < length, share[0, 0:1, :], 0.0)
    hat2, scale2 = normed(r2[...])
    grad_r2, gain2, shift2 = norm_back(grad_h2, hat2, scale2, small[12:13, :])
    add_row(sums, 12, gain2)
    add_row(sums, 13, shift2)
    add_row(sums, 11, jnp.sum(grad_r2, 0, keepdims=True))
    low_f = grad_r2.astype(jnp.bfloat16)
    f_out[...] = low_f
    grad_h1 = grad_r2
    for part in range(FF // D):
        span = slice(part * D, (part + 1) * D)
        grad_up = back_mul(low_f, down_w[span, :]) * slope[:, span].astype(jnp.float32)
        add_row(sums, 7 + part, jnp.sum(grad_up, 0, keepdims=True))
        low_u = grad_up.astype(jnp.bfloat16)
        u_out[:, span] = low_u
        grad_h1 = grad_h1 + back_mul(low_u, up_w[span, :])
    hat1, scale1 = normed(r1[...])
    grad_r1, gain1, shift1 = norm_back(grad_h1, hat1, scale1, small[5:6, :])
    add_row(sums, 5, gain1)
    add_row(sums, 6, shift1)
    add_row(sums, 4, jnp.sum(grad_r1, 0, keepdims=True))
    r1_grad[...] = grad_r1
    low_a = grad_r1.astype(jnp.bfloat16)
    a_out[...] = low_a
    mixed_out[...] = back_mul(low_a, out_w[...]).astype(jnp.bfloat16)


def feed_back(lengths, share, r1, r2, slope, first, second, small):
    tokens = r1.shape[0]
    turns = LEN // TILE
    return call(
        feed_back_kernel,
        "feed_forward_back",
        (tokens // TILE,),
        [
            pl.BlockSpec((1, 8, D), lambda i, *_: (i // turns, 0, 0)),
            rows_spec(D),
            rows_spec(D),
            rows_spec(FF),
            weight_spec(D, 3),
            weight_spec(FF, 0),
            weight_spec(FF, 1),
            whole_spec(small.shape),
        ],
        [
            rows_spec(D),
            rows_spec(FF),
            rows_spec(D),
            rows_spec(D),
            rows_spec(D),
            whole_spec((16, D)),
        ],
        [
            jax.ShapeDtypeStruct((tokens, D), jnp.bfloat16),
            jax.ShapeDtypeStruct((tokens, FF), jnp.bfloat16),
            jax.ShapeDtypeStruct((tokens, D), jnp.float32),
            jax.ShapeDtypeStruct((tokens, D), jnp.bfloat16),
            jax.ShapeDtypeStruct((tokens, D), jnp.bfloat16),
            jax.ShapeDtypeStruct((16, D), jnp.float32),
        ],
        prefetch=1,
        flops=2 * tokens * D * (D + 2 * FF),
        moved=tokens * D * 32,
    )(lengths, share, r1, r2, slope, first, second, second, small)


def outer_kernel(act, low_f, low_h1, low_u, mixed, low_a, out):
    step = pl.program_id(0)
    parts = FF // D

    @pl.when(step < parts)
    def _():
        out[...] = outer_sum(act[...], low_f[...]).astype(jnp.bfloat16)

    @pl.when((step >= parts) & (step < 2 * parts))
    def _():
        out[...] = outer_sum(low_h1[...], low_u[...]).astype(jnp.bfloat16)

    @pl.when(step == 2 * parts)
    def _():
        out[...] = outer_sum(mixed[...], low_a[...]).astype(jnp.bfloat16)


def feed_weights(act, low_f, low_h1, low_u, mixed, low_a):
    tokens = act.shape[0]
    parts = FF // D
    return call(
        outer_kernel,
        "feed_forward_weights",
        (2 * parts + 1,),
        [
            pl.BlockSpec((tokens, D), lambda i: (0, jnp.minimum(i, parts - 1))),
            whole_spec((tokens, D)),
            whole_spec((tokens, D)),
            pl.BlockSpec((tokens, D), lambda i: (0, jnp.clip(i - parts, 0, parts - 1))),
            whole_spec((tokens, D)),
            whole_spec((tokens, D)),
        ],
        [pl.BlockSpec((D, D), lambda i: (i, 0))],
        [jax.ShapeDtypeStruct(((2 * parts + 1) * D, D), jnp.bfloat16)],
        flops=2 * tokens * D * (D + 2 * FF),
        moved=tokens * D * 24,
    )(act, low_f, low_h1, low_u, mixed, low_a)[0]


def attend_back_kernel(lengths, qkv, grad_mixed, logs, out, sums):
    seq = qkv.shape[0]
    bias = live_row(lengths[pl.program_id(0)], seq)
    masks = head_masks(seq)

    @pl.when(pl.program_id(0) == 0)
    def _():
        sums[...] = jnp.zeros_like(sums)

    for pair in range(H // 2):
        attend_back_pair(
            qkv, grad_mixed, logs, bias, masks, out, sums, slice(0, seq), pair
        )


def attend_back(lengths, qkv, grad_mixed, logs, seq):
    tokens = qkv.shape[0]
    return call(
        attend_back_kernel,
        "attention_back",
        (tokens // seq,),
        [rows_spec(3 * D, seq), rows_spec(D, seq), rows_spec(128, seq)],
        [rows_spec(3 * D, seq), whole_spec((16, D))],
        [
            jax.ShapeDtypeStruct((tokens, 3 * D), jnp.bfloat16),
            jax.ShapeDtypeStruct((16, D), jnp.float32),
        ],
        prefetch=1,
        flops=10 * tokens * seq * D,
        moved=tokens * D * 16,
    )(lengths, qkv, grad_mixed, logs)


def embed_back_kernel(grad_r1, grad_qkv, weight, x, small, x_out, pos_out, sums):
    spot, sentence = pl.program_id(0), pl.program_id(1)

    @pl.when((spot == 0) & (sentence == 0))
    def _():
        sums[...] = jnp.zeros_like(sums)

    @pl.when(sentence == 0)
    def _():
        pos_out[...] = jnp.zeros_like(pos_out)

    grad_h0 = grad_r1[...]
    for third in range(3):
        span = slice(third * D, (third + 1) * D)
        grad_h0 = grad_h0 + back_mul(grad_qkv[:, span], weight[span, :])
    hat, scale = normed(x[...])
    grad_x, gain, shift = norm_back(grad_h0, hat, scale, small[0:1, :])
    add_row(sums, 0, gain)
    add_row(sums, 1, shift)
    x_out[...] = grad_x.astype(jnp.bfloat16)
    pos_out[...] += grad_x


def embed_back(grad_r1, grad_qkv, weight, x, small, seq):
    tokens = x.shape[0]
    turns = seq // TILE

    def rows(width):
        return pl.BlockSpec((TILE, width), lambda p, b: (b * turns + p, 0))

    return call(
        embed_back_kernel,
        "embed_back",
        (turns, tokens // seq),
        [rows(D), rows(3 * D), whole_spec((3 * D, D)), rows(D), whole_spec(small.shape)],
        [rows(D), pl.BlockSpec((TILE, D), lambda p, b: (p, 0)), whole_spec((16, D))],
        [
            jax.ShapeDtypeStruct((tokens, D), jnp.bfloat16),
            jax.ShapeDtypeStruct((seq, D), jnp.float32),
            jax.ShapeDtypeStruct((16, D), jnp.float32),
        ],
        flops=6 * tokens * D * D,
        moved=tokens * D * 20,
    )(grad_r1, grad_qkv, weight, x, small)


def qkv_outer_kernel(h0, grad_qkv, out, low):
    @pl.when(pl.program_id(0) == 0)
    def _():
        low[...] = h0[...].astype(jnp.bfloat16)

    out[...] = outer_sum(low[...], grad_qkv[...]).astype(jnp.bfloat16)


def qkv_weights(h0, grad_qkv):
    tokens = h0.shape[0]
    return call(
        qkv_outer_kernel,
        "qkv_weights",
        (3,),
        [whole_spec((tokens, D)), pl.BlockSpec((tokens, D), lambda i: (0, i))],
        [pl.BlockSpec((D, D), lambda i: (i, 0))],
        [jax.ShapeDtypeStruct((3 * D, D), jnp.bfloat16)],
        scratch=[pltpu.VMEM((tokens, D), jnp.bfloat16)],
        flops=6 * tokens * D * D,
        moved=tokens * D * 12,
    )(h0, grad_qkv)[0]


def bucket_kernel(slot, grad, out):
    size = out.shape[0]
    at = pl.program_id(0) * size + lax.broadcasted_iota(jnp.int32, (size, slot.shape[1]), 0)
    pick = (slot[...] == at).astype(jnp.bfloat16)
    out[...] = matmul(pick, grad[...]).astype(jnp.bfloat16)


def bucket_rows(slot, grad, count):
    tokens = grad.shape[0]
    size = count // 4
    return call(
        bucket_kernel,
        "bucket_rows",
        (count // size,),
        [whole_spec((1, tokens)), whole_spec((tokens, D))],
        [pl.BlockSpec((size, D), lambda i: (i, 0))],
        [jax.ShapeDtypeStruct((count, D), jnp.bfloat16)],
        flops=2 * tokens * D * count,
        moved=tokens * D * 4,
    )(slot, grad)[0]


def scatter_kernel(row, got, out):
    size = out.shape[0]
    at = pl.program_id(0) * size + lax.broadcasted_iota(jnp.int32, (size, row.shape[1]), 0)
    pick = (row[...] == at).astype(jnp.bfloat16)
    out[...] = matmul(pick, got[...])


def scatter_rows(row, got, rows):
    size = math.gcd(rows, 480)
    count = got.shape[0]
    return call(
        scatter_kernel,
        "scatter_rows",
        (rows // size,),
        [whole_spec((1, count)), whole_spec((count, D))],
        [pl.BlockSpec((size, D), lambda i: (i, 0))],
        [jax.ShapeDtypeStruct((rows, D), jnp.float32)],
        flops=2 * rows * D * count,
        moved=rows * D * 8,
    )(row, got)[0]


MESH = pl.DeviceIdType.MESH


def gather_kernel(sizes, whole, src, out, send, recv, local):
    dp, fsdp = sizes
    count = dp * fsdp if whole else fsdp
    row, col = lax.axis_index("dp"), lax.axis_index("fsdp")
    me = row * fsdp + col if whole else col

    def target(step):
        other = lax.rem(me + step, count)
        return (other // fsdp, lax.rem(other, fsdp)) if whole else (row, other)

    barrier = pltpu.get_barrier_semaphore()

    def greet(step, carry):
        pl.semaphore_signal(barrier, inc=1, device_id=target(step), device_id_type=MESH)
        return carry

    lax.fori_loop(1, count, greet, 0)
    pl.semaphore_wait(barrier, count - 1)
    own = pltpu.make_async_copy(src, out.at[me], local)
    own.start()

    def copy(step):
        return pltpu.make_async_remote_copy(
            src_ref=src,
            dst_ref=out.at[me],
            send_sem=send.at[step],
            recv_sem=recv.at[step],
            device_id=target(step),
            device_id_type=MESH,
        )

    def begin(step, carry):
        copy(step).start()
        return carry

    def end(step, carry):
        copy(step).wait()
        return carry

    lax.fori_loop(1, count, begin, 0)
    lax.fori_loop(1, count, end, 0)
    own.wait()


def gather_small(value, whole, collective):
    dp, fsdp = lax.axis_size("dp"), lax.axis_size("fsdp")
    count = dp * fsdp if whole else fsdp
    return pl.pallas_call(
        functools.partial(gather_kernel, (dp, fsdp), whole),
        out_shape=jax.ShapeDtypeStruct((count,) + value.shape, value.dtype),
        in_specs=[pl.BlockSpec(memory_space=pltpu.VMEM)],
        out_specs=pl.BlockSpec(memory_space=pltpu.VMEM),
        scratch_shapes=[
            pltpu.SemaphoreType.DMA((count,)),
            pltpu.SemaphoreType.DMA((count,)),
            pltpu.SemaphoreType.DMA,
        ],
        compiler_params=pltpu.CompilerParams(collective_id=collective, has_side_effects=True),
    )(value)


LOOP_SIZE = 8
AHEAD = 2
CHUNK = 480


def grid_place(device):
    z, y = device // 2, lax.rem(device, 2)
    return z + y * (LOOP_SIZE - 1 - 2 * z)


def grid_device(place):
    place = lax.rem(place + LOOP_SIZE, LOOP_SIZE)
    y = place // (LOOP_SIZE // 2)
    return 2 * (place + y * (LOOP_SIZE - 1 - 2 * place)) + y


def front_kernel(
    cap,
    own_rows,
    lengths,
    ids,
    small,
    pieces,
    pos_low,
    table,
    everyone,
    first,
    second,
    small_out,
    held_rows,
    asker_row,
    most,
    x_out,
    h0_out,
    qkv_out,
    mixed_out,
    log_out,
    stage,
    table_low,
    sent,
    got,
    before,
    asker_col,
    smalls,
    small_sum,
    pos,
    x_in,
    h0_in,
    qkv,
    id_send,
    id_recv,
    hop_send,
    hop_recv,
    word_send,
    word_recv,
    small_send,
    small_recv,
    held_send,
    held_recv,
    stage_sem,
    local_sem,
):
    fsdp = LOOP_SIZE
    row, col = lax.axis_index("dp"), lax.axis_index("fsdp")
    count = lax.axis_size("dp") * fsdp
    tokens = ids.shape[1]
    seq = LEN
    me = row * fsdp + col
    shard = pieces.shape[0] // 12
    pos_rows = pos_low.shape[0]
    quarter = row
    place = grid_place(col)
    core_mate = row + 1 - 2 * lax.rem(row, 2)
    x_mate = lax.rem(row + 2, 4)
    far_mate = lax.rem(core_mate + 2, 4)
    right = (row, grid_device(place + 1))
    left = (row, grid_device(place - 1))

    def anyone(step):
        other = lax.rem(me + step, count)
        return (other // fsdp, lax.rem(other, fsdp))

    barrier = pltpu.get_barrier_semaphore()

    def greet(step, carry):
        pl.semaphore_signal(barrier, inc=1, device_id=anyone(step), device_id_type=MESH)
        return carry

    lax.fori_loop(1, count, greet, 0)
    pl.semaphore_wait(barrier, count - 1)

    def remote(src, dst, sems, index, target):
        return pltpu.make_async_remote_copy(
            src_ref=src,
            dst_ref=dst,
            send_sem=sems[0].at[index],
            recv_sem=sems[1].at[index],
            device_id=target,
            device_id_type=MESH,
        )

    def id_copy(step):
        return remote(ids, everyone.at[me], (id_send, id_recv), step, anyone(step))

    def id_start(step, carry):
        id_copy(step).start()
        return carry

    lax.fori_loop(1, count, id_start, 0)
    everyone[pl.ds(me, 1)] = ids[...][None]

    def aligned(at):
        return pl.multiple_of(at, 16)

    def hop_refs(phase, block, part, own):
        if phase == 0:
            size = pos_rows // 4
            there = [
                first.at[pl.ds(aligned(part * D + block * shard), shard), :],
                pos.at[pl.ds(aligned(block * pos_rows + part * size), size), :],
            ]
            here = [
                pieces.at[pl.ds(aligned(part * shard), shard), :],
                pos_low.at[pl.ds(aligned(part * size), size), :],
            ]
        else:
            there, here = [], []
            late = part // 2
            for i in range(2):
                piece = part * 2 + i
                early_at = piece * D + block * shard
                late_at = FF + block * 4 * shard + (piece - 4) * shard
                there.append(
                    second.at[pl.ds(aligned(early_at + late * (late_at - early_at)), shard), :]
                )
                here.append(pieces.at[pl.ds(aligned((4 + piece) * shard), shard), :])
        return there, here if own else there

    def hop(phase, slot, block, part, target, own=False):
        there, here = hop_refs(phase, block, part, own)
        return [
            remote(src, dst, (hop_send, hop_recv), 56 * phase + 2 * slot + i, target)
            for i, (src, dst) in enumerate(zip(here, there))
        ]

    started = []

    def begin(copies):
        for copy in copies:
            copy.start()
        started.extend(copies)

    def arrive(copies):
        for copy in copies:
            copy.wait_recv()

    events = []
    for k in range(1, LOOP_SIZE // 2 + 1):
        events.append((k, 1))
        if k < LOOP_SIZE // 2:
            events.append((k, -1))
    slot_of = {event: i for i, event in enumerate(events)}
    total = len(events)

    def block_of(event):
        return grid_device(place - event[0] * event[1])

    def begin_ring(phase):
        begin(hop(phase, slot_of[(1, 1)], col, quarter, right, own=True))
        begin(hop(phase, slot_of[(1, -1)], col, quarter, left, own=True))

    def spread(phase, index):
        event = events[index]
        hops, sign = event
        block = block_of(event)
        arrive(hop(phase, index, block, quarter, right))
        follow = (hops + 1, sign)
        if follow in slot_of:
            begin(hop(phase, slot_of[follow], block, quarter, right if sign == 1 else left))
        begin(hop(phase, total + index, block, quarter, (x_mate, col)))
        begin(hop(phase, 2 * total + index, block, quarter, (core_mate, col)))

    def pass_on(phase, index):
        block = block_of(events[index])
        arrive(hop(phase, total + index, block, x_mate, (x_mate, col)))
        begin(hop(phase, 3 * total + index, block, x_mate, (core_mate, col)))

    def settle(phase):
        for index in range(total):
            block = block_of(events[index])
            arrive(hop(phase, 2 * total + index, block, core_mate, (core_mate, col)))
            arrive(hop(phase, 3 * total + index, block, far_mate, (core_mate, col)))

    begin_ring(0)

    def small_copy(step):
        return remote(
            small, smalls.at[col], (small_send, small_recv), step, (row, lax.rem(col + step, fsdp))
        )

    for step in range(1, fsdp):
        small_copy(step).start()
    begin_ring(1)
    local = [
        pltpu.make_async_copy(small, smalls.at[col], local_sem.at[0]),
        pltpu.make_async_copy(
            pos_low, pos.at[pl.ds(aligned(col * pos_rows), pos_rows), :], local_sem.at[1]
        ),
        pltpu.make_async_copy(
            pieces.at[pl.ds(8 * shard, 4 * shard), :],
            second.at[pl.ds(aligned(FF + col * 4 * shard), 4 * shard), :],
            local_sem.at[2],
        ),
    ]
    for piece in range(4):
        span = pl.ds(aligned(piece * D + col * shard), shard)
        here = pieces.at[pl.ds(piece * shard, shard), :]
        local.append(pltpu.make_async_copy(here, first.at[span, :], local_sem.at[3 + piece]))
        here = pieces.at[pl.ds((4 + piece) * shard, shard), :]
        local.append(pltpu.make_async_copy(here, second.at[span, :], local_sem.at[7 + piece]))
    for copy in local:
        copy.start()

    chunks = own_rows // CHUNK

    def stage_copy(chunk, slot):
        return pltpu.make_async_copy(
            table.at[pl.ds(chunk * CHUNK, CHUNK), :], stage.at[slot], stage_sem.at[slot]
        )

    stage_copy(0, 0).start()
    across = lax.broadcasted_iota(jnp.int32, (tokens, tokens), 1)
    down = lax.broadcasted_iota(jnp.int32, (tokens, tokens), 0)
    before[...] = (down <= across).astype(jnp.float32).astype(jnp.bfloat16)
    for chunk in range(chunks):
        if chunk + 1 < chunks:
            stage_copy(chunk + 1, (chunk + 1) % 2).start()
        stage_copy(chunk, chunk % 2).wait()
        table_low[chunk * CHUNK : (chunk + 1) * CHUNK, :] = stage[chunk % 2].astype(jnp.bfloat16)

    def words_at(device):
        return got.at[pl.ds(aligned(device * cap), cap), :]

    def word_copy(step):
        other = lax.rem(col + step, fsdp)
        return remote(sent.at[other], words_at(col), (word_send, word_recv), step, (row, other))

    def bucket(step):
        asker = lax.rem(col + step, fsdp)
        if step:
            id_copy(lax.rem(me - row * fsdp - asker + count, count)).wait_recv()
        theirs = everyone[row * fsdp + asker] - col * own_rows
        held = (theirs >= 0) & (theirs < own_rows)
        flag = jnp.broadcast_to(held, (8, tokens)).astype(jnp.float32).astype(jnp.bfloat16)
        rank = matmul(flag, before[...])[0:1, :].astype(jnp.int32) - 1
        rank = jnp.where(held, rank, -1)
        hit = lax.broadcasted_iota(jnp.int32, (cap, tokens), 0) == rank
        inner = jnp.sum(jnp.where(hit, theirs + 1, 0), 1, keepdims=True) - 1
        held_rows[pl.ds(row, 1), step] = jnp.broadcast_to(inner, (cap, 128)).T[0:1, :][None]
        rows = jnp.zeros((cap, D), jnp.float32)
        wide = own_rows // 4
        for part in range(4):
            pick = inner == part * wide + lax.broadcasted_iota(jnp.int32, (cap, wide), 1)
            rows = rows + matmul(
                pick.astype(jnp.float32).astype(jnp.bfloat16),
                table_low[part * wide : (part + 1) * wide, :],
            )
        if step:
            sent[pl.ds(asker, 1)] = rows.astype(jnp.bfloat16)[None]
            if step > AHEAD:
                word_copy(step - AHEAD).wait_send()
            word_copy(step).start()
        else:
            words_at(col)[...] = rows.astype(jnp.bfloat16)

    for step, chores in (
        (1, ()),
        (2, ((spread, 0, 0), (spread, 0, 1), (spread, 1, 0), (spread, 1, 1))),
        (3, ((pass_on, 0, 0), (spread, 0, 2), (spread, 0, 3))),
        (4, ((pass_on, 0, 1), (pass_on, 1, 0), (spread, 0, 4), (spread, 0, 5))),
        (5, ((spread, 1, 2), (spread, 1, 3), (pass_on, 0, 2), (pass_on, 0, 3), (pass_on, 1, 1))),
        (6, ((spread, 0, 6),)),
        (7, ((pass_on, 0, 4), (pass_on, 0, 5))),
        (0, ((spread, 1, 4), (spread, 1, 5), (pass_on, 1, 2), (pass_on, 0, 6))),
    ):
        bucket(step)
        for chore, phase, index in chores:
            chore(phase, index)

    mine = jnp.broadcast_to(ids[...], (8, tokens))
    owner = lax.broadcasted_iota(jnp.int32, (8, tokens), 0)
    hot = (mine >= owner * own_rows) & (mine < (owner + 1) * own_rows)
    so_far = matmul(hot.astype(jnp.float32).astype(jnp.bfloat16), before[...]).astype(jnp.int32) - 1
    slot = jnp.sum(
        jnp.where(hot & (so_far < cap), owner * cap + so_far + 1, 0), 0, keepdims=True
    ) - 1
    asker_row[...] = slot
    asker_col[...] = jnp.broadcast_to(slot, (128, tokens)).T

    def held_copy(index):
        target = (core_mate, x_mate, far_mate)[index]
        return remote(
            held_rows.at[row], held_rows.at[row], (held_send, held_recv), index, (target, col)
        )

    for index in range(3):
        held_copy(index).start()

    def id_end(step, carry):
        copy = id_copy(step)
        copy.wait_send()

        @pl.when(lax.rem(lax.rem(me - step + count, count) // fsdp - row + count, count) != 0)
        def _():
            copy.wait_recv()

        return carry

    lax.fori_loop(1, count, id_end, 0)
    ids_all = everyone[...]
    largest = jnp.zeros((1, 1), jnp.int32)
    for part in range(fsdp):
        inside = (ids_all >= part * own_rows) & (ids_all < (part + 1) * own_rows)
        number = jnp.sum(inside.astype(jnp.int32), -1)
        largest = jnp.maximum(largest, jnp.max(number, 0, keepdims=True))
    most[...] = jnp.broadcast_to(largest, (8, 128))
    for step in range(1, fsdp):
        small_copy(step).wait()
    for copy in local:
        copy.wait()
    small_sum[...] = jnp.zeros_like(small_sum)
    for device in range(fsdp):
        at = device * (D // fsdp) // 128 * 128
        small_sum[:, at : at + 256] += smalls[device].astype(jnp.float32)
    gains = small_sum[:, 0:D]
    small_out[...] = gains
    settle(0)
    for step in range(1, fsdp):
        word_copy(step).wait_recv()
    for step in range(fsdp - AHEAD, fsdp):
        word_copy(step).wait_send()

    def embed_tile(i, carry):
        span = pl.ds(pl.multiple_of(i * TILE, TILE), TILE)
        slots = fsdp * cap
        pick = asker_col[span, 0:1] == lax.broadcasted_iota(jnp.int32, (TILE, slots), 1)
        words = matmul(pick.astype(jnp.float32).astype(jnp.bfloat16), got[...])
        spot = pl.ds(pl.multiple_of(lax.rem(i, seq // TILE) * TILE, TILE), TILE)
        x = words + pos[spot, :].astype(jnp.float32)
        hat, _ = normed(x)
        h0 = hat * small_sum[0:1, 0:D] + small_sum[1:2, 0:D]
        x_in[span, :] = x
        h0_in[span, :] = h0
        low = h0.astype(jnp.bfloat16)
        for third, bias in enumerate((2, None, 3)):
            value = matmul(low, first[third * D : (third + 1) * D, :])
            if bias is not None:
                value = value + small_sum[bias : bias + 1, 0:D]
            qkv[span, third * D : (third + 1) * D] = value.astype(jnp.bfloat16)
        return carry

    tiles = tokens // TILE
    lax.fori_loop(0, tiles // 2, embed_tile, 0)
    pass_on(1, 3)
    spread(1, 6)
    lax.fori_loop(tiles // 2, tiles, embed_tile, 0)
    written = [
        pltpu.make_async_copy(x_in, x_out, local_sem.at[0]),
        pltpu.make_async_copy(h0_in, h0_out, local_sem.at[1]),
        pltpu.make_async_copy(qkv, qkv_out, local_sem.at[2]),
    ]
    for copy in written:
        copy.start()
    masks = head_masks(seq)
    chores = {
        1: lambda: pass_on(1, 4),
        4: lambda: pass_on(1, 5),
        8: lambda: pass_on(1, 6),
    }
    done = 0
    for sentence in range(tokens // seq):
        bias = live_row(lengths[sentence], seq)
        rows = slice(sentence * seq, (sentence + 1) * seq)
        logs = jnp.zeros((seq, 128), jnp.float32)
        for pair in range(H // 2):
            logs = attend_pair(qkv, bias, masks, logs, mixed_out, rows, pair)
            done += 1
            if done in chores:
                chores[done]()
        log_out[rows, :] = logs
    settle(1)
    for index in range(3):
        held_copy(index).wait()
    for copy in written:
        copy.wait()
    for copy in started:
        copy.wait_send()


def front(lengths, ids, pieces, pos_low, small, table, cap):
    fsdp = LOOP_SIZE
    count = lax.axis_size("dp") * fsdp
    tokens = ids.shape[1]
    own_rows = table.shape[0]
    hops = 16 * (fsdp - 1)
    vmem = pl.BlockSpec(memory_space=pltpu.VMEM)
    anywhere = pl.BlockSpec(memory_space=pl.ANY)
    low, wide = jnp.bfloat16, jnp.float32
    dma = pltpu.SemaphoreType.DMA
    return pl.pallas_call(
        functools.partial(front_kernel, cap, own_rows),
        name="front",
        in_specs=[pl.BlockSpec(memory_space=pltpu.SMEM), vmem, vmem, anywhere, anywhere, anywhere],
        out_specs=[vmem, vmem, anywhere, vmem, vmem, vmem, vmem, anywhere, anywhere, anywhere, vmem, vmem],
        out_shape=[
            jax.ShapeDtypeStruct((count, 1, tokens), jnp.int32),
            jax.ShapeDtypeStruct((4 * D, D), low),
            jax.ShapeDtypeStruct((2 * FF, D), low),
            jax.ShapeDtypeStruct((16, D), wide),
            jax.ShapeDtypeStruct((4, fsdp, 1, cap), jnp.int32),
            jax.ShapeDtypeStruct((1, tokens), jnp.int32),
            jax.ShapeDtypeStruct((8, 128), jnp.int32),
            jax.ShapeDtypeStruct((tokens, D), wide),
            jax.ShapeDtypeStruct((tokens, D), wide),
            jax.ShapeDtypeStruct((tokens, 3 * D), low),
            jax.ShapeDtypeStruct((tokens, D), low),
            jax.ShapeDtypeStruct((tokens, 128), wide),
        ],
        scratch_shapes=[
            pltpu.VMEM((2, CHUNK, D), wide),
            pltpu.VMEM((own_rows, D), low),
            pltpu.VMEM((fsdp, cap, D), low),
            pltpu.VMEM((fsdp * cap, D), low),
            pltpu.VMEM((tokens, tokens), low),
            pltpu.VMEM((tokens, 128), jnp.int32),
            pltpu.VMEM((fsdp, 16, 256), low),
            pltpu.VMEM((16, D + 128), wide),
            pltpu.VMEM((LEN, D), low),
            pltpu.VMEM((tokens, D), wide),
            pltpu.VMEM((tokens, D), wide),
            pltpu.VMEM((tokens, 3 * D), low),
            dma((count,)),
            dma((count,)),
            dma((hops,)),
            dma((hops,)),
            dma((fsdp,)),
            dma((fsdp,)),
            dma((fsdp,)),
            dma((fsdp,)),
            dma((3,)),
            dma((3,)),
            dma((2,)),
            dma((12,)),
        ],
        compiler_params=pltpu.CompilerParams(
            collective_id=0, has_side_effects=True, vmem_limit_bytes=VMEM_GRANT
        ),
    )(lengths, ids, small, pieces, pos_low, table)


class Ring:
    def __init__(self, parts, sign, send, recv, base):
        self.parts, self.send, self.recv, self.base = parts, send, recv, base
        self.row, col = lax.axis_index("dp"), lax.axis_index("fsdp")
        self.col, self.place = col, grid_place(col)
        self.hops = {sign: LOOP_SIZE // 2, -sign: LOOP_SIZE - LOOP_SIZE // 2 - 1}
        self.events = []
        for k in range(1, LOOP_SIZE // 2 + 1):
            for direction in (sign, -sign):
                if k <= self.hops[direction]:
                    self.events.append((k, direction))
        self.slot = {event: i for i, event in enumerate(self.events)}
        self.sign = sign
        self.started = []

    def copies(self, source, event):
        slot = self.slot[event]
        target = (self.row, grid_device(self.place + event[1]))
        return [
            pltpu.make_async_remote_copy(
                src_ref=box.at[source],
                dst_ref=box.at[slot],
                send_sem=self.send.at[self.base + len(self.parts) * slot + i],
                recv_sem=self.recv.at[self.base + len(self.parts) * slot + i],
                device_id=target,
                device_id_type=MESH,
            )
            for i, (_, _, box) in enumerate(self.parts)
        ]

    def depart(self, source, event):
        for copy in self.copies(source, event):
            copy.start()
            self.started.append(copy)

    def add(self, slot, block, arrived):
        for keep, mate, box in self.parts:
            terms = [keep.at[block], mate.at[block]] + ([box.at[slot]] if arrived else [])
            sum_rows(box.at[slot], terms)

    def first(self):
        for i, direction in enumerate((self.sign, -self.sign)):
            block = grid_device(self.place + direction * self.hops[direction])
            self.add(len(self.events) + i, block, False)
            self.depart(len(self.events) + i, (1, direction))

    def step(self, index):
        hop, direction = self.events[index]
        for copy in self.copies(index, self.events[index]):
            copy.wait_recv()
        left = self.hops[direction] - hop
        if left:
            self.add(index, grid_device(self.place + direction * left), True)
            self.depart(index, (hop + 1, direction))

    def last(self, totals):
        far = self.slot[(self.hops[self.sign], self.sign)]
        near = self.slot[(self.hops[-self.sign], -self.sign)]
        for (keep, mate, box), total in zip(self.parts, totals):
            sum_rows(total, [keep.at[self.col], mate.at[self.col], box.at[far], box.at[near]])

    def drain(self):
        for copy in self.started:
            copy.wait_send()


def sum_rows(out, terms):
    rows = min(out.shape[0], 32)

    def body(i, carry):
        span = pl.ds(pl.multiple_of(i * rows, rows), rows)
        total = terms[0][span, :].astype(jnp.float32)
        for term in terms[1:]:
            total = total + term[span, :].astype(jnp.float32)
        out[span, :] = total.astype(out.dtype)
        return carry

    lax.fori_loop(0, out.shape[0] // rows, body, 0)


def add_squares(squares, value):
    rows = min(value.shape[0], 32)

    def body(i, carry):
        part = value[pl.ds(pl.multiple_of(i * rows, rows), rows), :].astype(jnp.float32)
        squares[0:1, 0 : part.shape[1]] += jnp.sum(part * part, 0, keepdims=True)
        return carry

    lax.fori_loop(0, value.shape[0] // rows, body, 0)


def finish_kernel(
    cap,
    own_rows,
    grad,
    slot,
    held,
    feed_grads,
    qkv_grads,
    pos_grads,
    small_grads,
    depart,
    own,
    table_out,
    sum_a,
    sum_b,
    sum_small,
    norm_out,
    got,
    sent,
    total,
    half_low,
    last_a,
    keep_b,
    mate_b,
    box_b,
    keep_s,
    mate_s,
    box_s,
    out_a,
    in_a,
    out_b,
    in_b,
    out_s,
    in_s,
    squares,
    share,
    shares,
    word_send,
    word_recv,
    ring_send,
    ring_recv,
    pair_send,
    pair_recv,
    norm_send,
    norm_recv,
    local_sem,
):
    fsdp = LOOP_SIZE
    row, col = lax.axis_index("dp"), lax.axis_index("fsdp")
    core = lax.rem(row, 2)
    core_mate = row + 1 - 2 * core
    x_mate = lax.rem(row + 2, 4)
    far_mate = lax.rem(core_mate + 2, 4)
    half = own_rows // 2
    tokens = grad.shape[0]

    barrier = pltpu.get_barrier_semaphore()
    for step in range(1, fsdp):
        there = (row, lax.rem(col + step, fsdp))
        pl.semaphore_signal(barrier, inc=1, device_id=there, device_id_type=MESH)
    for step in range(fsdp):
        there = (core_mate, lax.rem(col + step, fsdp))
        pl.semaphore_signal(barrier, inc=1, device_id=there, device_id_type=MESH)
    pl.semaphore_signal(barrier, inc=1, device_id=(x_mate, col), device_id_type=MESH)
    pl.semaphore_wait(barrier, 2 * fsdp)

    def remote(src, dst, sems, index, target):
        return pltpu.make_async_remote_copy(
            src_ref=src,
            dst_ref=dst,
            send_sem=sems[0].at[index],
            recv_sem=sems[1].at[index],
            device_id=target,
            device_id_type=MESH,
        )

    pair = (pair_send, pair_recv)
    mate = (core_mate, col)
    shard = feed_grads.shape[1]

    def b_parts(which, target):
        pos_half = pos_grads.shape[1] // 2
        if which == 0:
            first, second = qkv_grads.at[pl.ds(0, 8)], qkv_grads.at[pl.ds(8, 8)]
        else:
            first, second = qkv_grads.at[pl.ds(16, 8)], feed_grads.at[pl.ds(64, 8)]
        return [
            (first, target.at[:, pl.ds(0, shard)]),
            (second, target.at[:, pl.ds(shard, shard)]),
            (pos_grads.at[:, pl.ds(which * pos_half, pos_half)], target.at[:, pl.ds(2 * shard, pos_half)]),
        ]

    def s_parts(which, target):
        return [(small_grads.at[:, pl.ds(8 * which, 8)], target)]

    for which in range(2):

        @pl.when(core == which)
        def _(which=which):
            for index, (parts, keep, mates) in enumerate(
                ((b_parts, keep_b, mate_b), (s_parts, keep_s, mate_s))
            ):
                for src, dst in parts(1 - which, mates):
                    remote(src, dst, pair, index, mate).start()
                for src, dst in parts(which, keep):
                    pltpu.make_async_copy(src, dst, local_sem.at[index]).start()

    def halves_in(index):
        keep, mates = ((keep_b, mate_b), (keep_s, mate_s))[index]
        pltpu.make_async_copy(keep, keep, local_sem.at[index]).wait()
        remote(mates, mates, pair, index, mate).wait_recv()

    def word_copy(step):
        return remote(
            sent.at[step],
            got.at[row, step],
            (word_send, word_recv),
            step,
            (row, lax.rem(col - step + fsdp, fsdp)),
        )

    def word_hand(kind, step):
        group, target = ((row, (x_mate, col)), (row, mate), (x_mate, mate))[kind]
        place = got.at[group, step]
        return remote(place, place, (word_send, word_recv), fsdp * (kind + 1) + step, target)

    def bucket(step):
        base = lax.rem(col - step + fsdp, fsdp) * cap
        pick = slot[...] == base + lax.broadcasted_iota(jnp.int32, (cap, tokens), 0)
        rows = matmul(pick.astype(jnp.float32).astype(jnp.bfloat16), grad[...]).astype(jnp.bfloat16)
        if step:
            sent[step] = rows
            word_copy(step).start()
        else:
            got[pl.ds(row, 1), 0] = rows[None]

    handed = []

    def spread(step):
        if step:
            word_copy(step).wait_recv()
        for kind in (0, 1):
            copy = word_hand(kind, step)
            copy.start()
            handed.append(copy)

    def pass_on(step):
        place = got.at[x_mate, step]
        remote(place, place, (word_send, word_recv), fsdp + step, (x_mate, col)).wait_recv()
        copy = word_hand(2, step)
        copy.start()
        handed.append(copy)

    def from_mate(group, kind, step):
        place = got.at[group, step]
        remote(place, place, (word_send, word_recv), fsdp * (kind + 1) + step, mate).wait_recv()

    def accumulate(side, parity, part, fresh):
        chip = row - core if side == 0 else x_mate - core
        group = chip + parity
        width = 4 * cap
        size = half // 4

        def tile(i, carry):
            at = core * half + i * size + lax.broadcasted_iota(jnp.int32, (size, width), 0)
            pick = held[pl.ds(group, 1), 0, part * width : (part + 1) * width] == at
            rows = got[pl.ds(group, 1), 4 * part : 4 * part + 4].reshape(width, D)
            value = matmul(pick.astype(jnp.float32).astype(jnp.bfloat16), rows)
            span = pl.ds(pl.multiple_of(i * size, size), size)
            if fresh:
                total[side, span, :] = value
            else:
                total[side, span, :] += value
            return carry

        lax.fori_loop(0, 4, tile, 0)

    def arrived_here(part):
        for step in range(4 * part, 4 * part + 4):
            from_mate(core_mate, 1, step)

    def arrived_far(part):
        for step in range(4 * part, 4 * part + 4):
            from_mate(far_mate, 2, step)

    def last_hop():
        return remote(
            depart, last_a, (ring_send, ring_recv), 14, (row, grid_device(grid_place(col) + 1))
        )

    ring_b = Ring(
        [(keep_b, mate_b, box_b), (keep_s, mate_s, box_s)],
        -1,
        ring_send,
        ring_recv,
        0,
    )
    squares[...] = jnp.zeros_like(squares)

    def swap_x(ring, totals, incoming, index):
        ring.last(totals)
        for i, (mine, theirs) in enumerate(zip(totals, incoming)):
            remote(mine, theirs, pair, index + i, (x_mate, col)).start()

    def settle(totals, incoming, finals, index, back):
        for i, (mine, theirs, final) in enumerate(zip(totals, incoming, finals)):
            remote(mine, theirs, pair, index + i, (x_mate, col)).wait_recv()
            sum_rows(final.at[core], [mine, theirs])
            add_squares(squares, final.at[core])
            remote(final.at[core], final.at[core], pair, back + i, mate).start()

    last_hop().start()
    for step in range(1, fsdp):
        bucket(step)
    bucket(0)
    spread(0)
    halves_in(0)
    halves_in(1)
    ring_b.first()
    spread(1)
    last_hop().wait_recv()
    sum_rows(out_a, [own, last_a])
    remote(out_a, in_a, pair, 5, (x_mate, col)).start()
    spread(2)
    pass_on(0)
    spread(3)
    ring_b.step(0)
    ring_b.step(1)
    pass_on(1)
    pass_on(2)
    arrived_here(0)
    accumulate(0, 0, 0, True)
    accumulate(0, 1, 0, False)
    spread(4)
    pass_on(3)
    ring_b.step(2)
    ring_b.step(3)
    spread(5)
    arrived_far(0)
    accumulate(1, 0, 0, True)
    accumulate(1, 1, 0, False)
    spread(6)
    pass_on(4)
    ring_b.step(4)
    ring_b.step(5)
    spread(7)
    pass_on(5)
    arrived_here(1)
    accumulate(0, 0, 1, False)
    accumulate(0, 1, 1, False)
    ring_b.step(6)
    swap_x(ring_b, (out_b, out_s), (in_b, in_s), 3)
    pass_on(6)
    pass_on(7)
    settle((out_a,), (in_a,), (sum_a,), 5, 9)
    arrived_far(1)
    accumulate(1, 0, 1, False)
    accumulate(1, 1, 1, False)

    def close(i, carry):
        span = pl.ds(pl.multiple_of(i * 32, 32), 32)
        value = (total[0, span, :] + total[1, span, :]).astype(jnp.bfloat16)
        half_low[span, :] = value
        wide = value.astype(jnp.float32)
        squares[0:1, :] += jnp.sum(wide * wide, 0, keepdims=True)
        return carry

    lax.fori_loop(0, half // 32, close, 0)
    mine = table_out.at[pl.ds(pl.multiple_of(core * half, 32), half), :]
    kept = pltpu.make_async_copy(half_low, mine, local_sem.at[3])
    kept.start()
    given = remote(half_low, mine, pair, 6, mate)
    given.start()
    settle((out_b, out_s), (in_b, in_s), (sum_b, sum_small), 3, 7)

    here = core * fsdp + col
    share[...] = jnp.broadcast_to(jnp.sum(squares[0:1, :], 1, keepdims=True), (8, 128))
    shares[pl.ds(here, 1)] = share[...][None]

    def norm_copy(step):
        other = lax.rem(here + step, 2 * fsdp)
        target = (row - core + other // fsdp, lax.rem(other, fsdp))
        return remote(share, shares.at[here], (norm_send, norm_recv), step, target)

    for step in range(1, 2 * fsdp):
        norm_copy(step).start()
    for step in range(1, 2 * fsdp):
        norm_copy(step).wait()
    norm = shares[0]
    for step in range(1, 2 * fsdp):
        norm = norm + shares[step]
    norm_out[...] = norm

    kept.wait()
    given.wait()
    for i, final in enumerate((sum_b, sum_small, sum_a)):
        other = final.at[1 - core]
        remote(other, other, pair, 7 + i, mate).wait()
    for index, (mine_out, theirs) in enumerate(((out_b, in_b), (out_s, in_s), (out_a, in_a))):
        remote(mine_out, theirs, pair, 3 + index, (x_mate, col)).wait_send()
    for index, mates in enumerate((mate_b, mate_s)):
        remote(mates, mates, pair, index, mate).wait_send()
    for step in range(1, fsdp):
        word_copy(step).wait_send()
    for copy in handed:
        copy.wait_send()
    last_hop().wait_send()
    ring_b.drain()


class flat_blocks:
    def __init__(self, ref):
        self.ref = ref

    @property
    def at(self):
        return self

    def __getitem__(self, block):
        return flat_rows(self.ref, block)


class flat_rows:
    def __init__(self, ref, block):
        self.ref, self.block = ref, block

    def __getitem__(self, key):
        span = key[0]
        rows = self.ref.shape[2]
        return self.ref[self.block, span.start // rows, pl.ds(lax.rem(span.start, rows), span.size), :]


def finish(grad, slot, held, feed_grads, qkv_grads, pos_grads, small_grads, depart, own, own_rows, cap):
    fsdp = LOOP_SIZE
    tokens = grad.shape[0]
    shard = D // fsdp
    pos_rows = pos_grads.shape[0] // fsdp
    rows_a, rows_b = 4 * shard, 2 * shard + pos_rows // 2
    half = own_rows // 2
    vmem = pl.BlockSpec(memory_space=pltpu.VMEM)
    anywhere = pl.BlockSpec(memory_space=pl.ANY)
    low, wide = jnp.bfloat16, jnp.float32
    return pl.pallas_call(
        functools.partial(finish_kernel, cap, own_rows),
        name="finish",
        in_specs=[vmem, vmem, vmem, anywhere, anywhere, anywhere, anywhere, vmem, vmem],
        out_specs=[anywhere, vmem, vmem, vmem, vmem],
        out_shape=[
            jax.ShapeDtypeStruct((own_rows, D), low),
            jax.ShapeDtypeStruct((2, rows_a, D), low),
            jax.ShapeDtypeStruct((2, rows_b, D), low),
            jax.ShapeDtypeStruct((2, 8, 128), wide),
            jax.ShapeDtypeStruct((8, 128), wide),
        ],
        scratch_shapes=[
            pltpu.VMEM((4, fsdp, cap, D), low),
            pltpu.VMEM((fsdp, cap, D), low),
            pltpu.VMEM((2, half, D), wide),
            pltpu.VMEM((half, D), low),
            pltpu.VMEM((rows_a, D), low),
            pltpu.VMEM((fsdp, rows_b, D), low),
            pltpu.VMEM((fsdp, rows_b, D), low),
            pltpu.VMEM((fsdp + 1, rows_b, D), low),
            pltpu.VMEM((fsdp, 8, 128), wide),
            pltpu.VMEM((fsdp, 8, 128), wide),
            pltpu.VMEM((fsdp + 1, 8, 128), wide),
            pltpu.VMEM((rows_a, D), low),
            pltpu.VMEM((rows_a, D), low),
            pltpu.VMEM((rows_b, D), low),
            pltpu.VMEM((rows_b, D), low),
            pltpu.VMEM((8, 128), wide),
            pltpu.VMEM((8, 128), wide),
            pltpu.VMEM((8, D), wide),
            pltpu.VMEM((8, 128), wide),
            pltpu.VMEM((2 * fsdp, 8, 128), wide),
            pltpu.SemaphoreType.DMA((4 * fsdp,)),
            pltpu.SemaphoreType.DMA((4 * fsdp,)),
            pltpu.SemaphoreType.DMA((15,)),
            pltpu.SemaphoreType.DMA((15,)),
            pltpu.SemaphoreType.DMA((10,)),
            pltpu.SemaphoreType.DMA((10,)),
            pltpu.SemaphoreType.DMA((2 * fsdp,)),
            pltpu.SemaphoreType.DMA((2 * fsdp,)),
            pltpu.SemaphoreType.DMA((4,)),
        ],
        compiler_params=pltpu.CompilerParams(
            collective_id=3, has_side_effects=True, vmem_limit_bytes=VMEM_GRANT
        ),
    )(
        grad,
        slot,
        held,
        feed_grads.reshape(-1, shard, D),
        qkv_grads.reshape(-1, shard, D),
        pos_grads.reshape(fsdp, pos_rows, D),
        small_grads,
        depart,
        own,
    )


def attend_back_pair(qkv, grad_mixed, logs, bias, masks, out, sums, rows, pair):
    at = pair * 128
    query = qkv[rows, at : at + 128] * jnp.bfloat16(0.125)
    keys = qkv[rows, D + at : D + at + 128]
    values = qkv[rows, 2 * D + at : 2 * D + at + 128]
    above = grad_mixed[rows, at : at + 128]
    queries = []
    key_sum = value_sum = None
    for side, mask in enumerate(masks):
        head = 2 * pair + side
        side_query = jnp.where(mask, query, jnp.zeros_like(query))
        side_above = jnp.where(mask, above, jnp.zeros_like(above))
        probs = jnp.exp(back_mul(side_query, keys) + (bias - logs[rows, head : head + 1]))
        grad_probs = back_mul(side_above, values)
        inner = jnp.sum(probs * grad_probs, -1, keepdims=True)
        grad_logits = (probs * (grad_probs - inner)).astype(jnp.bfloat16)
        side_value = outer_sum(probs.astype(jnp.bfloat16), side_above)
        side_key = outer_sum(grad_logits, side_query)
        queries.append(matmul(grad_logits, keys))
        value_sum = side_value if side == 0 else value_sum + side_value
        key_sum = side_key if side == 0 else key_sum + side_key
    grad_query = jnp.where(masks[0], queries[0], queries[1]) * 0.125
    out[rows, at : at + 128] = grad_query.astype(jnp.bfloat16)
    out[rows, D + at : D + at + 128] = key_sum.astype(jnp.bfloat16)
    out[rows, 2 * D + at : 2 * D + at + 128] = value_sum.astype(jnp.bfloat16)
    sums[2:3, at : at + 128] += jnp.sum(grad_query, 0, keepdims=True)
    sums[3:4, at : at + 128] += jnp.sum(value_sum, 0, keepdims=True)


def back_kernel(
    lengths,
    qkv,
    grad_mixed,
    logs,
    small,
    grad_r1,
    x,
    weight,
    feed_grads,
    x_out,
    pos_out,
    qkv_out,
    sums,
    depart,
    own,
    grad_qkv,
    r1_in,
    x_in,
    weight_in,
    low_h0,
    pos_sum,
    keep,
    mates,
    box,
    ring_send,
    ring_recv,
    pair_send,
    pair_recv,
    local_sem,
):
    fsdp = LOOP_SIZE
    row, col = lax.axis_index("dp"), lax.axis_index("fsdp")
    core = lax.rem(row, 2)
    mate = (row + 1 - 2 * core, col)
    place = grid_place(col)
    seq = LEN
    sentences = qkv.shape[0] // seq

    barrier = pltpu.get_barrier_semaphore()
    for there in (mate, (row, grid_device(place + 1)), (row, grid_device(place - 1))):
        pl.semaphore_signal(barrier, inc=1, device_id=there, device_id_type=MESH)
    pl.semaphore_wait(barrier, 3)

    def pair_copy(src, dst):
        return pltpu.make_async_remote_copy(
            src_ref=src,
            dst_ref=dst,
            send_sem=pair_send,
            recv_sem=pair_recv,
            device_id=mate,
            device_id_type=MESH,
        )

    def halves(which, target):
        if which == 0:
            return [(feed_grads.at[pl.ds(4 * b, 4)], target.at[b]) for b in range(fsdp)]
        return [(feed_grads.at[pl.ds(32 + 8 * j, 8)], target.at[:, j]) for j in range(4)]

    for which in range(2):

        @pl.when(core == which)
        def _(which=which):
            for src, dst in halves(1 - which, mates):
                pair_copy(src, dst).start()
            for src, dst in halves(which, keep):
                pltpu.make_async_copy(src, dst, local_sem.at[0]).start()

    fills = [
        pltpu.make_async_copy(grad_r1, r1_in, local_sem.at[1]),
        pltpu.make_async_copy(x, x_in, local_sem.at[2]),
        pltpu.make_async_copy(weight.at[pl.ds(0, 3 * D), :], weight_in, local_sem.at[3]),
    ]
    for fill in fills:
        fill.start()

    ring = Ring([(flat_blocks(keep), flat_blocks(mates), box)], 1, ring_send, ring_recv, 0)
    sums[...] = jnp.zeros_like(sums)
    masks = head_masks(seq)
    done = 0
    for sentence in range(sentences):
        bias = live_row(lengths[sentence], seq)
        rows = slice(sentence * seq, (sentence + 1) * seq)
        for pair in range(H // 2):
            attend_back_pair(qkv, grad_mixed, logs, bias, masks, grad_qkv, sums, rows, pair)
            done += 1
            if done == 4:
                pltpu.make_async_copy(keep, keep, local_sem.at[0]).wait()
                pair_copy(mates, mates).wait_recv()
                ring.first()
            if done == 10:
                ring.step(0)
                ring.step(1)
    for fill in fills:
        fill.wait()
    pos_sum[...] = jnp.zeros_like(pos_sum)

    def tile(i, carry):
        span = pl.ds(pl.multiple_of(i * TILE, TILE), TILE)
        grad_h0 = r1_in[span, :]
        for third in range(3):
            cols = slice(third * D, (third + 1) * D)
            grad_h0 = grad_h0 + back_mul(grad_qkv[span, cols], weight_in[cols, :])
        hat, scale = normed(x_in[span, :])
        low_h0[span, :] = (hat * small[0:1, :] + small[1:2, :]).astype(jnp.bfloat16)
        grad_x, gain, shift = norm_back(grad_h0, hat, scale, small[0:1, :])
        add_row(sums, 0, gain)
        add_row(sums, 1, shift)
        x_out[span, :] = grad_x.astype(jnp.bfloat16)
        spot = pl.ds(pl.multiple_of(lax.rem(i, seq // TILE) * TILE, TILE), TILE)
        pos_sum[spot, :] += grad_x
        return carry

    lax.fori_loop(0, sentences * seq // TILE, tile, 0)
    pos_out[...] = pos_sum[...].astype(jnp.bfloat16)
    ring.step(2)
    ring.step(3)
    for third in range(3):
        cols = slice(third * D, (third + 1) * D)
        qkv_out[cols, :] = outer_sum(low_h0[...], grad_qkv[:, cols]).astype(jnp.bfloat16)
    right, left = ring.slot[(3, 1)], ring.slot[(3, -1)]
    for slot in (right, left):
        for copy in ring.copies(slot, ring.events[slot]):
            copy.wait_recv()
    ahead = grid_device(place + 1)
    sum_rows(depart, [ring.parts[0][0].at[ahead], ring.parts[0][1].at[ahead], box.at[right]])
    sum_rows(own, [ring.parts[0][0].at[col], ring.parts[0][1].at[col], box.at[left]])
    pair_copy(mates, mates).wait_send()
    ring.drain()


def back(lengths, qkv, grad_mixed, logs, small, grad_r1, x, weight, feed_grads):
    fsdp = LOOP_SIZE
    tokens = qkv.shape[0]
    shard = D // fsdp
    vmem = pl.BlockSpec(memory_space=pltpu.VMEM)
    anywhere = pl.BlockSpec(memory_space=pl.ANY)
    low, wide = jnp.bfloat16, jnp.float32
    return pl.pallas_call(
        back_kernel,
        name="back",
        in_specs=[pl.BlockSpec(memory_space=pltpu.SMEM)] + [vmem] * 4 + [anywhere] * 4,
        out_specs=[vmem] * 6,
        out_shape=[
            jax.ShapeDtypeStruct((tokens, D), low),
            jax.ShapeDtypeStruct((LEN, D), low),
            jax.ShapeDtypeStruct((3 * D, D), low),
            jax.ShapeDtypeStruct((16, D), wide),
            jax.ShapeDtypeStruct((4 * shard, D), low),
            jax.ShapeDtypeStruct((4 * shard, D), wide),
        ],
        scratch_shapes=[
            pltpu.VMEM((tokens, 3 * D), low),
            pltpu.VMEM((tokens, D), wide),
            pltpu.VMEM((tokens, D), wide),
            pltpu.VMEM((3 * D, D), low),
            pltpu.VMEM((tokens, D), low),
            pltpu.VMEM((LEN, D), wide),
            pltpu.VMEM((fsdp, 4, shard, D), low),
            pltpu.VMEM((fsdp, 4, shard, D), low),
            pltpu.VMEM((fsdp + 1, 4 * shard, D), low),
            pltpu.SemaphoreType.DMA((7,)),
            pltpu.SemaphoreType.DMA((7,)),
            pltpu.SemaphoreType.DMA,
            pltpu.SemaphoreType.DMA,
            pltpu.SemaphoreType.DMA((4,)),
        ],
        compiler_params=pltpu.CompilerParams(
            collective_id=4, has_side_effects=True, vmem_limit_bytes=VMEM_GRANT
        ),
    )(lengths, qkv, grad_mixed, logs, small, grad_r1, x, weight, feed_grads.reshape(-1, shard, D))


def exact_dot(left, right):
    return lax.dot_general(
        left,
        right,
        (((1,), (0,)), ((), ())),
        precision=lax.Precision.HIGHEST,
        preferred_element_type=jnp.float32,
    )


def cosine_parts(first, second):
    dots = jnp.sum(first * second, -1, keepdims=True)
    one = lax.rsqrt(jnp.sum(first * first, -1, keepdims=True) + 1e-06)
    two = lax.rsqrt(jnp.sum(second * second, -1, keepdims=True) + 1e-06)
    return dots * one * two, one, two


def cosine_back(grad, value, first, second, one, two):
    return (
        grad * one * (second * two - value * first * one),
        grad * two * (first * one - value * second * two),
    )


def loss_kernel(sizes, lengths, src, pair_ids, scores, loss_out, share_out, out, send, recv, local):
    gather_kernel(sizes, True, src, out, send, recv, local)
    count, batch = out.shape[0], out.shape[1]
    pooled = jnp.concatenate([out[:, i] for i in range(batch)], 0)
    rows = lax.broadcasted_iota(jnp.int32, (pair_ids.shape[1], count * batch), 1)
    sentence = lax.rem(rows, count) * batch + rows // count
    anchor, near, far = (
        exact_dot((pair_ids[i] == sentence).astype(jnp.float32), pooled) for i in range(3)
    )
    near_cos, near_one, near_two = cosine_parts(anchor, near)
    far_cos, far_one, far_two = cosine_parts(anchor, far)
    near_miss, far_miss = near_cos - scores[0], far_cos - scores[1]
    loss = jnp.sum(near_miss * near_miss + far_miss * far_miss, 0, keepdims=True)
    loss_out[...] = jnp.broadcast_to(loss, loss_out.shape)
    anchor_a, grad_near = cosine_back(
        2.0 * near_miss, near_cos, anchor, near, near_one, near_two
    )
    anchor_b, grad_far = cosine_back(2.0 * far_miss, far_cos, anchor, far, far_one, far_two)
    grads = (anchor_a + anchor_b, grad_near, grad_far)
    me = lax.axis_index("dp") * sizes[1] + lax.axis_index("fsdp")
    for i in range(batch):
        total = jnp.zeros((1, grads[0].shape[1]), jnp.float32)
        for part, grad in enumerate(grads):
            mine = pair_ids[part] == me * batch + i
            total = total + jnp.sum(jnp.where(mine, grad, 0.0), 0, keepdims=True)
        share_out[i] = jnp.broadcast_to(
            total / lengths[i].astype(jnp.float32), share_out.shape[1:]
        )


def pair_grads(lengths, pooled, pair_ids, scores):
    dp, fsdp = lax.axis_size("dp"), lax.axis_size("fsdp")
    count, (batch, width) = dp * fsdp, pooled.shape
    vmem = pl.BlockSpec(memory_space=pltpu.VMEM)
    return pl.pallas_call(
        functools.partial(loss_kernel, (dp, fsdp)),
        name="pair_loss",
        in_specs=[pl.BlockSpec(memory_space=pltpu.SMEM), vmem, vmem, vmem],
        out_specs=[vmem, vmem],
        out_shape=[
            jax.ShapeDtypeStruct((8, 128), jnp.float32),
            jax.ShapeDtypeStruct((batch, 8, width), jnp.float32),
        ],
        scratch_shapes=[
            pltpu.VMEM((count,) + pooled.shape, jnp.float32),
            pltpu.SemaphoreType.DMA((count,)),
            pltpu.SemaphoreType.DMA((count,)),
            pltpu.SemaphoreType.DMA,
        ],
        compiler_params=pltpu.CompilerParams(
            collective_id=1, has_side_effects=True, vmem_limit_bytes=VMEM_GRANT
        ),
    )(lengths, pooled, pair_ids[:, :, None], scores[:, :, None])


def pack_kernel(qkv, out_w, up, down, pos, pieces, low_pos):
    rows = qkv.shape[0]
    low = jnp.bfloat16
    for part in range(3):
        pieces[part * rows : (part + 1) * rows, :] = qkv[:, part * D : (part + 1) * D].astype(low)
    pieces[3 * rows : 4 * rows, :] = out_w[...].astype(low)
    for part in range(4):
        at = (4 + part) * rows
        pieces[at : at + rows, :] = up[:, part * D : (part + 1) * D].astype(low)
    pieces[8 * rows :, :] = down[...].astype(low)
    low_pos[...] = pos[...].astype(low)


def pack(qkv, out_w, up, down, pos):
    rows = qkv.shape[0]
    if rows % 16:
        pieces = jnp.concatenate(
            [split_rows(qkv, 3), out_w, split_rows(up, FF // D), down], 0
        ).astype(jnp.bfloat16)
        return pieces, pos.astype(jnp.bfloat16)
    vmem = pl.BlockSpec(memory_space=pltpu.VMEM)
    return pl.pallas_call(
        pack_kernel,
        name="pack",
        in_specs=[vmem] * 5,
        out_specs=[vmem] * 2,
        out_shape=[
            jax.ShapeDtypeStruct((12 * rows, D), jnp.bfloat16),
            jax.ShapeDtypeStruct(pos.shape, jnp.bfloat16),
        ],
        compiler_params=pltpu.CompilerParams(vmem_limit_bytes=VMEM_GRANT),
    )(qkv, out_w, up, down, pos)


LOOP = {8: (0, 2, 4, 6, 7, 5, 3, 1)}


def swap_core(value):
    return lax.ppermute(value, "dp", [(i, i ^ 1) for i in range(lax.axis_size("dp"))])


def swap_x(value):
    count = lax.axis_size("dp")
    return lax.ppermute(value, "dp", [(i, (i + 2) % count) for i in range(count)])


def sum_x(value):
    count = lax.axis_size("dp")
    total = value
    for hop in range(2, count, 2):
        moved = lax.ppermute(value, "dp", [(i, (i + hop) % count) for i in range(count)])
        total = total.astype(jnp.float32) + moved.astype(jnp.float32)
    return total


def shift(value, step):
    loop = LOOP[lax.axis_size("fsdp")]
    size = len(loop)
    return lax.ppermute(
        value, "fsdp", [(loop[i], loop[(i + step) % size]) for i in range(size)]
    )


def loop_place():
    loop = LOOP[lax.axis_size("fsdp")]
    place = [0] * len(loop)
    for i, device in enumerate(loop):
        place[device] = i
    return jnp.array(place, jnp.int32)[lax.axis_index("fsdp")], jnp.array(loop, jnp.int32)


def ring_gather(part, sign):
    size = lax.axis_size("fsdp")
    place, loop = loop_place()
    out = jnp.zeros((size,) + part.shape, part.dtype)

    def put(out, block, offset):
        at = loop[lax.rem(place + offset + size, size)]
        return lax.dynamic_update_slice(out, block[None], (at, 0, 0))

    out = put(out, part, 0)
    ahead = behind = part
    for hop in range(1, size // 2 + 1):
        ahead = shift(ahead, sign)
        out = put(out, ahead, -sign * hop)
        if hop < size - size // 2:
            behind = shift(behind, -sign)
            out = put(out, behind, sign * hop)
    return out


def ring_reduce(parts, sign):
    size = lax.axis_size("fsdp")
    place, loop = loop_place()

    def local(offset):
        at = loop[lax.rem(place + offset + size, size)]
        return lax.dynamic_index_in_dim(parts, at, 0, keepdims=False).astype(jnp.float32)

    def flow(direction, hops):
        arrived = None
        for hop in range(hops):
            value = local(direction * (hops - hop))
            if arrived is not None:
                value = value + arrived.astype(jnp.float32)
            arrived = shift(value.astype(jnp.bfloat16), direction)
        return arrived

    far = flow(sign, size // 2)
    near = flow(-sign, size - size // 2 - 1)
    return local(0) + far.astype(jnp.float32) + near.astype(jnp.float32)


def gather_halves(first, second, sign):
    core = lax.rem(lax.axis_index("dp"), 2)
    if lax.axis_size("fsdp") not in LOOP:
        return lax.all_gather(first, "fsdp", axis=0), lax.all_gather(second, "fsdp", axis=0)
    mine = ring_gather(jnp.where(core == 0, first, second), sign)
    other = swap_core(mine)
    return jnp.where(core == 0, mine, other), jnp.where(core == 0, other, mine)


def reduce_halves(first, second, sign):
    core = lax.rem(lax.axis_index("dp"), 2)
    give = jnp.where(core == 0, second, first).astype(jnp.bfloat16)
    keep = jnp.where(core == 0, first, second).astype(jnp.float32)
    chip = (keep + swap_core(give).astype(jnp.float32)).astype(jnp.bfloat16)
    if lax.axis_size("fsdp") in LOOP:
        block = ring_reduce(chip, sign)
    else:
        block = lax.psum_scatter(chip.astype(jnp.float32), "fsdp", scatter_dimension=0)
    total = sum_x(block.astype(jnp.bfloat16)).astype(jnp.bfloat16)
    other = swap_core(total)
    low = jnp.where(core == 0, total, other).astype(jnp.float32)
    high = jnp.where(core == 0, other, total).astype(jnp.float32)
    return low, high


def split_rows(weight, parts):
    return jnp.concatenate(jnp.split(weight, parts, axis=1), axis=0)


def join_rows(blocks, parts):
    count, rows, width = blocks.shape
    return (
        blocks.reshape(count, parts, rows // parts, width)
        .transpose(0, 2, 1, 3)
        .reshape(count * rows // parts, parts * width)
    )


def cut_parts(grad, count, parts):
    width = grad.shape[-1]
    return (
        grad.reshape(parts, count, -1, width).transpose(1, 0, 2, 3).reshape(count, -1, width)
    )


def pad_rows(value, rows):
    return jnp.pad(value, [(0, 0)] * (value.ndim - 2) + [(0, rows - value.shape[-2]), (0, 0)])


def round_up(value, step):
    return -(-value // step) * step


def bucket_size(tokens, owners):
    mean = tokens / owners
    return min(tokens, round_up(int(mean + 5.6 * math.sqrt(mean)), 16))


def one_hot(index, count):
    return (index[:, None] == lax.iota(jnp.int32, count)[None, :]).astype(jnp.bfloat16)


class Routes:
    def __init__(self, everyone, own_rows):
        fsdp = lax.axis_size("fsdp")
        self.rows = own_rows
        tokens = everyone.shape[1]
        self.cap = bucket_size(tokens, fsdp)
        me = lax.axis_index("fsdp")
        group = lax.dynamic_slice_in_dim(everyone, lax.axis_index("dp") * fsdp, fsdp, 0)
        mine = lax.dynamic_index_in_dim(group, me, 0, keepdims=False)
        owners = lax.iota(jnp.int32, fsdp)
        every_count = jnp.sum(
            (everyone // own_rows)[:, :, None] == owners[None, None, :], 1, dtype=jnp.int32
        )
        self.rounds = (jnp.max(every_count) + self.cap - 1) // self.cap
        self.inner = group - me * own_rows
        self.held = (self.inner >= 0) & (self.inner < own_rows)
        self.held_place = jnp.cumsum(self.held.astype(jnp.int32), 1) - 1
        self.owner = mine // own_rows
        hot = (self.owner[None, :] == owners[:, None])
        place = jnp.cumsum(hot.astype(jnp.int32), 1) - 1
        self.hot = hot
        self.place = place
        self.my_place = jnp.sum(jnp.where(hot, place, 0), 0)

    def slots(self, flag, place, value, turn):
        slot = lax.iota(jnp.int32, self.cap)[None, :, None] + turn * self.cap
        hit = flag[:, None, :] & (place[:, None, :] == slot)
        return (jnp.sum(jnp.where(hit, value[:, None, :] + 1, 0), -1) - 1).reshape(-1)

    def owner_rows(self, turn):
        return self.slots(self.held, self.held_place, self.inner, turn)

    def asker_tokens(self, turn):
        tokens = lax.iota(jnp.int32, self.owner.shape[0])[None, :]
        return self.slots(self.hot, self.place, tokens, turn)

    def asker_slots(self, turn):
        place = self.my_place - turn * self.cap
        inside = (place >= 0) & (place < self.cap)
        return jnp.where(inside, self.owner * self.cap + place, -1)


def exchange(rows):
    fsdp = lax.axis_size("fsdp")
    blocks = rows.reshape(fsdp, rows.shape[0] // fsdp, rows.shape[1])
    return lax.all_to_all(blocks, "fsdp", 0, 0).reshape(rows.shape)


def pick_kernel(index, table, out):
    rows = lax.broadcasted_iota(jnp.int32, (index.shape[0], table.shape[0]), 1)
    pick = (index[:, 0:1] == rows).astype(jnp.bfloat16)
    out[...] = matmul(pick, table[...].astype(jnp.bfloat16)).astype(jnp.bfloat16)


def gather_table(table, routes, turn):
    index = routes.owner_rows(turn)
    size = routes.cap
    return call(
        pick_kernel,
        "pick_rows",
        (index.shape[0] // size,),
        [rows_spec(128, size), whole_spec(table.shape)],
        [rows_spec(D, size)],
        [jax.ShapeDtypeStruct((index.shape[0], D), jnp.bfloat16)],
        flops=2 * index.shape[0] * D * table.shape[0],
        moved=table.shape[0] * D * 4,
    )(jnp.broadcast_to(index[:, None], (index.shape[0], 128)), table)[0]


def all_words(everyone, table, rounds, tokens):
    def more(carry):
        return carry[0] < rounds

    def body(carry):
        turn, words = carry
        ids, turn, rows = lax.optimization_barrier((everyone, turn, table))
        routes = Routes(ids, table.shape[0])
        got = exchange(gather_table(rows, routes, turn))
        mine = matmul(one_hot(routes.asker_slots(turn), got.shape[0]), got)
        return turn + 1, words + mine.astype(jnp.bfloat16)

    start = (jnp.int32(0), jnp.zeros((tokens, D), jnp.bfloat16))
    return lax.while_loop(more, body, start)[1]


def return_round(grad_low, everyone, turn, rows):
    routes = Routes(everyone, rows)
    held = routes.owner_rows(turn)[None, :]
    sent = bucket_rows(routes.asker_slots(turn)[None, :], grad_low, held.shape[1])
    return scatter_rows(held, exchange(sent), rows)


def return_rows(grad_low, everyone, rounds, rows):
    def more(carry):
        return carry[0] < rounds

    def body(carry):
        turn, total = carry
        ids, turn = lax.optimization_barrier((everyone, turn))
        return turn + 1, total + return_round(grad_low, ids, turn, rows)

    return lax.while_loop(more, body, (jnp.int32(0), jnp.zeros((rows, D), jnp.float32)))[1]


def more_grads(grad_low, plan, table, squares):
    def more(carry):
        return carry[0] < plan.rounds

    def body(carry):
        turn, table, squares = carry
        ids, turn = lax.optimization_barrier((plan.everyone, turn))
        before = table.astype(jnp.float32)
        after = (before + sum_groups(return_round(grad_low, ids, turn, table.shape[0]))).astype(
            jnp.bfloat16
        )
        change = jnp.sum(after.astype(jnp.float32) ** 2) - jnp.sum(before * before)
        return turn + 1, after, squares + lax.psum(change, "fsdp")

    return lax.while_loop(more, body, (jnp.int32(1), table, squares))[1:]


def total_grads(everyone, rounds, grad_x, feed_grads, qkv_grads, grad_pos, grad_small, own_rows):
    fsdp = lax.axis_size("fsdp")
    down, up = reduce_halves(
        feed_grads[:FF].reshape(fsdp, -1, D), cut_parts(feed_grads[FF : 2 * FF], fsdp, 4), 1
    )
    qkv_cut = cut_parts(qkv_grads, fsdp, 3)
    shard = qkv_cut.shape[1] // 3
    pos_cut = grad_pos.reshape(fsdp, -1, D)
    half_pos = pos_cut.shape[1] // 2
    low, high = reduce_halves(
        jnp.concatenate([qkv_cut[:, : 2 * shard], pos_cut[:, :half_pos]], 1),
        jnp.concatenate(
            [
                qkv_cut[:, 2 * shard :],
                feed_grads[2 * FF :].reshape(fsdp, shard, D),
                pos_cut[:, half_pos:],
            ],
            1,
        ),
        -1,
    )
    cols = D // fsdp
    small = lax.dynamic_slice_in_dim(
        lax.psum(grad_small, ("dp", "fsdp")), lax.axis_index("fsdp") * cols, cols, 1
    )
    small = jnp.pad(small, ((0, 0), (0, 128 - cols)))
    table = sum_groups(return_rows(grad_x, everyone, rounds, own_rows))
    squares = sum(jnp.sum(part * part) for part in (table, down, up, low, high, small))
    squares = jnp.sum(gather_small(jnp.full((8, 128), squares), False, 2)[:, 0, 0])
    return (
        table.astype(jnp.bfloat16),
        jnp.stack([down, up]).astype(jnp.bfloat16),
        jnp.stack([low, high]).astype(jnp.bfloat16),
        small,
        squares,
    )


class Plan:
    def __init__(self, lengths, ids, pieces, pos_low, small, table):
        fsdp = lax.axis_size("fsdp")
        seq = ids.shape[1]
        tokens = ids.size
        cap = self.cap = bucket_size(tokens, fsdp)
        cols = small.shape[1]
        self.direct = fsdp == LOOP_SIZE and lax.axis_size("dp") == 4 and tokens == 1024
        if self.direct:
            block = lax.dynamic_update_slice(
                jnp.zeros((16, 256), jnp.bfloat16),
                small,
                (0, lax.rem(lax.axis_index("fsdp") * cols, 128)),
            )
            everyone, self.first, self.second, self.small, held, self.asker_row, most, *state = front(
                lengths, ids.reshape(1, tokens), pieces, pos_low, block, table, cap
            )
            self.everyone = everyone.reshape(-1, tokens)
            self.rounds = (most[0, 0] + cap - 1) // cap
            self.held = held.reshape(4, 1, -1)
            self.state = self.redo(lengths, table, seq, state, pos_low)
        else:
            self.everyone = gather_small(ids.reshape(-1, 128), True, 0).reshape(-1, tokens)
            self.rounds = Routes(self.everyone, table.shape[0]).rounds
            both = lax.all_gather(pieces, "fsdp", axis=0)
            shard = pieces.shape[0] // 12
            columns = both[:, : 8 * shard].reshape(fsdp, 8, shard, D).transpose(1, 0, 2, 3)
            self.first = columns[:4].reshape(-1, D)
            self.second = jnp.concatenate(
                [columns[4:].reshape(-1, D), both[:, 8 * shard :].reshape(-1, D)], 0
            )
            smalls = lax.all_gather(jnp.pad(small, ((0, 2), (0, 128 - cols))), "fsdp", axis=0)
            self.small = (
                smalls[:, :, :cols].transpose(1, 0, 2).reshape(16, D).astype(jnp.float32)
            )
            self.state = self.again(lengths, table, seq, pos_low, self.everyone)

    def again(self, lengths, table, seq, pos_low, everyone):
        tokens = everyone.shape[1]
        words = all_words(everyone, table, self.rounds, tokens)
        pos = lax.all_gather(pos_low, "fsdp", axis=0, tiled=True)
        nowhere = jnp.full((tokens, 128), -1, jnp.int32)
        x, h0, qkv = embed(nowhere, jnp.zeros((128, D), jnp.bfloat16), words, pos, self.first, self.small)
        return [x, h0, qkv, *attend(lengths, qkv, seq)]

    def redo(self, lengths, table, seq, state, pos_low):
        def more(carry):
            return carry[0] < self.rounds

        def once(carry):
            everyone, low, _ = lax.optimization_barrier((self.everyone, pos_low, carry[0]))
            return [self.rounds] + self.again(lengths, table, seq, low, everyone)

        return lax.while_loop(more, once, [jnp.int32(1)] + state)[1:]


def sum_groups(table):
    core = lax.rem(lax.axis_index("dp"), 2)
    half = table.shape[0] // 2
    low = table.astype(jnp.bfloat16)
    keep = lax.dynamic_slice_in_dim(table, core * half, half, 0)
    give = lax.dynamic_slice_in_dim(low, (1 - core) * half, half, 0)
    chip = (keep + swap_core(give).astype(jnp.float32)).astype(jnp.bfloat16)
    total = sum_x(chip).astype(jnp.bfloat16)
    other = swap_core(total)
    return jnp.concatenate(
        [jnp.where(core == 0, total, other), jnp.where(core == 0, other, total)], 0
    ).astype(jnp.float32)


def renew(weight, moment, average, grad, factor):
    step = factor * grad
    buffer = MOMENTUM * moment + step
    fresh = weight - RATE * (step + MOMENTUM * buffer)
    return (fresh, buffer, KEEP * average + (1.0 - KEEP) * fresh)


def renew_kernel(factor, *refs):
    kinds = len(refs) // 7
    scale = factor[0, 0]
    for kind in range(kinds):
        weight, moment, average, grad = refs[4 * kind : 4 * kind + 4]
        outs = refs[4 * kinds + 3 * kind : 4 * kinds + 3 * kind + 3]
        shape = weight.shape
        value = grad[...] if len(grad.shape) == 2 else grad[0]
        value = value[: shape[0], : shape[1]].astype(jnp.float32)
        results = renew(weight[...], moment[...], average[...], value, scale)
        for out, result in zip(outs, results):
            out[...] = result


def renew_all(factor, groups, table, sum_a, sum_b, small):
    steps = 12
    own_rows = table.shape[0]
    rows = groups[2][0].shape[0]
    half_pos = groups[1][0].shape[0] // 2
    down_rows = groups[5][0].shape[0]
    cols = 256

    def piece(i):
        return jnp.minimum(i // 3, 2)

    def third(i):
        return lax.rem(jnp.minimum(i, 8), 3)

    def late(i):
        return jnp.clip(i - 9, 0, 2)

    specs = [
        (pl.BlockSpec((own_rows // steps, D), lambda i: (i, 0)), None, table),
        (
            pl.BlockSpec((half_pos, D), lambda i: (jnp.minimum(i, 1), 0)),
            pl.BlockSpec((1, half_pos, D), lambda i: (jnp.minimum(i, 1), 2 * rows // half_pos, 0)),
            sum_b,
        ),
        (
            pl.BlockSpec((rows, cols), lambda i: (0, jnp.minimum(i, 8))),
            pl.BlockSpec(
                (1, rows, cols), lambda i: (piece(i) // 2, lax.rem(piece(i), 2), third(i))
            ),
            sum_b,
        ),
        (
            pl.BlockSpec((rows, cols), lambda i: (0, late(i))),
            pl.BlockSpec((1, rows, cols), lambda i: (1, 1, late(i))),
            sum_b,
        ),
        (
            pl.BlockSpec((rows, cols), lambda i: (0, i)),
            pl.BlockSpec((1, rows, cols), lambda i: (1, i // 3, lax.rem(i, 3))),
            sum_a,
        ),
        (
            pl.BlockSpec((down_rows // steps, D), lambda i: (i, 0)),
            pl.BlockSpec((1, down_rows // steps, D), lambda i: (0, i, 0)),
            sum_a,
        ),
        (whole_spec(groups[6][0].shape), whole_spec(small.shape), small),
    ]
    in_specs = [pl.BlockSpec(memory_space=pltpu.SMEM)]
    out_specs, shapes, operands = [], [], [factor.reshape(1, 1)]
    for (spec, grad_spec, grad), group in zip(specs, groups):
        in_specs += [spec] * 3 + [grad_spec or spec]
        operands += [*group, grad]
        out_specs += [spec] * 3
        shapes += [jax.ShapeDtypeStruct(group[0].shape, jnp.float32)] * 3
    size = sum(group[0].size for group in groups)
    results = call(
        renew_kernel, "renew", (steps,), in_specs, out_specs, shapes, flops=8 * size, moved=26 * size
    )(*operands)
    return results[0::3], results[1::3], results[2::3]


def shards(
    token_ids,
    lengths,
    pair_ids,
    scores,
    word_table,
    pos_table,
    qkv_weight,
    out_weight,
    up_weight,
    down_weight,
    small_params,
    word_moment,
    pos_moment,
    qkv_moment,
    out_moment,
    up_moment,
    down_moment,
    small_moment,
    word_average,
    pos_average,
    qkv_average,
    out_average,
    up_average,
    down_average,
    small_average,
):
    batch, seq = token_ids.shape
    width = D
    fsdp = lax.axis_size("fsdp")
    tokens = batch * seq
    shard = qkv_weight.shape[0]
    pos_rows = pos_table.shape[0]
    small_cols = small_params.shape[1]
    pieces, pos_low = pack(qkv_weight, out_weight, up_weight, down_weight, pos_table)
    plan = Plan(
        lengths,
        token_ids,
        pieces,
        pos_low,
        small_params.astype(jnp.bfloat16),
        word_table,
    )
    first, second, small_full = plan.first, plan.second, plan.small
    x, h0, qkv, mixed, logs = plan.state
    r1, low_h1, act, slope, r2, pooled = feed(lengths, mixed, h0, first, second, small_full)
    loss, share = pair_grads(lengths, pooled[:, 0], pair_ids, scores)
    low_f, low_u, grad_r1, low_a, grad_mixed, sums_feed = feed_back(
        lengths, share, r1, r2, slope, first, second, small_full
    )
    feed_grads = feed_weights(act, low_f, low_h1, low_u, mixed, low_a)
    own_rows = word_table.shape[0]
    if plan.direct:
        grad_x, low_pos, qkv_grads, sums_back, depart, own = back(
            lengths, qkv, grad_mixed, logs, small_full, grad_r1, x, first, feed_grads
        )
        grad_small = sums_feed + sums_back
        small_cut = jnp.pad(
            grad_small.reshape(16, fsdp, small_cols).transpose(1, 0, 2),
            ((0, 0), (0, 0), (0, 128 - small_cols)),
        )
        table, sum_a, sum_b, small, squares = finish(
            grad_x,
            plan.asker_row,
            plan.held,
            feed_grads,
            qkv_grads,
            low_pos,
            small_cut,
            depart,
            own,
            own_rows,
            plan.cap,
        )
        small = small.reshape(16, 128)
        table, total = more_grads(grad_x, plan, table, squares[0, 0])
    else:
        grad_qkv, sums_attend = attend_back(lengths, qkv, grad_mixed, logs, seq)
        grad_x, grad_pos, sums_embed = embed_back(grad_r1, grad_qkv, first, x, small_full, seq)
        qkv_grads = qkv_weights(h0, grad_qkv)
        grad_small = sums_feed + sums_attend + sums_embed
        table, sum_a, sum_b, small, total = total_grads(
            plan.everyone,
            plan.rounds,
            grad_x,
            feed_grads,
            qkv_grads,
            grad_pos.astype(jnp.bfloat16),
            grad_small,
            own_rows,
        )
    norm = jnp.sqrt(total)
    limit = 1e-05 * math.sqrt((VOCAB + LEN + 4 * D + 2 * FF + 14) * D)
    factor = jnp.minimum(1.0, limit / (norm + 1e-06))
    weights = (word_table, pos_table, qkv_weight, out_weight, up_weight, down_weight, small_params)
    moments = (
        word_moment,
        pos_moment,
        qkv_moment,
        out_moment,
        up_moment,
        down_moment,
        small_moment,
    )
    averages = (
        word_average,
        pos_average,
        qkv_average,
        out_average,
        up_average,
        down_average,
        small_average,
    )
    if plan.direct:
        groups = list(zip(weights, moments, averages))
        new_w, new_m, new_a = renew_all(factor, groups, table, sum_a, sum_b, small)
    else:
        wide_b = sum_b.astype(jnp.float32)
        summed = (
            table.astype(jnp.float32),
            wide_b[:, 2 * shard :].reshape(pos_rows, width),
            jnp.concatenate([wide_b[0, :shard], wide_b[0, shard : 2 * shard], wide_b[1, :shard]], 1),
            wide_b[1, shard : 2 * shard],
            join_rows(sum_a[1][None], 4).astype(jnp.float32),
            sum_a[0].astype(jnp.float32),
            small[:14, :small_cols],
        )
        new_w = []
        new_m = []
        new_a = []
        for weight, moment, average, grad in zip(weights, moments, averages, summed):
            fresh, buffer, mean_new = renew(weight, moment, average, grad, factor)
            new_w.append(fresh)
            new_m.append(buffer)
            new_a.append(mean_new)
    return (
        loss[0, 0],
        norm,
        new_w[0],
        new_w[1],
        new_w[2],
        new_w[3],
        new_w[4],
        new_w[5],
        new_w[6],
        new_m[0],
        new_m[1],
        new_m[2],
        new_m[3],
        new_m[4],
        new_m[5],
        new_m[6],
        new_a[0],
        new_a[1],
        new_a[2],
        new_a[3],
        new_a[4],
        new_a[5],
        new_a[6],
    )


def solution(mesh):
    placed = (
        P(("dp", "fsdp"), None),
        P(("dp", "fsdp")),
        P(),
        P(),
        P("fsdp", None),
        P("fsdp", None),
        P("fsdp", None),
        P("fsdp", None),
        P("fsdp", None),
        P("fsdp", None),
        P(None, "fsdp"),
        P("fsdp", None),
        P("fsdp", None),
        P("fsdp", None),
        P("fsdp", None),
        P("fsdp", None),
        P("fsdp", None),
        P(None, "fsdp"),
        P("fsdp", None),
        P("fsdp", None),
        P("fsdp", None),
        P("fsdp", None),
        P("fsdp", None),
        P("fsdp", None),
        P(None, "fsdp"),
    )
    return jax.shard_map(
        shards,
        mesh=mesh,
        in_specs=placed,
        out_specs=(
            P(),
            P(),
            P("fsdp", None),
            P("fsdp", None),
            P("fsdp", None),
            P("fsdp", None),
            P("fsdp", None),
            P("fsdp", None),
            P(None, "fsdp"),
            P("fsdp", None),
            P("fsdp", None),
            P("fsdp", None),
            P("fsdp", None),
            P("fsdp", None),
            P("fsdp", None),
            P(None, "fsdp"),
            P("fsdp", None),
            P("fsdp", None),
            P("fsdp", None),
            P("fsdp", None),
            P("fsdp", None),
            P("fsdp", None),
            P(None, "fsdp"),
        ),
        check_vma=False,
    )
```

```python
import functools
import math

import jax
import jax.numpy as jnp
from jax import lax
from jax.experimental import pallas as pl
from jax.experimental.pallas import tpu as pltpu
from jax.sharding import PartitionSpec as P

D = 768
H = 12
FF = 3072
VOCAB = 30720
LEN = 512


MOMENTUM = 0.9
RATE = 3000.0
KEEP = 0.9


def matmul(left, right):
    return jnp.dot(left, right, preferred_element_type=jnp.float32)


def outer_sum(left, right):
    return lax.dot_general(
        left, right, (((0,), (0,)), ((), ())), preferred_element_type=jnp.float32
    )


def back_mul(grad, weight):
    return lax.dot_general(
        grad, weight, (((1,), (1,)), ((), ())), preferred_element_type=jnp.float32
    )


TILE = 256
EPS = 1e-12
VMEM_GRANT = 60 * 1024 * 1024


def whole_spec(shape):
    return pl.BlockSpec(shape, lambda *_: (0,) * len(shape))


def rows_spec(width, rows=TILE):
    return pl.BlockSpec((rows, width), lambda i, *_: (i, 0))


def weight_spec(rows, at):
    return pl.BlockSpec((rows, D), lambda i, *_: (at, 0))


def call(kernel, name, grid, in_specs, out_specs, out_shape, scratch=(), prefetch=0, flops=0, moved=0):
    return pl.pallas_call(
        kernel,
        name=name,
        grid_spec=pltpu.PrefetchScalarGridSpec(
            num_scalar_prefetch=prefetch,
            grid=grid,
            in_specs=in_specs,
            out_specs=out_specs,
            scratch_shapes=scratch,
        ),
        out_shape=out_shape,
        compiler_params=pltpu.CompilerParams(vmem_limit_bytes=VMEM_GRANT),
        cost_estimate=pl.CostEstimate(flops=flops, bytes_accessed=moved, transcendentals=0),
    )


def normed(v):
    mean = jnp.mean(v, -1, keepdims=True)
    cent = v - mean
    scale = lax.rsqrt(jnp.mean(cent * cent, -1, keepdims=True) + EPS)
    return cent * scale, scale


def norm_back(grad, hat, scale, gain):
    inner = grad * gain
    middle = jnp.mean(inner, -1, keepdims=True)
    along = jnp.mean(inner * hat, -1, keepdims=True)
    return (
        scale * (inner - middle - hat * along),
        jnp.sum(grad * hat, 0, keepdims=True),
        jnp.sum(grad, 0, keepdims=True),
    )


def add_row(ref, row, value):
    ref[row : row + 1, :] += value


def embed_kernel(slot, got, extra, pos, weight, small, x_out, h0_out, qkv_out):
    count = got.shape[0]
    pick = (slot[:, 0:1] == lax.broadcasted_iota(jnp.int32, (slot.shape[0], count), 1)).astype(
        jnp.bfloat16
    )
    words = matmul(pick, got[...]) + extra[...].astype(jnp.float32)
    x = words + pos[...].astype(jnp.float32)
    hat, _ = normed(x)
    h0 = hat * small[0:1, :] + small[1:2, :]
    x_out[...] = x
    h0_out[...] = h0
    low = h0.astype(jnp.bfloat16)
    for third, bias in enumerate((2, None, 3)):
        value = matmul(low, weight[third * D : (third + 1) * D, :])
        if bias is not None:
            value = value + small[bias : bias + 1, :]
        qkv_out[:, third * D : (third + 1) * D] = value.astype(jnp.bfloat16)


def embed(slot, got, extra, pos, weight, small):
    tokens = slot.shape[0]
    turns = pos.shape[0] // TILE
    return call(
        embed_kernel,
        "embed_qkv",
        (tokens // TILE,),
        [
            rows_spec(128),
            whole_spec(got.shape),
            rows_spec(D),
            pl.BlockSpec((TILE, D), lambda i: (lax.rem(i, turns), 0)),
            weight_spec(3 * D, 0),
            whole_spec(small.shape),
        ],
        [rows_spec(D), rows_spec(D), rows_spec(3 * D)],
        [
            jax.ShapeDtypeStruct((tokens, D), jnp.float32),
            jax.ShapeDtypeStruct((tokens, D), jnp.float32),
            jax.ShapeDtypeStruct((tokens, 3 * D), jnp.bfloat16),
        ],
        flops=2 * tokens * D * (3 * D + got.shape[0]),
        moved=tokens * D * 20,
    )(slot, got, extra, pos, weight, small)


def head_masks(rows):
    lane = lax.broadcasted_iota(jnp.int32, (rows, 128), 1)
    return (lane < 64, lane >= 64)


def live_row(length, seq):
    return jnp.where(
        lax.broadcasted_iota(jnp.int32, (1, seq), 1) < length, 0.0, -1000000000.0
    ).astype(jnp.float32)


def attend_pair(qkv, bias, masks, logs, mixed_out, rows, pair):
    at = pair * 128
    query = qkv[rows, at : at + 128] * jnp.bfloat16(0.125)
    keys = qkv[rows, D + at : D + at + 128]
    values = qkv[rows, 2 * D + at : 2 * D + at + 128]
    lane = lax.broadcasted_iota(jnp.int32, logs.shape, 1)
    sides = []
    for side, mask in enumerate(masks):
        logits = back_mul(jnp.where(mask, query, jnp.zeros_like(query)), keys) + bias
        top = jnp.max(logits, -1, keepdims=True)
        raised = jnp.exp(logits - top)
        total = jnp.sum(raised, -1, keepdims=True)
        probs = (raised * (1.0 / total)).astype(jnp.bfloat16)
        sides.append(matmul(probs, values))
        logs = jnp.where(lane == 2 * pair + side, top + jnp.log(total), logs)
    mixed_out[rows, at : at + 128] = jnp.where(masks[0], sides[0], sides[1]).astype(jnp.bfloat16)
    return logs


def attend_kernel(lengths, qkv, mixed_out, log_out):
    seq = qkv.shape[0]
    bias = live_row(lengths[pl.program_id(0)], seq)
    masks = head_masks(seq)
    logs = jnp.zeros((seq, 128), jnp.float32)
    for pair in range(H // 2):
        logs = attend_pair(qkv, bias, masks, logs, mixed_out, slice(0, seq), pair)
    log_out[...] = logs


def attend(lengths, qkv, seq):
    tokens = qkv.shape[0]
    return call(
        attend_kernel,
        "attention",
        (tokens // seq,),
        [rows_spec(3 * D, seq)],
        [rows_spec(D, seq), rows_spec(128, seq)],
        [
            jax.ShapeDtypeStruct((tokens, D), jnp.bfloat16),
            jax.ShapeDtypeStruct((tokens, 128), jnp.float32),
        ],
        prefetch=1,
        flops=4 * tokens * seq * D,
        moved=tokens * D * 8,
    )(lengths, qkv)


def feed_kernel(
    lengths, mixed, h0, out_w, up_w, down_w, small, r1_out, h1_out, act_out, slope_out, r2_out, pooled
):
    step = pl.program_id(0)
    turns = LEN // TILE
    r1 = h0[...] + (matmul(mixed[...], out_w[...]) + small[4:5, :])
    hat, _ = normed(r1)
    h1 = hat * small[5:6, :] + small[6:7, :]
    low = h1.astype(jnp.bfloat16)
    r1_out[...] = r1
    h1_out[...] = low
    ffn = jnp.zeros(r1.shape, jnp.float32)
    for part in range(FF // D):
        up = matmul(low, up_w[part * D : (part + 1) * D, :]) + small[7 + part : 8 + part, :]
        below = 0.5 * (1.0 + lax.erf(up * math.sqrt(0.5)))
        act = (up * below).astype(jnp.bfloat16)
        slope = below + up * jnp.exp(-0.5 * up * up) * (1.0 / math.sqrt(2.0 * math.pi))
        act_out[:, part * D : (part + 1) * D] = act
        slope_out[:, part * D : (part + 1) * D] = slope.astype(jnp.bfloat16)
        ffn = ffn + matmul(act, down_w[part * D : (part + 1) * D, :])
    r2 = h1 + (ffn + small[11:12, :])
    r2_out[...] = r2
    hat2, _ = normed(r2)
    h2 = hat2 * small[12:13, :] + small[13:14, :]
    length = lengths[step // turns]
    at = lax.rem(step, turns) * TILE + lax.broadcasted_iota(jnp.int32, (TILE, 1), 0)
    part_sum = jnp.sum(jnp.where(at < length, h2, 0.0), 0, keepdims=True)

    @pl.when(lax.rem(step, turns) == 0)
    def _():
        pooled[...] = jnp.zeros_like(pooled)

    pooled[0, 0:1, :] += part_sum / length.astype(jnp.float32)


def feed(lengths, mixed, h0, first, second, small):
    tokens = mixed.shape[0]
    turns = LEN // TILE
    return call(
        feed_kernel,
        "feed_forward",
        (tokens // TILE,),
        [
            rows_spec(D),
            rows_spec(D),
            weight_spec(D, 3),
            weight_spec(FF, 0),
            weight_spec(FF, 1),
            whole_spec(small.shape),
        ],
        [
            rows_spec(D),
            rows_spec(D),
            rows_spec(FF),
            rows_spec(FF),
            rows_spec(D),
            pl.BlockSpec((1, 8, D), lambda i, *_: (i // turns, 0, 0)),
        ],
        [
            jax.ShapeDtypeStruct((tokens, D), jnp.float32),
            jax.ShapeDtypeStruct((tokens, D), jnp.bfloat16),
            jax.ShapeDtypeStruct((tokens, FF), jnp.bfloat16),
            jax.ShapeDtypeStruct((tokens, FF), jnp.bfloat16),
            jax.ShapeDtypeStruct((tokens, D), jnp.float32),
            jax.ShapeDtypeStruct((tokens // LEN, 8, D), jnp.float32),
        ],
        prefetch=1,
        flops=2 * tokens * D * (D + 2 * FF),
        moved=tokens * D * 32,
    )(lengths, mixed, h0, first, second, second, small)


def feed_back_kernel(
    lengths,
    share,
    r1,
    r2,
    slope,
    out_w,
    up_w,
    down_w,
    small,
    act,
    low_h1,
    mixed,
    r1_grad,
    mixed_out,
    sums,
    weights_out,
    low_f,
    low_u,
    low_a,
):
    step = pl.program_id(0)
    turns = LEN // TILE
    tiles = low_f.shape[0] // TILE
    parts = FF // D

    @pl.when(step == 0)
    def _():
        sums[...] = jnp.zeros_like(sums)

    @pl.when(step < tiles)
    def _():
        rows = pl.ds(pl.multiple_of(step * TILE, TILE), TILE)
        length = lengths[jnp.minimum(step, tiles - 1) // turns]
        at = lax.rem(step, turns) * TILE + lax.broadcasted_iota(jnp.int32, (TILE, 1), 0)
        grad_h2 = jnp.where(at < length, share[0, 0:1, :], 0.0)
        hat2, scale2 = normed(r2[...])
        grad_r2, gain2, shift2 = norm_back(grad_h2, hat2, scale2, small[12:13, :])
        add_row(sums, 12, gain2)
        add_row(sums, 13, shift2)
        add_row(sums, 11, jnp.sum(grad_r2, 0, keepdims=True))
        tile_f = grad_r2.astype(jnp.bfloat16)
        low_f[rows, :] = tile_f
        grad_h1 = grad_r2
        for part in range(parts):
            span = slice(part * D, (part + 1) * D)
            grad_up = back_mul(tile_f, down_w[span, :]) * slope[:, span].astype(jnp.float32)
            add_row(sums, 7 + part, jnp.sum(grad_up, 0, keepdims=True))
            tile_u = grad_up.astype(jnp.bfloat16)
            low_u[part, rows, :] = tile_u
            grad_h1 = grad_h1 + back_mul(tile_u, up_w[span, :])
        hat1, scale1 = normed(r1[...])
        grad_r1, gain1, shift1 = norm_back(grad_h1, hat1, scale1, small[5:6, :])
        add_row(sums, 5, gain1)
        add_row(sums, 6, shift1)
        add_row(sums, 4, jnp.sum(grad_r1, 0, keepdims=True))
        r1_grad[...] = grad_r1
        tile_a = grad_r1.astype(jnp.bfloat16)
        low_a[rows, :] = tile_a
        mixed_out[...] = back_mul(tile_a, out_w[...]).astype(jnp.bfloat16)

    turn = step - tiles

    @pl.when((turn >= 0) & (turn < parts))
    def _():
        weights_out[...] = outer_sum(act[...], low_f[...]).astype(jnp.bfloat16)

    @pl.when((turn >= parts) & (turn < 2 * parts))
    def _():
        part = jnp.clip(turn - parts, 0, parts - 1)
        weights_out[...] = outer_sum(low_h1[...], low_u[part]).astype(jnp.bfloat16)

    @pl.when(turn == 2 * parts)
    def _():
        weights_out[...] = outer_sum(mixed[...], low_a[...]).astype(jnp.bfloat16)


def feed_back(lengths, share, r1, r2, slope, first, second, small, act, low_h1, mixed):
    tokens = r1.shape[0]
    turns = LEN // TILE
    tiles = tokens // TILE
    parts = FF // D

    def rows(width):
        return pl.BlockSpec((TILE, width), lambda i, *_: (jnp.minimum(i, tiles - 1), 0))

    return call(
        feed_back_kernel,
        "feed_forward_back",
        (tiles + 2 * parts + 1,),
        [
            pl.BlockSpec((1, 8, D), lambda i, *_: (jnp.minimum(i, tiles - 1) // turns, 0, 0)),
            rows(D),
            rows(D),
            rows(FF),
            weight_spec(D, 3),
            weight_spec(FF, 0),
            weight_spec(FF, 1),
            whole_spec(small.shape),
            pl.BlockSpec((tokens, D), lambda i, *_: (0, jnp.clip(i - tiles, 0, parts - 1))),
            whole_spec((tokens, D)),
            whole_spec((tokens, D)),
        ],
        [
            rows(D),
            rows(D),
            whole_spec((16, D)),
            pl.BlockSpec((D, D), lambda i, *_: (jnp.maximum(i - tiles, 0), 0)),
        ],
        [
            jax.ShapeDtypeStruct((tokens, D), jnp.float32),
            jax.ShapeDtypeStruct((tokens, D), jnp.bfloat16),
            jax.ShapeDtypeStruct((16, D), jnp.float32),
            jax.ShapeDtypeStruct(((2 * parts + 1) * D, D), jnp.bfloat16),
        ],
        scratch=[
            pltpu.VMEM((tokens, D), jnp.bfloat16),
            pltpu.VMEM((parts, tokens, D), jnp.bfloat16),
            pltpu.VMEM((tokens, D), jnp.bfloat16),
        ],
        prefetch=1,
        flops=4 * tokens * D * (D + 2 * FF),
        moved=tokens * D * 48,
    )(lengths, share, r1, r2, slope, first, second, second, small, act, low_h1, mixed)


def attend_back_kernel(lengths, qkv, grad_mixed, logs, out, sums):
    seq = qkv.shape[0]
    bias = live_row(lengths[pl.program_id(0)], seq)
    masks = head_masks(seq)

    @pl.when(pl.program_id(0) == 0)
    def _():
        sums[...] = jnp.zeros_like(sums)

    for pair in range(H // 2):
        attend_back_pair(
            qkv, grad_mixed, logs, bias, masks, out, sums, slice(0, seq), pair
        )


def attend_back(lengths, qkv, grad_mixed, logs, seq):
    tokens = qkv.shape[0]
    return call(
        attend_back_kernel,
        "attention_back",
        (tokens // seq,),
        [rows_spec(3 * D, seq), rows_spec(D, seq), rows_spec(128, seq)],
        [rows_spec(3 * D, seq), whole_spec((16, D))],
        [
            jax.ShapeDtypeStruct((tokens, 3 * D), jnp.bfloat16),
            jax.ShapeDtypeStruct((16, D), jnp.float32),
        ],
        prefetch=1,
        flops=10 * tokens * seq * D,
        moved=tokens * D * 16,
    )(lengths, qkv, grad_mixed, logs)


def embed_back_kernel(grad_r1, grad_qkv, weight, x, small, x_out, pos_out, sums):
    spot, sentence = pl.program_id(0), pl.program_id(1)

    @pl.when((spot == 0) & (sentence == 0))
    def _():
        sums[...] = jnp.zeros_like(sums)

    @pl.when(sentence == 0)
    def _():
        pos_out[...] = jnp.zeros_like(pos_out)

    grad_h0 = grad_r1[...]
    for third in range(3):
        span = slice(third * D, (third + 1) * D)
        grad_h0 = grad_h0 + back_mul(grad_qkv[:, span], weight[span, :])
    hat, scale = normed(x[...])
    grad_x, gain, shift = norm_back(grad_h0, hat, scale, small[0:1, :])
    add_row(sums, 0, gain)
    add_row(sums, 1, shift)
    x_out[...] = grad_x.astype(jnp.bfloat16)
    pos_out[...] += grad_x


def embed_back(grad_r1, grad_qkv, weight, x, small, seq):
    tokens = x.shape[0]
    turns = seq // TILE

    def rows(width):
        return pl.BlockSpec((TILE, width), lambda p, b: (b * turns + p, 0))

    return call(
        embed_back_kernel,
        "embed_back",
        (turns, tokens // seq),
        [rows(D), rows(3 * D), whole_spec((3 * D, D)), rows(D), whole_spec(small.shape)],
        [rows(D), pl.BlockSpec((TILE, D), lambda p, b: (p, 0)), whole_spec((16, D))],
        [
            jax.ShapeDtypeStruct((tokens, D), jnp.bfloat16),
            jax.ShapeDtypeStruct((seq, D), jnp.float32),
            jax.ShapeDtypeStruct((16, D), jnp.float32),
        ],
        flops=6 * tokens * D * D,
        moved=tokens * D * 20,
    )(grad_r1, grad_qkv, weight, x, small)


def qkv_outer_kernel(h0, grad_qkv, out, low):
    @pl.when(pl.program_id(0) == 0)
    def _():
        low[...] = h0[...].astype(jnp.bfloat16)

    out[...] = outer_sum(low[...], grad_qkv[...]).astype(jnp.bfloat16)


def qkv_weights(h0, grad_qkv):
    tokens = h0.shape[0]
    return call(
        qkv_outer_kernel,
        "qkv_weights",
        (3,),
        [whole_spec((tokens, D)), pl.BlockSpec((tokens, D), lambda i: (0, i))],
        [pl.BlockSpec((D, D), lambda i: (i, 0))],
        [jax.ShapeDtypeStruct((3 * D, D), jnp.bfloat16)],
        scratch=[pltpu.VMEM((tokens, D), jnp.bfloat16)],
        flops=6 * tokens * D * D,
        moved=tokens * D * 12,
    )(h0, grad_qkv)[0]


def bucket_kernel(slot, grad, out):
    size = out.shape[0]
    at = pl.program_id(0) * size + lax.broadcasted_iota(jnp.int32, (size, slot.shape[1]), 0)
    pick = (slot[...] == at).astype(jnp.bfloat16)
    out[...] = matmul(pick, grad[...]).astype(jnp.bfloat16)


def bucket_rows(slot, grad, count):
    tokens = grad.shape[0]
    size = count // 4
    return call(
        bucket_kernel,
        "bucket_rows",
        (count // size,),
        [whole_spec((1, tokens)), whole_spec((tokens, D))],
        [pl.BlockSpec((size, D), lambda i: (i, 0))],
        [jax.ShapeDtypeStruct((count, D), jnp.bfloat16)],
        flops=2 * tokens * D * count,
        moved=tokens * D * 4,
    )(slot, grad)[0]


def scatter_kernel(row, got, out):
    size = out.shape[0]
    at = pl.program_id(0) * size + lax.broadcasted_iota(jnp.int32, (size, row.shape[1]), 0)
    pick = (row[...] == at).astype(jnp.bfloat16)
    out[...] = matmul(pick, got[...])


def scatter_rows(row, got, rows):
    size = math.gcd(rows, 480)
    count = got.shape[0]
    return call(
        scatter_kernel,
        "scatter_rows",
        (rows // size,),
        [whole_spec((1, count)), whole_spec((count, D))],
        [pl.BlockSpec((size, D), lambda i: (i, 0))],
        [jax.ShapeDtypeStruct((rows, D), jnp.float32)],
        flops=2 * rows * D * count,
        moved=rows * D * 8,
    )(row, got)[0]


MESH = pl.DeviceIdType.MESH


def gather_kernel(sizes, whole, src, out, send, recv, local):
    dp, fsdp = sizes
    count = dp * fsdp if whole else fsdp
    row, col = lax.axis_index("dp"), lax.axis_index("fsdp")
    me = row * fsdp + col if whole else col

    def target(step):
        other = lax.rem(me + step, count)
        return (other // fsdp, lax.rem(other, fsdp)) if whole else (row, other)

    barrier = pltpu.get_barrier_semaphore()

    def greet(step, carry):
        pl.semaphore_signal(barrier, inc=1, device_id=target(step), device_id_type=MESH)
        return carry

    lax.fori_loop(1, count, greet, 0)
    pl.semaphore_wait(barrier, count - 1)
    own = pltpu.make_async_copy(src, out.at[me], local)
    own.start()

    def copy(step):
        return pltpu.make_async_remote_copy(
            src_ref=src,
            dst_ref=out.at[me],
            send_sem=send.at[step],
            recv_sem=recv.at[step],
            device_id=target(step),
            device_id_type=MESH,
        )

    def begin(step, carry):
        copy(step).start()
        return carry

    def end(step, carry):
        copy(step).wait()
        return carry

    lax.fori_loop(1, count, begin, 0)
    lax.fori_loop(1, count, end, 0)
    own.wait()


def gather_small(value, whole, collective):
    dp, fsdp = lax.axis_size("dp"), lax.axis_size("fsdp")
    count = dp * fsdp if whole else fsdp
    return pl.pallas_call(
        functools.partial(gather_kernel, (dp, fsdp), whole),
        out_shape=jax.ShapeDtypeStruct((count,) + value.shape, value.dtype),
        in_specs=[pl.BlockSpec(memory_space=pltpu.VMEM)],
        out_specs=pl.BlockSpec(memory_space=pltpu.VMEM),
        scratch_shapes=[
            pltpu.SemaphoreType.DMA((count,)),
            pltpu.SemaphoreType.DMA((count,)),
            pltpu.SemaphoreType.DMA,
        ],
        compiler_params=pltpu.CompilerParams(collective_id=collective, has_side_effects=True),
    )(value)


LOOP_SIZE = 8
AHEAD = 2
CHUNK = 480


def grid_place(device):
    z, y = device // 2, lax.rem(device, 2)
    return z + y * (LOOP_SIZE - 1 - 2 * z)


def grid_device(place):
    place = lax.rem(place + LOOP_SIZE, LOOP_SIZE)
    y = place // (LOOP_SIZE // 2)
    return 2 * (place + y * (LOOP_SIZE - 1 - 2 * place)) + y


def front_kernel(
    cap,
    own_rows,
    lengths,
    ids,
    small,
    pieces,
    pos_low,
    table,
    everyone,
    first,
    second,
    small_out,
    held_rows,
    asker_row,
    most,
    x_out,
    h0_out,
    qkv_out,
    mixed_out,
    log_out,
    stage,
    table_low,
    sent,
    got,
    before,
    asker_col,
    smalls,
    small_sum,
    pos,
    x_in,
    h0_in,
    qkv,
    id_send,
    id_recv,
    hop_send,
    hop_recv,
    word_send,
    word_recv,
    small_send,
    small_recv,
    held_send,
    held_recv,
    stage_sem,
    local_sem,
):
    fsdp = LOOP_SIZE
    row, col = lax.axis_index("dp"), lax.axis_index("fsdp")
    count = lax.axis_size("dp") * fsdp
    tokens = ids.shape[1]
    seq = LEN
    me = row * fsdp + col
    shard = pieces.shape[0] // 12
    pos_rows = pos_low.shape[0]
    quarter = row
    place = grid_place(col)
    core_mate = row + 1 - 2 * lax.rem(row, 2)
    x_mate = lax.rem(row + 2, 4)
    far_mate = lax.rem(core_mate + 2, 4)
    right = (row, grid_device(place + 1))
    left = (row, grid_device(place - 1))

    def anyone(step):
        other = lax.rem(me + step, count)
        return (other // fsdp, lax.rem(other, fsdp))

    barrier = pltpu.get_barrier_semaphore()

    def greet(step, carry):
        pl.semaphore_signal(barrier, inc=1, device_id=anyone(step), device_id_type=MESH)
        return carry

    lax.fori_loop(1, count, greet, 0)
    pl.semaphore_wait(barrier, count - 1)

    def remote(src, dst, sems, index, target):
        return pltpu.make_async_remote_copy(
            src_ref=src,
            dst_ref=dst,
            send_sem=sems[0].at[index],
            recv_sem=sems[1].at[index],
            device_id=target,
            device_id_type=MESH,
        )

    def id_copy(step):
        return remote(ids, everyone.at[me], (id_send, id_recv), step, anyone(step))

    def id_start(step, carry):
        id_copy(step).start()
        return carry

    lax.fori_loop(1, count, id_start, 0)
    everyone[pl.ds(me, 1)] = ids[...][None]

    def aligned(at):
        return pl.multiple_of(at, 16)

    def hop_refs(phase, block, part, own):
        if phase == 0:
            size = pos_rows // 4
            there = [
                first.at[pl.ds(aligned(part * D + block * shard), shard), :],
                pos.at[pl.ds(aligned(block * pos_rows + part * size), size), :],
            ]
            here = [
                pieces.at[pl.ds(aligned(part * shard), shard), :],
                pos_low.at[pl.ds(aligned(part * size), size), :],
            ]
        else:
            there, here = [], []
            late = part // 2
            for i in range(2):
                piece = part * 2 + i
                early_at = piece * D + block * shard
                late_at = FF + block * 4 * shard + (piece - 4) * shard
                there.append(
                    second.at[pl.ds(aligned(early_at + late * (late_at - early_at)), shard), :]
                )
                here.append(pieces.at[pl.ds(aligned((4 + piece) * shard), shard), :])
        return there, here if own else there

    def hop(phase, slot, block, part, target, own=False):
        there, here = hop_refs(phase, block, part, own)
        return [
            remote(src, dst, (hop_send, hop_recv), 56 * phase + 2 * slot + i, target)
            for i, (src, dst) in enumerate(zip(here, there))
        ]

    started = []

    def begin(copies):
        for copy in copies:
            copy.start()
        started.extend(copies)

    def arrive(copies):
        for copy in copies:
            copy.wait_recv()

    events = []
    for k in range(1, LOOP_SIZE // 2 + 1):
        events.append((k, 1))
        if k < LOOP_SIZE // 2:
            events.append((k, -1))
    slot_of = {event: i for i, event in enumerate(events)}
    total = len(events)

    def block_of(event):
        return grid_device(place - event[0] * event[1])

    def begin_ring(phase):
        begin(hop(phase, slot_of[(1, 1)], col, quarter, right, own=True))
        begin(hop(phase, slot_of[(1, -1)], col, quarter, left, own=True))

    def spread(phase, index):
        event = events[index]
        hops, sign = event
        block = block_of(event)
        arrive(hop(phase, index, block, quarter, right))
        follow = (hops + 1, sign)
        if follow in slot_of:
            begin(hop(phase, slot_of[follow], block, quarter, right if sign == 1 else left))
        begin(hop(phase, total + index, block, quarter, (x_mate, col)))
        begin(hop(phase, 2 * total + index, block, quarter, (core_mate, col)))

    def pass_on(phase, index):
        block = block_of(events[index])
        arrive(hop(phase, total + index, block, x_mate, (x_mate, col)))
        begin(hop(phase, 3 * total + index, block, x_mate, (core_mate, col)))

    def settle(phase):
        for index in range(total):
            block = block_of(events[index])
            arrive(hop(phase, 2 * total + index, block, core_mate, (core_mate, col)))
            arrive(hop(phase, 3 * total + index, block, far_mate, (core_mate, col)))

    begin_ring(0)

    def small_copy(step):
        return remote(
            small, smalls.at[col], (small_send, small_recv), step, (row, lax.rem(col + step, fsdp))
        )

    for step in range(1, fsdp):
        small_copy(step).start()
    begin_ring(1)
    local = [
        pltpu.make_async_copy(small, smalls.at[col], local_sem.at[0]),
        pltpu.make_async_copy(
            pos_low, pos.at[pl.ds(aligned(col * pos_rows), pos_rows), :], local_sem.at[1]
        ),
        pltpu.make_async_copy(
            pieces.at[pl.ds(8 * shard, 4 * shard), :],
            second.at[pl.ds(aligned(FF + col * 4 * shard), 4 * shard), :],
            local_sem.at[2],
        ),
    ]
    for piece in range(4):
        span = pl.ds(aligned(piece * D + col * shard), shard)
        here = pieces.at[pl.ds(piece * shard, shard), :]
        local.append(pltpu.make_async_copy(here, first.at[span, :], local_sem.at[3 + piece]))
        here = pieces.at[pl.ds((4 + piece) * shard, shard), :]
        local.append(pltpu.make_async_copy(here, second.at[span, :], local_sem.at[7 + piece]))
    for copy in local:
        copy.start()

    chunks = own_rows // CHUNK

    def stage_copy(chunk, slot):
        return pltpu.make_async_copy(
            table.at[pl.ds(chunk * CHUNK, CHUNK), :], stage.at[slot], stage_sem.at[slot]
        )

    stage_copy(0, 0).start()
    across = lax.broadcasted_iota(jnp.int32, (tokens, tokens), 1)
    down = lax.broadcasted_iota(jnp.int32, (tokens, tokens), 0)
    before[...] = (down <= across).astype(jnp.float32).astype(jnp.bfloat16)
    for chunk in range(chunks):
        if chunk + 1 < chunks:
            stage_copy(chunk + 1, (chunk + 1) % 2).start()
        stage_copy(chunk, chunk % 2).wait()
        table_low[chunk * CHUNK : (chunk + 1) * CHUNK, :] = stage[chunk % 2].astype(jnp.bfloat16)

    def words_at(device):
        return got.at[pl.ds(aligned(device * cap), cap), :]

    def word_copy(step):
        other = lax.rem(col + step, fsdp)
        return remote(sent.at[other], words_at(col), (word_send, word_recv), step, (row, other))

    def bucket(step):
        asker = lax.rem(col + step, fsdp)
        if step:
            id_copy(lax.rem(me - row * fsdp - asker + count, count)).wait_recv()
        theirs = everyone[row * fsdp + asker] - col * own_rows
        held = (theirs >= 0) & (theirs < own_rows)
        flag = jnp.broadcast_to(held, (8, tokens)).astype(jnp.float32).astype(jnp.bfloat16)
        rank = matmul(flag, before[...])[0:1, :].astype(jnp.int32) - 1
        rank = jnp.where(held, rank, -1)
        hit = lax.broadcasted_iota(jnp.int32, (cap, tokens), 0) == rank
        inner = jnp.sum(jnp.where(hit, theirs + 1, 0), 1, keepdims=True) - 1
        held_rows[pl.ds(row, 1), step] = jnp.broadcast_to(inner, (cap, 128)).T[0:1, :][None]
        rows = jnp.zeros((cap, D), jnp.float32)
        wide = own_rows // 4
        for part in range(4):
            pick = inner == part * wide + lax.broadcasted_iota(jnp.int32, (cap, wide), 1)
            rows = rows + matmul(
                pick.astype(jnp.float32).astype(jnp.bfloat16),
                table_low[part * wide : (part + 1) * wide, :],
            )
        if step:
            sent[pl.ds(asker, 1)] = rows.astype(jnp.bfloat16)[None]
            if step > AHEAD:
                word_copy(step - AHEAD).wait_send()
            word_copy(step).start()
        else:
            words_at(col)[...] = rows.astype(jnp.bfloat16)

    for step, chores in (
        (1, ()),
        (2, ((spread, 0, 0), (spread, 0, 1), (spread, 1, 0), (spread, 1, 1))),
        (3, ((pass_on, 0, 0), (spread, 0, 2), (spread, 0, 3))),
        (4, ((pass_on, 0, 1), (pass_on, 1, 0), (spread, 0, 4), (spread, 0, 5))),
        (5, ((spread, 1, 2), (spread, 1, 3), (pass_on, 0, 2), (pass_on, 0, 3), (pass_on, 1, 1))),
        (6, ((spread, 0, 6),)),
        (7, ((pass_on, 0, 4), (pass_on, 0, 5))),
        (0, ((spread, 1, 4), (spread, 1, 5), (pass_on, 1, 2), (pass_on, 0, 6))),
    ):
        bucket(step)
        for chore, phase, index in chores:
            chore(phase, index)

    mine = jnp.broadcast_to(ids[...], (8, tokens))
    owner = lax.broadcasted_iota(jnp.int32, (8, tokens), 0)
    hot = (mine >= owner * own_rows) & (mine < (owner + 1) * own_rows)
    so_far = matmul(hot.astype(jnp.float32).astype(jnp.bfloat16), before[...]).astype(jnp.int32) - 1
    slot = jnp.sum(
        jnp.where(hot & (so_far < cap), owner * cap + so_far + 1, 0), 0, keepdims=True
    ) - 1
    asker_row[...] = slot
    asker_col[...] = jnp.broadcast_to(slot, (128, tokens)).T

    def held_copy(index):
        target = (core_mate, x_mate, far_mate)[index]
        return remote(
            held_rows.at[row], held_rows.at[row], (held_send, held_recv), index, (target, col)
        )

    for index in range(3):
        held_copy(index).start()

    def id_end(step, carry):
        copy = id_copy(step)
        copy.wait_send()

        @pl.when(lax.rem(lax.rem(me - step + count, count) // fsdp - row + count, count) != 0)
        def _():
            copy.wait_recv()

        return carry

    lax.fori_loop(1, count, id_end, 0)
    ids_all = everyone[...]
    largest = jnp.zeros((1, 1), jnp.int32)
    for part in range(fsdp):
        inside = (ids_all >= part * own_rows) & (ids_all < (part + 1) * own_rows)
        number = jnp.sum(inside.astype(jnp.int32), -1)
        largest = jnp.maximum(largest, jnp.max(number, 0, keepdims=True))
    most[...] = jnp.broadcast_to(largest, (8, 128))
    for step in range(1, fsdp):
        small_copy(step).wait()
    for copy in local:
        copy.wait()
    small_sum[...] = jnp.zeros_like(small_sum)
    for device in range(fsdp):
        at = device * (D // fsdp) // 128 * 128
        small_sum[:, at : at + 256] += smalls[device].astype(jnp.float32)
    gains = small_sum[:, 0:D]
    small_out[...] = gains
    settle(0)
    for step in range(1, fsdp):
        word_copy(step).wait_recv()
    for step in range(fsdp - AHEAD, fsdp):
        word_copy(step).wait_send()

    def embed_tile(i, carry):
        span = pl.ds(pl.multiple_of(i * TILE, TILE), TILE)
        slots = fsdp * cap
        pick = asker_col[span, 0:1] == lax.broadcasted_iota(jnp.int32, (TILE, slots), 1)
        words = matmul(pick.astype(jnp.float32).astype(jnp.bfloat16), got[...])
        spot = pl.ds(pl.multiple_of(lax.rem(i, seq // TILE) * TILE, TILE), TILE)
        x = words + pos[spot, :].astype(jnp.float32)
        hat, _ = normed(x)
        h0 = hat * small_sum[0:1, 0:D] + small_sum[1:2, 0:D]
        x_in[span, :] = x
        h0_in[span, :] = h0
        low = h0.astype(jnp.bfloat16)
        for third, bias in enumerate((2, None, 3)):
            value = matmul(low, first[third * D : (third + 1) * D, :])
            if bias is not None:
                value = value + small_sum[bias : bias + 1, 0:D]
            qkv[span, third * D : (third + 1) * D] = value.astype(jnp.bfloat16)
        return carry

    tiles = tokens // TILE
    lax.fori_loop(0, tiles // 2, embed_tile, 0)
    pass_on(1, 3)
    spread(1, 6)
    lax.fori_loop(tiles // 2, tiles, embed_tile, 0)
    written = [
        pltpu.make_async_copy(x_in, x_out, local_sem.at[0]),
        pltpu.make_async_copy(h0_in, h0_out, local_sem.at[1]),
        pltpu.make_async_copy(qkv, qkv_out, local_sem.at[2]),
    ]
    for copy in written:
        copy.start()
    masks = head_masks(seq)
    chores = {
        1: lambda: pass_on(1, 4),
        4: lambda: pass_on(1, 5),
        8: lambda: pass_on(1, 6),
    }
    done = 0
    for sentence in range(tokens // seq):
        bias = live_row(lengths[sentence], seq)
        rows = slice(sentence * seq, (sentence + 1) * seq)
        logs = jnp.zeros((seq, 128), jnp.float32)
        for pair in range(H // 2):
            logs = attend_pair(qkv, bias, masks, logs, mixed_out, rows, pair)
            done += 1
            if done in chores:
                chores[done]()
        log_out[rows, :] = logs
    settle(1)
    for index in range(3):
        held_copy(index).wait()
    for copy in written:
        copy.wait()
    for copy in started:
        copy.wait_send()


def front(lengths, ids, pieces, pos_low, small, table, cap):
    fsdp = LOOP_SIZE
    count = lax.axis_size("dp") * fsdp
    tokens = ids.shape[1]
    own_rows = table.shape[0]
    hops = 16 * (fsdp - 1)
    vmem = pl.BlockSpec(memory_space=pltpu.VMEM)
    anywhere = pl.BlockSpec(memory_space=pl.ANY)
    low, wide = jnp.bfloat16, jnp.float32
    dma = pltpu.SemaphoreType.DMA
    return pl.pallas_call(
        functools.partial(front_kernel, cap, own_rows),
        name="front",
        in_specs=[pl.BlockSpec(memory_space=pltpu.SMEM), vmem, vmem, anywhere, anywhere, anywhere],
        out_specs=[vmem, vmem, anywhere, vmem, vmem, vmem, vmem, anywhere, anywhere, anywhere, vmem, vmem],
        out_shape=[
            jax.ShapeDtypeStruct((count, 1, tokens), jnp.int32),
            jax.ShapeDtypeStruct((4 * D, D), low),
            jax.ShapeDtypeStruct((2 * FF, D), low),
            jax.ShapeDtypeStruct((16, D), wide),
            jax.ShapeDtypeStruct((4, fsdp, 1, cap), jnp.int32),
            jax.ShapeDtypeStruct((1, tokens), jnp.int32),
            jax.ShapeDtypeStruct((8, 128), jnp.int32),
            jax.ShapeDtypeStruct((tokens, D), wide),
            jax.ShapeDtypeStruct((tokens, D), wide),
            jax.ShapeDtypeStruct((tokens, 3 * D), low),
            jax.ShapeDtypeStruct((tokens, D), low),
            jax.ShapeDtypeStruct((tokens, 128), wide),
        ],
        scratch_shapes=[
            pltpu.VMEM((2, CHUNK, D), wide),
            pltpu.VMEM((own_rows, D), low),
            pltpu.VMEM((fsdp, cap, D), low),
            pltpu.VMEM((fsdp * cap, D), low),
            pltpu.VMEM((tokens, tokens), low),
            pltpu.VMEM((tokens, 128), jnp.int32),
            pltpu.VMEM((fsdp, 16, 256), low),
            pltpu.VMEM((16, D + 128), wide),
            pltpu.VMEM((LEN, D), low),
            pltpu.VMEM((tokens, D), wide),
            pltpu.VMEM((tokens, D), wide),
            pltpu.VMEM((tokens, 3 * D), low),
            dma((count,)),
            dma((count,)),
            dma((hops,)),
            dma((hops,)),
            dma((fsdp,)),
            dma((fsdp,)),
            dma((fsdp,)),
            dma((fsdp,)),
            dma((3,)),
            dma((3,)),
            dma((2,)),
            dma((12,)),
        ],
        compiler_params=pltpu.CompilerParams(
            collective_id=0, has_side_effects=True, vmem_limit_bytes=VMEM_GRANT
        ),
    )(lengths, ids, small, pieces, pos_low, table)


class Ring:
    def __init__(self, parts, sign, send, recv, base):
        self.parts, self.send, self.recv, self.base = parts, send, recv, base
        self.row, col = lax.axis_index("dp"), lax.axis_index("fsdp")
        self.col, self.place = col, grid_place(col)
        self.hops = {sign: LOOP_SIZE // 2, -sign: LOOP_SIZE - LOOP_SIZE // 2 - 1}
        self.events = []
        for k in range(1, LOOP_SIZE // 2 + 1):
            for direction in (sign, -sign):
                if k <= self.hops[direction]:
                    self.events.append((k, direction))
        self.slot = {event: i for i, event in enumerate(self.events)}
        self.sign = sign
        self.started = []

    def copies(self, source, event):
        slot = self.slot[event]
        target = (self.row, grid_device(self.place + event[1]))
        return [
            pltpu.make_async_remote_copy(
                src_ref=box.at[source],
                dst_ref=box.at[slot],
                send_sem=self.send.at[self.base + len(self.parts) * slot + i],
                recv_sem=self.recv.at[self.base + len(self.parts) * slot + i],
                device_id=target,
                device_id_type=MESH,
            )
            for i, (_, _, box) in enumerate(self.parts)
        ]

    def depart(self, source, event):
        for copy in self.copies(source, event):
            copy.start()
            self.started.append(copy)

    def add(self, slot, block, arrived):
        for keep, mate, box in self.parts:
            terms = [keep.at[block], mate.at[block]] + ([box.at[slot]] if arrived else [])
            sum_rows(box.at[slot], terms)

    def first(self):
        for i, direction in enumerate((self.sign, -self.sign)):
            block = grid_device(self.place + direction * self.hops[direction])
            self.add(len(self.events) + i, block, False)
            self.depart(len(self.events) + i, (1, direction))

    def step(self, index):
        hop, direction = self.events[index]
        for copy in self.copies(index, self.events[index]):
            copy.wait_recv()
        left = self.hops[direction] - hop
        if left:
            self.add(index, grid_device(self.place + direction * left), True)
            self.depart(index, (hop + 1, direction))

    def last(self, totals):
        far = self.slot[(self.hops[self.sign], self.sign)]
        near = self.slot[(self.hops[-self.sign], -self.sign)]
        for (keep, mate, box), total in zip(self.parts, totals):
            sum_rows(total, [keep.at[self.col], mate.at[self.col], box.at[far], box.at[near]])

    def drain(self):
        for copy in self.started:
            copy.wait_send()


def sum_rows(out, terms):
    rows = min(out.shape[0], 32)

    def body(i, carry):
        span = pl.ds(pl.multiple_of(i * rows, rows), rows)
        total = terms[0][span, :].astype(jnp.float32)
        for term in terms[1:]:
            total = total + term[span, :].astype(jnp.float32)
        out[span, :] = total.astype(out.dtype)
        return carry

    lax.fori_loop(0, out.shape[0] // rows, body, 0)


def add_squares(squares, value):
    rows = min(value.shape[0], 32)

    def body(i, carry):
        part = value[pl.ds(pl.multiple_of(i * rows, rows), rows), :].astype(jnp.float32)
        squares[0:1, 0 : part.shape[1]] += jnp.sum(part * part, 0, keepdims=True)
        return carry

    lax.fori_loop(0, value.shape[0] // rows, body, 0)


def finish_kernel(
    cap,
    own_rows,
    grad,
    slot,
    held,
    feed_grads,
    qkv_grads,
    pos_grads,
    small_grads,
    depart,
    own,
    table_out,
    sum_a,
    sum_b,
    sum_small,
    norm_out,
    got,
    sent,
    total,
    half_low,
    last_a,
    keep_b,
    mate_b,
    box_b,
    keep_s,
    mate_s,
    box_s,
    out_a,
    in_a,
    out_b,
    in_b,
    out_s,
    in_s,
    squares,
    share,
    shares,
    word_send,
    word_recv,
    ring_send,
    ring_recv,
    pair_send,
    pair_recv,
    norm_send,
    norm_recv,
    local_sem,
):
    fsdp = LOOP_SIZE
    row, col = lax.axis_index("dp"), lax.axis_index("fsdp")
    core = lax.rem(row, 2)
    core_mate = row + 1 - 2 * core
    x_mate = lax.rem(row + 2, 4)
    far_mate = lax.rem(core_mate + 2, 4)
    half = own_rows // 2
    tokens = grad.shape[0]

    barrier = pltpu.get_barrier_semaphore()
    for step in range(1, fsdp):
        there = (row, lax.rem(col + step, fsdp))
        pl.semaphore_signal(barrier, inc=1, device_id=there, device_id_type=MESH)
    for step in range(fsdp):
        there = (core_mate, lax.rem(col + step, fsdp))
        pl.semaphore_signal(barrier, inc=1, device_id=there, device_id_type=MESH)
    pl.semaphore_signal(barrier, inc=1, device_id=(x_mate, col), device_id_type=MESH)
    pl.semaphore_wait(barrier, 2 * fsdp)

    def remote(src, dst, sems, index, target):
        return pltpu.make_async_remote_copy(
            src_ref=src,
            dst_ref=dst,
            send_sem=sems[0].at[index],
            recv_sem=sems[1].at[index],
            device_id=target,
            device_id_type=MESH,
        )

    pair = (pair_send, pair_recv)
    mate = (core_mate, col)
    shard = feed_grads.shape[1]

    def b_parts(which, target):
        pos_half = pos_grads.shape[1] // 2
        if which == 0:
            first, second = qkv_grads.at[pl.ds(0, 8)], qkv_grads.at[pl.ds(8, 8)]
        else:
            first, second = qkv_grads.at[pl.ds(16, 8)], feed_grads.at[pl.ds(64, 8)]
        return [
            (first, target.at[:, pl.ds(0, shard)]),
            (second, target.at[:, pl.ds(shard, shard)]),
            (pos_grads.at[:, pl.ds(which * pos_half, pos_half)], target.at[:, pl.ds(2 * shard, pos_half)]),
        ]

    def s_parts(which, target):
        return [(small_grads.at[:, pl.ds(8 * which, 8)], target)]

    for which in range(2):

        @pl.when(core == which)
        def _(which=which):
            for index, (parts, keep, mates) in enumerate(
                ((b_parts, keep_b, mate_b), (s_parts, keep_s, mate_s))
            ):
                for src, dst in parts(1 - which, mates):
                    remote(src, dst, pair, index, mate).start()
                for src, dst in parts(which, keep):
                    pltpu.make_async_copy(src, dst, local_sem.at[index]).start()

    def halves_in(index):
        keep, mates = ((keep_b, mate_b), (keep_s, mate_s))[index]
        pltpu.make_async_copy(keep, keep, local_sem.at[index]).wait()
        remote(mates, mates, pair, index, mate).wait_recv()

    def word_copy(step):
        return remote(
            sent.at[step],
            got.at[row, step],
            (word_send, word_recv),
            step,
            (row, lax.rem(col - step + fsdp, fsdp)),
        )

    def word_hand(kind, step):
        group, target = ((row, (x_mate, col)), (row, mate), (x_mate, mate))[kind]
        place = got.at[group, step]
        return remote(place, place, (word_send, word_recv), fsdp * (kind + 1) + step, target)

    def bucket(step):
        base = lax.rem(col - step + fsdp, fsdp) * cap
        pick = slot[...] == base + lax.broadcasted_iota(jnp.int32, (cap, tokens), 0)
        rows = matmul(pick.astype(jnp.float32).astype(jnp.bfloat16), grad[...]).astype(jnp.bfloat16)
        if step:
            sent[step] = rows
            word_copy(step).start()
        else:
            got[pl.ds(row, 1), 0] = rows[None]

    handed = []

    def spread(step):
        if step:
            word_copy(step).wait_recv()
        for kind in (0, 1):
            copy = word_hand(kind, step)
            copy.start()
            handed.append(copy)

    def pass_on(step):
        place = got.at[x_mate, step]
        remote(place, place, (word_send, word_recv), fsdp + step, (x_mate, col)).wait_recv()
        copy = word_hand(2, step)
        copy.start()
        handed.append(copy)

    def from_mate(group, kind, step):
        place = got.at[group, step]
        remote(place, place, (word_send, word_recv), fsdp * (kind + 1) + step, mate).wait_recv()

    def accumulate(side, parity, part, fresh):
        chip = row - core if side == 0 else x_mate - core
        group = chip + parity
        width = 4 * cap
        size = half // 4

        def tile(i, carry):
            at = core * half + i * size + lax.broadcasted_iota(jnp.int32, (size, width), 0)
            pick = held[pl.ds(group, 1), 0, part * width : (part + 1) * width] == at
            rows = got[pl.ds(group, 1), 4 * part : 4 * part + 4].reshape(width, D)
            value = matmul(pick.astype(jnp.float32).astype(jnp.bfloat16), rows)
            span = pl.ds(pl.multiple_of(i * size, size), size)
            if fresh:
                total[side, span, :] = value
            else:
                total[side, span, :] += value
            return carry

        lax.fori_loop(0, 4, tile, 0)

    def arrived_here(part):
        for step in range(4 * part, 4 * part + 4):
            from_mate(core_mate, 1, step)

    def arrived_far(part):
        for step in range(4 * part, 4 * part + 4):
            from_mate(far_mate, 2, step)

    def last_hop():
        return remote(
            depart, last_a, (ring_send, ring_recv), 14, (row, grid_device(grid_place(col) + 1))
        )

    ring_b = Ring(
        [(keep_b, mate_b, box_b), (keep_s, mate_s, box_s)],
        -1,
        ring_send,
        ring_recv,
        0,
    )
    squares[...] = jnp.zeros_like(squares)

    def swap_x(ring, totals, incoming, index):
        ring.last(totals)
        for i, (mine, theirs) in enumerate(zip(totals, incoming)):
            remote(mine, theirs, pair, index + i, (x_mate, col)).start()

    def settle(totals, incoming, finals, index, back):
        for i, (mine, theirs, final) in enumerate(zip(totals, incoming, finals)):
            remote(mine, theirs, pair, index + i, (x_mate, col)).wait_recv()
            sum_rows(final.at[core], [mine, theirs])
            add_squares(squares, final.at[core])
            remote(final.at[core], final.at[core], pair, back + i, mate).start()

    last_hop().start()
    for step in range(1, fsdp):
        bucket(step)
    bucket(0)
    spread(0)
    halves_in(0)
    halves_in(1)
    ring_b.first()
    spread(1)
    last_hop().wait_recv()
    sum_rows(out_a, [own, last_a])
    remote(out_a, in_a, pair, 5, (x_mate, col)).start()
    spread(2)
    pass_on(0)
    spread(3)
    ring_b.step(0)
    ring_b.step(1)
    pass_on(1)
    pass_on(2)
    arrived_here(0)
    accumulate(0, 0, 0, True)
    accumulate(0, 1, 0, False)
    spread(4)
    pass_on(3)
    ring_b.step(2)
    ring_b.step(3)
    spread(5)
    arrived_far(0)
    accumulate(1, 0, 0, True)
    accumulate(1, 1, 0, False)
    spread(6)
    pass_on(4)
    ring_b.step(4)
    ring_b.step(5)
    spread(7)
    pass_on(5)
    arrived_here(1)
    accumulate(0, 0, 1, False)
    accumulate(0, 1, 1, False)
    ring_b.step(6)
    swap_x(ring_b, (out_b, out_s), (in_b, in_s), 3)
    pass_on(6)
    pass_on(7)
    settle((out_a,), (in_a,), (sum_a,), 5, 9)
    arrived_far(1)
    accumulate(1, 0, 1, False)
    accumulate(1, 1, 1, False)

    def close(i, carry):
        span = pl.ds(pl.multiple_of(i * 32, 32), 32)
        value = (total[0, span, :] + total[1, span, :]).astype(jnp.bfloat16)
        half_low[span, :] = value
        wide = value.astype(jnp.float32)
        squares[0:1, :] += jnp.sum(wide * wide, 0, keepdims=True)
        return carry

    lax.fori_loop(0, half // 32, close, 0)
    mine = table_out.at[pl.ds(pl.multiple_of(core * half, 32), half), :]
    kept = pltpu.make_async_copy(half_low, mine, local_sem.at[3])
    kept.start()
    given = remote(half_low, mine, pair, 6, mate)
    given.start()
    settle((out_b, out_s), (in_b, in_s), (sum_b, sum_small), 3, 7)

    here = core * fsdp + col
    share[...] = jnp.broadcast_to(jnp.sum(squares[0:1, :], 1, keepdims=True), (8, 128))
    shares[pl.ds(here, 1)] = share[...][None]

    def norm_copy(step):
        other = lax.rem(here + step, 2 * fsdp)
        target = (row - core + other // fsdp, lax.rem(other, fsdp))
        return remote(share, shares.at[here], (norm_send, norm_recv), step, target)

    for step in range(1, 2 * fsdp):
        norm_copy(step).start()
    for step in range(1, 2 * fsdp):
        norm_copy(step).wait()
    norm = shares[0]
    for step in range(1, 2 * fsdp):
        norm = norm + shares[step]
    norm_out[...] = norm

    kept.wait()
    given.wait()
    for i, final in enumerate((sum_b, sum_small, sum_a)):
        other = final.at[1 - core]
        remote(other, other, pair, 7 + i, mate).wait()
    for index, (mine_out, theirs) in enumerate(((out_b, in_b), (out_s, in_s), (out_a, in_a))):
        remote(mine_out, theirs, pair, 3 + index, (x_mate, col)).wait_send()
    for index, mates in enumerate((mate_b, mate_s)):
        remote(mates, mates, pair, index, mate).wait_send()
    for step in range(1, fsdp):
        word_copy(step).wait_send()
    for copy in handed:
        copy.wait_send()
    last_hop().wait_send()
    ring_b.drain()


class flat_blocks:
    def __init__(self, ref):
        self.ref = ref

    @property
    def at(self):
        return self

    def __getitem__(self, block):
        return flat_rows(self.ref, block)


class flat_rows:
    def __init__(self, ref, block):
        self.ref, self.block = ref, block

    def __getitem__(self, key):
        span = key[0]
        rows = self.ref.shape[2]
        return self.ref[self.block, span.start // rows, pl.ds(lax.rem(span.start, rows), span.size), :]


def finish(grad, slot, held, feed_grads, qkv_grads, pos_grads, small_grads, depart, own, own_rows, cap):
    fsdp = LOOP_SIZE
    tokens = grad.shape[0]
    shard = D // fsdp
    pos_rows = pos_grads.shape[0] // fsdp
    rows_a, rows_b = 4 * shard, 2 * shard + pos_rows // 2
    half = own_rows // 2
    vmem = pl.BlockSpec(memory_space=pltpu.VMEM)
    anywhere = pl.BlockSpec(memory_space=pl.ANY)
    low, wide = jnp.bfloat16, jnp.float32
    return pl.pallas_call(
        functools.partial(finish_kernel, cap, own_rows),
        name="finish",
        in_specs=[vmem, vmem, vmem, anywhere, anywhere, anywhere, anywhere, vmem, vmem],
        out_specs=[anywhere, vmem, vmem, vmem, vmem],
        out_shape=[
            jax.ShapeDtypeStruct((own_rows, D), low),
            jax.ShapeDtypeStruct((2, rows_a, D), low),
            jax.ShapeDtypeStruct((2, rows_b, D), low),
            jax.ShapeDtypeStruct((2, 8, 128), wide),
            jax.ShapeDtypeStruct((8, 128), wide),
        ],
        scratch_shapes=[
            pltpu.VMEM((4, fsdp, cap, D), low),
            pltpu.VMEM((fsdp, cap, D), low),
            pltpu.VMEM((2, half, D), wide),
            pltpu.VMEM((half, D), low),
            pltpu.VMEM((rows_a, D), low),
            pltpu.VMEM((fsdp, rows_b, D), low),
            pltpu.VMEM((fsdp, rows_b, D), low),
            pltpu.VMEM((fsdp + 1, rows_b, D), low),
            pltpu.VMEM((fsdp, 8, 128), wide),
            pltpu.VMEM((fsdp, 8, 128), wide),
            pltpu.VMEM((fsdp + 1, 8, 128), wide),
            pltpu.VMEM((rows_a, D), low),
            pltpu.VMEM((rows_a, D), low),
            pltpu.VMEM((rows_b, D), low),
            pltpu.VMEM((rows_b, D), low),
            pltpu.VMEM((8, 128), wide),
            pltpu.VMEM((8, 128), wide),
            pltpu.VMEM((8, D), wide),
            pltpu.VMEM((8, 128), wide),
            pltpu.VMEM((2 * fsdp, 8, 128), wide),
            pltpu.SemaphoreType.DMA((4 * fsdp,)),
            pltpu.SemaphoreType.DMA((4 * fsdp,)),
            pltpu.SemaphoreType.DMA((15,)),
            pltpu.SemaphoreType.DMA((15,)),
            pltpu.SemaphoreType.DMA((10,)),
            pltpu.SemaphoreType.DMA((10,)),
            pltpu.SemaphoreType.DMA((2 * fsdp,)),
            pltpu.SemaphoreType.DMA((2 * fsdp,)),
            pltpu.SemaphoreType.DMA((4,)),
        ],
        compiler_params=pltpu.CompilerParams(
            collective_id=3, has_side_effects=True, vmem_limit_bytes=VMEM_GRANT
        ),
    )(
        grad,
        slot,
        held,
        feed_grads.reshape(-1, shard, D),
        qkv_grads.reshape(-1, shard, D),
        pos_grads.reshape(fsdp, pos_rows, D),
        small_grads,
        depart,
        own,
    )


def attend_back_pair(qkv, grad_mixed, logs, bias, masks, out, sums, rows, pair):
    at = pair * 128
    query = qkv[rows, at : at + 128] * jnp.bfloat16(0.125)
    keys = qkv[rows, D + at : D + at + 128]
    values = qkv[rows, 2 * D + at : 2 * D + at + 128]
    above = grad_mixed[rows, at : at + 128]
    queries = []
    key_sum = value_sum = None
    for side, mask in enumerate(masks):
        head = 2 * pair + side
        side_query = jnp.where(mask, query, jnp.zeros_like(query))
        side_above = jnp.where(mask, above, jnp.zeros_like(above))
        probs = jnp.exp(back_mul(side_query, keys) + (bias - logs[rows, head : head + 1]))
        grad_probs = back_mul(side_above, values)
        inner = jnp.sum(probs * grad_probs, -1, keepdims=True)
        grad_logits = (probs * (grad_probs - inner)).astype(jnp.bfloat16)
        side_value = outer_sum(probs.astype(jnp.bfloat16), side_above)
        side_key = outer_sum(grad_logits, side_query)
        queries.append(matmul(grad_logits, keys))
        value_sum = side_value if side == 0 else value_sum + side_value
        key_sum = side_key if side == 0 else key_sum + side_key
    grad_query = jnp.where(masks[0], queries[0], queries[1]) * 0.125
    out[rows, at : at + 128] = grad_query.astype(jnp.bfloat16)
    out[rows, D + at : D + at + 128] = key_sum.astype(jnp.bfloat16)
    out[rows, 2 * D + at : 2 * D + at + 128] = value_sum.astype(jnp.bfloat16)
    sums[2:3, at : at + 128] += jnp.sum(grad_query, 0, keepdims=True)
    sums[3:4, at : at + 128] += jnp.sum(value_sum, 0, keepdims=True)


def back_kernel(
    lengths,
    qkv,
    grad_mixed,
    logs,
    small,
    grad_r1,
    x,
    weight,
    feed_grads,
    x_out,
    pos_out,
    qkv_out,
    sums,
    depart,
    own,
    grad_qkv,
    r1_in,
    x_in,
    weight_in,
    low_h0,
    pos_sum,
    keep,
    mates,
    box,
    ring_send,
    ring_recv,
    pair_send,
    pair_recv,
    local_sem,
):
    fsdp = LOOP_SIZE
    row, col = lax.axis_index("dp"), lax.axis_index("fsdp")
    core = lax.rem(row, 2)
    mate = (row + 1 - 2 * core, col)
    place = grid_place(col)
    seq = LEN
    sentences = qkv.shape[0] // seq

    barrier = pltpu.get_barrier_semaphore()
    for there in (mate, (row, grid_device(place + 1)), (row, grid_device(place - 1))):
        pl.semaphore_signal(barrier, inc=1, device_id=there, device_id_type=MESH)
    pl.semaphore_wait(barrier, 3)

    def pair_copy(src, dst, index):
        return pltpu.make_async_remote_copy(
            src_ref=src,
            dst_ref=dst,
            send_sem=pair_send.at[index],
            recv_sem=pair_recv.at[index],
            device_id=mate,
            device_id_type=MESH,
        )

    offsets = (4, -3, 3, -2, 2, -1, 1, 0)

    def halves(which, block, target):
        if which == 0:
            return [(feed_grads.at[pl.ds(4 * block, 4)], target.at[block])]
        return [(feed_grads.at[32 + 8 * j + block], target.at[block, j]) for j in range(4)]

    for which in range(2):

        @pl.when(core == which)
        def _(which=which):
            for index, offset in enumerate(offsets):
                block = grid_device(place + offset)
                for src, dst in halves(1 - which, block, mates):
                    pair_copy(src, dst, index).start()
                for src, dst in halves(which, block, keep):
                    pltpu.make_async_copy(src, dst, local_sem.at[0]).start()

    def mate_block(index):
        block = grid_device(place + offsets[index])
        return pair_copy(mates.at[block], mates.at[block], index)

    fills = [
        pltpu.make_async_copy(grad_r1, r1_in, local_sem.at[1]),
        pltpu.make_async_copy(x, x_in, local_sem.at[2]),
        pltpu.make_async_copy(weight.at[pl.ds(0, 3 * D), :], weight_in, local_sem.at[3]),
    ]
    for fill in fills:
        fill.start()

    ring = Ring([(flat_blocks(keep), flat_blocks(mates), box)], 1, ring_send, ring_recv, 0)
    sums[...] = jnp.zeros_like(sums)
    masks = head_masks(seq)
    done = 0
    for sentence in range(sentences):
        bias = live_row(lengths[sentence], seq)
        rows = slice(sentence * seq, (sentence + 1) * seq)
        for pair in range(H // 2):
            attend_back_pair(qkv, grad_mixed, logs, bias, masks, grad_qkv, sums, rows, pair)
            done += 1
            if done == 1:
                pltpu.make_async_copy(keep, keep, local_sem.at[0]).wait()
                mate_block(0).wait_recv()
                mate_block(1).wait_recv()
                ring.first()
            if done == 8:
                mate_block(2).wait_recv()
                mate_block(3).wait_recv()
                ring.step(0)
                ring.step(1)
    for fill in fills:
        fill.wait()
    pos_sum[...] = jnp.zeros_like(pos_sum)

    def tile(i, carry):
        span = pl.ds(pl.multiple_of(i * TILE, TILE), TILE)
        grad_h0 = r1_in[span, :]
        for third in range(3):
            cols = slice(third * D, (third + 1) * D)
            grad_h0 = grad_h0 + back_mul(grad_qkv[span, cols], weight_in[cols, :])
        hat, scale = normed(x_in[span, :])
        low_h0[span, :] = (hat * small[0:1, :] + small[1:2, :]).astype(jnp.bfloat16)
        grad_x, gain, shift = norm_back(grad_h0, hat, scale, small[0:1, :])
        add_row(sums, 0, gain)
        add_row(sums, 1, shift)
        x_out[span, :] = grad_x.astype(jnp.bfloat16)
        spot = pl.ds(pl.multiple_of(lax.rem(i, seq // TILE) * TILE, TILE), TILE)
        pos_sum[spot, :] += grad_x
        return carry

    tiles = sentences * seq // TILE
    lax.fori_loop(0, tiles // 2, tile, 0)
    mate_block(4).wait_recv()
    mate_block(5).wait_recv()
    ring.step(2)
    ring.step(3)
    lax.fori_loop(tiles // 2, tiles, tile, 0)
    pos_out[...] = pos_sum[...].astype(jnp.bfloat16)
    for third in range(3):
        cols = slice(third * D, (third + 1) * D)
        qkv_out[cols, :] = outer_sum(low_h0[...], grad_qkv[:, cols]).astype(jnp.bfloat16)
    right, left = ring.slot[(3, 1)], ring.slot[(3, -1)]
    for slot in (right, left):
        for copy in ring.copies(slot, ring.events[slot]):
            copy.wait_recv()
    mate_block(6).wait_recv()
    mate_block(7).wait_recv()
    ahead = grid_device(place + 1)
    sum_rows(depart, [ring.parts[0][0].at[ahead], ring.parts[0][1].at[ahead], box.at[right]])
    sum_rows(own, [ring.parts[0][0].at[col], ring.parts[0][1].at[col], box.at[left]])
    for index in range(8):
        mate_block(index).wait_send()
    ring.drain()


def back(lengths, qkv, grad_mixed, logs, small, grad_r1, x, weight, feed_grads):
    fsdp = LOOP_SIZE
    tokens = qkv.shape[0]
    shard = D // fsdp
    vmem = pl.BlockSpec(memory_space=pltpu.VMEM)
    anywhere = pl.BlockSpec(memory_space=pl.ANY)
    low, wide = jnp.bfloat16, jnp.float32
    return pl.pallas_call(
        back_kernel,
        name="back",
        in_specs=[pl.BlockSpec(memory_space=pltpu.SMEM)] + [vmem] * 4 + [anywhere] * 4,
        out_specs=[vmem] * 6,
        out_shape=[
            jax.ShapeDtypeStruct((tokens, D), low),
            jax.ShapeDtypeStruct((LEN, D), low),
            jax.ShapeDtypeStruct((3 * D, D), low),
            jax.ShapeDtypeStruct((16, D), wide),
            jax.ShapeDtypeStruct((4 * shard, D), low),
            jax.ShapeDtypeStruct((4 * shard, D), wide),
        ],
        scratch_shapes=[
            pltpu.VMEM((tokens, 3 * D), low),
            pltpu.VMEM((tokens, D), wide),
            pltpu.VMEM((tokens, D), wide),
            pltpu.VMEM((3 * D, D), low),
            pltpu.VMEM((tokens, D), low),
            pltpu.VMEM((LEN, D), wide),
            pltpu.VMEM((fsdp, 4, shard, D), low),
            pltpu.VMEM((fsdp, 4, shard, D), low),
            pltpu.VMEM((fsdp + 1, 4 * shard, D), low),
            pltpu.SemaphoreType.DMA((7,)),
            pltpu.SemaphoreType.DMA((7,)),
            pltpu.SemaphoreType.DMA((8,)),
            pltpu.SemaphoreType.DMA((8,)),
            pltpu.SemaphoreType.DMA((4,)),
        ],
        compiler_params=pltpu.CompilerParams(
            collective_id=4, has_side_effects=True, vmem_limit_bytes=VMEM_GRANT
        ),
    )(lengths, qkv, grad_mixed, logs, small, grad_r1, x, weight, feed_grads.reshape(-1, shard, D))


def exact_dot(left, right):
    return lax.dot_general(
        left,
        right,
        (((1,), (0,)), ((), ())),
        precision=lax.Precision.HIGHEST,
        preferred_element_type=jnp.float32,
    )


def cosine_parts(first, second):
    dots = jnp.sum(first * second, -1, keepdims=True)
    one = lax.rsqrt(jnp.sum(first * first, -1, keepdims=True) + 1e-06)
    two = lax.rsqrt(jnp.sum(second * second, -1, keepdims=True) + 1e-06)
    return dots * one * two, one, two


def cosine_back(grad, value, first, second, one, two):
    return (
        grad * one * (second * two - value * first * one),
        grad * two * (first * one - value * second * two),
    )


def loss_kernel(sizes, lengths, src, pair_ids, scores, loss_out, share_out, out, send, recv, local):
    gather_kernel(sizes, True, src, out, send, recv, local)
    count, batch = out.shape[0], out.shape[1]
    pooled = jnp.concatenate([out[:, i] for i in range(batch)], 0)
    rows = lax.broadcasted_iota(jnp.int32, (pair_ids.shape[1], count * batch), 1)
    sentence = lax.rem(rows, count) * batch + rows // count
    anchor, near, far = (
        exact_dot((pair_ids[i] == sentence).astype(jnp.float32), pooled) for i in range(3)
    )
    near_cos, near_one, near_two = cosine_parts(anchor, near)
    far_cos, far_one, far_two = cosine_parts(anchor, far)
    near_miss, far_miss = near_cos - scores[0], far_cos - scores[1]
    loss = jnp.sum(near_miss * near_miss + far_miss * far_miss, 0, keepdims=True)
    loss_out[...] = jnp.broadcast_to(loss, loss_out.shape)
    anchor_a, grad_near = cosine_back(
        2.0 * near_miss, near_cos, anchor, near, near_one, near_two
    )
    anchor_b, grad_far = cosine_back(2.0 * far_miss, far_cos, anchor, far, far_one, far_two)
    grads = (anchor_a + anchor_b, grad_near, grad_far)
    me = lax.axis_index("dp") * sizes[1] + lax.axis_index("fsdp")
    for i in range(batch):
        total = jnp.zeros((1, grads[0].shape[1]), jnp.float32)
        for part, grad in enumerate(grads):
            mine = pair_ids[part] == me * batch + i
            total = total + jnp.sum(jnp.where(mine, grad, 0.0), 0, keepdims=True)
        share_out[i] = jnp.broadcast_to(
            total / lengths[i].astype(jnp.float32), share_out.shape[1:]
        )


def pair_grads(lengths, pooled, pair_ids, scores):
    dp, fsdp = lax.axis_size("dp"), lax.axis_size("fsdp")
    count, (batch, width) = dp * fsdp, pooled.shape
    vmem = pl.BlockSpec(memory_space=pltpu.VMEM)
    return pl.pallas_call(
        functools.partial(loss_kernel, (dp, fsdp)),
        name="pair_loss",
        in_specs=[pl.BlockSpec(memory_space=pltpu.SMEM), vmem, vmem, vmem],
        out_specs=[vmem, vmem],
        out_shape=[
            jax.ShapeDtypeStruct((8, 128), jnp.float32),
            jax.ShapeDtypeStruct((batch, 8, width), jnp.float32),
        ],
        scratch_shapes=[
            pltpu.VMEM((count,) + pooled.shape, jnp.float32),
            pltpu.SemaphoreType.DMA((count,)),
            pltpu.SemaphoreType.DMA((count,)),
            pltpu.SemaphoreType.DMA,
        ],
        compiler_params=pltpu.CompilerParams(
            collective_id=1, has_side_effects=True, vmem_limit_bytes=VMEM_GRANT
        ),
    )(lengths, pooled, pair_ids[:, :, None], scores[:, :, None])


def pack_kernel(qkv, out_w, up, down, pos, pieces, low_pos):
    rows = qkv.shape[0]
    low = jnp.bfloat16
    for part in range(3):
        pieces[part * rows : (part + 1) * rows, :] = qkv[:, part * D : (part + 1) * D].astype(low)
    pieces[3 * rows : 4 * rows, :] = out_w[...].astype(low)
    for part in range(4):
        at = (4 + part) * rows
        pieces[at : at + rows, :] = up[:, part * D : (part + 1) * D].astype(low)
    pieces[8 * rows :, :] = down[...].astype(low)
    low_pos[...] = pos[...].astype(low)


def pack(qkv, out_w, up, down, pos):
    rows = qkv.shape[0]
    if rows % 16:
        pieces = jnp.concatenate(
            [split_rows(qkv, 3), out_w, split_rows(up, FF // D), down], 0
        ).astype(jnp.bfloat16)
        return pieces, pos.astype(jnp.bfloat16)
    vmem = pl.BlockSpec(memory_space=pltpu.VMEM)
    return pl.pallas_call(
        pack_kernel,
        name="pack",
        in_specs=[vmem] * 5,
        out_specs=[vmem] * 2,
        out_shape=[
            jax.ShapeDtypeStruct((12 * rows, D), jnp.bfloat16),
            jax.ShapeDtypeStruct(pos.shape, jnp.bfloat16),
        ],
        compiler_params=pltpu.CompilerParams(vmem_limit_bytes=VMEM_GRANT),
    )(qkv, out_w, up, down, pos)


LOOP = {8: (0, 2, 4, 6, 7, 5, 3, 1)}


def swap_core(value):
    return lax.ppermute(value, "dp", [(i, i ^ 1) for i in range(lax.axis_size("dp"))])


def swap_x(value):
    count = lax.axis_size("dp")
    return lax.ppermute(value, "dp", [(i, (i + 2) % count) for i in range(count)])


def sum_x(value):
    count = lax.axis_size("dp")
    total = value
    for hop in range(2, count, 2):
        moved = lax.ppermute(value, "dp", [(i, (i + hop) % count) for i in range(count)])
        total = total.astype(jnp.float32) + moved.astype(jnp.float32)
    return total


def shift(value, step):
    loop = LOOP[lax.axis_size("fsdp")]
    size = len(loop)
    return lax.ppermute(
        value, "fsdp", [(loop[i], loop[(i + step) % size]) for i in range(size)]
    )


def loop_place():
    loop = LOOP[lax.axis_size("fsdp")]
    place = [0] * len(loop)
    for i, device in enumerate(loop):
        place[device] = i
    return jnp.array(place, jnp.int32)[lax.axis_index("fsdp")], jnp.array(loop, jnp.int32)


def ring_gather(part, sign):
    size = lax.axis_size("fsdp")
    place, loop = loop_place()
    out = jnp.zeros((size,) + part.shape, part.dtype)

    def put(out, block, offset):
        at = loop[lax.rem(place + offset + size, size)]
        return lax.dynamic_update_slice(out, block[None], (at, 0, 0))

    out = put(out, part, 0)
    ahead = behind = part
    for hop in range(1, size // 2 + 1):
        ahead = shift(ahead, sign)
        out = put(out, ahead, -sign * hop)
        if hop < size - size // 2:
            behind = shift(behind, -sign)
            out = put(out, behind, sign * hop)
    return out


def ring_reduce(parts, sign):
    size = lax.axis_size("fsdp")
    place, loop = loop_place()

    def local(offset):
        at = loop[lax.rem(place + offset + size, size)]
        return lax.dynamic_index_in_dim(parts, at, 0, keepdims=False).astype(jnp.float32)

    def flow(direction, hops):
        arrived = None
        for hop in range(hops):
            value = local(direction * (hops - hop))
            if arrived is not None:
                value = value + arrived.astype(jnp.float32)
            arrived = shift(value.astype(jnp.bfloat16), direction)
        return arrived

    far = flow(sign, size // 2)
    near = flow(-sign, size - size // 2 - 1)
    return local(0) + far.astype(jnp.float32) + near.astype(jnp.float32)


def gather_halves(first, second, sign):
    core = lax.rem(lax.axis_index("dp"), 2)
    if lax.axis_size("fsdp") not in LOOP:
        return lax.all_gather(first, "fsdp", axis=0), lax.all_gather(second, "fsdp", axis=0)
    mine = ring_gather(jnp.where(core == 0, first, second), sign)
    other = swap_core(mine)
    return jnp.where(core == 0, mine, other), jnp.where(core == 0, other, mine)


def reduce_halves(first, second, sign):
    core = lax.rem(lax.axis_index("dp"), 2)
    give = jnp.where(core == 0, second, first).astype(jnp.bfloat16)
    keep = jnp.where(core == 0, first, second).astype(jnp.float32)
    chip = (keep + swap_core(give).astype(jnp.float32)).astype(jnp.bfloat16)
    if lax.axis_size("fsdp") in LOOP:
        block = ring_reduce(chip, sign)
    else:
        block = lax.psum_scatter(chip.astype(jnp.float32), "fsdp", scatter_dimension=0)
    total = sum_x(block.astype(jnp.bfloat16)).astype(jnp.bfloat16)
    other = swap_core(total)
    low = jnp.where(core == 0, total, other).astype(jnp.float32)
    high = jnp.where(core == 0, other, total).astype(jnp.float32)
    return low, high


def split_rows(weight, parts):
    return jnp.concatenate(jnp.split(weight, parts, axis=1), axis=0)


def join_rows(blocks, parts):
    count, rows, width = blocks.shape
    return (
        blocks.reshape(count, parts, rows // parts, width)
        .transpose(0, 2, 1, 3)
        .reshape(count * rows // parts, parts * width)
    )


def cut_parts(grad, count, parts):
    width = grad.shape[-1]
    return (
        grad.reshape(parts, count, -1, width).transpose(1, 0, 2, 3).reshape(count, -1, width)
    )


def pad_rows(value, rows):
    return jnp.pad(value, [(0, 0)] * (value.ndim - 2) + [(0, rows - value.shape[-2]), (0, 0)])


def round_up(value, step):
    return -(-value // step) * step


def bucket_size(tokens, owners):
    mean = tokens / owners
    return min(tokens, round_up(int(mean + 5.6 * math.sqrt(mean)), 16))


def one_hot(index, count):
    return (index[:, None] == lax.iota(jnp.int32, count)[None, :]).astype(jnp.bfloat16)


class Routes:
    def __init__(self, everyone, own_rows):
        fsdp = lax.axis_size("fsdp")
        self.rows = own_rows
        tokens = everyone.shape[1]
        self.cap = bucket_size(tokens, fsdp)
        me = lax.axis_index("fsdp")
        group = lax.dynamic_slice_in_dim(everyone, lax.axis_index("dp") * fsdp, fsdp, 0)
        mine = lax.dynamic_index_in_dim(group, me, 0, keepdims=False)
        owners = lax.iota(jnp.int32, fsdp)
        every_count = jnp.sum(
            (everyone // own_rows)[:, :, None] == owners[None, None, :], 1, dtype=jnp.int32
        )
        self.rounds = (jnp.max(every_count) + self.cap - 1) // self.cap
        self.inner = group - me * own_rows
        self.held = (self.inner >= 0) & (self.inner < own_rows)
        self.held_place = jnp.cumsum(self.held.astype(jnp.int32), 1) - 1
        self.owner = mine // own_rows
        hot = (self.owner[None, :] == owners[:, None])
        place = jnp.cumsum(hot.astype(jnp.int32), 1) - 1
        self.hot = hot
        self.place = place
        self.my_place = jnp.sum(jnp.where(hot, place, 0), 0)

    def slots(self, flag, place, value, turn):
        slot = lax.iota(jnp.int32, self.cap)[None, :, None] + turn * self.cap
        hit = flag[:, None, :] & (place[:, None, :] == slot)
        return (jnp.sum(jnp.where(hit, value[:, None, :] + 1, 0), -1) - 1).reshape(-1)

    def owner_rows(self, turn):
        return self.slots(self.held, self.held_place, self.inner, turn)

    def asker_tokens(self, turn):
        tokens = lax.iota(jnp.int32, self.owner.shape[0])[None, :]
        return self.slots(self.hot, self.place, tokens, turn)

    def asker_slots(self, turn):
        place = self.my_place - turn * self.cap
        inside = (place >= 0) & (place < self.cap)
        return jnp.where(inside, self.owner * self.cap + place, -1)


def exchange(rows):
    fsdp = lax.axis_size("fsdp")
    blocks = rows.reshape(fsdp, rows.shape[0] // fsdp, rows.shape[1])
    return lax.all_to_all(blocks, "fsdp", 0, 0).reshape(rows.shape)


def pick_kernel(index, table, out):
    rows = lax.broadcasted_iota(jnp.int32, (index.shape[0], table.shape[0]), 1)
    pick = (index[:, 0:1] == rows).astype(jnp.bfloat16)
    out[...] = matmul(pick, table[...].astype(jnp.bfloat16)).astype(jnp.bfloat16)


def gather_table(table, routes, turn):
    index = routes.owner_rows(turn)
    size = routes.cap
    return call(
        pick_kernel,
        "pick_rows",
        (index.shape[0] // size,),
        [rows_spec(128, size), whole_spec(table.shape)],
        [rows_spec(D, size)],
        [jax.ShapeDtypeStruct((index.shape[0], D), jnp.bfloat16)],
        flops=2 * index.shape[0] * D * table.shape[0],
        moved=table.shape[0] * D * 4,
    )(jnp.broadcast_to(index[:, None], (index.shape[0], 128)), table)[0]


def all_words(everyone, table, rounds, tokens):
    def more(carry):
        return carry[0] < rounds

    def body(carry):
        turn, words = carry
        ids, turn, rows = lax.optimization_barrier((everyone, turn, table))
        routes = Routes(ids, table.shape[0])
        got = exchange(gather_table(rows, routes, turn))
        mine = matmul(one_hot(routes.asker_slots(turn), got.shape[0]), got)
        return turn + 1, words + mine.astype(jnp.bfloat16)

    start = (jnp.int32(0), jnp.zeros((tokens, D), jnp.bfloat16))
    return lax.while_loop(more, body, start)[1]


def return_round(grad_low, everyone, turn, rows):
    routes = Routes(everyone, rows)
    held = routes.owner_rows(turn)[None, :]
    sent = bucket_rows(routes.asker_slots(turn)[None, :], grad_low, held.shape[1])
    return scatter_rows(held, exchange(sent), rows)


def return_rows(grad_low, everyone, rounds, rows):
    def more(carry):
        return carry[0] < rounds

    def body(carry):
        turn, total = carry
        ids, turn = lax.optimization_barrier((everyone, turn))
        return turn + 1, total + return_round(grad_low, ids, turn, rows)

    return lax.while_loop(more, body, (jnp.int32(0), jnp.zeros((rows, D), jnp.float32)))[1]


def more_grads(grad_low, plan, table, squares):
    def more(carry):
        return carry[0] < plan.rounds

    def body(carry):
        turn, table, squares = carry
        ids, turn = lax.optimization_barrier((plan.everyone, turn))
        before = table.astype(jnp.float32)
        after = (before + sum_groups(return_round(grad_low, ids, turn, table.shape[0]))).astype(
            jnp.bfloat16
        )
        change = jnp.sum(after.astype(jnp.float32) ** 2) - jnp.sum(before * before)
        return turn + 1, after, squares + lax.psum(change, "fsdp")

    return lax.while_loop(more, body, (jnp.int32(1), table, squares))[1:]


def total_grads(everyone, rounds, grad_x, feed_grads, qkv_grads, grad_pos, grad_small, own_rows):
    fsdp = lax.axis_size("fsdp")
    down, up = reduce_halves(
        feed_grads[:FF].reshape(fsdp, -1, D), cut_parts(feed_grads[FF : 2 * FF], fsdp, 4), 1
    )
    qkv_cut = cut_parts(qkv_grads, fsdp, 3)
    shard = qkv_cut.shape[1] // 3
    pos_cut = grad_pos.reshape(fsdp, -1, D)
    half_pos = pos_cut.shape[1] // 2
    low, high = reduce_halves(
        jnp.concatenate([qkv_cut[:, : 2 * shard], pos_cut[:, :half_pos]], 1),
        jnp.concatenate(
            [
                qkv_cut[:, 2 * shard :],
                feed_grads[2 * FF :].reshape(fsdp, shard, D),
                pos_cut[:, half_pos:],
            ],
            1,
        ),
        -1,
    )
    cols = D // fsdp
    small = lax.dynamic_slice_in_dim(
        lax.psum(grad_small, ("dp", "fsdp")), lax.axis_index("fsdp") * cols, cols, 1
    )
    small = jnp.pad(small, ((0, 0), (0, 128 - cols)))
    table = sum_groups(return_rows(grad_x, everyone, rounds, own_rows))
    squares = sum(jnp.sum(part * part) for part in (table, down, up, low, high, small))
    squares = jnp.sum(gather_small(jnp.full((8, 128), squares), False, 2)[:, 0, 0])
    return (
        table.astype(jnp.bfloat16),
        jnp.stack([down, up]).astype(jnp.bfloat16),
        jnp.stack([low, high]).astype(jnp.bfloat16),
        small,
        squares,
    )


class Plan:
    def __init__(self, lengths, ids, pieces, pos_low, small, table):
        fsdp = lax.axis_size("fsdp")
        seq = ids.shape[1]
        tokens = ids.size
        cap = self.cap = bucket_size(tokens, fsdp)
        cols = small.shape[1]
        self.direct = fsdp == LOOP_SIZE and lax.axis_size("dp") == 4 and tokens == 1024
        if self.direct:
            block = lax.dynamic_update_slice(
                jnp.zeros((16, 256), jnp.bfloat16),
                small,
                (0, lax.rem(lax.axis_index("fsdp") * cols, 128)),
            )
            everyone, self.first, self.second, self.small, held, self.asker_row, most, *state = front(
                lengths, ids.reshape(1, tokens), pieces, pos_low, block, table, cap
            )
            self.everyone = everyone.reshape(-1, tokens)
            self.rounds = (most[0, 0] + cap - 1) // cap
            self.held = held.reshape(4, 1, -1)
            self.state = self.redo(lengths, table, seq, state, pos_low)
        else:
            self.everyone = gather_small(ids.reshape(-1, 128), True, 0).reshape(-1, tokens)
            self.rounds = Routes(self.everyone, table.shape[0]).rounds
            both = lax.all_gather(pieces, "fsdp", axis=0)
            shard = pieces.shape[0] // 12
            columns = both[:, : 8 * shard].reshape(fsdp, 8, shard, D).transpose(1, 0, 2, 3)
            self.first = columns[:4].reshape(-1, D)
            self.second = jnp.concatenate(
                [columns[4:].reshape(-1, D), both[:, 8 * shard :].reshape(-1, D)], 0
            )
            smalls = lax.all_gather(jnp.pad(small, ((0, 2), (0, 128 - cols))), "fsdp", axis=0)
            self.small = (
                smalls[:, :, :cols].transpose(1, 0, 2).reshape(16, D).astype(jnp.float32)
            )
            self.state = self.again(lengths, table, seq, pos_low, self.everyone)

    def again(self, lengths, table, seq, pos_low, everyone):
        tokens = everyone.shape[1]
        words = all_words(everyone, table, self.rounds, tokens)
        pos = lax.all_gather(pos_low, "fsdp", axis=0, tiled=True)
        nowhere = jnp.full((tokens, 128), -1, jnp.int32)
        x, h0, qkv = embed(nowhere, jnp.zeros((128, D), jnp.bfloat16), words, pos, self.first, self.small)
        return [x, h0, qkv, *attend(lengths, qkv, seq)]

    def redo(self, lengths, table, seq, state, pos_low):
        def more(carry):
            return carry[0] < self.rounds

        def once(carry):
            everyone, low, _ = lax.optimization_barrier((self.everyone, pos_low, carry[0]))
            return [self.rounds] + self.again(lengths, table, seq, low, everyone)

        return lax.while_loop(more, once, [jnp.int32(1)] + state)[1:]


def sum_groups(table):
    core = lax.rem(lax.axis_index("dp"), 2)
    half = table.shape[0] // 2
    low = table.astype(jnp.bfloat16)
    keep = lax.dynamic_slice_in_dim(table, core * half, half, 0)
    give = lax.dynamic_slice_in_dim(low, (1 - core) * half, half, 0)
    chip = (keep + swap_core(give).astype(jnp.float32)).astype(jnp.bfloat16)
    total = sum_x(chip).astype(jnp.bfloat16)
    other = swap_core(total)
    return jnp.concatenate(
        [jnp.where(core == 0, total, other), jnp.where(core == 0, other, total)], 0
    ).astype(jnp.float32)


def renew(weight, moment, average, grad, factor):
    step = factor * grad
    buffer = MOMENTUM * moment + step
    fresh = weight - RATE * (step + MOMENTUM * buffer)
    return (fresh, buffer, KEEP * average + (1.0 - KEEP) * fresh)


def renew_kernel(factor, *refs):
    kinds = len(refs) // 7
    scale = factor[0, 0]
    for kind in range(kinds):
        weight, moment, average, grad = refs[4 * kind : 4 * kind + 4]
        outs = refs[4 * kinds + 3 * kind : 4 * kinds + 3 * kind + 3]
        shape = weight.shape
        value = grad[...] if len(grad.shape) == 2 else grad[0]
        value = value[: shape[0], : shape[1]].astype(jnp.float32)
        results = renew(weight[...], moment[...], average[...], value, scale)
        for out, result in zip(outs, results):
            out[...] = result


def renew_all(factor, groups, table, sum_a, sum_b, small):
    steps = 12
    own_rows = table.shape[0]
    rows = groups[2][0].shape[0]
    half_pos = groups[1][0].shape[0] // 2
    down_rows = groups[5][0].shape[0]
    cols = 256

    def piece(i):
        return jnp.minimum(i // 3, 2)

    def third(i):
        return lax.rem(jnp.minimum(i, 8), 3)

    def late(i):
        return jnp.clip(i - 9, 0, 2)

    specs = [
        (pl.BlockSpec((own_rows // steps, D), lambda i: (i, 0)), None, table),
        (
            pl.BlockSpec((half_pos, D), lambda i: (jnp.minimum(i, 1), 0)),
            pl.BlockSpec((1, half_pos, D), lambda i: (jnp.minimum(i, 1), 2 * rows // half_pos, 0)),
            sum_b,
        ),
        (
            pl.BlockSpec((rows, cols), lambda i: (0, jnp.minimum(i, 8))),
            pl.BlockSpec(
                (1, rows, cols), lambda i: (piece(i) // 2, lax.rem(piece(i), 2), third(i))
            ),
            sum_b,
        ),
        (
            pl.BlockSpec((rows, cols), lambda i: (0, late(i))),
            pl.BlockSpec((1, rows, cols), lambda i: (1, 1, late(i))),
            sum_b,
        ),
        (
            pl.BlockSpec((rows, cols), lambda i: (0, i)),
            pl.BlockSpec((1, rows, cols), lambda i: (1, i // 3, lax.rem(i, 3))),
            sum_a,
        ),
        (
            pl.BlockSpec((down_rows // steps, D), lambda i: (i, 0)),
            pl.BlockSpec((1, down_rows // steps, D), lambda i: (0, i, 0)),
            sum_a,
        ),
        (whole_spec(groups[6][0].shape), whole_spec(small.shape), small),
    ]
    in_specs = [pl.BlockSpec(memory_space=pltpu.SMEM)]
    out_specs, shapes, operands = [], [], [factor.reshape(1, 1)]
    for (spec, grad_spec, grad), group in zip(specs, groups):
        in_specs += [spec] * 3 + [grad_spec or spec]
        operands += [*group, grad]
        out_specs += [spec] * 3
        shapes += [jax.ShapeDtypeStruct(group[0].shape, jnp.float32)] * 3
    size = sum(group[0].size for group in groups)
    results = call(
        renew_kernel, "renew", (steps,), in_specs, out_specs, shapes, flops=8 * size, moved=26 * size
    )(*operands)
    return results[0::3], results[1::3], results[2::3]


def shards(
    token_ids,
    lengths,
    pair_ids,
    scores,
    word_table,
    pos_table,
    qkv_weight,
    out_weight,
    up_weight,
    down_weight,
    small_params,
    word_moment,
    pos_moment,
    qkv_moment,
    out_moment,
    up_moment,
    down_moment,
    small_moment,
    word_average,
    pos_average,
    qkv_average,
    out_average,
    up_average,
    down_average,
    small_average,
):
    batch, seq = token_ids.shape
    width = D
    fsdp = lax.axis_size("fsdp")
    tokens = batch * seq
    shard = qkv_weight.shape[0]
    pos_rows = pos_table.shape[0]
    small_cols = small_params.shape[1]
    pieces, pos_low = pack(qkv_weight, out_weight, up_weight, down_weight, pos_table)
    plan = Plan(
        lengths,
        token_ids,
        pieces,
        pos_low,
        small_params.astype(jnp.bfloat16),
        word_table,
    )
    first, second, small_full = plan.first, plan.second, plan.small
    x, h0, qkv, mixed, logs = plan.state
    r1, low_h1, act, slope, r2, pooled = feed(lengths, mixed, h0, first, second, small_full)
    loss, share = pair_grads(lengths, pooled[:, 0], pair_ids, scores)
    grad_r1, grad_mixed, sums_feed, feed_grads = feed_back(
        lengths, share, r1, r2, slope, first, second, small_full, act, low_h1, mixed
    )
    own_rows = word_table.shape[0]
    if plan.direct:
        grad_x, low_pos, qkv_grads, sums_back, depart, own = back(
            lengths, qkv, grad_mixed, logs, small_full, grad_r1, x, first, feed_grads
        )
        grad_small = sums_feed + sums_back
        small_cut = jnp.pad(
            grad_small.reshape(16, fsdp, small_cols).transpose(1, 0, 2),
            ((0, 0), (0, 0), (0, 128 - small_cols)),
        )
        table, sum_a, sum_b, small, squares = finish(
            grad_x,
            plan.asker_row,
            plan.held,
            feed_grads,
            qkv_grads,
            low_pos,
            small_cut,
            depart,
            own,
            own_rows,
            plan.cap,
        )
        small = small.reshape(16, 128)
        table, total = more_grads(grad_x, plan, table, squares[0, 0])
    else:
        grad_qkv, sums_attend = attend_back(lengths, qkv, grad_mixed, logs, seq)
        grad_x, grad_pos, sums_embed = embed_back(grad_r1, grad_qkv, first, x, small_full, seq)
        qkv_grads = qkv_weights(h0, grad_qkv)
        grad_small = sums_feed + sums_attend + sums_embed
        table, sum_a, sum_b, small, total = total_grads(
            plan.everyone,
            plan.rounds,
            grad_x,
            feed_grads,
            qkv_grads,
            grad_pos.astype(jnp.bfloat16),
            grad_small,
            own_rows,
        )
    norm = jnp.sqrt(total)
    limit = 1e-05 * math.sqrt((VOCAB + LEN + 4 * D + 2 * FF + 14) * D)
    factor = jnp.minimum(1.0, limit / (norm + 1e-06))
    weights = (word_table, pos_table, qkv_weight, out_weight, up_weight, down_weight, small_params)
    moments = (
        word_moment,
        pos_moment,
        qkv_moment,
        out_moment,
        up_moment,
        down_moment,
        small_moment,
    )
    averages = (
        word_average,
        pos_average,
        qkv_average,
        out_average,
        up_average,
        down_average,
        small_average,
    )
    if plan.direct:
        groups = list(zip(weights, moments, averages))
        new_w, new_m, new_a = renew_all(factor, groups, table, sum_a, sum_b, small)
    else:
        wide_b = sum_b.astype(jnp.float32)
        summed = (
            table.astype(jnp.float32),
            wide_b[:, 2 * shard :].reshape(pos_rows, width),
            jnp.concatenate([wide_b[0, :shard], wide_b[0, shard : 2 * shard], wide_b[1, :shard]], 1),
            wide_b[1, shard : 2 * shard],
            join_rows(sum_a[1][None], 4).astype(jnp.float32),
            sum_a[0].astype(jnp.float32),
            small[:14, :small_cols],
        )
        new_w = []
        new_m = []
        new_a = []
        for weight, moment, average, grad in zip(weights, moments, averages, summed):
            fresh, buffer, mean_new = renew(weight, moment, average, grad, factor)
            new_w.append(fresh)
            new_m.append(buffer)
            new_a.append(mean_new)
    return (
        loss[0, 0],
        norm,
        new_w[0],
        new_w[1],
        new_w[2],
        new_w[3],
        new_w[4],
        new_w[5],
        new_w[6],
        new_m[0],
        new_m[1],
        new_m[2],
        new_m[3],
        new_m[4],
        new_m[5],
        new_m[6],
        new_a[0],
        new_a[1],
        new_a[2],
        new_a[3],
        new_a[4],
        new_a[5],
        new_a[6],
    )


def solution(mesh):
    placed = (
        P(("dp", "fsdp"), None),
        P(("dp", "fsdp")),
        P(),
        P(),
        P("fsdp", None),
        P("fsdp", None),
        P("fsdp", None),
        P("fsdp", None),
        P("fsdp", None),
        P("fsdp", None),
        P(None, "fsdp"),
        P("fsdp", None),
        P("fsdp", None),
        P("fsdp", None),
        P("fsdp", None),
        P("fsdp", None),
        P("fsdp", None),
        P(None, "fsdp"),
        P("fsdp", None),
        P("fsdp", None),
        P("fsdp", None),
        P("fsdp", None),
        P("fsdp", None),
        P("fsdp", None),
        P(None, "fsdp"),
    )
    return jax.shard_map(
        shards,
        mesh=mesh,
        in_specs=placed,
        out_specs=(
            P(),
            P(),
            P("fsdp", None),
            P("fsdp", None),
            P("fsdp", None),
            P("fsdp", None),
            P("fsdp", None),
            P("fsdp", None),
            P(None, "fsdp"),
            P("fsdp", None),
            P("fsdp", None),
            P("fsdp", None),
            P("fsdp", None),
            P("fsdp", None),
            P("fsdp", None),
            P(None, "fsdp"),
            P("fsdp", None),
            P("fsdp", None),
            P("fsdp", None),
            P("fsdp", None),
            P("fsdp", None),
            P("fsdp", None),
            P(None, "fsdp"),
        ),
        check_vma=False,
    )
```

```python
import functools
import math

import jax
import jax.numpy as jnp
from jax import lax
from jax.experimental import pallas as pl
from jax.experimental.pallas import tpu as pltpu
from jax.sharding import PartitionSpec as P

D = 768
H = 12
FF = 3072
VOCAB = 30720
LEN = 512


MOMENTUM = 0.9
RATE = 3000.0
KEEP = 0.9


def matmul(left, right):
    return jnp.dot(left, right, preferred_element_type=jnp.float32)


def outer_sum(left, right):
    return lax.dot_general(
        left, right, (((0,), (0,)), ((), ())), preferred_element_type=jnp.float32
    )


def back_mul(grad, weight):
    return lax.dot_general(
        grad, weight, (((1,), (1,)), ((), ())), preferred_element_type=jnp.float32
    )


TILE = 256
EPS = 1e-12
VMEM_GRANT = 60 * 1024 * 1024


def whole_spec(shape):
    return pl.BlockSpec(shape, lambda *_: (0,) * len(shape))


def rows_spec(width, rows=TILE):
    return pl.BlockSpec((rows, width), lambda i, *_: (i, 0))


def weight_spec(rows, at):
    return pl.BlockSpec((rows, D), lambda i, *_: (at, 0))


def call(kernel, name, grid, in_specs, out_specs, out_shape, scratch=(), prefetch=0, flops=0, moved=0):
    return pl.pallas_call(
        kernel,
        name=name,
        grid_spec=pltpu.PrefetchScalarGridSpec(
            num_scalar_prefetch=prefetch,
            grid=grid,
            in_specs=in_specs,
            out_specs=out_specs,
            scratch_shapes=scratch,
        ),
        out_shape=out_shape,
        compiler_params=pltpu.CompilerParams(vmem_limit_bytes=VMEM_GRANT),
        cost_estimate=pl.CostEstimate(flops=flops, bytes_accessed=moved, transcendentals=0),
    )


def normed(v):
    mean = jnp.mean(v, -1, keepdims=True)
    cent = v - mean
    scale = lax.rsqrt(jnp.mean(cent * cent, -1, keepdims=True) + EPS)
    return cent * scale, scale


def norm_back(grad, hat, scale, gain):
    inner = grad * gain
    middle = jnp.mean(inner, -1, keepdims=True)
    along = jnp.mean(inner * hat, -1, keepdims=True)
    return (
        scale * (inner - middle - hat * along),
        jnp.sum(grad * hat, 0, keepdims=True),
        jnp.sum(grad, 0, keepdims=True),
    )


def add_row(ref, row, value):
    ref[row : row + 1, :] += value


def embed_kernel(slot, got, extra, pos, weight, small, x_out, h0_out, qkv_out):
    count = got.shape[0]
    pick = (slot[:, 0:1] == lax.broadcasted_iota(jnp.int32, (slot.shape[0], count), 1)).astype(
        jnp.bfloat16
    )
    words = matmul(pick, got[...]) + extra[...].astype(jnp.float32)
    x = words + pos[...].astype(jnp.float32)
    hat, _ = normed(x)
    h0 = hat * small[0:1, :] + small[1:2, :]
    x_out[...] = x
    h0_out[...] = h0
    low = h0.astype(jnp.bfloat16)
    for third, bias in enumerate((2, None, 3)):
        value = matmul(low, weight[third * D : (third + 1) * D, :])
        if bias is not None:
            value = value + small[bias : bias + 1, :]
        qkv_out[:, third * D : (third + 1) * D] = value.astype(jnp.bfloat16)


def embed(slot, got, extra, pos, weight, small):
    tokens = slot.shape[0]
    turns = pos.shape[0] // TILE
    return call(
        embed_kernel,
        "embed_qkv",
        (tokens // TILE,),
        [
            rows_spec(128),
            whole_spec(got.shape),
            rows_spec(D),
            pl.BlockSpec((TILE, D), lambda i: (lax.rem(i, turns), 0)),
            weight_spec(3 * D, 0),
            whole_spec(small.shape),
        ],
        [rows_spec(D), rows_spec(D), rows_spec(3 * D)],
        [
            jax.ShapeDtypeStruct((tokens, D), jnp.float32),
            jax.ShapeDtypeStruct((tokens, D), jnp.float32),
            jax.ShapeDtypeStruct((tokens, 3 * D), jnp.bfloat16),
        ],
        flops=2 * tokens * D * (3 * D + got.shape[0]),
        moved=tokens * D * 20,
    )(slot, got, extra, pos, weight, small)


def head_masks(rows):
    lane = lax.broadcasted_iota(jnp.int32, (rows, 128), 1)
    return (lane < 64, lane >= 64)


def live_row(length, seq):
    return jnp.where(
        lax.broadcasted_iota(jnp.int32, (1, seq), 1) < length, 0.0, -1000000000.0
    ).astype(jnp.float32)


def attend_pair(qkv, bias, masks, logs, mixed_out, rows, pair):
    at = pair * 128
    query = qkv[rows, at : at + 128] * jnp.bfloat16(0.125)
    keys = qkv[rows, D + at : D + at + 128]
    values = qkv[rows, 2 * D + at : 2 * D + at + 128]
    lane = lax.broadcasted_iota(jnp.int32, logs.shape, 1)
    sides = []
    for side, mask in enumerate(masks):
        logits = back_mul(jnp.where(mask, query, jnp.zeros_like(query)), keys) + bias
        top = jnp.max(logits, -1, keepdims=True)
        raised = jnp.exp(logits - top)
        total = jnp.sum(raised, -1, keepdims=True)
        probs = (raised * (1.0 / total)).astype(jnp.bfloat16)
        sides.append(matmul(probs, values))
        logs = jnp.where(lane == 2 * pair + side, top + jnp.log(total), logs)
    mixed_out[rows, at : at + 128] = jnp.where(masks[0], sides[0], sides[1]).astype(jnp.bfloat16)
    return logs


def attend_kernel(lengths, qkv, mixed_out, log_out):
    seq = qkv.shape[0]
    bias = live_row(lengths[pl.program_id(0)], seq)
    masks = head_masks(seq)
    logs = jnp.zeros((seq, 128), jnp.float32)
    for pair in range(H // 2):
        logs = attend_pair(qkv, bias, masks, logs, mixed_out, slice(0, seq), pair)
    log_out[...] = logs


def attend(lengths, qkv, seq):
    tokens = qkv.shape[0]
    return call(
        attend_kernel,
        "attention",
        (tokens // seq,),
        [rows_spec(3 * D, seq)],
        [rows_spec(D, seq), rows_spec(128, seq)],
        [
            jax.ShapeDtypeStruct((tokens, D), jnp.bfloat16),
            jax.ShapeDtypeStruct((tokens, 128), jnp.float32),
        ],
        prefetch=1,
        flops=4 * tokens * seq * D,
        moved=tokens * D * 8,
    )(lengths, qkv)


def feed_kernel(
    lengths, mixed, h0, out_w, up_w, down_w, small, r1_out, h1_out, act_out, slope_out, r2_out, pooled
):
    step = pl.program_id(0)
    turns = LEN // TILE
    r1 = h0[...] + (matmul(mixed[...], out_w[...]) + small[4:5, :])
    hat, _ = normed(r1)
    h1 = hat * small[5:6, :] + small[6:7, :]
    low = h1.astype(jnp.bfloat16)
    r1_out[...] = r1
    h1_out[...] = low
    ffn = jnp.zeros(r1.shape, jnp.float32)
    for part in range(FF // D):
        up = matmul(low, up_w[part * D : (part + 1) * D, :]) + small[7 + part : 8 + part, :]
        below = 0.5 * (1.0 + lax.erf(up * math.sqrt(0.5)))
        act = (up * below).astype(jnp.bfloat16)
        slope = below + up * jnp.exp(-0.5 * up * up) * (1.0 / math.sqrt(2.0 * math.pi))
        act_out[:, part * D : (part + 1) * D] = act
        slope_out[:, part * D : (part + 1) * D] = slope.astype(jnp.bfloat16)
        ffn = ffn + matmul(act, down_w[part * D : (part + 1) * D, :])
    r2 = h1 + (ffn + small[11:12, :])
    r2_out[...] = r2
    hat2, _ = normed(r2)
    h2 = hat2 * small[12:13, :] + small[13:14, :]
    length = lengths[step // turns]
    at = lax.rem(step, turns) * TILE + lax.broadcasted_iota(jnp.int32, (TILE, 1), 0)
    part_sum = jnp.sum(jnp.where(at < length, h2, 0.0), 0, keepdims=True)

    @pl.when(lax.rem(step, turns) == 0)
    def _():
        pooled[...] = jnp.zeros_like(pooled)

    pooled[0, 0:1, :] += part_sum / length.astype(jnp.float32)


def feed(lengths, mixed, h0, first, second, small):
    tokens = mixed.shape[0]
    turns = LEN // TILE
    return call(
        feed_kernel,
        "feed_forward",
        (tokens // TILE,),
        [
            rows_spec(D),
            rows_spec(D),
            weight_spec(D, 3),
            weight_spec(FF, 0),
            weight_spec(FF, 1),
            whole_spec(small.shape),
        ],
        [
            rows_spec(D),
            rows_spec(D),
            rows_spec(FF),
            rows_spec(FF),
            rows_spec(D),
            pl.BlockSpec((1, 8, D), lambda i, *_: (i // turns, 0, 0)),
        ],
        [
            jax.ShapeDtypeStruct((tokens, D), jnp.float32),
            jax.ShapeDtypeStruct((tokens, D), jnp.bfloat16),
            jax.ShapeDtypeStruct((tokens, FF), jnp.bfloat16),
            jax.ShapeDtypeStruct((tokens, FF), jnp.bfloat16),
            jax.ShapeDtypeStruct((tokens, D), jnp.float32),
            jax.ShapeDtypeStruct((tokens // LEN, 8, D), jnp.float32),
        ],
        prefetch=1,
        flops=2 * tokens * D * (D + 2 * FF),
        moved=tokens * D * 32,
    )(lengths, mixed, h0, first, second, second, small)


def feed_back_kernel(
    lengths,
    share,
    r1,
    r2,
    slope,
    out_w,
    up_w,
    down_w,
    small,
    act,
    low_h1,
    mixed,
    r1_grad,
    mixed_out,
    sums,
    weights_out,
    low_f,
    low_u,
    low_a,
):
    step = pl.program_id(0)
    turns = LEN // TILE
    tiles = low_f.shape[0] // TILE
    parts = FF // D

    @pl.when(step == 0)
    def _():
        sums[...] = jnp.zeros_like(sums)

    @pl.when(step < tiles)
    def _():
        rows = pl.ds(pl.multiple_of(step * TILE, TILE), TILE)
        length = lengths[jnp.minimum(step, tiles - 1) // turns]
        at = lax.rem(step, turns) * TILE + lax.broadcasted_iota(jnp.int32, (TILE, 1), 0)
        grad_h2 = jnp.where(at < length, share[0, 0:1, :], 0.0)
        hat2, scale2 = normed(r2[...])
        grad_r2, gain2, shift2 = norm_back(grad_h2, hat2, scale2, small[12:13, :])
        add_row(sums, 12, gain2)
        add_row(sums, 13, shift2)
        add_row(sums, 11, jnp.sum(grad_r2, 0, keepdims=True))
        tile_f = grad_r2.astype(jnp.bfloat16)
        low_f[rows, :] = tile_f
        grad_h1 = grad_r2
        for part in range(parts):
            span = slice(part * D, (part + 1) * D)
            grad_up = back_mul(tile_f, down_w[span, :]) * slope[:, span].astype(jnp.float32)
            add_row(sums, 7 + part, jnp.sum(grad_up, 0, keepdims=True))
            tile_u = grad_up.astype(jnp.bfloat16)
            low_u[part, rows, :] = tile_u
            grad_h1 = grad_h1 + back_mul(tile_u, up_w[span, :])
        hat1, scale1 = normed(r1[...])
        grad_r1, gain1, shift1 = norm_back(grad_h1, hat1, scale1, small[5:6, :])
        add_row(sums, 5, gain1)
        add_row(sums, 6, shift1)
        add_row(sums, 4, jnp.sum(grad_r1, 0, keepdims=True))
        r1_grad[...] = grad_r1
        tile_a = grad_r1.astype(jnp.bfloat16)
        low_a[rows, :] = tile_a
        mixed_out[...] = back_mul(tile_a, out_w[...]).astype(jnp.bfloat16)

    turn = step - tiles

    @pl.when((turn >= 0) & (turn < parts))
    def _():
        weights_out[...] = outer_sum(act[...], low_f[...]).astype(jnp.bfloat16)

    @pl.when((turn >= parts) & (turn < 2 * parts))
    def _():
        part = jnp.clip(turn - parts, 0, parts - 1)
        weights_out[...] = outer_sum(low_h1[...], low_u[part]).astype(jnp.bfloat16)

    @pl.when(turn == 2 * parts)
    def _():
        weights_out[...] = outer_sum(mixed[...], low_a[...]).astype(jnp.bfloat16)


def feed_back(lengths, share, r1, r2, slope, first, second, small, act, low_h1, mixed):
    tokens = r1.shape[0]
    turns = LEN // TILE
    tiles = tokens // TILE
    parts = FF // D

    def rows(width):
        return pl.BlockSpec((TILE, width), lambda i, *_: (jnp.minimum(i, tiles - 1), 0))

    return call(
        feed_back_kernel,
        "feed_forward_back",
        (tiles + 2 * parts + 1,),
        [
            pl.BlockSpec((1, 8, D), lambda i, *_: (jnp.minimum(i, tiles - 1) // turns, 0, 0)),
            rows(D),
            rows(D),
            rows(FF),
            weight_spec(D, 3),
            weight_spec(FF, 0),
            weight_spec(FF, 1),
            whole_spec(small.shape),
            pl.BlockSpec((tokens, D), lambda i, *_: (0, jnp.clip(i - tiles, 0, parts - 1))),
            whole_spec((tokens, D)),
            whole_spec((tokens, D)),
        ],
        [
            rows(D),
            rows(D),
            whole_spec((16, D)),
            pl.BlockSpec((D, D), lambda i, *_: (jnp.maximum(i - tiles, 0), 0)),
        ],
        [
            jax.ShapeDtypeStruct((tokens, D), jnp.float32),
            jax.ShapeDtypeStruct((tokens, D), jnp.bfloat16),
            jax.ShapeDtypeStruct((16, D), jnp.float32),
            jax.ShapeDtypeStruct(((2 * parts + 1) * D, D), jnp.bfloat16),
        ],
        scratch=[
            pltpu.VMEM((tokens, D), jnp.bfloat16),
            pltpu.VMEM((parts, tokens, D), jnp.bfloat16),
            pltpu.VMEM((tokens, D), jnp.bfloat16),
        ],
        prefetch=1,
        flops=4 * tokens * D * (D + 2 * FF),
        moved=tokens * D * 48,
    )(lengths, share, r1, r2, slope, first, second, second, small, act, low_h1, mixed)


def attend_back_kernel(lengths, qkv, grad_mixed, logs, out, sums):
    seq = qkv.shape[0]
    bias = live_row(lengths[pl.program_id(0)], seq)
    masks = head_masks(seq)

    @pl.when(pl.program_id(0) == 0)
    def _():
        sums[...] = jnp.zeros_like(sums)

    for pair in range(H // 2):
        attend_back_pair(
            qkv, grad_mixed, logs, bias, masks, out, sums, slice(0, seq), pair
        )


def attend_back(lengths, qkv, grad_mixed, logs, seq):
    tokens = qkv.shape[0]
    return call(
        attend_back_kernel,
        "attention_back",
        (tokens // seq,),
        [rows_spec(3 * D, seq), rows_spec(D, seq), rows_spec(128, seq)],
        [rows_spec(3 * D, seq), whole_spec((16, D))],
        [
            jax.ShapeDtypeStruct((tokens, 3 * D), jnp.bfloat16),
            jax.ShapeDtypeStruct((16, D), jnp.float32),
        ],
        prefetch=1,
        flops=10 * tokens * seq * D,
        moved=tokens * D * 16,
    )(lengths, qkv, grad_mixed, logs)


def embed_back_kernel(grad_r1, grad_qkv, weight, x, small, x_out, pos_out, sums):
    spot, sentence = pl.program_id(0), pl.program_id(1)

    @pl.when((spot == 0) & (sentence == 0))
    def _():
        sums[...] = jnp.zeros_like(sums)

    @pl.when(sentence == 0)
    def _():
        pos_out[...] = jnp.zeros_like(pos_out)

    grad_h0 = grad_r1[...]
    for third in range(3):
        span = slice(third * D, (third + 1) * D)
        grad_h0 = grad_h0 + back_mul(grad_qkv[:, span], weight[span, :])
    hat, scale = normed(x[...])
    grad_x, gain, shift = norm_back(grad_h0, hat, scale, small[0:1, :])
    add_row(sums, 0, gain)
    add_row(sums, 1, shift)
    x_out[...] = grad_x.astype(jnp.bfloat16)
    pos_out[...] += grad_x


def embed_back(grad_r1, grad_qkv, weight, x, small, seq):
    tokens = x.shape[0]
    turns = seq // TILE

    def rows(width):
        return pl.BlockSpec((TILE, width), lambda p, b: (b * turns + p, 0))

    return call(
        embed_back_kernel,
        "embed_back",
        (turns, tokens // seq),
        [rows(D), rows(3 * D), whole_spec((3 * D, D)), rows(D), whole_spec(small.shape)],
        [rows(D), pl.BlockSpec((TILE, D), lambda p, b: (p, 0)), whole_spec((16, D))],
        [
            jax.ShapeDtypeStruct((tokens, D), jnp.bfloat16),
            jax.ShapeDtypeStruct((seq, D), jnp.float32),
            jax.ShapeDtypeStruct((16, D), jnp.float32),
        ],
        flops=6 * tokens * D * D,
        moved=tokens * D * 20,
    )(grad_r1, grad_qkv, weight, x, small)


def qkv_outer_kernel(h0, grad_qkv, out, low):
    @pl.when(pl.program_id(0) == 0)
    def _():
        low[...] = h0[...].astype(jnp.bfloat16)

    out[...] = outer_sum(low[...], grad_qkv[...]).astype(jnp.bfloat16)


def qkv_weights(h0, grad_qkv):
    tokens = h0.shape[0]
    return call(
        qkv_outer_kernel,
        "qkv_weights",
        (3,),
        [whole_spec((tokens, D)), pl.BlockSpec((tokens, D), lambda i: (0, i))],
        [pl.BlockSpec((D, D), lambda i: (i, 0))],
        [jax.ShapeDtypeStruct((3 * D, D), jnp.bfloat16)],
        scratch=[pltpu.VMEM((tokens, D), jnp.bfloat16)],
        flops=6 * tokens * D * D,
        moved=tokens * D * 12,
    )(h0, grad_qkv)[0]


def bucket_kernel(slot, grad, out):
    size = out.shape[0]
    at = pl.program_id(0) * size + lax.broadcasted_iota(jnp.int32, (size, slot.shape[1]), 0)
    pick = (slot[...] == at).astype(jnp.bfloat16)
    out[...] = matmul(pick, grad[...]).astype(jnp.bfloat16)


def bucket_rows(slot, grad, count):
    tokens = grad.shape[0]
    size = count // 4
    return call(
        bucket_kernel,
        "bucket_rows",
        (count // size,),
        [whole_spec((1, tokens)), whole_spec((tokens, D))],
        [pl.BlockSpec((size, D), lambda i: (i, 0))],
        [jax.ShapeDtypeStruct((count, D), jnp.bfloat16)],
        flops=2 * tokens * D * count,
        moved=tokens * D * 4,
    )(slot, grad)[0]


def scatter_kernel(row, got, out):
    size = out.shape[0]
    at = pl.program_id(0) * size + lax.broadcasted_iota(jnp.int32, (size, row.shape[1]), 0)
    pick = (row[...] == at).astype(jnp.bfloat16)
    out[...] = matmul(pick, got[...])


def scatter_rows(row, got, rows):
    size = math.gcd(rows, 480)
    count = got.shape[0]
    return call(
        scatter_kernel,
        "scatter_rows",
        (rows // size,),
        [whole_spec((1, count)), whole_spec((count, D))],
        [pl.BlockSpec((size, D), lambda i: (i, 0))],
        [jax.ShapeDtypeStruct((rows, D), jnp.float32)],
        flops=2 * rows * D * count,
        moved=rows * D * 8,
    )(row, got)[0]


MESH = pl.DeviceIdType.MESH


def gather_kernel(sizes, whole, src, out, send, recv, local):
    dp, fsdp = sizes
    count = dp * fsdp if whole else fsdp
    row, col = lax.axis_index("dp"), lax.axis_index("fsdp")
    me = row * fsdp + col if whole else col

    def target(step):
        other = lax.rem(me + step, count)
        return (other // fsdp, lax.rem(other, fsdp)) if whole else (row, other)

    barrier = pltpu.get_barrier_semaphore()

    def greet(step, carry):
        pl.semaphore_signal(barrier, inc=1, device_id=target(step), device_id_type=MESH)
        return carry

    lax.fori_loop(1, count, greet, 0)
    pl.semaphore_wait(barrier, count - 1)
    own = pltpu.make_async_copy(src, out.at[me], local)
    own.start()

    def copy(step):
        return pltpu.make_async_remote_copy(
            src_ref=src,
            dst_ref=out.at[me],
            send_sem=send.at[step],
            recv_sem=recv.at[step],
            device_id=target(step),
            device_id_type=MESH,
        )

    def begin(step, carry):
        copy(step).start()
        return carry

    def end(step, carry):
        copy(step).wait()
        return carry

    lax.fori_loop(1, count, begin, 0)
    lax.fori_loop(1, count, end, 0)
    own.wait()


def gather_small(value, whole, collective):
    dp, fsdp = lax.axis_size("dp"), lax.axis_size("fsdp")
    count = dp * fsdp if whole else fsdp
    return pl.pallas_call(
        functools.partial(gather_kernel, (dp, fsdp), whole),
        out_shape=jax.ShapeDtypeStruct((count,) + value.shape, value.dtype),
        in_specs=[pl.BlockSpec(memory_space=pltpu.VMEM)],
        out_specs=pl.BlockSpec(memory_space=pltpu.VMEM),
        scratch_shapes=[
            pltpu.SemaphoreType.DMA((count,)),
            pltpu.SemaphoreType.DMA((count,)),
            pltpu.SemaphoreType.DMA,
        ],
        compiler_params=pltpu.CompilerParams(collective_id=collective, has_side_effects=True),
    )(value)


LOOP_SIZE = 8
AHEAD = 2
CHUNK = 480


def grid_place(device):
    z, y = device // 2, lax.rem(device, 2)
    return z + y * (LOOP_SIZE - 1 - 2 * z)


def grid_device(place):
    place = lax.rem(place + LOOP_SIZE, LOOP_SIZE)
    y = place // (LOOP_SIZE // 2)
    return 2 * (place + y * (LOOP_SIZE - 1 - 2 * place)) + y


def front_kernel(
    cap,
    own_rows,
    lengths,
    ids,
    small,
    pieces,
    pos_low,
    table,
    everyone,
    first,
    second,
    small_out,
    held_rows,
    asker_row,
    most,
    x_out,
    h0_out,
    qkv_out,
    mixed_out,
    log_out,
    stage,
    table_low,
    sent,
    got,
    before,
    asker_col,
    smalls,
    small_sum,
    pos,
    x_in,
    h0_in,
    qkv,
    id_send,
    id_recv,
    hop_send,
    hop_recv,
    word_send,
    word_recv,
    small_send,
    small_recv,
    held_send,
    held_recv,
    stage_sem,
    local_sem,
):
    fsdp = LOOP_SIZE
    row, col = lax.axis_index("dp"), lax.axis_index("fsdp")
    count = lax.axis_size("dp") * fsdp
    tokens = ids.shape[1]
    seq = LEN
    me = row * fsdp + col
    shard = pieces.shape[0] // 12
    pos_rows = pos_low.shape[0]
    quarter = row
    place = grid_place(col)
    core_mate = row + 1 - 2 * lax.rem(row, 2)
    x_mate = lax.rem(row + 2, 4)
    far_mate = lax.rem(core_mate + 2, 4)
    right = (row, grid_device(place + 1))
    left = (row, grid_device(place - 1))

    def anyone(step):
        other = lax.rem(me + step, count)
        return (other // fsdp, lax.rem(other, fsdp))

    barrier = pltpu.get_barrier_semaphore()

    def greet(step, carry):
        pl.semaphore_signal(barrier, inc=1, device_id=anyone(step), device_id_type=MESH)
        return carry

    lax.fori_loop(1, count, greet, 0)
    pl.semaphore_wait(barrier, count - 1)

    def remote(src, dst, sems, index, target):
        return pltpu.make_async_remote_copy(
            src_ref=src,
            dst_ref=dst,
            send_sem=sems[0].at[index],
            recv_sem=sems[1].at[index],
            device_id=target,
            device_id_type=MESH,
        )

    def id_copy(step):
        return remote(ids, everyone.at[me], (id_send, id_recv), step, anyone(step))

    def id_start(step, carry):
        id_copy(step).start()
        return carry

    lax.fori_loop(1, count, id_start, 0)
    everyone[pl.ds(me, 1)] = ids[...][None]

    def aligned(at):
        return pl.multiple_of(at, 16)

    def hop_refs(phase, block, part, own):
        if phase == 0:
            size = pos_rows // 4
            there = [
                first.at[pl.ds(aligned(part * D + block * shard), shard), :],
                pos.at[pl.ds(aligned(block * pos_rows + part * size), size), :],
            ]
            here = [
                pieces.at[pl.ds(aligned(part * shard), shard), :],
                pos_low.at[pl.ds(aligned(part * size), size), :],
            ]
        else:
            there, here = [], []
            late = part // 2
            for i in range(2):
                piece = part * 2 + i
                early_at = piece * D + block * shard
                late_at = FF + block * 4 * shard + (piece - 4) * shard
                there.append(
                    second.at[pl.ds(aligned(early_at + late * (late_at - early_at)), shard), :]
                )
                here.append(pieces.at[pl.ds(aligned((4 + piece) * shard), shard), :])
        return there, here if own else there

    def hop(phase, slot, block, part, target, own=False):
        there, here = hop_refs(phase, block, part, own)
        return [
            remote(src, dst, (hop_send, hop_recv), 56 * phase + 2 * slot + i, target)
            for i, (src, dst) in enumerate(zip(here, there))
        ]

    started = []

    def begin(copies):
        for copy in copies:
            copy.start()
        started.extend(copies)

    def arrive(copies):
        for copy in copies:
            copy.wait_recv()

    events = []
    for k in range(1, LOOP_SIZE // 2 + 1):
        events.append((k, 1))
        if k < LOOP_SIZE // 2:
            events.append((k, -1))
    slot_of = {event: i for i, event in enumerate(events)}
    total = len(events)

    def block_of(event):
        return grid_device(place - event[0] * event[1])

    def begin_ring(phase):
        begin(hop(phase, slot_of[(1, 1)], col, quarter, right, own=True))
        begin(hop(phase, slot_of[(1, -1)], col, quarter, left, own=True))

    def spread(phase, index):
        event = events[index]
        hops, sign = event
        block = block_of(event)
        arrive(hop(phase, index, block, quarter, right))
        follow = (hops + 1, sign)
        if follow in slot_of:
            begin(hop(phase, slot_of[follow], block, quarter, right if sign == 1 else left))
        begin(hop(phase, total + index, block, quarter, (x_mate, col)))
        begin(hop(phase, 2 * total + index, block, quarter, (core_mate, col)))

    def pass_on(phase, index):
        block = block_of(events[index])
        arrive(hop(phase, total + index, block, x_mate, (x_mate, col)))
        begin(hop(phase, 3 * total + index, block, x_mate, (core_mate, col)))

    def settle(phase):
        for index in range(total):
            block = block_of(events[index])
            arrive(hop(phase, 2 * total + index, block, core_mate, (core_mate, col)))
            arrive(hop(phase, 3 * total + index, block, far_mate, (core_mate, col)))

    begin_ring(0)

    def small_copy(step):
        return remote(
            small, smalls.at[col], (small_send, small_recv), step, (row, lax.rem(col + step, fsdp))
        )

    for step in range(1, fsdp):
        small_copy(step).start()
    begin_ring(1)
    local = [
        pltpu.make_async_copy(small, smalls.at[col], local_sem.at[0]),
        pltpu.make_async_copy(
            pos_low, pos.at[pl.ds(aligned(col * pos_rows), pos_rows), :], local_sem.at[1]
        ),
        pltpu.make_async_copy(
            pieces.at[pl.ds(8 * shard, 4 * shard), :],
            second.at[pl.ds(aligned(FF + col * 4 * shard), 4 * shard), :],
            local_sem.at[2],
        ),
    ]
    for piece in range(4):
        span = pl.ds(aligned(piece * D + col * shard), shard)
        here = pieces.at[pl.ds(piece * shard, shard), :]
        local.append(pltpu.make_async_copy(here, first.at[span, :], local_sem.at[3 + piece]))
        here = pieces.at[pl.ds((4 + piece) * shard, shard), :]
        local.append(pltpu.make_async_copy(here, second.at[span, :], local_sem.at[7 + piece]))
    for copy in local:
        copy.start()

    chunks = own_rows // CHUNK

    def stage_copy(chunk, slot):
        return pltpu.make_async_copy(
            table.at[pl.ds(chunk * CHUNK, CHUNK), :], stage.at[slot], stage_sem.at[slot]
        )

    stage_copy(0, 0).start()
    across = lax.broadcasted_iota(jnp.int32, (tokens, tokens), 1)
    down = lax.broadcasted_iota(jnp.int32, (tokens, tokens), 0)
    before[...] = (down <= across).astype(jnp.float32).astype(jnp.bfloat16)
    for chunk in range(chunks):
        if chunk + 1 < chunks:
            stage_copy(chunk + 1, (chunk + 1) % 2).start()
        stage_copy(chunk, chunk % 2).wait()
        table_low[chunk * CHUNK : (chunk + 1) * CHUNK, :] = stage[chunk % 2].astype(jnp.bfloat16)

    def words_at(device):
        return got.at[pl.ds(aligned(device * cap), cap), :]

    def word_copy(step):
        other = lax.rem(col + step, fsdp)
        return remote(sent.at[other], words_at(col), (word_send, word_recv), step, (row, other))

    def bucket(step):
        asker = lax.rem(col + step, fsdp)
        if step:
            id_copy(lax.rem(me - row * fsdp - asker + count, count)).wait_recv()
        theirs = everyone[row * fsdp + asker] - col * own_rows
        held = (theirs >= 0) & (theirs < own_rows)
        flag = jnp.broadcast_to(held, (8, tokens)).astype(jnp.float32).astype(jnp.bfloat16)
        rank = matmul(flag, before[...])[0:1, :].astype(jnp.int32) - 1
        rank = jnp.where(held, rank, -1)
        hit = lax.broadcasted_iota(jnp.int32, (cap, tokens), 0) == rank
        inner = jnp.sum(jnp.where(hit, theirs + 1, 0), 1, keepdims=True) - 1
        held_rows[pl.ds(row, 1), step] = jnp.broadcast_to(inner, (cap, 128)).T[0:1, :][None]
        rows = jnp.zeros((cap, D), jnp.float32)
        wide = own_rows // 4
        for part in range(4):
            pick = inner == part * wide + lax.broadcasted_iota(jnp.int32, (cap, wide), 1)
            rows = rows + matmul(
                pick.astype(jnp.float32).astype(jnp.bfloat16),
                table_low[part * wide : (part + 1) * wide, :],
            )
        if step:
            sent[pl.ds(asker, 1)] = rows.astype(jnp.bfloat16)[None]
            if step > AHEAD:
                word_copy(step - AHEAD).wait_send()
            word_copy(step).start()
        else:
            words_at(col)[...] = rows.astype(jnp.bfloat16)

    for step, chores in (
        (1, ()),
        (2, ((spread, 0, 0), (spread, 0, 1), (spread, 1, 0), (spread, 1, 1))),
        (3, ((pass_on, 0, 0), (spread, 0, 2), (spread, 0, 3))),
        (4, ((pass_on, 0, 1), (pass_on, 1, 0), (spread, 0, 4), (spread, 0, 5))),
        (5, ((spread, 1, 2), (spread, 1, 3), (pass_on, 0, 2), (pass_on, 0, 3), (pass_on, 1, 1))),
        (6, ((spread, 0, 6),)),
        (7, ((pass_on, 0, 4), (pass_on, 0, 5))),
        (0, ((spread, 1, 4), (spread, 1, 5), (pass_on, 1, 2), (pass_on, 0, 6))),
    ):
        bucket(step)
        for chore, phase, index in chores:
            chore(phase, index)

    mine = jnp.broadcast_to(ids[...], (8, tokens))
    owner = lax.broadcasted_iota(jnp.int32, (8, tokens), 0)
    hot = (mine >= owner * own_rows) & (mine < (owner + 1) * own_rows)
    so_far = matmul(hot.astype(jnp.float32).astype(jnp.bfloat16), before[...]).astype(jnp.int32) - 1
    slot = jnp.sum(
        jnp.where(hot & (so_far < cap), owner * cap + so_far + 1, 0), 0, keepdims=True
    ) - 1
    asker_row[...] = slot
    asker_col[...] = jnp.broadcast_to(slot, (128, tokens)).T

    def held_copy(index):
        target = (core_mate, x_mate, far_mate)[index]
        return remote(
            held_rows.at[row], held_rows.at[row], (held_send, held_recv), index, (target, col)
        )

    for index in range(3):
        held_copy(index).start()

    def id_end(step, carry):
        copy = id_copy(step)
        copy.wait_send()

        @pl.when(lax.rem(lax.rem(me - step + count, count) // fsdp - row + count, count) != 0)
        def _():
            copy.wait_recv()

        return carry

    lax.fori_loop(1, count, id_end, 0)
    ids_all = everyone[...]
    largest = jnp.zeros((1, 1), jnp.int32)
    for part in range(fsdp):
        inside = (ids_all >= part * own_rows) & (ids_all < (part + 1) * own_rows)
        number = jnp.sum(inside.astype(jnp.int32), -1)
        largest = jnp.maximum(largest, jnp.max(number, 0, keepdims=True))
    most[...] = jnp.broadcast_to(largest, (8, 128))
    for step in range(1, fsdp):
        small_copy(step).wait()
    for copy in local:
        copy.wait()
    small_sum[...] = jnp.zeros_like(small_sum)
    for device in range(fsdp):
        at = device * (D // fsdp) // 128 * 128
        small_sum[:, at : at + 256] += smalls[device].astype(jnp.float32)
    gains = small_sum[:, 0:D]
    small_out[...] = gains
    settle(0)
    for step in range(1, fsdp):
        word_copy(step).wait_recv()
    for step in range(fsdp - AHEAD, fsdp):
        word_copy(step).wait_send()

    def embed_tile(i, carry):
        span = pl.ds(pl.multiple_of(i * TILE, TILE), TILE)
        slots = fsdp * cap
        pick = asker_col[span, 0:1] == lax.broadcasted_iota(jnp.int32, (TILE, slots), 1)
        words = matmul(pick.astype(jnp.float32).astype(jnp.bfloat16), got[...])
        spot = pl.ds(pl.multiple_of(lax.rem(i, seq // TILE) * TILE, TILE), TILE)
        x = words + pos[spot, :].astype(jnp.float32)
        hat, _ = normed(x)
        h0 = hat * small_sum[0:1, 0:D] + small_sum[1:2, 0:D]
        x_in[span, :] = x
        h0_in[span, :] = h0
        low = h0.astype(jnp.bfloat16)
        for third, bias in enumerate((2, None, 3)):
            value = matmul(low, first[third * D : (third + 1) * D, :])
            if bias is not None:
                value = value + small_sum[bias : bias + 1, 0:D]
            qkv[span, third * D : (third + 1) * D] = value.astype(jnp.bfloat16)
        return carry

    tiles = tokens // TILE
    lax.fori_loop(0, tiles // 2, embed_tile, 0)
    pass_on(1, 3)
    spread(1, 6)
    lax.fori_loop(tiles // 2, tiles, embed_tile, 0)
    written = [
        pltpu.make_async_copy(x_in, x_out, local_sem.at[0]),
        pltpu.make_async_copy(h0_in, h0_out, local_sem.at[1]),
        pltpu.make_async_copy(qkv, qkv_out, local_sem.at[2]),
    ]
    for copy in written:
        copy.start()
    masks = head_masks(seq)
    chores = {
        1: lambda: pass_on(1, 4),
        4: lambda: pass_on(1, 5),
        8: lambda: pass_on(1, 6),
    }
    done = 0
    for sentence in range(tokens // seq):
        bias = live_row(lengths[sentence], seq)
        rows = slice(sentence * seq, (sentence + 1) * seq)
        logs = jnp.zeros((seq, 128), jnp.float32)
        for pair in range(H // 2):
            logs = attend_pair(qkv, bias, masks, logs, mixed_out, rows, pair)
            done += 1
            if done in chores:
                chores[done]()
        log_out[rows, :] = logs
    settle(1)
    for index in range(3):
        held_copy(index).wait()
    for copy in written:
        copy.wait()
    for copy in started:
        copy.wait_send()


def front(lengths, ids, pieces, pos_low, small, table, cap):
    fsdp = LOOP_SIZE
    count = lax.axis_size("dp") * fsdp
    tokens = ids.shape[1]
    own_rows = table.shape[0]
    hops = 16 * (fsdp - 1)
    vmem = pl.BlockSpec(memory_space=pltpu.VMEM)
    anywhere = pl.BlockSpec(memory_space=pl.ANY)
    low, wide = jnp.bfloat16, jnp.float32
    dma = pltpu.SemaphoreType.DMA
    return pl.pallas_call(
        functools.partial(front_kernel, cap, own_rows),
        name="front",
        in_specs=[pl.BlockSpec(memory_space=pltpu.SMEM), vmem, vmem, anywhere, anywhere, anywhere],
        out_specs=[vmem, vmem, anywhere, vmem, vmem, vmem, vmem, anywhere, anywhere, anywhere, vmem, vmem],
        out_shape=[
            jax.ShapeDtypeStruct((count, 1, tokens), jnp.int32),
            jax.ShapeDtypeStruct((4 * D, D), low),
            jax.ShapeDtypeStruct((2 * FF, D), low),
            jax.ShapeDtypeStruct((16, D), wide),
            jax.ShapeDtypeStruct((4, fsdp, 1, cap), jnp.int32),
            jax.ShapeDtypeStruct((1, tokens), jnp.int32),
            jax.ShapeDtypeStruct((8, 128), jnp.int32),
            jax.ShapeDtypeStruct((tokens, D), wide),
            jax.ShapeDtypeStruct((tokens, D), wide),
            jax.ShapeDtypeStruct((tokens, 3 * D), low),
            jax.ShapeDtypeStruct((tokens, D), low),
            jax.ShapeDtypeStruct((tokens, 128), wide),
        ],
        scratch_shapes=[
            pltpu.VMEM((2, CHUNK, D), wide),
            pltpu.VMEM((own_rows, D), low),
            pltpu.VMEM((fsdp, cap, D), low),
            pltpu.VMEM((fsdp * cap, D), low),
            pltpu.VMEM((tokens, tokens), low),
            pltpu.VMEM((tokens, 128), jnp.int32),
            pltpu.VMEM((fsdp, 16, 256), low),
            pltpu.VMEM((16, D + 128), wide),
            pltpu.VMEM((LEN, D), low),
            pltpu.VMEM((tokens, D), wide),
            pltpu.VMEM((tokens, D), wide),
            pltpu.VMEM((tokens, 3 * D), low),
            dma((count,)),
            dma((count,)),
            dma((hops,)),
            dma((hops,)),
            dma((fsdp,)),
            dma((fsdp,)),
            dma((fsdp,)),
            dma((fsdp,)),
            dma((3,)),
            dma((3,)),
            dma((2,)),
            dma((12,)),
        ],
        compiler_params=pltpu.CompilerParams(
            collective_id=0, has_side_effects=True, vmem_limit_bytes=VMEM_GRANT
        ),
    )(lengths, ids, small, pieces, pos_low, table)


class Ring:
    def __init__(self, parts, sign, send, recv, base):
        self.parts, self.send, self.recv, self.base = parts, send, recv, base
        self.row, col = lax.axis_index("dp"), lax.axis_index("fsdp")
        self.col, self.place = col, grid_place(col)
        self.hops = {sign: LOOP_SIZE // 2, -sign: LOOP_SIZE - LOOP_SIZE // 2 - 1}
        self.events = []
        for k in range(1, LOOP_SIZE // 2 + 1):
            for direction in (sign, -sign):
                if k <= self.hops[direction]:
                    self.events.append((k, direction))
        self.slot = {event: i for i, event in enumerate(self.events)}
        self.sign = sign
        self.started = []

    def copies(self, source, event):
        slot = self.slot[event]
        target = (self.row, grid_device(self.place + event[1]))
        return [
            pltpu.make_async_remote_copy(
                src_ref=box.at[source],
                dst_ref=box.at[slot],
                send_sem=self.send.at[self.base + len(self.parts) * slot + i],
                recv_sem=self.recv.at[self.base + len(self.parts) * slot + i],
                device_id=target,
                device_id_type=MESH,
            )
            for i, (_, _, box) in enumerate(self.parts)
        ]

    def depart(self, source, event):
        for copy in self.copies(source, event):
            copy.start()
            self.started.append(copy)

    def add(self, slot, block, arrived):
        for keep, mate, box in self.parts:
            terms = [keep.at[block], mate.at[block]] + ([box.at[slot]] if arrived else [])
            sum_rows(box.at[slot], terms)

    def first(self):
        for i, direction in enumerate((self.sign, -self.sign)):
            block = grid_device(self.place + direction * self.hops[direction])
            self.add(len(self.events) + i, block, False)
            self.depart(len(self.events) + i, (1, direction))

    def step(self, index):
        hop, direction = self.events[index]
        for copy in self.copies(index, self.events[index]):
            copy.wait_recv()
        left = self.hops[direction] - hop
        if left:
            self.add(index, grid_device(self.place + direction * left), True)
            self.depart(index, (hop + 1, direction))

    def last(self, totals):
        far = self.slot[(self.hops[self.sign], self.sign)]
        near = self.slot[(self.hops[-self.sign], -self.sign)]
        for (keep, mate, box), total in zip(self.parts, totals):
            sum_rows(total, [keep.at[self.col], mate.at[self.col], box.at[far], box.at[near]])

    def drain(self):
        for copy in self.started:
            copy.wait_send()


def sum_rows(out, terms):
    rows = min(out.shape[0], 32)

    def body(i, carry):
        span = pl.ds(pl.multiple_of(i * rows, rows), rows)
        total = terms[0][span, :].astype(jnp.float32)
        for term in terms[1:]:
            total = total + term[span, :].astype(jnp.float32)
        out[span, :] = total.astype(out.dtype)
        return carry

    lax.fori_loop(0, out.shape[0] // rows, body, 0)


def add_squares(squares, value):
    rows = min(value.shape[0], 32)

    def body(i, carry):
        part = value[pl.ds(pl.multiple_of(i * rows, rows), rows), :].astype(jnp.float32)
        squares[0:1, 0 : part.shape[1]] += jnp.sum(part * part, 0, keepdims=True)
        return carry

    lax.fori_loop(0, value.shape[0] // rows, body, 0)


def finish_kernel(
    cap,
    own_rows,
    grad,
    slot,
    held,
    feed_grads,
    qkv_grads,
    pos_grads,
    small_grads,
    depart,
    own,
    table_out,
    sum_a,
    sum_b,
    sum_small,
    norm_out,
    got,
    sent,
    total,
    half_low,
    last_a,
    keep_b,
    mate_b,
    box_b,
    keep_s,
    mate_s,
    box_s,
    out_a,
    in_a,
    out_b,
    in_b,
    out_s,
    in_s,
    squares,
    share,
    shares,
    word_send,
    word_recv,
    ring_send,
    ring_recv,
    pair_send,
    pair_recv,
    norm_send,
    norm_recv,
    local_sem,
):
    fsdp = LOOP_SIZE
    row, col = lax.axis_index("dp"), lax.axis_index("fsdp")
    core = lax.rem(row, 2)
    core_mate = row + 1 - 2 * core
    x_mate = lax.rem(row + 2, 4)
    far_mate = lax.rem(core_mate + 2, 4)
    half = own_rows // 2
    tokens = grad.shape[0]

    barrier = pltpu.get_barrier_semaphore()
    for step in range(1, fsdp):
        there = (row, lax.rem(col + step, fsdp))
        pl.semaphore_signal(barrier, inc=1, device_id=there, device_id_type=MESH)
    for step in range(fsdp):
        there = (core_mate, lax.rem(col + step, fsdp))
        pl.semaphore_signal(barrier, inc=1, device_id=there, device_id_type=MESH)
    pl.semaphore_signal(barrier, inc=1, device_id=(x_mate, col), device_id_type=MESH)
    pl.semaphore_wait(barrier, 2 * fsdp)

    def remote(src, dst, sems, index, target):
        return pltpu.make_async_remote_copy(
            src_ref=src,
            dst_ref=dst,
            send_sem=sems[0].at[index],
            recv_sem=sems[1].at[index],
            device_id=target,
            device_id_type=MESH,
        )

    pair = (pair_send, pair_recv)
    mate = (core_mate, col)
    shard = feed_grads.shape[1]

    def b_parts(which, target):
        pos_half = pos_grads.shape[1] // 2
        if which == 0:
            first, second = qkv_grads.at[pl.ds(0, 8)], qkv_grads.at[pl.ds(8, 8)]
        else:
            first, second = qkv_grads.at[pl.ds(16, 8)], feed_grads.at[pl.ds(64, 8)]
        return [
            (first, target.at[:, pl.ds(0, shard)]),
            (second, target.at[:, pl.ds(shard, shard)]),
            (pos_grads.at[:, pl.ds(which * pos_half, pos_half)], target.at[:, pl.ds(2 * shard, pos_half)]),
        ]

    def s_parts(which, target):
        return [(small_grads.at[:, pl.ds(8 * which, 8)], target)]

    for which in range(2):

        @pl.when(core == which)
        def _(which=which):
            for index, (parts, keep, mates) in enumerate(
                ((b_parts, keep_b, mate_b), (s_parts, keep_s, mate_s))
            ):
                for src, dst in parts(1 - which, mates):
                    remote(src, dst, pair, index, mate).start()
                for src, dst in parts(which, keep):
                    pltpu.make_async_copy(src, dst, local_sem.at[index]).start()

    def halves_in(index):
        keep, mates = ((keep_b, mate_b), (keep_s, mate_s))[index]
        pltpu.make_async_copy(keep, keep, local_sem.at[index]).wait()
        remote(mates, mates, pair, index, mate).wait_recv()

    def word_copy(step):
        return remote(
            sent.at[step],
            got.at[row, step],
            (word_send, word_recv),
            step,
            (row, lax.rem(col - step + fsdp, fsdp)),
        )

    def word_hand(kind, step):
        group, target = ((row, (x_mate, col)), (row, mate), (x_mate, mate))[kind]
        place = got.at[group, step]
        return remote(place, place, (word_send, word_recv), fsdp * (kind + 1) + step, target)

    def bucket(step):
        base = lax.rem(col - step + fsdp, fsdp) * cap
        pick = slot[...] == base + lax.broadcasted_iota(jnp.int32, (cap, tokens), 0)
        rows = matmul(pick.astype(jnp.float32).astype(jnp.bfloat16), grad[...]).astype(jnp.bfloat16)
        if step:
            sent[step] = rows
            word_copy(step).start()
        else:
            got[pl.ds(row, 1), 0] = rows[None]

    handed = []

    def spread(step):
        if step:
            word_copy(step).wait_recv()
        for kind in (0, 1):
            copy = word_hand(kind, step)
            copy.start()
            handed.append(copy)

    def pass_on(step):
        place = got.at[x_mate, step]
        remote(place, place, (word_send, word_recv), fsdp + step, (x_mate, col)).wait_recv()
        copy = word_hand(2, step)
        copy.start()
        handed.append(copy)

    def from_mate(group, kind, step):
        place = got.at[group, step]
        remote(place, place, (word_send, word_recv), fsdp * (kind + 1) + step, mate).wait_recv()

    def accumulate(side, parity, part, fresh):
        chip = row - core if side == 0 else x_mate - core
        group = chip + parity
        width = 4 * cap
        size = half // 4

        def tile(i, carry):
            at = core * half + i * size + lax.broadcasted_iota(jnp.int32, (size, width), 0)
            pick = held[pl.ds(group, 1), 0, part * width : (part + 1) * width] == at
            rows = got[pl.ds(group, 1), 4 * part : 4 * part + 4].reshape(width, D)
            value = matmul(pick.astype(jnp.float32).astype(jnp.bfloat16), rows)
            span = pl.ds(pl.multiple_of(i * size, size), size)
            if fresh:
                total[side, span, :] = value
            else:
                total[side, span, :] += value
            return carry

        lax.fori_loop(0, 4, tile, 0)

    def arrived_here(part):
        for step in range(4 * part, 4 * part + 4):
            from_mate(core_mate, 1, step)

    def arrived_far(part):
        for step in range(4 * part, 4 * part + 4):
            from_mate(far_mate, 2, step)

    def last_hop():
        return remote(
            depart, last_a, (ring_send, ring_recv), 14, (row, grid_device(grid_place(col) + 1))
        )

    ring_b = Ring(
        [(keep_b, mate_b, box_b), (keep_s, mate_s, box_s)],
        -1,
        ring_send,
        ring_recv,
        0,
    )
    squares[...] = jnp.zeros_like(squares)

    def swap_x(ring, totals, incoming, index):
        ring.last(totals)
        for i, (mine, theirs) in enumerate(zip(totals, incoming)):
            remote(mine, theirs, pair, index + i, (x_mate, col)).start()

    def settle(totals, incoming, finals, index, back):
        for i, (mine, theirs, final) in enumerate(zip(totals, incoming, finals)):
            remote(mine, theirs, pair, index + i, (x_mate, col)).wait_recv()
            sum_rows(final.at[core], [mine, theirs])
            add_squares(squares, final.at[core])
            remote(final.at[core], final.at[core], pair, back + i, mate).start()

    last_hop().start()
    halves_in(0)
    halves_in(1)
    ring_b.first()
    for step in range(1, fsdp):
        bucket(step)
    bucket(0)
    ring_b.step(0)
    ring_b.step(1)
    spread(0)
    spread(1)
    last_hop().wait_recv()
    sum_rows(out_a, [own, last_a])
    remote(out_a, in_a, pair, 5, (x_mate, col)).start()
    spread(2)
    pass_on(0)
    spread(3)
    pass_on(1)
    pass_on(2)
    arrived_here(0)
    accumulate(0, 0, 0, True)
    accumulate(0, 1, 0, False)
    spread(4)
    pass_on(3)
    ring_b.step(2)
    ring_b.step(3)
    spread(5)
    arrived_far(0)
    accumulate(1, 0, 0, True)
    accumulate(1, 1, 0, False)
    spread(6)
    pass_on(4)
    ring_b.step(4)
    ring_b.step(5)
    spread(7)
    pass_on(5)
    arrived_here(1)
    accumulate(0, 0, 1, False)
    accumulate(0, 1, 1, False)
    ring_b.step(6)
    swap_x(ring_b, (out_b, out_s), (in_b, in_s), 3)
    pass_on(6)
    pass_on(7)
    settle((out_a,), (in_a,), (sum_a,), 5, 9)
    arrived_far(1)
    accumulate(1, 0, 1, False)
    accumulate(1, 1, 1, False)

    def close(i, carry):
        span = pl.ds(pl.multiple_of(i * 32, 32), 32)
        value = (total[0, span, :] + total[1, span, :]).astype(jnp.bfloat16)
        half_low[span, :] = value
        wide = value.astype(jnp.float32)
        squares[0:1, :] += jnp.sum(wide * wide, 0, keepdims=True)
        return carry

    lax.fori_loop(0, half // 32, close, 0)
    mine = table_out.at[pl.ds(pl.multiple_of(core * half, 32), half), :]
    kept = pltpu.make_async_copy(half_low, mine, local_sem.at[3])
    kept.start()
    given = remote(half_low, mine, pair, 6, mate)
    given.start()
    settle((out_b, out_s), (in_b, in_s), (sum_b, sum_small), 3, 7)

    here = core * fsdp + col
    share[...] = jnp.broadcast_to(jnp.sum(squares[0:1, :], 1, keepdims=True), (8, 128))
    shares[pl.ds(here, 1)] = share[...][None]

    def norm_copy(step):
        other = lax.rem(here + step, 2 * fsdp)
        target = (row - core + other // fsdp, lax.rem(other, fsdp))
        return remote(share, shares.at[here], (norm_send, norm_recv), step, target)

    for step in range(1, 2 * fsdp):
        norm_copy(step).start()
    for step in range(1, 2 * fsdp):
        norm_copy(step).wait()
    norm = shares[0]
    for step in range(1, 2 * fsdp):
        norm = norm + shares[step]
    norm_out[...] = norm

    kept.wait()
    given.wait()
    for i, final in enumerate((sum_b, sum_small, sum_a)):
        other = final.at[1 - core]
        remote(other, other, pair, 7 + i, mate).wait()
    for index, (mine_out, theirs) in enumerate(((out_b, in_b), (out_s, in_s), (out_a, in_a))):
        remote(mine_out, theirs, pair, 3 + index, (x_mate, col)).wait_send()
    for index, mates in enumerate((mate_b, mate_s)):
        remote(mates, mates, pair, index, mate).wait_send()
    for step in range(1, fsdp):
        word_copy(step).wait_send()
    for copy in handed:
        copy.wait_send()
    last_hop().wait_send()
    ring_b.drain()


class flat_blocks:
    def __init__(self, ref):
        self.ref = ref

    @property
    def at(self):
        return self

    def __getitem__(self, block):
        return flat_rows(self.ref, block)


class flat_rows:
    def __init__(self, ref, block):
        self.ref, self.block = ref, block

    def __getitem__(self, key):
        span = key[0]
        rows = self.ref.shape[2]
        return self.ref[self.block, span.start // rows, pl.ds(lax.rem(span.start, rows), span.size), :]


def finish(grad, slot, held, feed_grads, qkv_grads, pos_grads, small_grads, depart, own, own_rows, cap):
    fsdp = LOOP_SIZE
    tokens = grad.shape[0]
    shard = D // fsdp
    pos_rows = pos_grads.shape[0] // fsdp
    rows_a, rows_b = 4 * shard, 2 * shard + pos_rows // 2
    half = own_rows // 2
    vmem = pl.BlockSpec(memory_space=pltpu.VMEM)
    anywhere = pl.BlockSpec(memory_space=pl.ANY)
    low, wide = jnp.bfloat16, jnp.float32
    return pl.pallas_call(
        functools.partial(finish_kernel, cap, own_rows),
        name="finish",
        in_specs=[vmem, vmem, vmem, anywhere, anywhere, anywhere, anywhere, vmem, vmem],
        out_specs=[anywhere, vmem, vmem, vmem, vmem],
        out_shape=[
            jax.ShapeDtypeStruct((own_rows, D), low),
            jax.ShapeDtypeStruct((2, rows_a, D), low),
            jax.ShapeDtypeStruct((2, rows_b, D), low),
            jax.ShapeDtypeStruct((2, 8, 128), wide),
            jax.ShapeDtypeStruct((8, 128), wide),
        ],
        scratch_shapes=[
            pltpu.VMEM((4, fsdp, cap, D), low),
            pltpu.VMEM((fsdp, cap, D), low),
            pltpu.VMEM((2, half, D), wide),
            pltpu.VMEM((half, D), low),
            pltpu.VMEM((rows_a, D), low),
            pltpu.VMEM((fsdp, rows_b, D), low),
            pltpu.VMEM((fsdp, rows_b, D), low),
            pltpu.VMEM((fsdp + 1, rows_b, D), low),
            pltpu.VMEM((fsdp, 8, 128), wide),
            pltpu.VMEM((fsdp, 8, 128), wide),
            pltpu.VMEM((fsdp + 1, 8, 128), wide),
            pltpu.VMEM((rows_a, D), low),
            pltpu.VMEM((rows_a, D), low),
            pltpu.VMEM((rows_b, D), low),
            pltpu.VMEM((rows_b, D), low),
            pltpu.VMEM((8, 128), wide),
            pltpu.VMEM((8, 128), wide),
            pltpu.VMEM((8, D), wide),
            pltpu.VMEM((8, 128), wide),
            pltpu.VMEM((2 * fsdp, 8, 128), wide),
            pltpu.SemaphoreType.DMA((4 * fsdp,)),
            pltpu.SemaphoreType.DMA((4 * fsdp,)),
            pltpu.SemaphoreType.DMA((15,)),
            pltpu.SemaphoreType.DMA((15,)),
            pltpu.SemaphoreType.DMA((10,)),
            pltpu.SemaphoreType.DMA((10,)),
            pltpu.SemaphoreType.DMA((2 * fsdp,)),
            pltpu.SemaphoreType.DMA((2 * fsdp,)),
            pltpu.SemaphoreType.DMA((4,)),
        ],
        compiler_params=pltpu.CompilerParams(
            collective_id=3, has_side_effects=True, vmem_limit_bytes=VMEM_GRANT
        ),
    )(
        grad,
        slot,
        held,
        feed_grads.reshape(-1, shard, D),
        qkv_grads.reshape(-1, shard, D),
        pos_grads.reshape(fsdp, pos_rows, D),
        small_grads,
        depart,
        own,
    )


def attend_back_pair(qkv, grad_mixed, logs, bias, masks, out, sums, rows, pair):
    at = pair * 128
    query = qkv[rows, at : at + 128] * jnp.bfloat16(0.125)
    keys = qkv[rows, D + at : D + at + 128]
    values = qkv[rows, 2 * D + at : 2 * D + at + 128]
    above = grad_mixed[rows, at : at + 128]
    queries = []
    key_sum = value_sum = None
    for side, mask in enumerate(masks):
        head = 2 * pair + side
        side_query = jnp.where(mask, query, jnp.zeros_like(query))
        side_above = jnp.where(mask, above, jnp.zeros_like(above))
        probs = jnp.exp(back_mul(side_query, keys) + (bias - logs[rows, head : head + 1]))
        grad_probs = back_mul(side_above, values)
        inner = jnp.sum(probs * grad_probs, -1, keepdims=True)
        grad_logits = (probs * (grad_probs - inner)).astype(jnp.bfloat16)
        side_value = outer_sum(probs.astype(jnp.bfloat16), side_above)
        side_key = outer_sum(grad_logits, side_query)
        queries.append(matmul(grad_logits, keys))
        value_sum = side_value if side == 0 else value_sum + side_value
        key_sum = side_key if side == 0 else key_sum + side_key
    grad_query = jnp.where(masks[0], queries[0], queries[1]) * 0.125
    out[rows, at : at + 128] = grad_query.astype(jnp.bfloat16)
    out[rows, D + at : D + at + 128] = key_sum.astype(jnp.bfloat16)
    out[rows, 2 * D + at : 2 * D + at + 128] = value_sum.astype(jnp.bfloat16)
    sums[2:3, at : at + 128] += jnp.sum(grad_query, 0, keepdims=True)
    sums[3:4, at : at + 128] += jnp.sum(value_sum, 0, keepdims=True)


def back_kernel(
    lengths,
    qkv,
    grad_mixed,
    logs,
    small,
    grad_r1,
    x,
    weight,
    feed_grads,
    x_out,
    pos_out,
    qkv_out,
    sums,
    depart,
    own,
    grad_qkv,
    r1_in,
    x_in,
    weight_in,
    low_h0,
    pos_sum,
    keep,
    mates,
    box,
    ring_send,
    ring_recv,
    pair_send,
    pair_recv,
    local_sem,
):
    fsdp = LOOP_SIZE
    row, col = lax.axis_index("dp"), lax.axis_index("fsdp")
    core = lax.rem(row, 2)
    mate = (row + 1 - 2 * core, col)
    place = grid_place(col)
    seq = LEN
    sentences = qkv.shape[0] // seq

    barrier = pltpu.get_barrier_semaphore()
    for there in (mate, (row, grid_device(place + 1)), (row, grid_device(place - 1))):
        pl.semaphore_signal(barrier, inc=1, device_id=there, device_id_type=MESH)
    pl.semaphore_wait(barrier, 3)

    def pair_copy(src, dst, index):
        return pltpu.make_async_remote_copy(
            src_ref=src,
            dst_ref=dst,
            send_sem=pair_send.at[index],
            recv_sem=pair_recv.at[index],
            device_id=mate,
            device_id_type=MESH,
        )

    offsets = (4, -3, 3, -2, 2, -1, 1, 0)

    def halves(which, block, target):
        if which == 0:
            return [(feed_grads.at[pl.ds(4 * block, 4)], target.at[block])]
        return [(feed_grads.at[32 + 8 * j + block], target.at[block, j]) for j in range(4)]

    for which in range(2):

        @pl.when(core == which)
        def _(which=which):
            for index, offset in enumerate(offsets):
                block = grid_device(place + offset)
                for src, dst in halves(1 - which, block, mates):
                    pair_copy(src, dst, index).start()
                for src, dst in halves(which, block, keep):
                    pltpu.make_async_copy(src, dst, local_sem.at[0]).start()

    def mate_block(index):
        block = grid_device(place + offsets[index])
        return pair_copy(mates.at[block], mates.at[block], index)

    fills = [
        pltpu.make_async_copy(grad_r1, r1_in, local_sem.at[1]),
        pltpu.make_async_copy(x, x_in, local_sem.at[2]),
        pltpu.make_async_copy(weight.at[pl.ds(0, 3 * D), :], weight_in, local_sem.at[3]),
    ]
    for fill in fills:
        fill.start()

    ring = Ring([(flat_blocks(keep), flat_blocks(mates), box)], 1, ring_send, ring_recv, 0)
    sums[...] = jnp.zeros_like(sums)
    masks = head_masks(seq)
    done = 0
    for sentence in range(sentences):
        bias = live_row(lengths[sentence], seq)
        rows = slice(sentence * seq, (sentence + 1) * seq)
        for pair in range(H // 2):
            attend_back_pair(qkv, grad_mixed, logs, bias, masks, grad_qkv, sums, rows, pair)
            done += 1
            if done == 1:
                pltpu.make_async_copy(keep, keep, local_sem.at[0]).wait()
                mate_block(0).wait_recv()
                mate_block(1).wait_recv()
                ring.first()
            if done == 8:
                mate_block(2).wait_recv()
                mate_block(3).wait_recv()
                ring.step(0)
                ring.step(1)
    for fill in fills:
        fill.wait()
    pos_sum[...] = jnp.zeros_like(pos_sum)

    def tile(i, carry):
        span = pl.ds(pl.multiple_of(i * TILE, TILE), TILE)
        grad_h0 = r1_in[span, :]
        for third in range(3):
            cols = slice(third * D, (third + 1) * D)
            grad_h0 = grad_h0 + back_mul(grad_qkv[span, cols], weight_in[cols, :])
        hat, scale = normed(x_in[span, :])
        low_h0[span, :] = (hat * small[0:1, :] + small[1:2, :]).astype(jnp.bfloat16)
        grad_x, gain, shift = norm_back(grad_h0, hat, scale, small[0:1, :])
        add_row(sums, 0, gain)
        add_row(sums, 1, shift)
        x_out[span, :] = grad_x.astype(jnp.bfloat16)
        spot = pl.ds(pl.multiple_of(lax.rem(i, seq // TILE) * TILE, TILE), TILE)
        pos_sum[spot, :] += grad_x
        return carry

    tiles = sentences * seq // TILE
    lax.fori_loop(0, tiles // 2, tile, 0)
    mate_block(4).wait_recv()
    mate_block(5).wait_recv()
    ring.step(2)
    ring.step(3)
    lax.fori_loop(tiles // 2, tiles, tile, 0)
    pos_out[...] = pos_sum[...].astype(jnp.bfloat16)
    for third in range(3):
        cols = slice(third * D, (third + 1) * D)
        qkv_out[cols, :] = outer_sum(low_h0[...], grad_qkv[:, cols]).astype(jnp.bfloat16)
    right, left = ring.slot[(3, 1)], ring.slot[(3, -1)]
    for slot in (right, left):
        for copy in ring.copies(slot, ring.events[slot]):
            copy.wait_recv()
    mate_block(6).wait_recv()
    mate_block(7).wait_recv()
    ahead = grid_device(place + 1)
    sum_rows(depart, [ring.parts[0][0].at[ahead], ring.parts[0][1].at[ahead], box.at[right]])
    sum_rows(own, [ring.parts[0][0].at[col], ring.parts[0][1].at[col], box.at[left]])
    for index in range(8):
        mate_block(index).wait_send()
    ring.drain()


def back(lengths, qkv, grad_mixed, logs, small, grad_r1, x, weight, feed_grads):
    fsdp = LOOP_SIZE
    tokens = qkv.shape[0]
    shard = D // fsdp
    vmem = pl.BlockSpec(memory_space=pltpu.VMEM)
    anywhere = pl.BlockSpec(memory_space=pl.ANY)
    low, wide = jnp.bfloat16, jnp.float32
    return pl.pallas_call(
        back_kernel,
        name="back",
        in_specs=[pl.BlockSpec(memory_space=pltpu.SMEM)] + [vmem] * 4 + [anywhere] * 4,
        out_specs=[vmem] * 6,
        out_shape=[
            jax.ShapeDtypeStruct((tokens, D), low),
            jax.ShapeDtypeStruct((LEN, D), low),
            jax.ShapeDtypeStruct((3 * D, D), low),
            jax.ShapeDtypeStruct((16, D), wide),
            jax.ShapeDtypeStruct((4 * shard, D), low),
            jax.ShapeDtypeStruct((4 * shard, D), wide),
        ],
        scratch_shapes=[
            pltpu.VMEM((tokens, 3 * D), low),
            pltpu.VMEM((tokens, D), wide),
            pltpu.VMEM((tokens, D), wide),
            pltpu.VMEM((3 * D, D), low),
            pltpu.VMEM((tokens, D), low),
            pltpu.VMEM((LEN, D), wide),
            pltpu.VMEM((fsdp, 4, shard, D), low),
            pltpu.VMEM((fsdp, 4, shard, D), low),
            pltpu.VMEM((fsdp + 1, 4 * shard, D), low),
            pltpu.SemaphoreType.DMA((7,)),
            pltpu.SemaphoreType.DMA((7,)),
            pltpu.SemaphoreType.DMA((8,)),
            pltpu.SemaphoreType.DMA((8,)),
            pltpu.SemaphoreType.DMA((4,)),
        ],
        compiler_params=pltpu.CompilerParams(
            collective_id=4, has_side_effects=True, vmem_limit_bytes=VMEM_GRANT
        ),
    )(lengths, qkv, grad_mixed, logs, small, grad_r1, x, weight, feed_grads.reshape(-1, shard, D))


def exact_dot(left, right):
    return lax.dot_general(
        left,
        right,
        (((1,), (0,)), ((), ())),
        precision=lax.Precision.HIGHEST,
        preferred_element_type=jnp.float32,
    )


def cosine_parts(first, second):
    dots = jnp.sum(first * second, -1, keepdims=True)
    one = lax.rsqrt(jnp.sum(first * first, -1, keepdims=True) + 1e-06)
    two = lax.rsqrt(jnp.sum(second * second, -1, keepdims=True) + 1e-06)
    return dots * one * two, one, two


def cosine_back(grad, value, first, second, one, two):
    return (
        grad * one * (second * two - value * first * one),
        grad * two * (first * one - value * second * two),
    )


def loss_kernel(sizes, lengths, src, pair_ids, scores, loss_out, share_out, out, send, recv, local):
    gather_kernel(sizes, True, src, out, send, recv, local)
    count, batch = out.shape[0], out.shape[1]
    pooled = jnp.concatenate([out[:, i] for i in range(batch)], 0)
    rows = lax.broadcasted_iota(jnp.int32, (pair_ids.shape[1], count * batch), 1)
    sentence = lax.rem(rows, count) * batch + rows // count
    anchor, near, far = (
        exact_dot((pair_ids[i] == sentence).astype(jnp.float32), pooled) for i in range(3)
    )
    near_cos, near_one, near_two = cosine_parts(anchor, near)
    far_cos, far_one, far_two = cosine_parts(anchor, far)
    near_miss, far_miss = near_cos - scores[0], far_cos - scores[1]
    loss = jnp.sum(near_miss * near_miss + far_miss * far_miss, 0, keepdims=True)
    loss_out[...] = jnp.broadcast_to(loss, loss_out.shape)
    anchor_a, grad_near = cosine_back(
        2.0 * near_miss, near_cos, anchor, near, near_one, near_two
    )
    anchor_b, grad_far = cosine_back(2.0 * far_miss, far_cos, anchor, far, far_one, far_two)
    grads = (anchor_a + anchor_b, grad_near, grad_far)
    me = lax.axis_index("dp") * sizes[1] + lax.axis_index("fsdp")
    for i in range(batch):
        total = jnp.zeros((1, grads[0].shape[1]), jnp.float32)
        for part, grad in enumerate(grads):
            mine = pair_ids[part] == me * batch + i
            total = total + jnp.sum(jnp.where(mine, grad, 0.0), 0, keepdims=True)
        share_out[i] = jnp.broadcast_to(
            total / lengths[i].astype(jnp.float32), share_out.shape[1:]
        )


def pair_grads(lengths, pooled, pair_ids, scores):
    dp, fsdp = lax.axis_size("dp"), lax.axis_size("fsdp")
    count, (batch, width) = dp * fsdp, pooled.shape
    vmem = pl.BlockSpec(memory_space=pltpu.VMEM)
    return pl.pallas_call(
        functools.partial(loss_kernel, (dp, fsdp)),
        name="pair_loss",
        in_specs=[pl.BlockSpec(memory_space=pltpu.SMEM), vmem, vmem, vmem],
        out_specs=[vmem, vmem],
        out_shape=[
            jax.ShapeDtypeStruct((8, 128), jnp.float32),
            jax.ShapeDtypeStruct((batch, 8, width), jnp.float32),
        ],
        scratch_shapes=[
            pltpu.VMEM((count,) + pooled.shape, jnp.float32),
            pltpu.SemaphoreType.DMA((count,)),
            pltpu.SemaphoreType.DMA((count,)),
            pltpu.SemaphoreType.DMA,
        ],
        compiler_params=pltpu.CompilerParams(
            collective_id=1, has_side_effects=True, vmem_limit_bytes=VMEM_GRANT
        ),
    )(lengths, pooled, pair_ids[:, :, None], scores[:, :, None])


def pack_kernel(qkv, out_w, up, down, pos, pieces, low_pos):
    rows = qkv.shape[0]
    low = jnp.bfloat16
    for part in range(3):
        pieces[part * rows : (part + 1) * rows, :] = qkv[:, part * D : (part + 1) * D].astype(low)
    pieces[3 * rows : 4 * rows, :] = out_w[...].astype(low)
    for part in range(4):
        at = (4 + part) * rows
        pieces[at : at + rows, :] = up[:, part * D : (part + 1) * D].astype(low)
    pieces[8 * rows :, :] = down[...].astype(low)
    low_pos[...] = pos[...].astype(low)


def pack(qkv, out_w, up, down, pos):
    rows = qkv.shape[0]
    if rows % 16:
        pieces = jnp.concatenate(
            [split_rows(qkv, 3), out_w, split_rows(up, FF // D), down], 0
        ).astype(jnp.bfloat16)
        return pieces, pos.astype(jnp.bfloat16)
    vmem = pl.BlockSpec(memory_space=pltpu.VMEM)
    return pl.pallas_call(
        pack_kernel,
        name="pack",
        in_specs=[vmem] * 5,
        out_specs=[vmem] * 2,
        out_shape=[
            jax.ShapeDtypeStruct((12 * rows, D), jnp.bfloat16),
            jax.ShapeDtypeStruct(pos.shape, jnp.bfloat16),
        ],
        compiler_params=pltpu.CompilerParams(vmem_limit_bytes=VMEM_GRANT),
    )(qkv, out_w, up, down, pos)


LOOP = {8: (0, 2, 4, 6, 7, 5, 3, 1)}


def swap_core(value):
    return lax.ppermute(value, "dp", [(i, i ^ 1) for i in range(lax.axis_size("dp"))])


def swap_x(value):
    count = lax.axis_size("dp")
    return lax.ppermute(value, "dp", [(i, (i + 2) % count) for i in range(count)])


def sum_x(value):
    count = lax.axis_size("dp")
    total = value
    for hop in range(2, count, 2):
        moved = lax.ppermute(value, "dp", [(i, (i + hop) % count) for i in range(count)])
        total = total.astype(jnp.float32) + moved.astype(jnp.float32)
    return total


def shift(value, step):
    loop = LOOP[lax.axis_size("fsdp")]
    size = len(loop)
    return lax.ppermute(
        value, "fsdp", [(loop[i], loop[(i + step) % size]) for i in range(size)]
    )


def loop_place():
    loop = LOOP[lax.axis_size("fsdp")]
    place = [0] * len(loop)
    for i, device in enumerate(loop):
        place[device] = i
    return jnp.array(place, jnp.int32)[lax.axis_index("fsdp")], jnp.array(loop, jnp.int32)


def ring_gather(part, sign):
    size = lax.axis_size("fsdp")
    place, loop = loop_place()
    out = jnp.zeros((size,) + part.shape, part.dtype)

    def put(out, block, offset):
        at = loop[lax.rem(place + offset + size, size)]
        return lax.dynamic_update_slice(out, block[None], (at, 0, 0))

    out = put(out, part, 0)
    ahead = behind = part
    for hop in range(1, size // 2 + 1):
        ahead = shift(ahead, sign)
        out = put(out, ahead, -sign * hop)
        if hop < size - size // 2:
            behind = shift(behind, -sign)
            out = put(out, behind, sign * hop)
    return out


def ring_reduce(parts, sign):
    size = lax.axis_size("fsdp")
    place, loop = loop_place()

    def local(offset):
        at = loop[lax.rem(place + offset + size, size)]
        return lax.dynamic_index_in_dim(parts, at, 0, keepdims=False).astype(jnp.float32)

    def flow(direction, hops):
        arrived = None
        for hop in range(hops):
            value = local(direction * (hops - hop))
            if arrived is not None:
                value = value + arrived.astype(jnp.float32)
            arrived = shift(value.astype(jnp.bfloat16), direction)
        return arrived

    far = flow(sign, size // 2)
    near = flow(-sign, size - size // 2 - 1)
    return local(0) + far.astype(jnp.float32) + near.astype(jnp.float32)


def gather_halves(first, second, sign):
    core = lax.rem(lax.axis_index("dp"), 2)
    if lax.axis_size("fsdp") not in LOOP:
        return lax.all_gather(first, "fsdp", axis=0), lax.all_gather(second, "fsdp", axis=0)
    mine = ring_gather(jnp.where(core == 0, first, second), sign)
    other = swap_core(mine)
    return jnp.where(core == 0, mine, other), jnp.where(core == 0, other, mine)


def reduce_halves(first, second, sign):
    core = lax.rem(lax.axis_index("dp"), 2)
    give = jnp.where(core == 0, second, first).astype(jnp.bfloat16)
    keep = jnp.where(core == 0, first, second).astype(jnp.float32)
    chip = (keep + swap_core(give).astype(jnp.float32)).astype(jnp.bfloat16)
    if lax.axis_size("fsdp") in LOOP:
        block = ring_reduce(chip, sign)
    else:
        block = lax.psum_scatter(chip.astype(jnp.float32), "fsdp", scatter_dimension=0)
    total = sum_x(block.astype(jnp.bfloat16)).astype(jnp.bfloat16)
    other = swap_core(total)
    low = jnp.where(core == 0, total, other).astype(jnp.float32)
    high = jnp.where(core == 0, other, total).astype(jnp.float32)
    return low, high


def split_rows(weight, parts):
    return jnp.concatenate(jnp.split(weight, parts, axis=1), axis=0)


def join_rows(blocks, parts):
    count, rows, width = blocks.shape
    return (
        blocks.reshape(count, parts, rows // parts, width)
        .transpose(0, 2, 1, 3)
        .reshape(count * rows // parts, parts * width)
    )


def cut_parts(grad, count, parts):
    width = grad.shape[-1]
    return (
        grad.reshape(parts, count, -1, width).transpose(1, 0, 2, 3).reshape(count, -1, width)
    )


def pad_rows(value, rows):
    return jnp.pad(value, [(0, 0)] * (value.ndim - 2) + [(0, rows - value.shape[-2]), (0, 0)])


def round_up(value, step):
    return -(-value // step) * step


def bucket_size(tokens, owners):
    mean = tokens / owners
    return min(tokens, round_up(int(mean + 5.6 * math.sqrt(mean)), 16))


def one_hot(index, count):
    return (index[:, None] == lax.iota(jnp.int32, count)[None, :]).astype(jnp.bfloat16)


class Routes:
    def __init__(self, everyone, own_rows):
        fsdp = lax.axis_size("fsdp")
        self.rows = own_rows
        tokens = everyone.shape[1]
        self.cap = bucket_size(tokens, fsdp)
        me = lax.axis_index("fsdp")
        group = lax.dynamic_slice_in_dim(everyone, lax.axis_index("dp") * fsdp, fsdp, 0)
        mine = lax.dynamic_index_in_dim(group, me, 0, keepdims=False)
        owners = lax.iota(jnp.int32, fsdp)
        every_count = jnp.sum(
            (everyone // own_rows)[:, :, None] == owners[None, None, :], 1, dtype=jnp.int32
        )
        self.rounds = (jnp.max(every_count) + self.cap - 1) // self.cap
        self.inner = group - me * own_rows
        self.held = (self.inner >= 0) & (self.inner < own_rows)
        self.held_place = jnp.cumsum(self.held.astype(jnp.int32), 1) - 1
        self.owner = mine // own_rows
        hot = (self.owner[None, :] == owners[:, None])
        place = jnp.cumsum(hot.astype(jnp.int32), 1) - 1
        self.hot = hot
        self.place = place
        self.my_place = jnp.sum(jnp.where(hot, place, 0), 0)

    def slots(self, flag, place, value, turn):
        slot = lax.iota(jnp.int32, self.cap)[None, :, None] + turn * self.cap
        hit = flag[:, None, :] & (place[:, None, :] == slot)
        return (jnp.sum(jnp.where(hit, value[:, None, :] + 1, 0), -1) - 1).reshape(-1)

    def owner_rows(self, turn):
        return self.slots(self.held, self.held_place, self.inner, turn)

    def asker_tokens(self, turn):
        tokens = lax.iota(jnp.int32, self.owner.shape[0])[None, :]
        return self.slots(self.hot, self.place, tokens, turn)

    def asker_slots(self, turn):
        place = self.my_place - turn * self.cap
        inside = (place >= 0) & (place < self.cap)
        return jnp.where(inside, self.owner * self.cap + place, -1)


def exchange(rows):
    fsdp = lax.axis_size("fsdp")
    blocks = rows.reshape(fsdp, rows.shape[0] // fsdp, rows.shape[1])
    return lax.all_to_all(blocks, "fsdp", 0, 0).reshape(rows.shape)


def pick_kernel(index, table, out):
    rows = lax.broadcasted_iota(jnp.int32, (index.shape[0], table.shape[0]), 1)
    pick = (index[:, 0:1] == rows).astype(jnp.bfloat16)
    out[...] = matmul(pick, table[...].astype(jnp.bfloat16)).astype(jnp.bfloat16)


def gather_table(table, routes, turn):
    index = routes.owner_rows(turn)
    size = routes.cap
    return call(
        pick_kernel,
        "pick_rows",
        (index.shape[0] // size,),
        [rows_spec(128, size), whole_spec(table.shape)],
        [rows_spec(D, size)],
        [jax.ShapeDtypeStruct((index.shape[0], D), jnp.bfloat16)],
        flops=2 * index.shape[0] * D * table.shape[0],
        moved=table.shape[0] * D * 4,
    )(jnp.broadcast_to(index[:, None], (index.shape[0], 128)), table)[0]


def all_words(everyone, table, rounds, tokens):
    def more(carry):
        return carry[0] < rounds

    def body(carry):
        turn, words = carry
        ids, turn, rows = lax.optimization_barrier((everyone, turn, table))
        routes = Routes(ids, table.shape[0])
        got = exchange(gather_table(rows, routes, turn))
        mine = matmul(one_hot(routes.asker_slots(turn), got.shape[0]), got)
        return turn + 1, words + mine.astype(jnp.bfloat16)

    start = (jnp.int32(0), jnp.zeros((tokens, D), jnp.bfloat16))
    return lax.while_loop(more, body, start)[1]


def return_round(grad_low, everyone, turn, rows):
    routes = Routes(everyone, rows)
    held = routes.owner_rows(turn)[None, :]
    sent = bucket_rows(routes.asker_slots(turn)[None, :], grad_low, held.shape[1])
    return scatter_rows(held, exchange(sent), rows)


def return_rows(grad_low, everyone, rounds, rows):
    def more(carry):
        return carry[0] < rounds

    def body(carry):
        turn, total = carry
        ids, turn = lax.optimization_barrier((everyone, turn))
        return turn + 1, total + return_round(grad_low, ids, turn, rows)

    return lax.while_loop(more, body, (jnp.int32(0), jnp.zeros((rows, D), jnp.float32)))[1]


def more_grads(grad_low, plan, table, squares):
    def more(carry):
        return carry[0] < plan.rounds

    def body(carry):
        turn, table, squares = carry
        ids, turn = lax.optimization_barrier((plan.everyone, turn))
        before = table.astype(jnp.float32)
        after = (before + sum_groups(return_round(grad_low, ids, turn, table.shape[0]))).astype(
            jnp.bfloat16
        )
        change = jnp.sum(after.astype(jnp.float32) ** 2) - jnp.sum(before * before)
        return turn + 1, after, squares + lax.psum(change, "fsdp")

    return lax.while_loop(more, body, (jnp.int32(1), table, squares))[1:]


def total_grads(everyone, rounds, grad_x, feed_grads, qkv_grads, grad_pos, grad_small, own_rows):
    fsdp = lax.axis_size("fsdp")
    down, up = reduce_halves(
        feed_grads[:FF].reshape(fsdp, -1, D), cut_parts(feed_grads[FF : 2 * FF], fsdp, 4), 1
    )
    qkv_cut = cut_parts(qkv_grads, fsdp, 3)
    shard = qkv_cut.shape[1] // 3
    pos_cut = grad_pos.reshape(fsdp, -1, D)
    half_pos = pos_cut.shape[1] // 2
    low, high = reduce_halves(
        jnp.concatenate([qkv_cut[:, : 2 * shard], pos_cut[:, :half_pos]], 1),
        jnp.concatenate(
            [
                qkv_cut[:, 2 * shard :],
                feed_grads[2 * FF :].reshape(fsdp, shard, D),
                pos_cut[:, half_pos:],
            ],
            1,
        ),
        -1,
    )
    cols = D // fsdp
    small = lax.dynamic_slice_in_dim(
        lax.psum(grad_small, ("dp", "fsdp")), lax.axis_index("fsdp") * cols, cols, 1
    )
    small = jnp.pad(small, ((0, 0), (0, 128 - cols)))
    table = sum_groups(return_rows(grad_x, everyone, rounds, own_rows))
    squares = sum(jnp.sum(part * part) for part in (table, down, up, low, high, small))
    squares = jnp.sum(gather_small(jnp.full((8, 128), squares), False, 2)[:, 0, 0])
    return (
        table.astype(jnp.bfloat16),
        jnp.stack([down, up]).astype(jnp.bfloat16),
        jnp.stack([low, high]).astype(jnp.bfloat16),
        small,
        squares,
    )


class Plan:
    def __init__(self, lengths, ids, pieces, pos_low, small, table):
        fsdp = lax.axis_size("fsdp")
        seq = ids.shape[1]
        tokens = ids.size
        cap = self.cap = bucket_size(tokens, fsdp)
        cols = small.shape[1]
        self.direct = fsdp == LOOP_SIZE and lax.axis_size("dp") == 4 and tokens == 1024
        if self.direct:
            block = lax.dynamic_update_slice(
                jnp.zeros((16, 256), jnp.bfloat16),
                small,
                (0, lax.rem(lax.axis_index("fsdp") * cols, 128)),
            )
            everyone, self.first, self.second, self.small, held, self.asker_row, most, *state = front(
                lengths, ids.reshape(1, tokens), pieces, pos_low, block, table, cap
            )
            self.everyone = everyone.reshape(-1, tokens)
            self.rounds = (most[0, 0] + cap - 1) // cap
            self.held = held.reshape(4, 1, -1)
            self.state = self.redo(lengths, table, seq, state, pos_low)
        else:
            self.everyone = gather_small(ids.reshape(-1, 128), True, 0).reshape(-1, tokens)
            self.rounds = Routes(self.everyone, table.shape[0]).rounds
            both = lax.all_gather(pieces, "fsdp", axis=0)
            shard = pieces.shape[0] // 12
            columns = both[:, : 8 * shard].reshape(fsdp, 8, shard, D).transpose(1, 0, 2, 3)
            self.first = columns[:4].reshape(-1, D)
            self.second = jnp.concatenate(
                [columns[4:].reshape(-1, D), both[:, 8 * shard :].reshape(-1, D)], 0
            )
            smalls = lax.all_gather(jnp.pad(small, ((0, 2), (0, 128 - cols))), "fsdp", axis=0)
            self.small = (
                smalls[:, :, :cols].transpose(1, 0, 2).reshape(16, D).astype(jnp.float32)
            )
            self.state = self.again(lengths, table, seq, pos_low, self.everyone)

    def again(self, lengths, table, seq, pos_low, everyone):
        tokens = everyone.shape[1]
        words = all_words(everyone, table, self.rounds, tokens)
        pos = lax.all_gather(pos_low, "fsdp", axis=0, tiled=True)
        nowhere = jnp.full((tokens, 128), -1, jnp.int32)
        x, h0, qkv = embed(nowhere, jnp.zeros((128, D), jnp.bfloat16), words, pos, self.first, self.small)
        return [x, h0, qkv, *attend(lengths, qkv, seq)]

    def redo(self, lengths, table, seq, state, pos_low):
        def more(carry):
            return carry[0] < self.rounds

        def once(carry):
            everyone, low, _ = lax.optimization_barrier((self.everyone, pos_low, carry[0]))
            return [self.rounds] + self.again(lengths, table, seq, low, everyone)

        return lax.while_loop(more, once, [jnp.int32(1)] + state)[1:]


def sum_groups(table):
    core = lax.rem(lax.axis_index("dp"), 2)
    half = table.shape[0] // 2
    low = table.astype(jnp.bfloat16)
    keep = lax.dynamic_slice_in_dim(table, core * half, half, 0)
    give = lax.dynamic_slice_in_dim(low, (1 - core) * half, half, 0)
    chip = (keep + swap_core(give).astype(jnp.float32)).astype(jnp.bfloat16)
    total = sum_x(chip).astype(jnp.bfloat16)
    other = swap_core(total)
    return jnp.concatenate(
        [jnp.where(core == 0, total, other), jnp.where(core == 0, other, total)], 0
    ).astype(jnp.float32)


def renew(weight, moment, average, grad, factor):
    step = factor * grad
    buffer = MOMENTUM * moment + step
    fresh = weight - RATE * (step + MOMENTUM * buffer)
    return (fresh, buffer, KEEP * average + (1.0 - KEEP) * fresh)


def renew_kernel(factor, *refs):
    kinds = len(refs) // 7
    scale = factor[0, 0]
    for kind in range(kinds):
        weight, moment, average, grad = refs[4 * kind : 4 * kind + 4]
        outs = refs[4 * kinds + 3 * kind : 4 * kinds + 3 * kind + 3]
        shape = weight.shape
        value = grad[...] if len(grad.shape) == 2 else grad[0]
        value = value[: shape[0], : shape[1]].astype(jnp.float32)
        results = renew(weight[...], moment[...], average[...], value, scale)
        for out, result in zip(outs, results):
            out[...] = result


def renew_all(factor, groups, table, sum_a, sum_b, small):
    steps = 12
    own_rows = table.shape[0]
    rows = groups[2][0].shape[0]
    half_pos = groups[1][0].shape[0] // 2
    down_rows = groups[5][0].shape[0]
    cols = 256

    def piece(i):
        return jnp.minimum(i // 3, 2)

    def third(i):
        return lax.rem(jnp.minimum(i, 8), 3)

    def late(i):
        return jnp.clip(i - 9, 0, 2)

    specs = [
        (pl.BlockSpec((own_rows // steps, D), lambda i: (i, 0)), None, table),
        (
            pl.BlockSpec((half_pos, D), lambda i: (jnp.minimum(i, 1), 0)),
            pl.BlockSpec((1, half_pos, D), lambda i: (jnp.minimum(i, 1), 2 * rows // half_pos, 0)),
            sum_b,
        ),
        (
            pl.BlockSpec((rows, cols), lambda i: (0, jnp.minimum(i, 8))),
            pl.BlockSpec(
                (1, rows, cols), lambda i: (piece(i) // 2, lax.rem(piece(i), 2), third(i))
            ),
            sum_b,
        ),
        (
            pl.BlockSpec((rows, cols), lambda i: (0, late(i))),
            pl.BlockSpec((1, rows, cols), lambda i: (1, 1, late(i))),
            sum_b,
        ),
        (
            pl.BlockSpec((rows, cols), lambda i: (0, i)),
            pl.BlockSpec((1, rows, cols), lambda i: (1, i // 3, lax.rem(i, 3))),
            sum_a,
        ),
        (
            pl.BlockSpec((down_rows // steps, D), lambda i: (i, 0)),
            pl.BlockSpec((1, down_rows // steps, D), lambda i: (0, i, 0)),
            sum_a,
        ),
        (whole_spec(groups[6][0].shape), whole_spec(small.shape), small),
    ]
    in_specs = [pl.BlockSpec(memory_space=pltpu.SMEM)]
    out_specs, shapes, operands = [], [], [factor.reshape(1, 1)]
    for (spec, grad_spec, grad), group in zip(specs, groups):
        in_specs += [spec] * 3 + [grad_spec or spec]
        operands += [*group, grad]
        out_specs += [spec] * 3
        shapes += [jax.ShapeDtypeStruct(group[0].shape, jnp.float32)] * 3
    size = sum(group[0].size for group in groups)
    results = call(
        renew_kernel, "renew", (steps,), in_specs, out_specs, shapes, flops=8 * size, moved=26 * size
    )(*operands)
    return results[0::3], results[1::3], results[2::3]


def shards(
    token_ids,
    lengths,
    pair_ids,
    scores,
    word_table,
    pos_table,
    qkv_weight,
    out_weight,
    up_weight,
    down_weight,
    small_params,
    word_moment,
    pos_moment,
    qkv_moment,
    out_moment,
    up_moment,
    down_moment,
    small_moment,
    word_average,
    pos_average,
    qkv_average,
    out_average,
    up_average,
    down_average,
    small_average,
):
    batch, seq = token_ids.shape
    width = D
    fsdp = lax.axis_size("fsdp")
    tokens = batch * seq
    shard = qkv_weight.shape[0]
    pos_rows = pos_table.shape[0]
    small_cols = small_params.shape[1]
    pieces, pos_low = pack(qkv_weight, out_weight, up_weight, down_weight, pos_table)
    plan = Plan(
        lengths,
        token_ids,
        pieces,
        pos_low,
        small_params.astype(jnp.bfloat16),
        word_table,
    )
    first, second, small_full = plan.first, plan.second, plan.small
    x, h0, qkv, mixed, logs = plan.state
    r1, low_h1, act, slope, r2, pooled = feed(lengths, mixed, h0, first, second, small_full)
    loss, share = pair_grads(lengths, pooled[:, 0], pair_ids, scores)
    grad_r1, grad_mixed, sums_feed, feed_grads = feed_back(
        lengths, share, r1, r2, slope, first, second, small_full, act, low_h1, mixed
    )
    own_rows = word_table.shape[0]
    if plan.direct:
        grad_x, low_pos, qkv_grads, sums_back, depart, own = back(
            lengths, qkv, grad_mixed, logs, small_full, grad_r1, x, first, feed_grads
        )
        grad_small = sums_feed + sums_back
        small_cut = jnp.pad(
            grad_small.reshape(16, fsdp, small_cols).transpose(1, 0, 2),
            ((0, 0), (0, 0), (0, 128 - small_cols)),
        )
        table, sum_a, sum_b, small, squares = finish(
            grad_x,
            plan.asker_row,
            plan.held,
            feed_grads,
            qkv_grads,
            low_pos,
            small_cut,
            depart,
            own,
            own_rows,
            plan.cap,
        )
        small = small.reshape(16, 128)
        table, total = more_grads(grad_x, plan, table, squares[0, 0])
    else:
        grad_qkv, sums_attend = attend_back(lengths, qkv, grad_mixed, logs, seq)
        grad_x, grad_pos, sums_embed = embed_back(grad_r1, grad_qkv, first, x, small_full, seq)
        qkv_grads = qkv_weights(h0, grad_qkv)
        grad_small = sums_feed + sums_attend + sums_embed
        table, sum_a, sum_b, small, total = total_grads(
            plan.everyone,
            plan.rounds,
            grad_x,
            feed_grads,
            qkv_grads,
            grad_pos.astype(jnp.bfloat16),
            grad_small,
            own_rows,
        )
    norm = jnp.sqrt(total)
    limit = 1e-05 * math.sqrt((VOCAB + LEN + 4 * D + 2 * FF + 14) * D)
    factor = jnp.minimum(1.0, limit / (norm + 1e-06))
    weights = (word_table, pos_table, qkv_weight, out_weight, up_weight, down_weight, small_params)
    moments = (
        word_moment,
        pos_moment,
        qkv_moment,
        out_moment,
        up_moment,
        down_moment,
        small_moment,
    )
    averages = (
        word_average,
        pos_average,
        qkv_average,
        out_average,
        up_average,
        down_average,
        small_average,
    )
    if plan.direct:
        groups = list(zip(weights, moments, averages))
        new_w, new_m, new_a = renew_all(factor, groups, table, sum_a, sum_b, small)
    else:
        wide_b = sum_b.astype(jnp.float32)
        summed = (
            table.astype(jnp.float32),
            wide_b[:, 2 * shard :].reshape(pos_rows, width),
            jnp.concatenate([wide_b[0, :shard], wide_b[0, shard : 2 * shard], wide_b[1, :shard]], 1),
            wide_b[1, shard : 2 * shard],
            join_rows(sum_a[1][None], 4).astype(jnp.float32),
            sum_a[0].astype(jnp.float32),
            small[:14, :small_cols],
        )
        new_w = []
        new_m = []
        new_a = []
        for weight, moment, average, grad in zip(weights, moments, averages, summed):
            fresh, buffer, mean_new = renew(weight, moment, average, grad, factor)
            new_w.append(fresh)
            new_m.append(buffer)
            new_a.append(mean_new)
    return (
        loss[0, 0],
        norm,
        new_w[0],
        new_w[1],
        new_w[2],
        new_w[3],
        new_w[4],
        new_w[5],
        new_w[6],
        new_m[0],
        new_m[1],
        new_m[2],
        new_m[3],
        new_m[4],
        new_m[5],
        new_m[6],
        new_a[0],
        new_a[1],
        new_a[2],
        new_a[3],
        new_a[4],
        new_a[5],
        new_a[6],
    )


def solution(mesh):
    placed = (
        P(("dp", "fsdp"), None),
        P(("dp", "fsdp")),
        P(),
        P(),
        P("fsdp", None),
        P("fsdp", None),
        P("fsdp", None),
        P("fsdp", None),
        P("fsdp", None),
        P("fsdp", None),
        P(None, "fsdp"),
        P("fsdp", None),
        P("fsdp", None),
        P("fsdp", None),
        P("fsdp", None),
        P("fsdp", None),
        P("fsdp", None),
        P(None, "fsdp"),
        P("fsdp", None),
        P("fsdp", None),
        P("fsdp", None),
        P("fsdp", None),
        P("fsdp", None),
        P("fsdp", None),
        P(None, "fsdp"),
    )
    return jax.shard_map(
        shards,
        mesh=mesh,
        in_specs=placed,
        out_specs=(
            P(),
            P(),
            P("fsdp", None),
            P("fsdp", None),
            P("fsdp", None),
            P("fsdp", None),
            P("fsdp", None),
            P("fsdp", None),
            P(None, "fsdp"),
            P("fsdp", None),
            P("fsdp", None),
            P("fsdp", None),
            P("fsdp", None),
            P("fsdp", None),
            P("fsdp", None),
            P(None, "fsdp"),
            P("fsdp", None),
            P("fsdp", None),
            P("fsdp", None),
            P("fsdp", None),
            P("fsdp", None),
            P("fsdp", None),
            P(None, "fsdp"),
        ),
        check_vma=False,
    )
```
